32 devices in a mesh: comp: 4 (over y, x), lat: 4 (over z), lon: 2 (over core).
Axes of the slice: x: 2, y: 2, z: 4, core: 2. Of those that a mesh axis runs over, the one named last changes fastest.
Arguments:
- state: float32 [2048, 256, 128], P(('comp', 'lat'), 'lon'), may hold values from -6 to 6
- land_mask: int32 [2048, 256], P(('comp', 'lat'), 'lon'), may hold values 0 or 1
- intersection_list: int32 [2048, 2, 2, 3], P(('comp', 'lat'), 'lon'), may hold values from 0 to 127, as said below
- mix_atm: float32 [128, 128], replicated, may hold values from -0.5 to 0.5
- mix_ocn: float32 [128, 128], replicated, may hold values from -0.5 to 0.5
- flux_map: float32 [128, 8], replicated, may hold values from -0.5 to 0.5
- ocean_map: float32 [8, 128], replicated, may hold values from -2 to 2
- regrid_weights: bfloat16 [32, 128, 128], replicated, may hold values from -0.25 to 0.25
Outputs:
- state_out: float32 [2048, 256, 128], P(('comp', 'lat'), 'lon')
- surface_out: float32 [2048, 256], P(('comp', 'lat'), 'lon')
The draws below stay inside these ranges and needn't reach their ends.
Inputs may be any that keep to these rules, and one draw needn't show every extreme that they name: `intersection_list`: entry 0 is an ocean tile lat * 2 + lon, entry 1 a row of that tile below 128, entry 2 a weight block below 32. With t the tile lat * 2 + lon of the list's own rows and r = min(4, 2), the entries of one tile name exactly the 2 r tiles (t + a * 2 + b - (r - 1) // 2) mod (4 * 2) for a in 0, 1 and b in 0 to r - 1, each by exactly 64 entries.
All inputs are finite; a program needn't handle non-finite values. No bound on the sum of `land_mask` on one device may be relied on, other than what follows from the above.
Results may differ from the reference program's by a relative error of at most 0.0012.
Values may be sent and summed in bfloat16 or wider, within the bound.
No kernel may reach another device: no remote copies, remote signals or barrier semaphores. Data moves between devices by JAX's collectives and lax.ppermute only.
A program may use at most 192 MiB of HBM per device.

```python
import jax
import jax.numpy as jnp
from jax import lax

RT = 128
CT = 128
LEV = 128
NF = 8
NW = 32
NOV = 2
NR = 2048
NC = 256
N_COMP = 4
N_LAT = 4
N_LON = 2


def draw_intersection_list(key, part):
    device_total = N_COMP * N_LAT * N_LON
    tile_total = N_LAT * N_LON
    entry_total = NOV * RT
    reach = min(4, N_LON)
    capacity = entry_total // (2 * reach)
    order_key, target_key, weight_key = jax.random.split(jax.random.fold_in(key, 11), 3)
    orders = jax.vmap(lambda one_key: jax.random.permutation(one_key, entry_total))(jax.random.split(order_key, device_total))
    neighbour = orders.astype(jnp.int32) // capacity
    device_ids = jnp.arange(device_total, dtype=jnp.int32)
    tile_ids = device_ids % tile_total
    offsets = neighbour // reach * N_LON + neighbour % reach - (reach - 1) // 2
    owners = (tile_ids[:, None] + offsets + tile_total) % tile_total
    targets = jax.random.randint(target_key, (device_total, entry_total), 0, RT)
    weights = jax.random.randint(weight_key, (device_total, entry_total), 0, NW)
    table = jnp.stack([owners, targets, weights], axis=-1).astype(jnp.int32)
    table = table.reshape(N_COMP, N_LAT, N_LON, RT, NOV, 3).transpose(0, 1, 3, 2, 4, 5)
    return table.reshape(N_COMP * N_LAT * RT, N_LON, NOV, 3)


def set_ends(result, stream_key, low, largest):
    extent = result.shape
    spot = [jax.random.randint(jax.random.fold_in(stream_key, axis), (), 0, extent[axis]) for axis in range(len(extent))]
    result = result.at[tuple(spot)].set(low)
    longest = extent.index(max(extent))
    spot[longest] = (spot[longest] + 1) % extent[longest]
    return result.at[tuple(spot)].set(largest)


def steps_of(key, extent, shards, low, largest):
    def one(axis_at, parts):
        draws = jax.random.uniform(jax.random.fold_in(jax.random.fold_in(key, 6), axis_at), (parts,), jnp.float32, low / len(shards), largest / len(shards))
        return jnp.repeat(jnp.exp(draws), extent[axis_at] // parts).reshape((-1,) + (1,) * (len(extent) - axis_at - 1))

    gain = one(*shards[0])
    for cut in shards[1:]:
        gain = gain * one(*cut)
    return gain


def normal_values(stream_key, dims, scale, most, cuts=(), kind=jnp.bfloat16):
    values = scale * jax.random.normal(stream_key, dims, jnp.float32)
    if cuts:
        values = values * steps_of(stream_key, dims, cuts, -0.22, 0.18)
    return jnp.clip(values, -most, most).astype(kind)


def setup_inputs(seed: int = 0) -> dict:
    keys = jax.random.split(jax.random.key(seed), 9)
    return {
        "state": normal_values(keys[0], (NR, NC, LEV), 1.0, 6.0, ((0, 16), (1, 2)), jnp.float32),
        "land_mask": set_ends((jax.random.randint(keys[1], (NR, NC), 0, 10) < 7).astype(jnp.int32), jax.random.fold_in(keys[1], 1), 0, 1),
        "intersection_list": draw_intersection_list(jax.random.fold_in(keys[8], 71), 0),
        "mix_atm": normal_values(keys[3], (LEV, LEV), LEV ** -0.5, 0.5, (), jnp.float32),
        "mix_ocn": normal_values(keys[4], (LEV, LEV), LEV ** -0.5, 0.5, (), jnp.float32),
        "flux_map": normal_values(keys[5], (LEV, NF), LEV ** -0.5, 0.5, (), jnp.float32),
        "ocean_map": normal_values(keys[6], (NF, LEV), NF ** -0.5, 2.0, (), jnp.float32),
        "regrid_weights": normal_values(keys[7], (NW, CT, CT), (4 * CT) ** -0.5, 0.25),
    }


SMOOTHING = 0.2
PHYSICS = 0.5
HIGHEST = lax.Precision.HIGHEST


def laplace(values):
    padded = jnp.pad(values, ((1, 1), (0, 0), (0, 0)))
    left_side = jnp.roll(values, 1, axis=1)
    right_side = jnp.roll(values, -1, axis=1)
    return padded[:-2] + padded[2:] + left_side + right_side - 4.0 * values


def column_physics(values, mixing):
    return jnp.tanh(jnp.einsum('rck,kj->rcj', values, mixing, precision=HIGHEST))


def reference(state, land_mask, intersection_list, mix_atm, mix_ocn, flux_map, ocean_map, regrid_weights):
    atm_rows = (N_COMP - 1) * N_LAT * RT
    tile_total = N_LAT * N_LON
    atmosphere = state[:atm_rows]
    ocean = state[atm_rows:]
    sea_atm = land_mask[:atm_rows] == 1
    sea_ocn = land_mask[atm_rows:] == 1
    flux_total = jnp.zeros((NF, atm_rows, N_LON * CT), jnp.float32)
    for substep in range(2):
        smooth = atmosphere + SMOOTHING * laplace(atmosphere)
        atmosphere = smooth + PHYSICS * column_physics(smooth, mix_atm)
        flux_total = flux_total + jnp.einsum('rck,kf->frc', atmosphere, flux_map, precision=HIGHEST)
    flux_sent = jnp.where(sea_atm[None], 0.5 * flux_total, 0.0).astype(jnp.bfloat16)
    blocks = flux_sent.astype(jnp.float32).reshape(NF, atm_rows, N_LON, CT).transpose(1, 2, 0, 3)
    lists = intersection_list[:atm_rows]
    owners = lists[..., 0].astype(jnp.int32)
    targets = lists[..., 1].astype(jnp.int32)
    weight_ids = lists[..., 2].astype(jnp.int32)
    segment = (weight_ids * tile_total + owners) * RT + targets
    entries = jnp.broadcast_to(blocks[:, :, None], (atm_rows, N_LON, NOV, NF, CT)).reshape(-1, NF * CT)
    binned = jax.ops.segment_sum(entries, segment.reshape(-1), num_segments=NW * tile_total * RT)
    binned = binned.reshape(NW, tile_total * RT, NF, CT)
    weights_wide = regrid_weights.astype(jnp.float32)

    def add_block(total, pair):
        part, weight = pair
        return total + jnp.einsum('qfa,ab->qfb', part, weight, precision=HIGHEST), None

    regridded, _ = lax.scan(add_block, jnp.zeros((tile_total * RT, NF, CT), jnp.float32), (binned, weights_wide))
    forcing = regridded.reshape(N_LAT, N_LON, RT, NF, CT).transpose(3, 0, 2, 1, 4).reshape(NF, N_LAT * RT, N_LON * CT)
    smooth = ocean + SMOOTHING * laplace(ocean)
    moved = smooth + jnp.einsum('frc,fk->rck', forcing, ocean_map, precision=HIGHEST) + PHYSICS * column_physics(smooth, mix_ocn)
    ocean_new = jnp.where(sea_ocn[..., None], moved, ocean)
    surface_ocean = ocean_new[..., 0]
    surface_blocks = surface_ocean.reshape(N_LAT, RT, N_LON, CT).transpose(0, 2, 1, 3).reshape(tile_total * RT, CT)
    picked = jnp.take(surface_blocks, (owners * RT + targets).reshape(-1), axis=0).reshape(-1, NOV, CT)
    flat_ids = weight_ids.reshape(-1, NOV)

    def pull(total, pair):
        index, weight = pair
        term = jnp.einsum('enb,ab->ena', picked, weight, precision=HIGHEST)
        return total + jnp.where((flat_ids == index)[..., None], term, 0.0), None

    pulled, _ = lax.scan(pull, jnp.zeros(picked.shape, jnp.float32), (jnp.arange(NW, dtype=jnp.int32), weights_wide))
    returned = pulled.sum(axis=1).reshape(atm_rows, N_LON * CT)
    surface_atm = jnp.where(sea_atm, returned, atmosphere[..., 0])
    state_out = jnp.concatenate([atmosphere, ocean_new], axis=0)
    surface_out = jnp.concatenate([surface_atm, surface_ocean], axis=0)
    return state_out, surface_out
```

```python
import functools

import jax
import jax.numpy as jnp
from jax import lax
from jax.experimental import pallas as pl
from jax.experimental.pallas import tpu as pltpu
from jax.sharding import PartitionSpec as P

SMOOTHING = 0.2
PHYSICS = 0.5
MIB = 1024 * 1024
F32 = jnp.float32
BF16 = jnp.bfloat16
EDGE = 8
CHUNK = 8
AXES = ("comp", "lat", "lon")


def split_two(x):
    high = x.astype(BF16)
    low = (x - high.astype(F32)).astype(BF16)
    return high, low


def side_by_side(x):
    return jnp.concatenate(split_two(x), axis=1)


def dot_nt(a, b):
    return lax.dot_general(a, b, (((1,), (1,)), ((), ())), preferred_element_type=F32)


def dot_nn(a, b):
    return jnp.dot(a, b, preferred_element_type=F32)


def edges_kernel(
    state, first_rows, last_rows, first_cols, last_cols, top_corners, low_corners, left, right, sems
):
    rows, cols, _ = state.shape
    copies = [
        pltpu.make_async_copy(state.at[:, pl.ds(0, EDGE)], left, sems.at[0]),
        pltpu.make_async_copy(state.at[:, pl.ds(cols - EDGE, EDGE)], right, sems.at[1]),
        pltpu.make_async_copy(state.at[pl.ds(0, 2)], first_rows, sems.at[2]),
        pltpu.make_async_copy(state.at[pl.ds(rows - 2, 2)], last_rows, sems.at[3]),
    ]
    for copy in copies:
        copy.start()
    for copy in copies:
        copy.wait()
    for i in range(2):
        first_cols[i] = left[:, i, :]
        last_cols[i] = right[:, EDGE - 2 + i, :]
    top_corners[...] = jnp.zeros(top_corners.shape, F32)
    low_corners[...] = jnp.zeros(low_corners.shape, F32)
    top_corners[0:1] = left[0, 0:1]
    top_corners[1:2] = right[0, EDGE - 1 :]
    low_corners[0:1] = left[rows - 1, 0:1]
    low_corners[1:2] = right[rows - 1, EDGE - 1 :]


def take_edges(state):
    rows, cols, levels = state.shape
    slab = jax.ShapeDtypeStruct((2, cols, levels), F32)
    side = jax.ShapeDtypeStruct((2, rows, levels), F32)
    corner = jax.ShapeDtypeStruct((EDGE, levels), F32)
    vmem = pl.BlockSpec(memory_space=pltpu.VMEM)
    return pl.pallas_call(
        edges_kernel,
        out_shape=(slab, slab, side, side, corner, corner),
        in_specs=[pl.BlockSpec(memory_space=pl.ANY)],
        out_specs=(vmem,) * 6,
        scratch_shapes=[
            pltpu.VMEM((rows, EDGE, levels), F32),
            pltpu.VMEM((rows, EDGE, levels), F32),
            pltpu.SemaphoreType.DMA((4,)),
        ],
        compiler_params=pltpu.CompilerParams(vmem_limit_bytes=16 * MIB),
        name="edges",
    )(state)


def advance_kernel(neighbours, capacity, *refs):
    (flags, sources, state, up_rows, low_rows, left_cols, right_cols, own_first, own_last) = refs[:9]
    (up_left, up_right, low_left, low_right, mask, mix_atm, mix_ocn, flux_map) = refs[9:17]
    out = refs[17]
    packed = refs[18 : 18 + neighbours]
    (values, moved, halo, halo_moved, smooth, pairs, mixed, weights, flux_weights, fluxes, staged) = refs[
        18 + neighbours : 29 + neighbours
    ]
    in_sems, out_sems = refs[29 + neighbours :]
    rows, cols, levels = state.shape
    chunks = rows // CHUNK
    inner = pl.ds(EDGE, cols)
    flux_count = flux_map.shape[0]

    def fetch(q):
        return pltpu.make_async_copy(
            state.at[pl.ds(q * CHUNK, CHUNK)],
            values.at[pl.ds(q * CHUNK + 2, CHUNK), inner],
            in_sems.at[q],
        )

    def put(q, slot):
        return pltpu.make_async_copy(
            staged.at[slot], out.at[pl.ds(q * CHUNK, CHUNK)], out_sems.at[slot]
        )

    def begin(q, _):
        fetch(q).start()
        return 0

    lax.fori_loop(0, chunks, begin, 0)
    ocean = flags[0] == 1
    mix = jnp.where(ocean, mix_ocn[...], mix_atm[...])
    mix_high, mix_low = split_two(mix)
    weights[:levels, :levels] = mix_high
    weights[levels:, :levels] = mix_high
    weights[:levels, levels:] = mix_low
    weights[levels:, levels:] = mix_low
    map_high, map_low = split_two(flux_map[...])
    flux_weights[...] = jnp.concatenate(
        [
            jnp.concatenate([map_high.astype(F32), map_high.astype(F32)], axis=1),
            jnp.concatenate([map_low.astype(F32), map_low.astype(F32)], axis=1),
        ],
        axis=0,
    ).astype(BF16)
    values[0:2, EDGE : EDGE + cols, :] = up_rows[...]
    values[rows + 2 : rows + 4, EDGE : EDGE + cols, :] = low_rows[...]
    values[1, EDGE - 1 : EDGE, :] = up_left[1:2]
    values[1, EDGE + cols : EDGE + cols + 1, :] = up_right[0:1]
    values[rows + 2, EDGE - 1 : EDGE, :] = low_left[1:2]
    values[rows + 2, EDGE + cols : EDGE + cols + 1, :] = low_right[0:1]

    def side_cells(r, _):
        values[r + 2, EDGE - 1 : EDGE, :] = left_cols[1, pl.ds(r, 1), :]
        values[r + 2, EDGE + cols : EDGE + cols + 1, :] = right_cols[0, pl.ds(r, 1), :]
        return 0

    lax.fori_loop(0, rows, side_cells, 0, unroll=8)

    def stage(row, total):
        line = SMOOTHING * total
        smooth[row] = line
        pairs[row * cols : (row + 1) * cols, :] = side_by_side(line)

    def mix_rows(count):
        mixed[: count * cols, :] = dot_nn(pairs[: count * cols, :], weights[...])

    def finish(row):
        part = mixed[row * cols : (row + 1) * cols, :]
        return smooth[row] + PHYSICS * jnp.tanh(part[:, :levels] + part[:, levels:])

    def gather_row(ref, i):
        here = ref[i, EDGE : EDGE + cols, :] + (
            ref[i - 1, EDGE : EDGE + cols, :] + ref[i + 1, EDGE : EDGE + cols, :]
        )
        return here + (
            ref[i, EDGE - 1 : EDGE - 1 + cols, :] + ref[i, EDGE + 1 : EDGE + 1 + cols, :]
        )

    @pl.when(jnp.logical_not(ocean))
    def atmosphere():
        halo[0, EDGE : EDGE + rows, :] = left_cols[1]
        halo[0, EDGE - 1 : EDGE, :] = up_left[1:2]
        halo[0, EDGE + rows : EDGE + rows + 1, :] = low_left[1:2]
        halo[1, EDGE : EDGE + rows, :] = right_cols[0]
        halo[1, EDGE - 1 : EDGE, :] = up_right[0:1]
        halo[1, EDGE + rows : EDGE + rows + 1, :] = low_right[0:1]
        beyond = (left_cols.at[0], right_cols.at[1])
        within = (own_first.at[0], own_last.at[1])
        for s in range(2):
            total = (
                halo[s, EDGE : EDGE + rows, :]
                + halo[s, EDGE - 1 : EDGE - 1 + rows, :]
                + halo[s, EDGE + 1 : EDGE + 1 + rows, :]
            )
            stage(s, total + (beyond[s][...] + within[s][...]))
        mix_rows(2)
        for s in range(2):
            halo_moved[s] = finish(s)

        def moved_sides(r, _):
            moved[r + 1, EDGE - 1 : EDGE, :] = halo_moved[0, pl.ds(r, 1), :]
            moved[r + 1, EDGE + cols : EDGE + cols + 1, :] = halo_moved[1, pl.ds(r, 1), :]
            return 0

        lax.fori_loop(0, rows, moved_sides, 0, unroll=8)
        fetch(0).wait()
        for row in range(2):
            stage(row, gather_row(values, row + 1))
        mix_rows(2)
        moved[0, EDGE : EDGE + cols, :] = finish(0)
        moved[1, EDGE : EDGE + cols, :] = finish(1)

        @pl.when(flags[1] == 0)
        def _():
            moved[0, EDGE : EDGE + cols, :] = jnp.zeros((cols, levels), F32)


        def one_chunk(q, _):
            base = q * CHUNK

            @pl.when(q + 1 < chunks)
            def _():
                fetch(q + 1).wait()

            for row in range(CHUNK):
                stage(row, gather_row(values, base + row + 3))
            mix_rows(CHUNK)
            for row in range(CHUNK):
                moved[base + row + 2, EDGE : EDGE + cols, :] = finish(row)

            @pl.when((q + 1 == chunks) & (flags[2] == 0))
            def _():
                moved[rows + 1, EDGE : EDGE + cols, :] = jnp.zeros((cols, levels), F32)

            for row in range(CHUNK):
                stage(row, gather_row(moved, base + row + 1))
            mix_rows(CHUNK)
            slot = q % 2

            @pl.when(q >= 2)
            def _():
                put(q - 2, slot).wait()

            for row in range(CHUNK):
                line = finish(row)
                staged[slot, row] = line
                both = line + moved[base + row + 1, EDGE : EDGE + cols, :]
                pairs[row * cols : (row + 1) * cols, :] = side_by_side(both)
            put(q, slot).start()
            flux = dot_nt(flux_weights[...], pairs[...])
            flux = flux[:flux_count] + flux[flux_count:]
            for row in range(CHUNK):
                block = PHYSICS * flux[:, row * cols : (row + 1) * cols]
                sea = jnp.broadcast_to(mask[pl.ds(base + row, 1), :], block.shape)
                block = jnp.where(sea > 0.5, block, 0.0)
                fluxes[base + row] = block.astype(BF16).astype(F32)
            return 0

        lax.fori_loop(0, chunks, one_chunk, 0)
        put(chunks - 2, (chunks - 2) % 2).wait()
        put(chunks - 1, (chunks - 1) % 2).wait()
        for n in range(neighbours):

            def pack(i, _, n=n):
                first = fluxes[sources[n * capacity + 2 * i]]
                second = fluxes[sources[n * capacity + 2 * i + 1]]
                packed[n][i] = jnp.concatenate([first, second], axis=0).astype(BF16)
                return 0

            lax.fori_loop(0, capacity // 2, pack, 0, unroll=8)

    @pl.when(ocean)
    def sea_side():
        fetch(0).wait()
        lanes = lax.broadcasted_iota(jnp.int32, (CHUNK, CHUNK * levels), 1) // levels
        lines = lax.broadcasted_iota(jnp.int32, (CHUNK, CHUNK * levels), 0)
        spreader = jnp.where(lanes == lines, 1.0, 0.0).astype(F32)

        def one_chunk(q, _):
            base = q * CHUNK

            @pl.when(q + 1 < chunks)
            def _():
                fetch(q + 1).wait()

            for row in range(CHUNK):
                stage(row, gather_row(values, base + row + 2))
            mix_rows(CHUNK)
            slot = q % 2

            @pl.when(q >= 2)
            def _():
                put(q - 2, slot).wait()

            sea = dot_nn(mask[pl.ds(pl.multiple_of(base, CHUNK), CHUNK), :].T, spreader)
            for row in range(CHUNK):
                chosen = sea[:, row * levels : (row + 1) * levels] > 0.5
                before = values[base + row + 2, EDGE : EDGE + cols, :]
                staged[slot, row] = jnp.where(chosen, finish(row), before)
            put(q, slot).start()
            return 0

        lax.fori_loop(0, chunks, one_chunk, 0)
        put(chunks - 2, (chunks - 2) % 2).wait()
        put(chunks - 1, (chunks - 1) % 2).wait()


def advance(flags, sources, state, halos, mask, mix_atm, mix_ocn, flux_map_t, neighbours, capacity):
    rows, cols, levels = state.shape
    fluxes = flux_map_t.shape[0]
    vmem = pl.BlockSpec(memory_space=pltpu.VMEM)
    smem = pl.BlockSpec(memory_space=pltpu.SMEM)
    hbm = pl.BlockSpec(memory_space=pl.ANY)
    entry = jax.ShapeDtypeStruct((capacity // 2, 2 * fluxes, cols), BF16)
    cells = rows * cols
    return pl.pallas_call(
        functools.partial(advance_kernel, neighbours, capacity),
        out_shape=(jax.ShapeDtypeStruct(state.shape, F32),) + (entry,) * neighbours,
        in_specs=[smem, smem, hbm] + [vmem] * (len(halos) + 4),
        out_specs=(hbm,) + (vmem,) * neighbours,
        scratch_shapes=[
            pltpu.VMEM((rows + 4, cols + 2 * EDGE, levels), F32),
            pltpu.VMEM((rows + 2, cols + 2 * EDGE, levels), F32),
            pltpu.VMEM((2, rows + 2 * EDGE, levels), F32),
            pltpu.VMEM((2, rows, levels), F32),
            pltpu.VMEM((CHUNK, cols, levels), F32),
            pltpu.VMEM((CHUNK * cols, 2 * levels), BF16),
            pltpu.VMEM((CHUNK * cols, 2 * levels), F32),
            pltpu.VMEM((2 * levels, 2 * levels), BF16),
            pltpu.VMEM((2 * fluxes, 2 * levels), BF16),
            pltpu.VMEM((rows, fluxes, cols), F32),
            pltpu.VMEM((2, CHUNK, cols, levels), F32),
            pltpu.SemaphoreType.DMA((rows // CHUNK,)),
            pltpu.SemaphoreType.DMA((2,)),
        ],
        compiler_params=pltpu.CompilerParams(vmem_limit_bytes=48 * MIB),
        cost_estimate=pl.CostEstimate(
            flops=8 * cells * levels * levels, bytes_accessed=8 * cells * levels, transcendentals=0
        ),
        name="advance",
    )(flags, sources, state, *halos, mask, mix_atm, mix_ocn, flux_map_t)


def regrid_kernel(groups, capacity, *refs):
    flags, labels = refs[:2]
    entries = refs[2 : 2 + groups]
    target_column, weights, surface, mask, ocean_first = refs[2 + groups : 7 + groups]
    forcing, new_surface = refs[7 + groups : 9 + groups]
    picked = refs[9 + groups : 9 + 2 * groups]
    (bins,) = refs[9 + 2 * groups :]
    rows, flux_count, cols = forcing.shape
    weight_count = weights.shape[0]

    @pl.when(flags[0] == 1)
    def ocean():
        def clear(i, _):
            bins[pl.ds(i * 32, 32)] = jnp.zeros((32, flux_count, cols), F32)
            return 0

        lax.fori_loop(0, weight_count * rows // 32, clear, 0)
        for j in range(groups):

            def add(i, _, j=j):
                pair = entries[j][i].astype(F32)
                bins[labels[j * capacity + 2 * i]] += pair[:flux_count]
                bins[labels[j * capacity + 2 * i + 1]] += pair[flux_count:]
                return 0

            lax.fori_loop(0, capacity // 2, add, 0, unroll=8)

        def products(w):
            block = bins[pl.ds(w * rows, rows)].reshape(rows * flux_count, cols)
            once = weights[w]
            return dot_nn(side_by_side(block), jnp.concatenate([once, once], axis=0))

        forcing[...] = products(0).reshape(forcing.shape)

        def accumulate(w, _):
            forcing[...] += products(w).reshape(forcing.shape)
            return 0

        lax.fori_loop(1, weight_count, accumulate, 0)
        change = jnp.sum(forcing[...] * ocean_first[...][None], axis=1)
        now = surface[...] + jnp.where(mask[...] > 0.5, change, 0.0)
        new_surface[...] = now
        now_pair = jnp.concatenate(split_two(now), axis=0)
        spots = lax.broadcasted_iota(jnp.int32, (capacity, rows), 1)
        for j in range(groups):
            chosen = target_column[j * capacity : (j + 1) * capacity, :] == spots
            chosen = jnp.where(chosen, 1.0, 0.0).astype(BF16)
            picked[j][...] = dot_nn(jnp.concatenate([chosen, chosen], axis=1), now_pair)


def regrid(flags, labels, entries, target_column, weights, surface, mask, ocean_first, capacity):
    groups = len(entries)
    rows, cols = mask.shape
    flux_count = ocean_first.shape[0]
    weight_count = weights.shape[0]
    vmem = pl.BlockSpec(memory_space=pltpu.VMEM)
    smem = pl.BlockSpec(memory_space=pltpu.SMEM)
    return pl.pallas_call(
        functools.partial(regrid_kernel, groups, capacity),
        out_shape=(
            jax.ShapeDtypeStruct((rows, flux_count, cols), F32),
            jax.ShapeDtypeStruct((rows, cols), F32),
        )
        + (jax.ShapeDtypeStruct((capacity, cols), F32),) * groups,
        in_specs=[smem, smem] + [vmem] * (groups + 5),
        out_specs=(vmem,) * (2 + groups),
        scratch_shapes=[pltpu.VMEM((weight_count * rows, flux_count, cols), F32)],
        compiler_params=pltpu.CompilerParams(vmem_limit_bytes=40 * MIB),
        cost_estimate=pl.CostEstimate(
            flops=4 * weight_count * rows * flux_count * cols * cols,
            bytes_accessed=8 * MIB,
            transcendentals=0,
        ),
        name="regrid",
    )(flags, labels, *entries, target_column, weights, surface, mask, ocean_first)


LINES = 16


def update_kernel(flags, state, forcing, mask, ocean_map, out, held, table, wide, in_sems, out_sems):
    rows, cols, levels = state.shape
    flux_count = forcing.shape[1]
    chunks = rows // LINES
    depth = LINES * flux_count

    def fetch(q):
        return pltpu.make_async_copy(
            state.at[pl.ds(q * LINES, LINES)], held.at[pl.ds(q * LINES, LINES)], in_sems.at[q]
        )

    def put(q):
        return pltpu.make_async_copy(
            held.at[pl.ds(q * LINES, LINES)], out.at[pl.ds(q * LINES, LINES)], out_sems.at[q]
        )

    @pl.when(flags[0] == 1)
    def ocean():
        for q in range(chunks):
            fetch(q).start()
        table[...] = jnp.zeros(table.shape, F32)
        for line in range(LINES):
            table[
                line * flux_count : (line + 1) * flux_count, line * levels : (line + 1) * levels
            ] = ocean_map[...]
        high, low = split_two(table[...])
        wide[:depth] = high
        wide[depth : 2 * depth] = high
        wide[2 * depth :] = low

        def one(q, _):
            start = pl.multiple_of(q * LINES, LINES)
            sea = mask[pl.ds(start, LINES), :]
            part = jnp.where(sea[:, None, :] > 0.5, forcing[pl.ds(start, LINES)], 0.0)
            turned = part.reshape(depth, cols).T
            first, second = split_two(turned)
            change = dot_nn(jnp.concatenate([first, second, first], axis=1), wide[...])
            fetch(q).wait()
            for line in range(LINES):
                held[start + line] += change[:, line * levels : (line + 1) * levels]
            put(q).start()
            return 0

        lax.fori_loop(0, chunks, one, 0)
        for q in range(chunks):
            put(q).wait()


def update(flags, state, forcing, mask, ocean_map):
    rows, cols, levels = state.shape
    depth = LINES * forcing.shape[1]
    vmem = pl.BlockSpec(memory_space=pltpu.VMEM)
    smem = pl.BlockSpec(memory_space=pltpu.SMEM)
    hbm = pl.BlockSpec(memory_space=pl.ANY)
    return pl.pallas_call(
        update_kernel,
        out_shape=jax.ShapeDtypeStruct(state.shape, F32),
        in_specs=[smem, hbm, vmem, vmem, vmem],
        out_specs=hbm,
        input_output_aliases={1: 0},
        scratch_shapes=[
            pltpu.VMEM(state.shape, F32),
            pltpu.VMEM((depth, LINES * levels), F32),
            pltpu.VMEM((3 * depth, LINES * levels), BF16),
            pltpu.SemaphoreType.DMA((rows // LINES,)),
            pltpu.SemaphoreType.DMA((rows // LINES,)),
        ],
        compiler_params=pltpu.CompilerParams(vmem_limit_bytes=24 * MIB),
        cost_estimate=pl.CostEstimate(
            flops=6 * rows * cols * depth * levels,
            bytes_accessed=8 * rows * cols * levels,
            transcendentals=0,
        ),
        name="update",
    )(flags, state, forcing, mask, ocean_map)


def returned_kernel(groups, flags, *refs):
    picked = refs[:groups]
    weight_column, row_line, weights, mask, surface, new_surface, out, total = refs[groups:]
    rows, cols = mask.shape
    weight_count = weights.shape[0]

    @pl.when(flags[0] == 1)
    def ocean():
        out[...] = new_surface[...]

    @pl.when(flags[0] == 0)
    def atmosphere():
        values = jnp.concatenate([p[...] for p in picked], axis=0)
        pair = side_by_side(values)
        which = jnp.broadcast_to(weight_column[...], values.shape)
        total[...] = jnp.zeros(values.shape, F32)

        def one(i, _):
            both = jnp.concatenate([weights[2 * i], weights[2 * i + 1]], axis=0)
            images = dot_nt(pair, jnp.concatenate([both, both], axis=1))
            total[...] += jnp.where(which == 2 * i, images[:, :cols], 0.0) + jnp.where(
                which == 2 * i + 1, images[:, cols:], 0.0
            )
            return 0

        lax.fori_loop(0, weight_count // 2, one, 0, unroll=2)
        spots = lax.broadcasted_iota(jnp.int32, (rows, values.shape[0]), 0)
        chosen = jnp.where(jnp.broadcast_to(row_line[...], spots.shape) == spots, 1.0, 0.0).astype(BF16)
        high, low = split_two(total[...])
        back = dot_nn(chosen, high) + dot_nn(chosen, low)
        out[...] = jnp.where(mask[...] > 0.5, back, surface[...])


def returned(flags, picked, weight_column, row_line, weights, mask, surface, new_surface):
    rows, cols = mask.shape
    entry_total = weight_column.shape[0]
    vmem = pl.BlockSpec(memory_space=pltpu.VMEM)
    smem = pl.BlockSpec(memory_space=pltpu.SMEM)
    return pl.pallas_call(
        functools.partial(returned_kernel, len(picked)),
        out_shape=jax.ShapeDtypeStruct((rows, cols), F32),
        in_specs=[smem] + [vmem] * (len(picked) + 6),
        out_specs=vmem,
        scratch_shapes=[pltpu.VMEM((entry_total, cols), F32)],
        compiler_params=pltpu.CompilerParams(vmem_limit_bytes=16 * MIB),
        name="returned",
    )(flags, *picked, weight_column, row_line, weights, mask, surface, new_surface)


def local(
    state, land_mask, intersection_list, mix_atm, mix_ocn, flux_map, ocean_map, regrid_weights
):
    rows, cols, levels = state.shape
    intersections = intersection_list.shape[2]
    comp_count = lax.axis_size("comp")
    lat_count = lax.axis_size("lat")
    lon_count = lax.axis_size("lon")
    tile_count = lat_count * lon_count
    reach = min(4, lon_count)
    neighbours = 2 * reach
    entry_total = intersections * rows
    capacity = entry_total // neighbours
    comp_index = lax.axis_index("comp")
    lat_index = lax.axis_index("lat")
    tile_index = lat_index * lon_count + lax.axis_index("lon")
    bands = comp_count * lat_count
    ocean_band = (comp_count - 1) * lat_count
    ocean_comp = comp_count - 1
    band = comp_index * lat_count + lat_index
    is_ocean = comp_index == ocean_comp
    upper_valid = (band > 0) & (band != ocean_band)
    lower_valid = (band < bands - 1) & (band != ocean_band - 1)
    flags = jnp.stack([is_ocean, upper_valid, lower_valid]).astype(jnp.int32)
    mask = (land_mask == 1).astype(F32)

    def band_shift(value, by, lon_by):
        pairs = []
        for b in range(bands):
            target = b + by
            if 0 <= target < bands and (b >= ocean_band) == (target >= ocean_band):
                for lon in range(lon_count):
                    pairs.append(
                        (b * lon_count + lon, target * lon_count + (lon + lon_by) % lon_count)
                    )
        return lax.ppermute(value, AXES, pairs)

    first_rows, last_rows, first_cols, last_cols, top_corners, low_corners = take_edges(state)
    up_rows = band_shift(last_rows, 1, 0)
    low_rows = band_shift(first_rows, -1, 0)
    left_cols = band_shift(last_cols, 0, 1)
    right_cols = band_shift(first_cols, 0, -1)
    up_left = band_shift(low_corners, 1, 1)
    low_left = band_shift(top_corners, -1, 1)
    if lon_count == 2:
        up_right, low_right = up_left, low_left
    else:
        up_right = band_shift(low_corners, 1, -1)
        low_right = band_shift(top_corners, -1, -1)

    entry_list = intersection_list.reshape(entry_total, 3)
    owners = entry_list[:, 0]
    labels = entry_list[:, 2] * rows + entry_list[:, 1]
    offsets = [
        (n // reach * lon_count + n % reach - (reach - 1) // 2) % tile_count
        for n in range(neighbours)
    ]
    distance = (owners - tile_index + tile_count) % tile_count
    hits = distance[:, None] == jnp.array(offsets, jnp.int32)[None, :]
    neighbour_ids = jnp.sum(
        jnp.where(hits, jnp.arange(neighbours, dtype=jnp.int32)[None, :], 0), axis=1
    )
    positions = jnp.arange(entry_total, dtype=jnp.int32)
    earlier = (neighbour_ids[None, :] == neighbour_ids[:, None]) & (
        positions[None, :] < positions[:, None]
    )
    slots = neighbour_ids * capacity + jnp.sum(earlier.astype(jnp.int32), axis=1)
    placing = positions[:, None] == slots[None, :]
    sources = jnp.sum(jnp.where(placing, (positions // intersections)[None, :], 0), axis=1)
    packed_labels = jnp.sum(jnp.where(placing, labels[None, :], 0), axis=1)

    def to_ocean(value, comp, offset):
        pairs = [
            (comp * tile_count + t, ocean_comp * tile_count + (t + offset) % tile_count)
            for t in range(tile_count)
        ]
        return lax.ppermute(value, AXES, pairs)

    def from_ocean(value, comp, offset):
        pairs = [
            (ocean_comp * tile_count + (t + offset) % tile_count, comp * tile_count + t)
            for t in range(tile_count)
        ]
        return lax.ppermute(value, AXES, pairs)

    order = [(c, n) for n in range(neighbours) for c in range(comp_count - 1)]
    arrived_labels = jnp.concatenate(
        [
            to_ocean(packed_labels[n * capacity : (n + 1) * capacity], c, offsets[n])
            for c, n in order
        ]
    )
    target_column = (arrived_labels % rows)[:, None]

    halos = (up_rows, low_rows, left_cols, right_cols, first_cols, last_cols)
    halos = halos + (up_left, up_right, low_left, low_right)
    moved = advance(
        flags, sources, state, halos, mask, mix_atm, mix_ocn, flux_map.T, neighbours, capacity
    )
    moved, packed = moved[0], moved[1:]
    entries = [to_ocean(packed[n], c, offsets[n]) for c, n in order]
    surface = moved[:, :, 0]
    ocean_first = jnp.broadcast_to(ocean_map[:, :1], (ocean_map.shape[0], cols))
    regridded = regrid(
        flags, arrived_labels, entries, target_column, regrid_weights, surface, mask,
        ocean_first, capacity,
    )
    forcing, new_surface, picked = regridded[0], regridded[1], regridded[2:]
    arrived = [None] * neighbours
    for (c, n), value in zip(order, picked):
        one = from_ocean(value, c, offsets[n])
        arrived[n] = one if arrived[n] is None else jnp.where(comp_index == c, one, arrived[n])
    final_state = update(flags, moved, forcing, mask, ocean_map)
    weight_column = (packed_labels // rows)[:, None]
    surface_out = returned(
        flags, arrived, weight_column, sources[None, :], regrid_weights, mask, surface, new_surface
    )
    return (final_state, surface_out)


def solution(mesh):
    placed = (
        P(("comp", "lat"), "lon", None),
        P(("comp", "lat"), "lon"),
        P(("comp", "lat"), "lon", None, None),
        P(),
        P(),
        P(),
        P(),
        P(),
    )
    return jax.shard_map(
        local,
        mesh=mesh,
        in_specs=placed,
        out_specs=(P(("comp", "lat"), "lon", None), P(("comp", "lat"), "lon")),
        check_vma=False,
    )
```

```python
import functools

import jax
import jax.numpy as jnp
from jax import lax
from jax.experimental import pallas as pl
from jax.experimental.pallas import tpu as pltpu
from jax.sharding import PartitionSpec as P

SMOOTHING = 0.2
PHYSICS = 0.5
MIB = 1024 * 1024
F32 = jnp.float32
BF16 = jnp.bfloat16
EDGE = 8
CHUNK = 8
AXES = ("comp", "lat", "lon")


def split_two(x):
    high = x.astype(BF16)
    low = (x - high.astype(F32)).astype(BF16)
    return high, low


def side_by_side(x):
    return jnp.concatenate(split_two(x), axis=1)


def dot_nt(a, b):
    return lax.dot_general(a, b, (((1,), (1,)), ((), ())), preferred_element_type=F32)


def dot_nn(a, b):
    return jnp.dot(a, b, preferred_element_type=F32)


def edges_kernel(state, first_rows, last_rows, sides, top_corners, low_corners, left, right, sems):
    rows, cols, _ = state.shape
    copies = [
        pltpu.make_async_copy(state.at[:, pl.ds(0, EDGE)], left, sems.at[0]),
        pltpu.make_async_copy(state.at[:, pl.ds(cols - EDGE, EDGE)], right, sems.at[1]),
        pltpu.make_async_copy(state.at[pl.ds(0, 2)], first_rows, sems.at[2]),
        pltpu.make_async_copy(state.at[pl.ds(rows - 2, 2)], last_rows, sems.at[3]),
    ]
    for copy in copies:
        copy.start()
    for copy in copies:
        copy.wait()
    for i in range(2):
        sides[i] = left[:, i, :]
        sides[2 + i] = right[:, EDGE - 2 + i, :]
    top_corners[...] = jnp.zeros(top_corners.shape, F32)
    low_corners[...] = jnp.zeros(low_corners.shape, F32)
    top_corners[0:1] = left[0, 0:1]
    top_corners[1:2] = right[0, EDGE - 1 :]
    low_corners[0:1] = left[rows - 1, 0:1]
    low_corners[1:2] = right[rows - 1, EDGE - 1 :]


def take_edges(state):
    rows, cols, levels = state.shape
    slab = jax.ShapeDtypeStruct((2, cols, levels), F32)
    side = jax.ShapeDtypeStruct((4, rows, levels), F32)
    corner = jax.ShapeDtypeStruct((EDGE, levels), F32)
    vmem = pl.BlockSpec(memory_space=pltpu.VMEM)
    return pl.pallas_call(
        edges_kernel,
        out_shape=(slab, slab, side, corner, corner),
        in_specs=[pl.BlockSpec(memory_space=pl.ANY)],
        out_specs=(vmem,) * 5,
        scratch_shapes=[
            pltpu.VMEM((rows, EDGE, levels), F32),
            pltpu.VMEM((rows, EDGE, levels), F32),
            pltpu.SemaphoreType.DMA((4,)),
        ],
        compiler_params=pltpu.CompilerParams(vmem_limit_bytes=16 * MIB),
        name="edges",
    )(state)


def advance_kernel(comp_count, left_at, right_at, *refs):
    (flags, source_column, state, up_rows, low_rows, left_in, right_in, own_sides) = refs[:8]
    (up_left, up_right, low_left, low_right, mask, mix_atm, mix_ocn, flux_map) = refs[8:16]
    out = refs[16]
    packed = refs[17 : 17 + comp_count]
    (values, moved, halo, halo_moved, smooth, pairs, mixed, weights, flux_weights, fluxes, staged) = refs[
        17 + comp_count : 28 + comp_count
    ]
    in_sems, out_sems = refs[28 + comp_count :]
    left_cols = left_in.at[left_at : left_at + 2]
    right_cols = right_in.at[right_at : right_at + 2]
    rows, cols, levels = state.shape
    chunks = rows // CHUNK
    inner = pl.ds(EDGE, cols)
    flux_count = flux_map.shape[0]

    def fetch(q):
        return pltpu.make_async_copy(
            state.at[pl.ds(q * CHUNK, CHUNK)],
            values.at[pl.ds(q * CHUNK + 2, CHUNK), inner],
            in_sems.at[q],
        )

    def put(q, slot):
        return pltpu.make_async_copy(
            staged.at[slot], out.at[pl.ds(q * CHUNK, CHUNK)], out_sems.at[slot]
        )

    def begin(q, _):
        fetch(q).start()
        return 0

    lax.fori_loop(0, chunks, begin, 0)
    ocean = flags[0] == 1
    mix = jnp.where(ocean, mix_ocn[...], mix_atm[...])
    mix_high, mix_low = split_two(mix)
    weights[:levels, :levels] = mix_high
    weights[levels:, :levels] = mix_high
    weights[:levels, levels:] = mix_low
    weights[levels:, levels:] = mix_low
    map_high, map_low = split_two(flux_map[...])
    flux_weights[...] = jnp.concatenate(
        [
            jnp.concatenate([map_high.astype(F32), map_high.astype(F32)], axis=1),
            jnp.concatenate([map_low.astype(F32), map_low.astype(F32)], axis=1),
        ],
        axis=0,
    ).astype(BF16)
    values[0:2, EDGE : EDGE + cols, :] = up_rows[...]
    values[rows + 2 : rows + 4, EDGE : EDGE + cols, :] = low_rows[...]
    values[1, EDGE - 1 : EDGE, :] = up_left[1:2]
    values[1, EDGE + cols : EDGE + cols + 1, :] = up_right[0:1]
    values[rows + 2, EDGE - 1 : EDGE, :] = low_left[1:2]
    values[rows + 2, EDGE + cols : EDGE + cols + 1, :] = low_right[0:1]

    def side_cells(r, _):
        values[r + 2, EDGE - 1 : EDGE, :] = left_cols[1, pl.ds(r, 1), :]
        values[r + 2, EDGE + cols : EDGE + cols + 1, :] = right_cols[0, pl.ds(r, 1), :]
        return 0

    lax.fori_loop(0, rows, side_cells, 0, unroll=8)

    def stage(row, total):
        line = SMOOTHING * total
        smooth[row] = line
        pairs[row * cols : (row + 1) * cols, :] = side_by_side(line)

    def mix_rows(count):
        mixed[: count * cols, :] = dot_nn(pairs[: count * cols, :], weights[...])

    def finish(row):
        part = mixed[row * cols : (row + 1) * cols, :]
        return smooth[row] + PHYSICS * jnp.tanh(part[:, :levels] + part[:, levels:])

    def gather_row(ref, i):
        here = ref[i, EDGE : EDGE + cols, :] + (
            ref[i - 1, EDGE : EDGE + cols, :] + ref[i + 1, EDGE : EDGE + cols, :]
        )
        return here + (
            ref[i, EDGE - 1 : EDGE - 1 + cols, :] + ref[i, EDGE + 1 : EDGE + 1 + cols, :]
        )

    @pl.when(jnp.logical_not(ocean))
    def atmosphere():
        halo[0, EDGE : EDGE + rows, :] = left_cols[1]
        halo[0, EDGE - 1 : EDGE, :] = up_left[1:2]
        halo[0, EDGE + rows : EDGE + rows + 1, :] = low_left[1:2]
        halo[1, EDGE : EDGE + rows, :] = right_cols[0]
        halo[1, EDGE - 1 : EDGE, :] = up_right[0:1]
        halo[1, EDGE + rows : EDGE + rows + 1, :] = low_right[0:1]
        beyond = (left_cols.at[0], right_cols.at[1])
        within = (own_sides.at[0], own_sides.at[3])
        for s in range(2):
            total = (
                halo[s, EDGE : EDGE + rows, :]
                + halo[s, EDGE - 1 : EDGE - 1 + rows, :]
                + halo[s, EDGE + 1 : EDGE + 1 + rows, :]
            )
            stage(s, total + (beyond[s][...] + within[s][...]))
        mix_rows(2)
        for s in range(2):
            halo_moved[s] = finish(s)

        def moved_sides(r, _):
            moved[r + 1, EDGE - 1 : EDGE, :] = halo_moved[0, pl.ds(r, 1), :]
            moved[r + 1, EDGE + cols : EDGE + cols + 1, :] = halo_moved[1, pl.ds(r, 1), :]
            return 0

        lax.fori_loop(0, rows, moved_sides, 0, unroll=8)
        fetch(0).wait()
        for row in range(2):
            stage(row, gather_row(values, row + 1))
        mix_rows(2)
        moved[0, EDGE : EDGE + cols, :] = finish(0)
        moved[1, EDGE : EDGE + cols, :] = finish(1)

        @pl.when(flags[1] == 0)
        def _():
            moved[0, EDGE : EDGE + cols, :] = jnp.zeros((cols, levels), F32)


        def one_chunk(q, _):
            base = q * CHUNK

            @pl.when(q + 1 < chunks)
            def _():
                fetch(q + 1).wait()

            for row in range(CHUNK):
                stage(row, gather_row(values, base + row + 3))
            mix_rows(CHUNK)
            for row in range(CHUNK):
                moved[base + row + 2, EDGE : EDGE + cols, :] = finish(row)

            @pl.when((q + 1 == chunks) & (flags[2] == 0))
            def _():
                moved[rows + 1, EDGE : EDGE + cols, :] = jnp.zeros((cols, levels), F32)

            for row in range(CHUNK):
                stage(row, gather_row(moved, base + row + 1))
            mix_rows(CHUNK)
            slot = q % 2

            @pl.when(q >= 2)
            def _():
                put(q - 2, slot).wait()

            for row in range(CHUNK):
                line = finish(row)
                staged[slot, row] = line
                both = line + moved[base + row + 1, EDGE : EDGE + cols, :]
                pairs[row * cols : (row + 1) * cols, :] = side_by_side(both)
            put(q, slot).start()
            flux = dot_nt(flux_weights[...], pairs[...])
            flux = flux[:flux_count] + flux[flux_count:]
            for row in range(CHUNK):
                block = PHYSICS * flux[:, row * cols : (row + 1) * cols]
                sea = jnp.broadcast_to(mask[pl.ds(base + row, 1), :], block.shape)
                block = jnp.where(sea > 0.5, block, 0.0)
                fluxes[pl.ds(pl.multiple_of((base + row) * flux_count, flux_count), flux_count), :] = block
            return 0

        lax.fori_loop(0, chunks, one_chunk, 0)
        put(chunks - 2, (chunks - 2) % 2).wait()
        put(chunks - 1, (chunks - 1) % 2).wait()
        spots = lax.broadcasted_iota(jnp.int32, (source_column.shape[0], rows), 1)
        placing = jnp.where(source_column[...] == spots, 1.0, 0.0).astype(BF16)
        share = flux_count // comp_count
        for shift in range(comp_count):
            first = lax.rem(flags[3] + shift, comp_count) * share
            for f in range(share):
                field = fluxes[pl.ds(first + f, rows, stride=flux_count), :].astype(BF16)
                packed[shift][:, f * cols : (f + 1) * cols] = dot_nn(placing, field).astype(BF16)

    @pl.when(ocean)
    def sea_side():
        fetch(0).wait()
        lanes = lax.broadcasted_iota(jnp.int32, (CHUNK, CHUNK * levels), 1) // levels
        lines = lax.broadcasted_iota(jnp.int32, (CHUNK, CHUNK * levels), 0)
        spreader = jnp.where(lanes == lines, 1.0, 0.0).astype(F32)

        def one_chunk(q, _):
            base = q * CHUNK

            @pl.when(q + 1 < chunks)
            def _():
                fetch(q + 1).wait()

            for row in range(CHUNK):
                stage(row, gather_row(values, base + row + 2))
            mix_rows(CHUNK)
            slot = q % 2

            @pl.when(q >= 2)
            def _():
                put(q - 2, slot).wait()

            sea = dot_nn(mask[pl.ds(pl.multiple_of(base, CHUNK), CHUNK), :].T, spreader)
            for row in range(CHUNK):
                chosen = sea[:, row * levels : (row + 1) * levels] > 0.5
                before = values[base + row + 2, EDGE : EDGE + cols, :]
                staged[slot, row] = jnp.where(chosen, finish(row), before)
            put(q, slot).start()
            return 0

        lax.fori_loop(0, chunks, one_chunk, 0)
        put(chunks - 2, (chunks - 2) % 2).wait()
        put(chunks - 1, (chunks - 1) % 2).wait()


def advance(
    flags, source_column, state, halos, mask, mix_atm, mix_ocn, flux_map_t, comp_count, left_at, right_at
):
    rows, cols, levels = state.shape
    fluxes = flux_map_t.shape[0]
    vmem = pl.BlockSpec(memory_space=pltpu.VMEM)
    smem = pl.BlockSpec(memory_space=pltpu.SMEM)
    hbm = pl.BlockSpec(memory_space=pl.ANY)
    entry = jax.ShapeDtypeStruct((source_column.shape[0], fluxes // comp_count * cols), BF16)
    cells = rows * cols
    return pl.pallas_call(
        functools.partial(advance_kernel, comp_count, left_at, right_at),
        out_shape=(jax.ShapeDtypeStruct(state.shape, F32),) + (entry,) * comp_count,
        in_specs=[smem, vmem, hbm] + [vmem] * (len(halos) + 4),
        out_specs=(hbm,) + (vmem,) * comp_count,
        scratch_shapes=[
            pltpu.VMEM((rows + 4, cols + 2 * EDGE, levels), F32),
            pltpu.VMEM((rows + 2, cols + 2 * EDGE, levels), F32),
            pltpu.VMEM((2, rows + 2 * EDGE, levels), F32),
            pltpu.VMEM((2, rows, levels), F32),
            pltpu.VMEM((CHUNK, cols, levels), F32),
            pltpu.VMEM((CHUNK * cols, 2 * levels), BF16),
            pltpu.VMEM((CHUNK * cols, 2 * levels), F32),
            pltpu.VMEM((2 * levels, 2 * levels), BF16),
            pltpu.VMEM((2 * fluxes, 2 * levels), BF16),
            pltpu.VMEM((rows * fluxes, cols), F32),
            pltpu.VMEM((2, CHUNK, cols, levels), F32),
            pltpu.SemaphoreType.DMA((rows // CHUNK,)),
            pltpu.SemaphoreType.DMA((2,)),
        ],
        compiler_params=pltpu.CompilerParams(vmem_limit_bytes=48 * MIB),
        cost_estimate=pl.CostEstimate(
            flops=8 * cells * levels * levels, bytes_accessed=8 * cells * levels, transcendentals=0
        ),
        name="advance",
    )(flags, source_column, state, *halos, mask, mix_atm, mix_ocn, flux_map_t)


BATCH = 8


def regrid_body(count, flags, ocean_first, *refs):
    blocks = refs[:count]
    target_line, weight_line, weights, surface, mask, forcing, shared, entries, chosen, binned = refs[count:]
    rows, cols = mask.shape
    share = forcing.shape[0]
    weight_count = weights.shape[0]
    size = blocks[0].shape[0]
    total = count * size
    for n in range(count):
        entries[n * size : (n + 1) * size, :] = blocks[n][...]
    spots = lax.broadcasted_iota(jnp.int32, (rows, total), 0)
    by_target = jnp.where(target_line[...] == spots, 1.0, 0.0).astype(BF16)
    numbers = lax.broadcasted_iota(jnp.int32, (weight_count, total), 0)
    by_weight = jnp.where(weight_line[...] == numbers, 1.0, 0.0).astype(BF16)
    for g in range(weight_count // BATCH):
        for i in range(BATCH):
            w = g * BATCH + i
            chosen[i * rows : (i + 1) * rows, :] = by_target * by_weight[w : w + 1, :]
        binned[...] = dot_nn(chosen[...], entries[...])
        wide = weights[g * BATCH : (g + 1) * BATCH].reshape(BATCH * cols, cols)
        for f in range(share):
            halves = [
                split_two(binned[i * rows : (i + 1) * rows, f * cols : (f + 1) * cols])
                for i in range(BATCH)
            ]
            part = dot_nn(jnp.concatenate([h for h, _ in halves], axis=1), wide) + dot_nn(
                jnp.concatenate([l for _, l in halves], axis=1), wide
            )
            forcing[f] = part if g == 0 else forcing[f] + part
    change = ocean_first[flags[3] * share] * forcing[0]
    for f in range(1, share):
        change = change + ocean_first[flags[3] * share + f] * forcing[f]
    base = jnp.where(flags[0] == 1, surface[...], 0.0)
    held = jnp.where((mask[...] > 0.5) | (flags[0] == 0), change, 0.0)
    shared[0] = base + held
    shared[1] = mask[...]


def regrid(flags, ocean_first, blocks, target_line, weight_line, weights, surface, mask):
    rows, cols = mask.shape
    count = len(blocks)
    size, width = blocks[0].shape
    share = width // cols
    weight_count = weights.shape[0]
    vmem = pl.BlockSpec(memory_space=pltpu.VMEM)
    smem = pl.BlockSpec(memory_space=pltpu.SMEM)
    return pl.pallas_call(
        functools.partial(regrid_body, count),
        out_shape=(
            jax.ShapeDtypeStruct((share, rows, cols), F32),
            jax.ShapeDtypeStruct((2, rows, cols), F32),
        ),
        in_specs=[smem, smem] + [vmem] * (count + 5),
        out_specs=(vmem, vmem),
        scratch_shapes=[
            pltpu.VMEM((count * size, width), BF16),
            pltpu.VMEM((BATCH * rows, count * size), BF16),
            pltpu.VMEM((BATCH * rows, width), F32),
        ],
        compiler_params=pltpu.CompilerParams(vmem_limit_bytes=32 * MIB),
        cost_estimate=pl.CostEstimate(
            flops=2 * weight_count * rows * width * (count * size + 2 * cols),
            bytes_accessed=2 * MIB,
            transcendentals=0,
        ),
        name="regrid",
    )(flags, ocean_first, *blocks, target_line, weight_line, weights, surface, mask)


def pick_kernel(comp_count, *refs):
    flags = refs[0]
    parts = refs[1 : 1 + comp_count]
    target_column, surface = refs[1 + comp_count : 3 + comp_count]
    picked = refs[3 + comp_count :]
    rows, cols = surface.shape
    from_ocean = lax.rem(flags[3] + 1, comp_count)
    base = jnp.zeros((rows, cols), F32)
    sea = base
    change = base
    for shift in range(comp_count):
        is_base = from_ocean == shift
        base = base + jnp.where(is_base, parts[shift][0], 0.0)
        sea = sea + jnp.where(is_base, parts[shift][1], 0.0)
        change = change + jnp.where(is_base, 0.0, parts[shift][0])
    now = base + jnp.where(sea > 0.5, change, 0.0)
    surface[...] = now
    pair = jnp.concatenate(split_two(now), axis=0)
    size = picked[0].shape[0]
    spots = lax.broadcasted_iota(jnp.int32, (size, rows), 1)
    for n in range(len(picked)):
        hits = target_column[n * size : (n + 1) * size, :] == spots
        hits = jnp.where(hits, 1.0, 0.0).astype(BF16)
        picked[n][...] = dot_nn(jnp.concatenate([hits, hits], axis=1), pair)


def pick(flags, parts, target_column, neighbours):
    _, rows, cols = parts[0].shape
    size = target_column.shape[0] // neighbours
    vmem = pl.BlockSpec(memory_space=pltpu.VMEM)
    smem = pl.BlockSpec(memory_space=pltpu.SMEM)
    return pl.pallas_call(
        functools.partial(pick_kernel, len(parts)),
        out_shape=(jax.ShapeDtypeStruct((rows, cols), F32),)
        + (jax.ShapeDtypeStruct((size, cols), F32),) * neighbours,
        in_specs=[smem] + [vmem] * (len(parts) + 1),
        out_specs=(vmem,) * (1 + neighbours),
        compiler_params=pltpu.CompilerParams(vmem_limit_bytes=16 * MIB),
        name="pick",
    )(flags, *parts, target_column)


LINES = 16


def update_kernel(groups, flags, state, *refs):
    parts = refs[:groups]
    mask, ocean_map, out, held, table, wide, in_sems, out_sems = refs[groups:]
    rows, cols, levels = state.shape
    share = parts[0].shape[0]
    flux_count = groups * share
    chunks = rows // LINES
    depth = LINES * flux_count

    def fetch(q):
        return pltpu.make_async_copy(
            state.at[pl.ds(q * LINES, LINES)], held.at[pl.ds(q * LINES, LINES)], in_sems.at[q]
        )

    def put(q):
        return pltpu.make_async_copy(
            held.at[pl.ds(q * LINES, LINES)], out.at[pl.ds(q * LINES, LINES)], out_sems.at[q]
        )

    @pl.when(flags[0] == 1)
    def ocean():
        for q in range(chunks):
            fetch(q).start()
        table[...] = jnp.zeros(table.shape, F32)
        for line in range(LINES):
            for f in range(flux_count):
                spot = f * LINES + line
                table[spot : spot + 1, line * levels : (line + 1) * levels] = ocean_map[f : f + 1]
        high, low = split_two(table[...])
        wide[:depth] = high
        wide[depth : 2 * depth] = high
        wide[2 * depth :] = low

        def one(q, _):
            start = pl.multiple_of(q * LINES, LINES)
            sea = mask[pl.ds(start, LINES), :] > 0.5
            part = jnp.concatenate(
                [
                    jnp.where(sea, parts[f // share][f % share, pl.ds(start, LINES), :], 0.0)
                    for f in range(flux_count)
                ],
                axis=0,
            )
            first, second = split_two(part.T)
            change = dot_nn(jnp.concatenate([first, second, first], axis=1), wide[...])
            fetch(q).wait()
            for line in range(LINES):
                held[start + line] += change[:, line * levels : (line + 1) * levels]
            put(q).start()
            return 0

        lax.fori_loop(0, chunks, one, 0)
        for q in range(chunks):
            put(q).wait()


def update(flags, state, parts, mask, ocean_map):
    rows, cols, levels = state.shape
    depth = LINES * ocean_map.shape[0]
    vmem = pl.BlockSpec(memory_space=pltpu.VMEM)
    smem = pl.BlockSpec(memory_space=pltpu.SMEM)
    hbm = pl.BlockSpec(memory_space=pl.ANY)
    return pl.pallas_call(
        functools.partial(update_kernel, len(parts)),
        out_shape=jax.ShapeDtypeStruct(state.shape, F32),
        in_specs=[smem, hbm] + [vmem] * (len(parts) + 2),
        out_specs=hbm,
        input_output_aliases={1: 0},
        scratch_shapes=[
            pltpu.VMEM(state.shape, F32),
            pltpu.VMEM((depth, LINES * levels), F32),
            pltpu.VMEM((3 * depth, LINES * levels), BF16),
            pltpu.SemaphoreType.DMA((rows // LINES,)),
            pltpu.SemaphoreType.DMA((rows // LINES,)),
        ],
        compiler_params=pltpu.CompilerParams(vmem_limit_bytes=24 * MIB),
        cost_estimate=pl.CostEstimate(
            flops=6 * rows * cols * depth * levels,
            bytes_accessed=8 * rows * cols * levels,
            transcendentals=0,
        ),
        name="update",
    )(flags, state, *parts, mask, ocean_map)


def returned_kernel(groups, flags, *refs):
    picked = refs[:groups]
    weight_column, row_line, weights, mask, surface, new_surface, out, total = refs[groups:]
    rows, cols = mask.shape
    weight_count = weights.shape[0]

    @pl.when(flags[0] == 1)
    def ocean():
        out[...] = new_surface[...]

    @pl.when(flags[0] == 0)
    def atmosphere():
        values = jnp.concatenate([p[...] for p in picked], axis=0)
        pair = side_by_side(values)
        which = jnp.broadcast_to(weight_column[...], values.shape)
        total[...] = jnp.zeros(values.shape, F32)

        def one(i, _):
            both = jnp.concatenate([weights[2 * i], weights[2 * i + 1]], axis=0)
            images = dot_nt(pair, jnp.concatenate([both, both], axis=1))
            total[...] += jnp.where(which == 2 * i, images[:, :cols], 0.0) + jnp.where(
                which == 2 * i + 1, images[:, cols:], 0.0
            )
            return 0

        lax.fori_loop(0, weight_count // 2, one, 0, unroll=2)
        spots = lax.broadcasted_iota(jnp.int32, (rows, values.shape[0]), 0)
        chosen = jnp.where(jnp.broadcast_to(row_line[...], spots.shape) == spots, 1.0, 0.0).astype(BF16)
        high, low = split_two(total[...])
        back = dot_nn(chosen, high) + dot_nn(chosen, low)
        out[...] = jnp.where(mask[...] > 0.5, back, surface[...])


def returned(flags, picked, weight_column, row_line, weights, mask, surface, new_surface):
    rows, cols = mask.shape
    entry_total = weight_column.shape[0]
    vmem = pl.BlockSpec(memory_space=pltpu.VMEM)
    smem = pl.BlockSpec(memory_space=pltpu.SMEM)
    return pl.pallas_call(
        functools.partial(returned_kernel, len(picked)),
        out_shape=jax.ShapeDtypeStruct((rows, cols), F32),
        in_specs=[smem] + [vmem] * (len(picked) + 6),
        out_specs=vmem,
        scratch_shapes=[pltpu.VMEM((entry_total, cols), F32)],
        compiler_params=pltpu.CompilerParams(vmem_limit_bytes=16 * MIB),
        name="returned",
    )(flags, *picked, weight_column, row_line, weights, mask, surface, new_surface)


def local(
    state, land_mask, intersection_list, mix_atm, mix_ocn, flux_map, ocean_map, regrid_weights
):
    rows, cols, levels = state.shape
    intersections = intersection_list.shape[2]
    comp_count = lax.axis_size("comp")
    lat_count = lax.axis_size("lat")
    lon_count = lax.axis_size("lon")
    tile_count = lat_count * lon_count
    reach = min(4, lon_count)
    neighbours = 2 * reach
    entry_total = intersections * rows
    capacity = entry_total // neighbours
    comp_index = lax.axis_index("comp")
    lat_index = lax.axis_index("lat")
    tile_index = lat_index * lon_count + lax.axis_index("lon")
    bands = comp_count * lat_count
    ocean_band = (comp_count - 1) * lat_count
    ocean_comp = comp_count - 1
    band = comp_index * lat_count + lat_index
    is_ocean = comp_index == ocean_comp
    upper_valid = (band > 0) & (band != ocean_band)
    lower_valid = (band < bands - 1) & (band != ocean_band - 1)
    flags = jnp.stack([is_ocean, upper_valid, lower_valid, comp_index]).astype(jnp.int32)
    mask = (land_mask == 1).astype(F32)

    def band_shift(value, by, lon_by):
        pairs = []
        for b in range(bands):
            target = b + by
            if 0 <= target < bands and (b >= ocean_band) == (target >= ocean_band):
                for lon in range(lon_count):
                    pairs.append(
                        (b * lon_count + lon, target * lon_count + (lon + lon_by) % lon_count)
                    )
        return lax.ppermute(value, AXES, pairs)

    first_rows, last_rows, sides, top_corners, low_corners = take_edges(state)
    up_rows = band_shift(last_rows, 1, 0)
    low_rows = band_shift(first_rows, -1, 0)
    if lon_count == 2:
        left_cols = right_cols = band_shift(sides, 0, 1)
        left_at, right_at = 2, 0
    else:
        left_cols = band_shift(sides[2:], 0, 1)
        right_cols = band_shift(sides[:2], 0, -1)
        left_at, right_at = 0, 0
    up_left = band_shift(low_corners, 1, 1)
    low_left = band_shift(top_corners, -1, 1)
    if lon_count == 2:
        up_right, low_right = up_left, low_left
    else:
        up_right = band_shift(low_corners, 1, -1)
        low_right = band_shift(top_corners, -1, -1)

    entry_list = intersection_list.reshape(entry_total, 3)
    owners = entry_list[:, 0]
    labels = entry_list[:, 2] * rows + entry_list[:, 1]
    offsets = [
        (n // reach * lon_count + n % reach - (reach - 1) // 2) % tile_count
        for n in range(neighbours)
    ]
    distance = (owners - tile_index + tile_count) % tile_count
    hits = distance[:, None] == jnp.array(offsets, jnp.int32)[None, :]
    neighbour_ids = jnp.sum(
        jnp.where(hits, jnp.arange(neighbours, dtype=jnp.int32)[None, :], 0), axis=1
    )
    positions = jnp.arange(entry_total, dtype=jnp.int32)
    earlier = (neighbour_ids[None, :] == neighbour_ids[:, None]) & (
        positions[None, :] < positions[:, None]
    )
    slots = neighbour_ids * capacity + jnp.sum(earlier.astype(jnp.int32), axis=1)
    placing = positions[:, None] == slots[None, :]
    sources = jnp.sum(jnp.where(placing, (positions // intersections)[None, :], 0), axis=1)
    packed_labels = jnp.sum(jnp.where(placing, labels[None, :], 0), axis=1)

    def over_comp(value, shift, last):
        pairs = [
            (c * tile_count + t, (c + shift) % comp_count * tile_count + t)
            for c in range(comp_count if last else comp_count - 1)
            for t in range(tile_count)
        ]
        return lax.ppermute(value, AXES, pairs)

    def over_tiles(value, offset):
        if offset % tile_count == 0:
            return value
        pairs = [
            (c * tile_count + t, c * tile_count + (t + offset) % tile_count)
            for c in range(comp_count)
            for t in range(tile_count)
        ]
        return lax.ppermute(value, AXES, pairs)

    def to_ocean(value, comp):
        pairs = [
            (comp * tile_count + t, ocean_comp * tile_count + t) for t in range(tile_count)
        ]
        return lax.ppermute(value, AXES, pairs)

    every = lax.all_gather(packed_labels, AXES).reshape(
        comp_count, tile_count, neighbours, capacity
    )
    ordered = (comp_index - jnp.arange(comp_count, dtype=jnp.int32) + comp_count) % comp_count
    from_tiles = [
        lax.dynamic_index_in_dim(
            every[:, :, n], (tile_index - offsets[n] + tile_count) % tile_count, 1, False
        )
        for n in range(neighbours)
    ]
    by_comp = jnp.stack(from_tiles)
    mine = by_comp[:, :, None, :]
    wanted = ordered[None, :, None, None] == jnp.arange(comp_count, dtype=jnp.int32)[None, None, :, None]
    arrived_labels = jnp.sum(jnp.where(wanted, mine.transpose(0, 2, 1, 3), 0), axis=2).reshape(1, -1)
    own_labels = jnp.sum(
        jnp.where((jnp.arange(comp_count, dtype=jnp.int32) == comp_index)[None, :, None], by_comp, 0),
        axis=1,
    )
    target_column = (own_labels % rows).reshape(-1, 1)

    halos = (up_rows, low_rows, left_cols, right_cols, sides)
    halos = halos + (up_left, up_right, low_left, low_right)
    moved = advance(
        flags, sources[:, None], state, halos, mask, mix_atm, mix_ocn, flux_map.T, comp_count,
        left_at, right_at,
    )
    moved, packed = moved[0], moved[1:]
    own = jnp.where(is_ocean, jnp.zeros((), BF16), packed[0])
    slabs = [own] + [over_comp(packed[s], s, False) for s in range(1, comp_count)]
    blocks = []
    for n in range(neighbours):
        block = jnp.concatenate([slab[n * capacity : (n + 1) * capacity] for slab in slabs])
        blocks.append(over_tiles(block, offsets[n]))
    surface = moved[:, :, 0]
    forcing, shared = regrid(
        flags, ocean_map[:, 0], blocks, arrived_labels % rows, arrived_labels // rows,
        regrid_weights, surface, mask,
    )
    parts = [shared] + [over_comp(shared, s, True) for s in range(1, comp_count)]
    picks = pick(flags, parts, target_column, neighbours)
    new_surface, picked = picks[0], picks[1:]
    arrived = [over_tiles(picked[n], -offsets[n]) for n in range(neighbours)]
    fields = [to_ocean(forcing, c) for c in range(comp_count - 1)] + [forcing]
    final_state = update(flags, moved, fields, mask, ocean_map)
    weight_column = (packed_labels // rows)[:, None]
    surface_out = returned(
        flags, arrived, weight_column, sources[None, :], regrid_weights, mask, surface, new_surface
    )
    return (final_state, surface_out)


def solution(mesh):
    placed = (
        P(("comp", "lat"), "lon", None),
        P(("comp", "lat"), "lon"),
        P(("comp", "lat"), "lon", None, None),
        P(),
        P(),
        P(),
        P(),
        P(),
    )
    return jax.shard_map(
        local,
        mesh=mesh,
        in_specs=placed,
        out_specs=(P(("comp", "lat"), "lon", None), P(("comp", "lat"), "lon")),
        check_vma=False,
    )
```

```python
import functools

import jax
import jax.numpy as jnp
from jax import lax
from jax.experimental import pallas as pl
from jax.experimental.pallas import tpu as pltpu
from jax.sharding import PartitionSpec as P

SMOOTHING = 0.2
PHYSICS = 0.5
MIB = 1024 * 1024
F32 = jnp.float32
BF16 = jnp.bfloat16
EDGE = 8
CHUNK = 8
AXES = ("comp", "lat", "lon")


def split_two(x):
    high = x.astype(BF16)
    low = (x - high.astype(F32)).astype(BF16)
    return high, low


def side_by_side(x):
    return jnp.concatenate(split_two(x), axis=1)


def dot_nt(a, b):
    return lax.dot_general(a, b, (((1,), (1,)), ((), ())), preferred_element_type=F32)


def dot_nn(a, b):
    return jnp.dot(a, b, preferred_element_type=F32)


def edges_kernel(state, first_rows, last_rows, sides, top_corners, low_corners, left, right, sems):
    rows, cols, _ = state.shape
    copies = [
        pltpu.make_async_copy(state.at[:, pl.ds(0, EDGE)], left, sems.at[0]),
        pltpu.make_async_copy(state.at[:, pl.ds(cols - EDGE, EDGE)], right, sems.at[1]),
        pltpu.make_async_copy(state.at[pl.ds(0, 2)], first_rows, sems.at[2]),
        pltpu.make_async_copy(state.at[pl.ds(rows - 2, 2)], last_rows, sems.at[3]),
    ]
    for copy in copies:
        copy.start()
    for copy in copies:
        copy.wait()
    for i in range(2):
        sides[i] = left[:, i, :]
        sides[2 + i] = right[:, EDGE - 2 + i, :]
    top_corners[...] = jnp.zeros(top_corners.shape, F32)
    low_corners[...] = jnp.zeros(low_corners.shape, F32)
    top_corners[0:1] = left[0, 0:1]
    top_corners[1:2] = right[0, EDGE - 1 :]
    low_corners[0:1] = left[rows - 1, 0:1]
    low_corners[1:2] = right[rows - 1, EDGE - 1 :]


def take_edges(state):
    rows, cols, levels = state.shape
    slab = jax.ShapeDtypeStruct((2, cols, levels), F32)
    side = jax.ShapeDtypeStruct((4, rows, levels), F32)
    corner = jax.ShapeDtypeStruct((EDGE, levels), F32)
    vmem = pl.BlockSpec(memory_space=pltpu.VMEM)
    return pl.pallas_call(
        edges_kernel,
        out_shape=(slab, slab, side, corner, corner),
        in_specs=[pl.BlockSpec(memory_space=pl.ANY)],
        out_specs=(vmem,) * 5,
        scratch_shapes=[
            pltpu.VMEM((rows, EDGE, levels), F32),
            pltpu.VMEM((rows, EDGE, levels), F32),
            pltpu.SemaphoreType.DMA((4,)),
        ],
        compiler_params=pltpu.CompilerParams(vmem_limit_bytes=56 * MIB),
        name="edges",
    )(state)


def advance_kernel(comp_count, left_at, right_at, *refs):
    (flags, source_column, labels, state, up_rows, low_rows, left_in, right_in, own_sides) = refs[:9]
    (up_left, up_right, low_left, low_right, mask, mix_atm, mix_ocn, flux_map) = refs[9:17]
    out, surface = refs[17:19]
    packed = refs[19 : 19 + comp_count]
    (values, moved, halo, halo_moved, smooth, pairs, mixed, weights, flux_weights, fluxes, staged) = refs[
        19 + comp_count : 30 + comp_count
    ]
    top, in_sems, out_sems = refs[30 + comp_count :]
    left_cols = left_in.at[left_at : left_at + 2]
    right_cols = right_in.at[right_at : right_at + 2]
    rows, cols, levels = state.shape
    chunks = rows // CHUNK
    inner = pl.ds(EDGE, cols)
    flux_count = flux_map.shape[0]

    def fetch(q):
        return pltpu.make_async_copy(
            state.at[pl.ds(q * CHUNK, CHUNK)],
            values.at[pl.ds(q * CHUNK + 2, CHUNK), inner],
            in_sems.at[q],
        )

    def put(q, slot):
        return pltpu.make_async_copy(
            staged.at[slot], out.at[pl.ds(q * CHUNK, CHUNK)], out_sems.at[slot]
        )

    def begin(q, _):
        fetch(q).start()
        return 0

    lax.fori_loop(0, chunks, begin, 0)
    ocean = flags[0] == 1
    mix = jnp.where(ocean, mix_ocn[...], mix_atm[...])
    mix_high, mix_low = split_two(mix)
    weights[:levels, :levels] = mix_high
    weights[levels:, :levels] = mix_high
    weights[:levels, levels:] = mix_low
    weights[levels:, levels:] = mix_low
    map_high, map_low = split_two(flux_map[...])
    flux_weights[...] = jnp.concatenate(
        [
            jnp.concatenate([map_high.astype(F32), map_high.astype(F32)], axis=1),
            jnp.concatenate([map_low.astype(F32), map_low.astype(F32)], axis=1),
        ],
        axis=0,
    ).astype(BF16)
    values[0:2, EDGE : EDGE + cols, :] = up_rows[...]
    values[rows + 2 : rows + 4, EDGE : EDGE + cols, :] = low_rows[...]
    values[1, EDGE - 1 : EDGE, :] = up_left[1:2]
    values[1, EDGE + cols : EDGE + cols + 1, :] = up_right[0:1]
    values[rows + 2, EDGE - 1 : EDGE, :] = low_left[1:2]
    values[rows + 2, EDGE + cols : EDGE + cols + 1, :] = low_right[0:1]

    def side_cells(r, _):
        values[r + 2, EDGE - 1 : EDGE, :] = left_cols[1, pl.ds(r, 1), :]
        values[r + 2, EDGE + cols : EDGE + cols + 1, :] = right_cols[0, pl.ds(r, 1), :]
        return 0

    lax.fori_loop(0, rows, side_cells, 0, unroll=8)

    def stage(row, total):
        line = SMOOTHING * total
        smooth[row] = line
        pairs[row * cols : (row + 1) * cols, :] = side_by_side(line)

    def note_top(q, lines):
        lanes = lax.broadcasted_iota(jnp.int32, (cols, levels), 1)
        kept = lines[0]
        for row in range(1, CHUNK):
            kept = jnp.where(lanes == row, pltpu.roll(lines[row], row, 1), kept)
        turned = pltpu.roll(kept, q * CHUNK, 1)
        top[...] = jnp.where(lanes // CHUNK == q, turned, top[...])

    def mix_rows(count):
        mixed[: count * cols, :] = dot_nn(pairs[: count * cols, :], weights[...])

    def finish(row):
        part = mixed[row * cols : (row + 1) * cols, :]
        return smooth[row] + PHYSICS * jnp.tanh(part[:, :levels] + part[:, levels:])

    def gather_row(ref, i):
        here = ref[i, EDGE : EDGE + cols, :] + (
            ref[i - 1, EDGE : EDGE + cols, :] + ref[i + 1, EDGE : EDGE + cols, :]
        )
        return here + (
            ref[i, EDGE - 1 : EDGE - 1 + cols, :] + ref[i, EDGE + 1 : EDGE + 1 + cols, :]
        )

    @pl.when(jnp.logical_not(ocean))
    def atmosphere():
        halo[0, EDGE : EDGE + rows, :] = left_cols[1]
        halo[0, EDGE - 1 : EDGE, :] = up_left[1:2]
        halo[0, EDGE + rows : EDGE + rows + 1, :] = low_left[1:2]
        halo[1, EDGE : EDGE + rows, :] = right_cols[0]
        halo[1, EDGE - 1 : EDGE, :] = up_right[0:1]
        halo[1, EDGE + rows : EDGE + rows + 1, :] = low_right[0:1]
        beyond = (left_cols.at[0], right_cols.at[1])
        within = (own_sides.at[0], own_sides.at[3])
        for s in range(2):
            total = (
                halo[s, EDGE : EDGE + rows, :]
                + halo[s, EDGE - 1 : EDGE - 1 + rows, :]
                + halo[s, EDGE + 1 : EDGE + 1 + rows, :]
            )
            stage(s, total + (beyond[s][...] + within[s][...]))
        mix_rows(2)
        for s in range(2):
            halo_moved[s] = finish(s)

        def moved_sides(r, _):
            moved[r + 1, EDGE - 1 : EDGE, :] = halo_moved[0, pl.ds(r, 1), :]
            moved[r + 1, EDGE + cols : EDGE + cols + 1, :] = halo_moved[1, pl.ds(r, 1), :]
            return 0

        lax.fori_loop(0, rows, moved_sides, 0, unroll=8)
        fetch(0).wait()
        for row in range(2):
            stage(row, gather_row(values, row + 1))
        mix_rows(2)
        moved[0, EDGE : EDGE + cols, :] = finish(0)
        moved[1, EDGE : EDGE + cols, :] = finish(1)

        @pl.when(flags[1] == 0)
        def _():
            moved[0, EDGE : EDGE + cols, :] = jnp.zeros((cols, levels), F32)


        def one_chunk(q, _):
            base = q * CHUNK

            @pl.when(q + 1 < chunks)
            def _():
                fetch(q + 1).wait()

            for row in range(CHUNK):
                stage(row, gather_row(values, base + row + 3))
            mix_rows(CHUNK)
            for row in range(CHUNK):
                moved[base + row + 2, EDGE : EDGE + cols, :] = finish(row)

            @pl.when((q + 1 == chunks) & (flags[2] == 0))
            def _():
                moved[rows + 1, EDGE : EDGE + cols, :] = jnp.zeros((cols, levels), F32)

            for row in range(CHUNK):
                stage(row, gather_row(moved, base + row + 1))
            mix_rows(CHUNK)
            slot = q % 2

            @pl.when(q >= 2)
            def _():
                put(q - 2, slot).wait()

            for row in range(CHUNK):
                line = finish(row)
                staged[slot, row] = line
                both = line + moved[base + row + 1, EDGE : EDGE + cols, :]
                pairs[row * cols : (row + 1) * cols, :] = side_by_side(both)
            put(q, slot).start()
            note_top(q, [staged[slot, row] for row in range(CHUNK)])
            flux = dot_nt(flux_weights[...], pairs[...])
            flux = flux[:flux_count] + flux[flux_count:]
            for row in range(CHUNK):
                block = PHYSICS * flux[:, row * cols : (row + 1) * cols]
                sea = jnp.broadcast_to(mask[pl.ds(base + row, 1), :], block.shape)
                block = jnp.where(sea > 0.5, block, 0.0)
                fluxes[pl.ds(pl.multiple_of((base + row) * flux_count, flux_count), flux_count), :] = block
            return 0

        lax.fori_loop(0, chunks, one_chunk, 0)
        put(chunks - 2, (chunks - 2) % 2).wait()
        put(chunks - 1, (chunks - 1) % 2).wait()
        spots = lax.broadcasted_iota(jnp.int32, (source_column.shape[0], rows), 1)
        placing = jnp.where(source_column[...] == spots, 1.0, 0.0).astype(BF16)
        share = flux_count // comp_count
        for shift in range(comp_count):
            first = lax.rem(flags[3] + shift, comp_count) * share
            for f in range(share):
                field = fluxes[pl.ds(first + f, rows, stride=flux_count), :].astype(BF16)
                packed[shift][: placing.shape[0], f * cols : (f + 1) * cols] = dot_nn(
                    placing, field
                ).astype(BF16)
            packed[shift][placing.shape[0] :, :] = labels[...]
        surface[...] = top[...].T

    @pl.when(ocean)
    def sea_side():
        fetch(0).wait()
        lanes = lax.broadcasted_iota(jnp.int32, (CHUNK, CHUNK * levels), 1) // levels
        lines = lax.broadcasted_iota(jnp.int32, (CHUNK, CHUNK * levels), 0)
        spreader = jnp.where(lanes == lines, 1.0, 0.0).astype(F32)

        def one_chunk(q, _):
            base = q * CHUNK

            @pl.when(q + 1 < chunks)
            def _():
                fetch(q + 1).wait()

            for row in range(CHUNK):
                stage(row, gather_row(values, base + row + 2))
            mix_rows(CHUNK)
            slot = q % 2

            @pl.when(q >= 2)
            def _():
                put(q - 2, slot).wait()

            sea = dot_nn(mask[pl.ds(pl.multiple_of(base, CHUNK), CHUNK), :].T, spreader)
            for row in range(CHUNK):
                chosen = sea[:, row * levels : (row + 1) * levels] > 0.5
                before = values[base + row + 2, EDGE : EDGE + cols, :]
                staged[slot, row] = jnp.where(chosen, finish(row), before)
            put(q, slot).start()
            note_top(q, [staged[slot, row] for row in range(CHUNK)])
            return 0

        lax.fori_loop(0, chunks, one_chunk, 0)
        put(chunks - 2, (chunks - 2) % 2).wait()
        put(chunks - 1, (chunks - 1) % 2).wait()
        surface[...] = top[...].T
        for shift in range(comp_count):
            packed[shift][...] = jnp.zeros(packed[shift].shape, BF16)


def advance(
    flags, source_column, labels, state, halos, mask, mix_atm, mix_ocn, flux_map_t, comp_count, left_at, right_at
):
    rows, cols, levels = state.shape
    fluxes = flux_map_t.shape[0]
    vmem = pl.BlockSpec(memory_space=pltpu.VMEM)
    smem = pl.BlockSpec(memory_space=pltpu.SMEM)
    hbm = pl.BlockSpec(memory_space=pl.ANY)
    entry = jax.ShapeDtypeStruct(
        (source_column.shape[0] + labels.shape[0], fluxes // comp_count * cols), BF16
    )
    cells = rows * cols
    return pl.pallas_call(
        functools.partial(advance_kernel, comp_count, left_at, right_at),
        out_shape=(
            jax.ShapeDtypeStruct(state.shape, F32),
            jax.ShapeDtypeStruct((rows, cols), F32),
        )
        + (entry,) * comp_count,
        in_specs=[smem, vmem, vmem, hbm] + [vmem] * (len(halos) + 4),
        out_specs=(hbm,) + (vmem,) * (1 + comp_count),
        scratch_shapes=[
            pltpu.VMEM((rows + 4, cols + 2 * EDGE, levels), F32),
            pltpu.VMEM((rows + 2, cols + 2 * EDGE, levels), F32),
            pltpu.VMEM((2, rows + 2 * EDGE, levels), F32),
            pltpu.VMEM((2, rows, levels), F32),
            pltpu.VMEM((CHUNK, cols, levels), F32),
            pltpu.VMEM((CHUNK * cols, 2 * levels), BF16),
            pltpu.VMEM((CHUNK * cols, 2 * levels), F32),
            pltpu.VMEM((2 * levels, 2 * levels), BF16),
            pltpu.VMEM((2 * fluxes, 2 * levels), BF16),
            pltpu.VMEM((rows * fluxes, cols), F32),
            pltpu.VMEM((2, CHUNK, cols, levels), F32),
            pltpu.VMEM((cols, levels), F32),
            pltpu.SemaphoreType.DMA((rows // CHUNK,)),
            pltpu.SemaphoreType.DMA((2,)),
        ],
        compiler_params=pltpu.CompilerParams(vmem_limit_bytes=48 * MIB),
        cost_estimate=pl.CostEstimate(
            flops=8 * cells * levels * levels, bytes_accessed=8 * cells * levels, transcendentals=0
        ),
        name="advance",
    )(flags, source_column, labels, state, *halos, mask, mix_atm, mix_ocn, flux_map_t)


BATCH = 8
LABEL_ROWS = 16


def regroup_kernel(count, *refs):
    slabs, blocks = refs[:-count], refs[-count:]
    comp_count = len(slabs)
    capacity = blocks[0].shape[0] // comp_count - LABEL_ROWS // comp_count
    size = count * capacity
    heads = [slab[size : size + LABEL_ROWS, :].astype(F32) for slab in slabs]
    lines = [head[i : i + 1] for i in range(2) for head in heads]
    spare = jnp.zeros((LABEL_ROWS - len(lines), heads[0].shape[1]), F32)
    labels = jnp.concatenate(lines + [spare], axis=0).astype(BF16)
    for n in range(count):
        for s in range(comp_count):
            blocks[n][s * capacity : (s + 1) * capacity, :] = slabs[s][
                n * capacity : (n + 1) * capacity, :
            ]
        blocks[n][comp_count * capacity :, :] = labels


def regroup(slabs, count):
    rows, width = slabs[0].shape
    size = (rows - LABEL_ROWS) // count * len(slabs) + LABEL_ROWS
    vmem = pl.BlockSpec(memory_space=pltpu.VMEM)
    return pl.pallas_call(
        functools.partial(regroup_kernel, count),
        out_shape=(jax.ShapeDtypeStruct((size, width), BF16),) * count,
        in_specs=[vmem] * len(slabs),
        out_specs=(vmem,) * count,
        compiler_params=pltpu.CompilerParams(vmem_limit_bytes=16 * MIB),
        name="regroup",
    )(*slabs)


def regrid_body(count, comp_count, flags, ocean_first, *refs):
    blocks = refs[:count]
    weights, surface, mask, forcing, shared, hits, entries, chosen, binned = refs[count:]
    rows, cols = mask.shape
    share = forcing.shape[0]
    weight_count = weights.shape[0]
    capacity = (blocks[0].shape[0] - LABEL_ROWS) // comp_count
    size = count * capacity
    total = comp_count * size
    width = blocks[0].shape[1]
    for s in range(comp_count):
        for n in range(count):
            start = s * size + n * capacity
            entries[start : start + capacity, :] = blocks[n][s * capacity : (s + 1) * capacity, :]
    lanes = lax.broadcasted_iota(jnp.int32, (LABEL_ROWS, width), 1) // capacity
    labels = jnp.zeros((LABEL_ROWS, width), F32)
    for n in range(count):
        labels = jnp.where(lanes == n, blocks[n][comp_count * capacity :, :].astype(F32), labels)
    labels = labels.astype(jnp.int32)
    weight_line = jnp.concatenate([labels[s : s + 1, :size] for s in range(comp_count)], axis=1)
    target_line = jnp.concatenate(
        [labels[comp_count + s : comp_count + s + 1, :size] for s in range(comp_count)], axis=1
    )
    spots = lax.broadcasted_iota(jnp.int32, (rows, total), 0)
    by_target = jnp.where(target_line == spots, 1.0, 0.0)
    hits[...] = by_target[:, :size].T.astype(BF16)
    by_target = by_target.astype(BF16)
    numbers = lax.broadcasted_iota(jnp.int32, (weight_count, total), 0)
    by_weight = jnp.where(weight_line == numbers, 1.0, 0.0).astype(BF16)
    for g in range(weight_count // BATCH):
        for i in range(BATCH):
            w = g * BATCH + i
            chosen[i * rows : (i + 1) * rows, :] = by_target * by_weight[w : w + 1, :]
        binned[...] = dot_nn(chosen[...], entries[...])
        wide = weights[g * BATCH : (g + 1) * BATCH].reshape(BATCH * cols, cols)
        for f in range(share):
            halves = [
                split_two(binned[i * rows : (i + 1) * rows, f * cols : (f + 1) * cols])
                for i in range(BATCH)
            ]
            part = dot_nn(jnp.concatenate([h for h, _ in halves], axis=1), wide) + dot_nn(
                jnp.concatenate([l for _, l in halves], axis=1), wide
            )
            forcing[f] = part if g == 0 else forcing[f] + part
    change = ocean_first[flags[3] * share] * forcing[0]
    for f in range(1, share):
        change = change + ocean_first[flags[3] * share + f] * forcing[f]
    base = jnp.where(flags[0] == 1, surface[...], 0.0)
    held = jnp.where((mask[...] > 0.5) | (flags[0] == 0), change, 0.0)
    shared[0] = base + held
    shared[1] = mask[...]


def regrid(flags, ocean_first, blocks, comp_count, weights, surface, mask):
    rows, cols = mask.shape
    count = len(blocks)
    height, width = blocks[0].shape
    size = (height - LABEL_ROWS) // comp_count * count
    total = size * comp_count
    share = width // cols
    weight_count = weights.shape[0]
    vmem = pl.BlockSpec(memory_space=pltpu.VMEM)
    smem = pl.BlockSpec(memory_space=pltpu.SMEM)
    return pl.pallas_call(
        functools.partial(regrid_body, count, comp_count),
        out_shape=(
            jax.ShapeDtypeStruct((share, rows, cols), F32),
            jax.ShapeDtypeStruct((2, rows, cols), F32),
            jax.ShapeDtypeStruct((size, rows), BF16),
        ),
        in_specs=[smem, smem] + [vmem] * (count + 3),
        out_specs=(vmem, vmem, vmem),
        scratch_shapes=[
            pltpu.VMEM((total, width), BF16),
            pltpu.VMEM((BATCH * rows, total), BF16),
            pltpu.VMEM((BATCH * rows, width), F32),
        ],
        compiler_params=pltpu.CompilerParams(vmem_limit_bytes=32 * MIB),
        cost_estimate=pl.CostEstimate(
            flops=2 * weight_count * rows * width * (total + 2 * cols),
            bytes_accessed=2 * MIB,
            transcendentals=0,
        ),
        name="regrid",
    )(flags, ocean_first, *blocks, weights, surface, mask)


def pick_kernel(comp_count, *refs):
    flags = refs[0]
    parts = refs[1 : 1 + comp_count]
    hits, surface = refs[1 + comp_count : 3 + comp_count]
    picked = refs[3 + comp_count :]
    rows, cols = surface.shape
    from_ocean = lax.rem(flags[3] + 1, comp_count)
    base = jnp.zeros((rows, cols), F32)
    sea = base
    change = base
    for shift in range(comp_count):
        is_base = from_ocean == shift
        base = base + jnp.where(is_base, parts[shift][0], 0.0)
        sea = sea + jnp.where(is_base, parts[shift][1], 0.0)
        change = change + jnp.where(is_base, 0.0, parts[shift][0])
    now = base + jnp.where(sea > 0.5, change, 0.0)
    surface[...] = now
    pair = jnp.concatenate(split_two(now), axis=0)
    size = picked[0].shape[0]
    for n in range(len(picked)):
        some = hits[n * size : (n + 1) * size, :]
        picked[n][...] = dot_nn(jnp.concatenate([some, some], axis=1), pair)


def pick(flags, parts, hits, neighbours):
    _, rows, cols = parts[0].shape
    size = hits.shape[0] // neighbours
    vmem = pl.BlockSpec(memory_space=pltpu.VMEM)
    smem = pl.BlockSpec(memory_space=pltpu.SMEM)
    return pl.pallas_call(
        functools.partial(pick_kernel, len(parts)),
        out_shape=(jax.ShapeDtypeStruct((rows, cols), F32),)
        + (jax.ShapeDtypeStruct((size, cols), F32),) * neighbours,
        in_specs=[smem] + [vmem] * (len(parts) + 1),
        out_specs=(vmem,) * (1 + neighbours),
        compiler_params=pltpu.CompilerParams(vmem_limit_bytes=16 * MIB),
        name="pick",
    )(flags, *parts, hits)


LINES = 16


def update_kernel(groups, flags, state, *refs):
    parts = refs[:groups]
    mask, ocean_map, out, held, table, wide, in_sems, out_sems = refs[groups:]
    rows, cols, levels = state.shape
    share = parts[0].shape[0]
    flux_count = groups * share
    chunks = rows // LINES
    depth = LINES * flux_count

    def fetch(q):
        return pltpu.make_async_copy(
            state.at[pl.ds(q * LINES, LINES)], held.at[pl.ds(q * LINES, LINES)], in_sems.at[q]
        )

    def put(q):
        return pltpu.make_async_copy(
            held.at[pl.ds(q * LINES, LINES)], out.at[pl.ds(q * LINES, LINES)], out_sems.at[q]
        )

    @pl.when(flags[0] == 1)
    def ocean():
        for q in range(chunks):
            fetch(q).start()
        table[...] = jnp.zeros(table.shape, F32)
        for line in range(LINES):
            for f in range(flux_count):
                spot = f * LINES + line
                table[spot : spot + 1, line * levels : (line + 1) * levels] = ocean_map[f : f + 1]
        high, low = split_two(table[...])
        wide[:depth] = high
        wide[depth : 2 * depth] = high
        wide[2 * depth :] = low

        def one(q, _):
            start = pl.multiple_of(q * LINES, LINES)
            sea = mask[pl.ds(start, LINES), :] > 0.5
            part = jnp.concatenate(
                [
                    jnp.where(sea, parts[f // share][f % share, pl.ds(start, LINES), :], 0.0)
                    for f in range(flux_count)
                ],
                axis=0,
            )
            first, second = split_two(part.T)
            change = dot_nn(jnp.concatenate([first, second, first], axis=1), wide[...])
            fetch(q).wait()
            for line in range(LINES):
                held[start + line] += change[:, line * levels : (line + 1) * levels]
            put(q).start()
            return 0

        lax.fori_loop(0, chunks, one, 0)
        for q in range(chunks):
            put(q).wait()


def update(flags, state, parts, mask, ocean_map):
    rows, cols, levels = state.shape
    depth = LINES * ocean_map.shape[0]
    vmem = pl.BlockSpec(memory_space=pltpu.VMEM)
    smem = pl.BlockSpec(memory_space=pltpu.SMEM)
    hbm = pl.BlockSpec(memory_space=pl.ANY)
    return pl.pallas_call(
        functools.partial(update_kernel, len(parts)),
        out_shape=jax.ShapeDtypeStruct(state.shape, F32),
        in_specs=[smem, hbm] + [vmem] * (len(parts) + 2),
        out_specs=hbm,
        input_output_aliases={1: 0},
        scratch_shapes=[
            pltpu.VMEM(state.shape, F32),
            pltpu.VMEM((depth, LINES * levels), F32),
            pltpu.VMEM((3 * depth, LINES * levels), BF16),
            pltpu.SemaphoreType.DMA((rows // LINES,)),
            pltpu.SemaphoreType.DMA((rows // LINES,)),
        ],
        compiler_params=pltpu.CompilerParams(vmem_limit_bytes=24 * MIB),
        cost_estimate=pl.CostEstimate(
            flops=6 * rows * cols * depth * levels,
            bytes_accessed=8 * rows * cols * levels,
            transcendentals=0,
        ),
        name="update",
    )(flags, state, *parts, mask, ocean_map)


def returned_kernel(groups, flags, *refs):
    picked = refs[:groups]
    weight_column, row_line, weights, mask, surface, new_surface, out, total = refs[groups:]
    rows, cols = mask.shape
    weight_count = weights.shape[0]

    @pl.when(flags[0] == 1)
    def ocean():
        out[...] = new_surface[...]

    @pl.when(flags[0] == 0)
    def atmosphere():
        values = jnp.concatenate([p[...] for p in picked], axis=0)
        pair = side_by_side(values)
        which = jnp.broadcast_to(weight_column[...], values.shape)
        total[...] = jnp.zeros(values.shape, F32)

        def one(i, _):
            both = jnp.concatenate([weights[2 * i], weights[2 * i + 1]], axis=0)
            images = dot_nt(pair, jnp.concatenate([both, both], axis=1))
            total[...] += jnp.where(which == 2 * i, images[:, :cols], 0.0) + jnp.where(
                which == 2 * i + 1, images[:, cols:], 0.0
            )
            return 0

        lax.fori_loop(0, weight_count // 2, one, 0, unroll=2)
        spots = lax.broadcasted_iota(jnp.int32, (rows, values.shape[0]), 0)
        chosen = jnp.where(jnp.broadcast_to(row_line[...], spots.shape) == spots, 1.0, 0.0).astype(BF16)
        high, low = split_two(total[...])
        back = dot_nn(chosen, high) + dot_nn(chosen, low)
        out[...] = jnp.where(mask[...] > 0.5, back, surface[...])


def returned(flags, picked, weight_column, row_line, weights, mask, surface, new_surface):
    rows, cols = mask.shape
    entry_total = weight_column.shape[0]
    vmem = pl.BlockSpec(memory_space=pltpu.VMEM)
    smem = pl.BlockSpec(memory_space=pltpu.SMEM)
    return pl.pallas_call(
        functools.partial(returned_kernel, len(picked)),
        out_shape=jax.ShapeDtypeStruct((rows, cols), F32),
        in_specs=[smem] + [vmem] * (len(picked) + 6),
        out_specs=vmem,
        scratch_shapes=[pltpu.VMEM((entry_total, cols), F32)],
        compiler_params=pltpu.CompilerParams(vmem_limit_bytes=16 * MIB),
        name="returned",
    )(flags, *picked, weight_column, row_line, weights, mask, surface, new_surface)


def local(
    state, land_mask, intersection_list, mix_atm, mix_ocn, flux_map, ocean_map, regrid_weights
):
    rows, cols, levels = state.shape
    intersections = intersection_list.shape[2]
    comp_count = lax.axis_size("comp")
    lat_count = lax.axis_size("lat")
    lon_count = lax.axis_size("lon")
    tile_count = lat_count * lon_count
    reach = min(4, lon_count)
    neighbours = 2 * reach
    entry_total = intersections * rows
    capacity = entry_total // neighbours
    comp_index = lax.axis_index("comp")
    lat_index = lax.axis_index("lat")
    tile_index = lat_index * lon_count + lax.axis_index("lon")
    bands = comp_count * lat_count
    ocean_band = (comp_count - 1) * lat_count
    ocean_comp = comp_count - 1
    band = comp_index * lat_count + lat_index
    is_ocean = comp_index == ocean_comp
    upper_valid = (band > 0) & (band != ocean_band)
    lower_valid = (band < bands - 1) & (band != ocean_band - 1)
    flags = jnp.stack([is_ocean, upper_valid, lower_valid, comp_index]).astype(jnp.int32)
    mask = (land_mask == 1).astype(F32)

    def band_shift(value, by, lon_by):
        pairs = []
        for b in range(bands):
            target = b + by
            if 0 <= target < bands and (b >= ocean_band) == (target >= ocean_band):
                for lon in range(lon_count):
                    pairs.append(
                        (b * lon_count + lon, target * lon_count + (lon + lon_by) % lon_count)
                    )
        return lax.ppermute(value, AXES, pairs)

    first_rows, last_rows, sides, top_corners, low_corners = take_edges(state)
    up_rows = band_shift(last_rows, 1, 0)
    low_rows = band_shift(first_rows, -1, 0)
    if lon_count == 2:
        left_cols = right_cols = band_shift(sides, 0, 1)
        left_at, right_at = 2, 0
    else:
        left_cols = band_shift(sides[2:], 0, 1)
        right_cols = band_shift(sides[:2], 0, -1)
        left_at, right_at = 0, 0
    up_left = band_shift(low_corners, 1, 1)
    low_left = band_shift(top_corners, -1, 1)
    if lon_count == 2:
        up_right, low_right = up_left, low_left
    else:
        up_right = band_shift(low_corners, 1, -1)
        low_right = band_shift(top_corners, -1, -1)

    entry_list = intersection_list.reshape(entry_total, 3)
    owners = entry_list[:, 0]
    labels = entry_list[:, 2] * rows + entry_list[:, 1]
    offsets = [
        (n // reach * lon_count + n % reach - (reach - 1) // 2) % tile_count
        for n in range(neighbours)
    ]
    distance = (owners - tile_index + tile_count) % tile_count
    hits = distance[:, None] == jnp.array(offsets, jnp.int32)[None, :]
    neighbour_ids = jnp.sum(
        jnp.where(hits, jnp.arange(neighbours, dtype=jnp.int32)[None, :], 0), axis=1
    )
    positions = jnp.arange(entry_total, dtype=jnp.int32)
    earlier = (neighbour_ids[None, :] == neighbour_ids[:, None]) & (
        positions[None, :] < positions[:, None]
    )
    slots = neighbour_ids * capacity + jnp.sum(earlier.astype(jnp.int32), axis=1)
    placing = positions[:, None] == slots[None, :]
    sources = jnp.sum(jnp.where(placing, (positions // intersections)[None, :], 0), axis=1)
    packed_labels = jnp.sum(jnp.where(placing, labels[None, :], 0), axis=1)

    def over_comp(value, shift, last):
        pairs = [
            (c * tile_count + t, (c + shift) % comp_count * tile_count + t)
            for c in range(comp_count if last else comp_count - 1)
            for t in range(tile_count)
        ]
        return lax.ppermute(value, AXES, pairs)

    def over_tiles(value, offset):
        if offset % tile_count == 0:
            return value
        pairs = [
            (c * tile_count + t, c * tile_count + (t + offset) % tile_count)
            for c in range(comp_count)
            for t in range(tile_count)
        ]
        return lax.ppermute(value, AXES, pairs)

    def to_ocean(value, comp):
        pairs = [
            (comp * tile_count + t, ocean_comp * tile_count + t) for t in range(tile_count)
        ]
        return lax.ppermute(value, AXES, pairs)

    label_lines = jnp.stack([packed_labels // rows, packed_labels % rows]).astype(BF16)
    label_lines = jnp.pad(label_lines, ((0, LABEL_ROWS - 2), (0, 0)))

    halos = (up_rows, low_rows, left_cols, right_cols, sides)
    halos = halos + (up_left, up_right, low_left, low_right)
    moved = advance(
        flags, sources[:, None], label_lines, state, halos, mask, mix_atm, mix_ocn, flux_map.T,
        comp_count, left_at, right_at,
    )
    moved, surface, packed = moved[0], moved[1], moved[2:]
    slabs = [packed[0]] + [over_comp(packed[s], s, False) for s in range(1, comp_count)]
    blocks = regroup(slabs, neighbours)
    blocks = [over_tiles(blocks[n], offsets[n]) for n in range(neighbours)]
    forcing, shared, hits = regrid(
        flags, ocean_map[:, 0], blocks, comp_count, regrid_weights, surface, mask
    )
    parts = [shared] + [over_comp(shared, s, True) for s in range(1, comp_count)]
    picks = pick(flags, parts, hits, neighbours)
    new_surface, picked = picks[0], picks[1:]
    arrived = [over_tiles(picked[n], -offsets[n]) for n in range(neighbours)]
    fields = [to_ocean(forcing, c) for c in range(comp_count - 1)] + [forcing]
    final_state = update(flags, moved, fields, mask, ocean_map)
    weight_column = (packed_labels // rows)[:, None]
    surface_out = returned(
        flags, arrived, weight_column, sources[None, :], regrid_weights, mask, surface, new_surface
    )
    return (final_state, surface_out)


def solution(mesh):
    placed = (
        P(("comp", "lat"), "lon", None),
        P(("comp", "lat"), "lon"),
        P(("comp", "lat"), "lon", None, None),
        P(),
        P(),
        P(),
        P(),
        P(),
    )
    return jax.shard_map(
        local,
        mesh=mesh,
        in_specs=placed,
        out_specs=(P(("comp", "lat"), "lon", None), P(("comp", "lat"), "lon")),
        check_vma=False,
    )
```

```python
import functools

import jax
import jax.numpy as jnp
from jax import lax
from jax.experimental import pallas as pl
from jax.experimental.pallas import tpu as pltpu
from jax.sharding import PartitionSpec as P

SMOOTHING = 0.2
PHYSICS = 0.5
MIB = 1024 * 1024
F32 = jnp.float32
BF16 = jnp.bfloat16
EDGE = 8
CHUNK = 8
AXES = ("comp", "lat", "lon")


def split_two(x):
    high = x.astype(BF16)
    low = (x - high.astype(F32)).astype(BF16)
    return high, low


def side_by_side(x):
    return jnp.concatenate(split_two(x), axis=1)


def dot_nt(a, b):
    return lax.dot_general(a, b, (((1,), (1,)), ((), ())), preferred_element_type=F32)


def dot_nn(a, b):
    return jnp.dot(a, b, preferred_element_type=F32)


def edges_kernel(state, first_rows, last_rows, sides, left, right, sems):
    rows, cols, _ = state.shape
    copies = [
        pltpu.make_async_copy(state.at[pl.ds(0, 2)], first_rows, sems.at[0]),
        pltpu.make_async_copy(state.at[pl.ds(rows - 2, 2)], last_rows, sems.at[1]),
        pltpu.make_async_copy(state.at[:, pl.ds(0, EDGE)], left, sems.at[2]),
        pltpu.make_async_copy(state.at[:, pl.ds(cols - EDGE, EDGE)], right, sems.at[3]),
    ]
    for copy in copies:
        copy.start()
    for copy in copies:
        copy.wait()
    for i in range(2):
        sides[i] = left[:, i, :]
        sides[2 + i] = right[:, EDGE - 2 + i, :]


def take_edges(state):
    rows, cols, levels = state.shape
    slab = jax.ShapeDtypeStruct((2, cols, levels), F32)
    side = jax.ShapeDtypeStruct((4, rows, levels), F32)
    vmem = pl.BlockSpec(memory_space=pltpu.VMEM)
    return pl.pallas_call(
        edges_kernel,
        out_shape=(slab, slab, side),
        in_specs=[pl.BlockSpec(memory_space=pl.ANY)],
        out_specs=(vmem,) * 3,
        scratch_shapes=[
            pltpu.VMEM((rows, EDGE, levels), F32),
            pltpu.VMEM((rows, EDGE, levels), F32),
            pltpu.SemaphoreType.DMA((4,)),
        ],
        compiler_params=pltpu.CompilerParams(vmem_limit_bytes=56 * MIB),
        name="edges",
    )(state)


def frame_kernel(sides, up_rows, low_rows, framed):
    _, rows, levels = sides.shape
    cols = up_rows.shape[1]
    framed[...] = jnp.zeros(framed.shape, F32)
    for i, col in enumerate((0, 1, cols - 2, cols - 1)):
        framed[i, EDGE : EDGE + rows, :] = sides[i]
        framed[i, EDGE - 1 : EDGE, :] = up_rows[1, col : col + 1, :]
        framed[i, EDGE + rows : EDGE + rows + 1, :] = low_rows[0, col : col + 1, :]


def frame_sides(sides, up_rows, low_rows):
    count, rows, levels = sides.shape
    vmem = pl.BlockSpec(memory_space=pltpu.VMEM)
    return pl.pallas_call(
        frame_kernel,
        out_shape=jax.ShapeDtypeStruct((count, rows + 2 * EDGE, levels), F32),
        in_specs=[vmem] * 3,
        out_specs=vmem,
        compiler_params=pltpu.CompilerParams(vmem_limit_bytes=56 * MIB),
        name="frame",
    )(sides, up_rows, low_rows)


def advance_kernel(comp_count, left_at, right_at, *refs):
    (flags, source_column, labels, state, up_rows, low_rows, left_in, right_in, own_sides) = refs[:9]
    (mask, mix_atm, mix_ocn, flux_map) = refs[9:13]
    out, surface, sea_copy = refs[13:16]
    packed = refs[16 : 16 + comp_count]
    (values, moved, halo_moved, smooth, pairs, mixed, later_smooth, later_pairs, later_mixed) = refs[
        16 + comp_count : 25 + comp_count
    ]
    (weights, flux_weights, fluxes, staged, top, in_sems, out_sems) = refs[25 + comp_count :]
    left_cols = left_in.at[left_at : left_at + 2]
    right_cols = right_in.at[right_at : right_at + 2]
    first = (smooth, pairs, mixed)
    second = (later_smooth, later_pairs, later_mixed)
    rows, cols, levels = state.shape
    chunks = rows // CHUNK
    inner = pl.ds(EDGE, cols)
    flux_count = flux_map.shape[0]

    def fetch(q):
        return pltpu.make_async_copy(
            state.at[pl.ds(q * CHUNK, CHUNK)],
            values.at[pl.ds(q * CHUNK + 2, CHUNK), inner],
            in_sems.at[q],
        )

    def put(q, slot):
        return pltpu.make_async_copy(
            staged.at[slot], out.at[pl.ds(q * CHUNK, CHUNK)], out_sems.at[slot]
        )

    def begin(q, _):
        fetch(q).start()
        return 0

    lax.fori_loop(0, chunks, begin, 0)
    ocean = flags[0] == 1
    mix = jnp.where(ocean, mix_ocn[...], mix_atm[...])
    mix_high, mix_low = split_two(mix)
    weights[:levels, :] = mix_high
    weights[levels : 2 * levels, :] = mix_high
    weights[2 * levels :, :] = mix_low
    sea_copy[...] = mask[...].astype(BF16)
    map_high, map_low = split_two(flux_map[...])
    flux_weights[...] = jnp.concatenate(
        [
            jnp.concatenate([map_high.astype(F32), map_high.astype(F32)], axis=1),
            jnp.concatenate([map_low.astype(F32), map_low.astype(F32)], axis=1),
        ],
        axis=0,
    ).astype(BF16)
    values[0:2, EDGE : EDGE + cols, :] = up_rows[...]
    values[rows + 2 : rows + 4, EDGE : EDGE + cols, :] = low_rows[...]
    for r, i in ((1, EDGE - 1), (rows + 2, EDGE + rows)):
        values[r, EDGE - 1 : EDGE, :] = left_cols[1, i : i + 1, :]
        values[r, EDGE + cols : EDGE + cols + 1, :] = right_cols[0, i : i + 1, :]

    def side_cells(r, _):
        values[r + 2, EDGE - 1 : EDGE, :] = left_cols[1, pl.ds(r + EDGE, 1), :]
        values[r + 2, EDGE + cols : EDGE + cols + 1, :] = right_cols[0, pl.ds(r + EDGE, 1), :]
        return 0

    lax.fori_loop(0, rows, side_cells, 0, unroll=8)

    def stage(refs, row, total):
        line = SMOOTHING * total
        high, low = split_two(line)
        refs[0][row] = line
        refs[1][row * cols : (row + 1) * cols, :] = jnp.concatenate([high, low, high], axis=1)

    def note_top(q, lines):
        lanes = lax.broadcasted_iota(jnp.int32, (cols, levels), 1)
        kept = lines[0]
        for row in range(1, CHUNK):
            kept = jnp.where(lanes == row, pltpu.roll(lines[row], row, 1), kept)
        turned = pltpu.roll(kept, q * CHUNK, 1)
        top[...] = jnp.where(lanes // CHUNK == q, turned, top[...])

    def mix_rows(refs, count):
        refs[2][: count * cols, :] = dot_nn(refs[1][: count * cols, :], weights[...])

    def finish(refs, row):
        return refs[0][row] + PHYSICS * jnp.tanh(refs[2][row * cols : (row + 1) * cols, :])

    def gather_row(ref, i):
        here = ref[i, EDGE : EDGE + cols, :] + (
            ref[i - 1, EDGE : EDGE + cols, :] + ref[i + 1, EDGE : EDGE + cols, :]
        )
        return here + (
            ref[i, EDGE - 1 : EDGE - 1 + cols, :] + ref[i, EDGE + 1 : EDGE + 1 + cols, :]
        )

    @pl.when(jnp.logical_not(ocean))
    def atmosphere():
        nearest = (left_cols.at[1], right_cols.at[0])
        beyond = (left_cols.at[0], right_cols.at[1])
        within = (own_sides.at[0], own_sides.at[3])
        for s in range(2):
            total = (
                nearest[s][EDGE : EDGE + rows, :]
                + nearest[s][EDGE - 1 : EDGE - 1 + rows, :]
                + nearest[s][EDGE + 1 : EDGE + 1 + rows, :]
            )
            stage(first, s, total + (beyond[s][EDGE : EDGE + rows, :] + within[s][...]))
        mix_rows(first, 2)
        for s in range(2):
            halo_moved[s] = finish(first, s)

        def moved_sides(r, _):
            moved[r + 1, EDGE - 1 : EDGE, :] = halo_moved[0, pl.ds(r, 1), :]
            moved[r + 1, EDGE + cols : EDGE + cols + 1, :] = halo_moved[1, pl.ds(r, 1), :]
            return 0

        lax.fori_loop(0, rows, moved_sides, 0, unroll=8)
        fetch(0).wait()
        fetch(1).wait()
        for row in range(2):
            stage(second, row, gather_row(values, row + 1))
        mix_rows(second, 2)
        moved[0, EDGE : EDGE + cols, :] = finish(second, 0)
        moved[1, EDGE : EDGE + cols, :] = finish(second, 1)

        @pl.when(flags[1] == 0)
        def _():
            moved[0, EDGE : EDGE + cols, :] = jnp.zeros((cols, levels), F32)

        def begin_first(q):
            for row in range(CHUNK):
                stage(first, row, gather_row(values, q * CHUNK + row + 3))
            mix_rows(first, CHUNK)

        def end_first(q):
            for row in range(CHUNK):
                moved[q * CHUNK + row + 2, EDGE : EDGE + cols, :] = finish(first, row)

        def begin_second(q):
            for row in range(CHUNK):
                stage(second, row, gather_row(moved, q * CHUNK + row + 1))

        def end_second(q, slot):
            for row in range(CHUNK):
                line = finish(second, row)
                staged[slot, row] = line
                both = line + moved[q * CHUNK + row + 1, EDGE : EDGE + cols, :]
                later_pairs[row * cols : (row + 1) * cols, : 2 * levels] = side_by_side(both)
            put(q, slot).start()
            note_top(q, [staged[slot, row] for row in range(CHUNK)])
            flux = dot_nt(flux_weights[...], later_pairs[:, : 2 * levels])
            flux = flux[:flux_count] + flux[flux_count:]
            for row in range(CHUNK):
                r = q * CHUNK + row
                block = PHYSICS * flux[:, row * cols : (row + 1) * cols]
                sea = jnp.broadcast_to(mask[pl.ds(r, 1), :], block.shape)
                block = jnp.where(sea > 0.5, block, 0.0)
                fluxes[pl.ds(pl.multiple_of(r * flux_count, flux_count), flux_count), :] = block

        begin_first(0)
        end_first(0)

        def one_chunk(q, _):
            @pl.when(q + 1 < chunks)
            def _():
                fetch(q + 1).wait()

            slot = (q - 1) % 2

            @pl.when(q >= 3)
            def _():
                put(q - 3, slot).wait()

            begin_first(q)
            begin_second(q - 1)
            end_first(q)
            mix_rows(second, CHUNK)
            end_second(q - 1, slot)
            return 0

        lax.fori_loop(1, chunks, one_chunk, 0)

        @pl.when(flags[2] == 0)
        def _():
            moved[rows + 1, EDGE : EDGE + cols, :] = jnp.zeros((cols, levels), F32)

        last = chunks - 1
        put(last - 2, last % 2).wait()
        begin_second(last)
        mix_rows(second, CHUNK)
        end_second(last, last % 2)
        put(last - 1, (last - 1) % 2).wait()
        put(last, last % 2).wait()
        spots = lax.broadcasted_iota(jnp.int32, (source_column.shape[0], rows), 1)
        placing = jnp.where(source_column[...] == spots, 1.0, 0.0).astype(BF16)
        share = flux_count // comp_count
        for shift in range(comp_count):
            begin_field = lax.rem(flags[3] + shift, comp_count) * share
            for f in range(share):
                field = fluxes[pl.ds(begin_field + f, rows, stride=flux_count), :].astype(BF16)
                packed[shift][: placing.shape[0], f * cols : (f + 1) * cols] = dot_nn(
                    placing, field
                ).astype(BF16)
            packed[shift][placing.shape[0] :, :] = labels[...]
        surface[...] = top[...].T

    @pl.when(ocean)
    def sea_side():
        fetch(0).wait()
        lanes = lax.broadcasted_iota(jnp.int32, (CHUNK, CHUNK * levels), 1) // levels
        lines = lax.broadcasted_iota(jnp.int32, (CHUNK, CHUNK * levels), 0)
        spreader = jnp.where(lanes == lines, 1.0, 0.0).astype(F32)

        def one_chunk(q, _):
            base = q * CHUNK

            @pl.when(q + 1 < chunks)
            def _():
                fetch(q + 1).wait()

            for row in range(CHUNK):
                stage(first, row, gather_row(values, base + row + 2))
            mix_rows(first, CHUNK)
            slot = q % 2

            @pl.when(q >= 2)
            def _():
                put(q - 2, slot).wait()

            sea = dot_nn(mask[pl.ds(pl.multiple_of(base, CHUNK), CHUNK), :].T, spreader)
            for row in range(CHUNK):
                chosen = sea[:, row * levels : (row + 1) * levels] > 0.5
                before = values[base + row + 2, EDGE : EDGE + cols, :]
                staged[slot, row] = jnp.where(chosen, finish(first, row), before)
            put(q, slot).start()
            note_top(q, [staged[slot, row] for row in range(CHUNK)])
            return 0

        lax.fori_loop(0, chunks, one_chunk, 0)
        put(chunks - 2, (chunks - 2) % 2).wait()
        put(chunks - 1, (chunks - 1) % 2).wait()
        surface[...] = top[...].T
        for shift in range(comp_count):
            packed[shift][...] = jnp.zeros(packed[shift].shape, BF16)


def advance(
    flags, source_column, labels, state, halos, mask, mix_atm, mix_ocn, flux_map_t, comp_count, left_at, right_at
):
    rows, cols, levels = state.shape
    fluxes = flux_map_t.shape[0]
    vmem = pl.BlockSpec(memory_space=pltpu.VMEM)
    smem = pl.BlockSpec(memory_space=pltpu.SMEM)
    hbm = pl.BlockSpec(memory_space=pl.ANY)
    entry = jax.ShapeDtypeStruct(
        (source_column.shape[0] + labels.shape[0], fluxes // comp_count * cols), BF16
    )
    cells = rows * cols
    return pl.pallas_call(
        functools.partial(advance_kernel, comp_count, left_at, right_at),
        out_shape=(
            jax.ShapeDtypeStruct(state.shape, F32),
            jax.ShapeDtypeStruct((rows, cols), F32),
            jax.ShapeDtypeStruct((rows, cols), BF16),
        )
        + (entry,) * comp_count,
        in_specs=[smem, vmem, vmem, hbm] + [vmem] * (len(halos) + 4),
        out_specs=(hbm,) + (vmem,) * (2 + comp_count),
        scratch_shapes=[
            pltpu.VMEM((rows + 4, cols + 2 * EDGE, levels), F32),
            pltpu.VMEM((rows + 2, cols + 2 * EDGE, levels), F32),
            pltpu.VMEM((2, rows, levels), F32),
            pltpu.VMEM((CHUNK, cols, levels), F32),
            pltpu.VMEM((CHUNK * cols, 3 * levels), BF16),
            pltpu.VMEM((CHUNK * cols, levels), F32),
            pltpu.VMEM((CHUNK, cols, levels), F32),
            pltpu.VMEM((CHUNK * cols, 3 * levels), BF16),
            pltpu.VMEM((CHUNK * cols, levels), F32),
            pltpu.VMEM((3 * levels, levels), BF16),
            pltpu.VMEM((2 * fluxes, 2 * levels), BF16),
            pltpu.VMEM((rows * fluxes, cols), F32),
            pltpu.VMEM((2, CHUNK, cols, levels), F32),
            pltpu.VMEM((cols, levels), F32),
            pltpu.SemaphoreType.DMA((rows // CHUNK,)),
            pltpu.SemaphoreType.DMA((2,)),
        ],
        compiler_params=pltpu.CompilerParams(vmem_limit_bytes=48 * MIB),
        cost_estimate=pl.CostEstimate(
            flops=8 * cells * levels * levels, bytes_accessed=8 * cells * levels, transcendentals=0
        ),
        name="advance",
    )(flags, source_column, labels, state, *halos, mask, mix_atm, mix_ocn, flux_map_t)


BATCH = 8
LABEL_ROWS = 16


def regroup_kernel(count, flags, *refs):
    slabs, blocks = refs[:-count], refs[-count:]
    sources = len(slabs) - 1
    capacity = (blocks[0].shape[0] - LABEL_ROWS) // sources
    size = count * capacity

    def chosen(c, start, stop):
        shift = lax.rem(flags[3] - c + len(slabs), len(slabs))
        value = slabs[0][start:stop, :].astype(F32)
        for s in range(1, len(slabs)):
            value = jnp.where(shift == s, slabs[s][start:stop, :].astype(F32), value)
        return value

    heads = [chosen(c, size, size + LABEL_ROWS) for c in range(sources)]
    lines = [head[i : i + 1] for i in range(2) for head in heads]
    spare = jnp.zeros((LABEL_ROWS - len(lines), heads[0].shape[1]), F32)
    labels = jnp.concatenate(lines + [spare], axis=0).astype(BF16)
    for n in range(count):
        for c in range(sources):
            blocks[n][c * capacity : (c + 1) * capacity, :] = chosen(
                c, n * capacity, (n + 1) * capacity
            ).astype(BF16)
        blocks[n][sources * capacity :, :] = labels


def regroup(flags, slabs, count):
    rows, width = slabs[0].shape
    size = (rows - LABEL_ROWS) // count * (len(slabs) - 1) + LABEL_ROWS
    vmem = pl.BlockSpec(memory_space=pltpu.VMEM)
    return pl.pallas_call(
        functools.partial(regroup_kernel, count),
        out_shape=(jax.ShapeDtypeStruct((size, width), BF16),) * count,
        in_specs=[pl.BlockSpec(memory_space=pltpu.SMEM)] + [vmem] * len(slabs),
        out_specs=(vmem,) * count,
        compiler_params=pltpu.CompilerParams(vmem_limit_bytes=16 * MIB),
        name="regroup",
    )(flags, *slabs)


def regrid_body(count, comp_count, flags, ocean_first, *refs):
    blocks = refs[:count]
    seas = refs[count : count + comp_count]
    weights, surface, mask, forcing, shared, hits, entries, chosen, binned = refs[count + comp_count :]
    sources = comp_count - 1
    rows, cols = mask.shape
    share = forcing.shape[0]
    weight_count = weights.shape[0]
    capacity = (blocks[0].shape[0] - LABEL_ROWS) // sources
    size = count * capacity
    total = sources * size
    width = blocks[0].shape[1]
    for c in range(sources):
        for n in range(count):
            start = c * size + n * capacity
            entries[start : start + capacity, :] = blocks[n][c * capacity : (c + 1) * capacity, :]
    lanes = lax.broadcasted_iota(jnp.int32, (LABEL_ROWS, width), 1) // capacity
    labels = jnp.zeros((LABEL_ROWS, width), F32)
    for n in range(count):
        labels = jnp.where(lanes == n, blocks[n][sources * capacity :, :].astype(F32), labels)
    labels = labels.astype(jnp.int32)
    weight_line = jnp.concatenate([labels[c : c + 1, :size] for c in range(sources)], axis=1)
    target_line = jnp.concatenate(
        [labels[sources + c : sources + c + 1, :size] for c in range(sources)], axis=1
    )
    spots = lax.broadcasted_iota(jnp.int32, (rows, total), 0)
    by_target = jnp.where(target_line == spots, 1.0, 0.0)
    own = by_target[:, :size]
    for c in range(1, sources):
        own = jnp.where(flags[3] == c, by_target[:, c * size : (c + 1) * size], own)
    hits[...] = own.T.astype(BF16)
    by_target = by_target.astype(BF16)
    numbers = lax.broadcasted_iota(jnp.int32, (weight_count, total), 0)
    by_weight = jnp.where(weight_line == numbers, 1.0, 0.0).astype(BF16)
    for g in range(weight_count // BATCH):
        for i in range(BATCH):
            w = g * BATCH + i
            chosen[i * rows : (i + 1) * rows, :] = by_target * by_weight[w : w + 1, :]
        binned[...] = dot_nn(chosen[...], entries[...])
        wide = weights[g * BATCH : (g + 1) * BATCH].reshape(BATCH * cols, cols)
        for f in range(share):
            halves = [
                split_two(binned[i * rows : (i + 1) * rows, f * cols : (f + 1) * cols])
                for i in range(BATCH)
            ]
            part = dot_nn(jnp.concatenate([h for h, _ in halves], axis=1), wide) + dot_nn(
                jnp.concatenate([l for _, l in halves], axis=1), wide
            )
            forcing[f] = part if g == 0 else forcing[f] + part
    change = ocean_first[flags[3] * share] * forcing[0]
    for f in range(1, share):
        change = change + ocean_first[flags[3] * share + f] * forcing[f]
    sea = jnp.where(flags[0] == 1, seas[sources][...].astype(F32), 0.0)
    for c in range(sources):
        sea = sea + jnp.where(flags[3] == c, seas[c][...].astype(F32), 0.0)
    base = jnp.where(flags[0] == 1, surface[...], 0.0)
    shared[...] = base + jnp.where(sea > 0.5, change, 0.0)


def regrid(flags, ocean_first, blocks, seas, weights, surface, mask):
    comp_count = len(seas)
    sources = comp_count - 1
    rows, cols = mask.shape
    count = len(blocks)
    height, width = blocks[0].shape
    size = (height - LABEL_ROWS) // sources * count
    total = size * sources
    share = width // cols
    weight_count = weights.shape[0]
    vmem = pl.BlockSpec(memory_space=pltpu.VMEM)
    smem = pl.BlockSpec(memory_space=pltpu.SMEM)
    return pl.pallas_call(
        functools.partial(regrid_body, count, comp_count),
        out_shape=(
            jax.ShapeDtypeStruct((share, rows, cols), F32),
            jax.ShapeDtypeStruct((rows, cols), F32),
            jax.ShapeDtypeStruct((size, rows), BF16),
        ),
        in_specs=[smem, smem] + [vmem] * (count + comp_count + 3),
        out_specs=(vmem, vmem, vmem),
        scratch_shapes=[
            pltpu.VMEM((total, width), BF16),
            pltpu.VMEM((BATCH * rows, total), BF16),
            pltpu.VMEM((BATCH * rows, width), F32),
        ],
        compiler_params=pltpu.CompilerParams(vmem_limit_bytes=32 * MIB),
        cost_estimate=pl.CostEstimate(
            flops=2 * weight_count * rows * width * (total + 2 * cols),
            bytes_accessed=2 * MIB,
            transcendentals=0,
        ),
        name="regrid",
    )(flags, ocean_first, *blocks, *seas, weights, surface, mask)


def pick_kernel(count, *refs):
    parts = refs[:count]
    hits, surface = refs[count : count + 2]
    picked = refs[count + 2 :]
    now = parts[0][...]
    for part in parts[1:]:
        now = now + part[...]
    surface[...] = now
    pair = jnp.concatenate(split_two(now), axis=0)
    size = picked[0].shape[0]
    for n in range(len(picked)):
        some = hits[n * size : (n + 1) * size, :]
        picked[n][...] = dot_nn(jnp.concatenate([some, some], axis=1), pair)


def pick(parts, hits, neighbours):
    rows, cols = parts[0].shape
    size = hits.shape[0] // neighbours
    vmem = pl.BlockSpec(memory_space=pltpu.VMEM)
    return pl.pallas_call(
        functools.partial(pick_kernel, len(parts)),
        out_shape=(jax.ShapeDtypeStruct((rows, cols), F32),)
        + (jax.ShapeDtypeStruct((size, cols), F32),) * neighbours,
        in_specs=[vmem] * (len(parts) + 1),
        out_specs=(vmem,) * (1 + neighbours),
        compiler_params=pltpu.CompilerParams(vmem_limit_bytes=16 * MIB),
        name="pick",
    )(*parts, hits)


LINES = 8


def update_kernel(groups, flags, state, *refs):
    parts = refs[:groups]
    mask, ocean_map, out, held, table, wide, in_sems, out_sems = refs[groups:]
    rows, cols, levels = state.shape
    share = parts[0].shape[0]
    flux_count = groups * share
    chunks = rows // LINES
    depth = LINES * flux_count

    def fetch(q):
        return pltpu.make_async_copy(
            state.at[pl.ds(q * LINES, LINES)], held.at[pl.ds(q * LINES, LINES)], in_sems.at[q]
        )

    def put(q):
        return pltpu.make_async_copy(
            held.at[pl.ds(q * LINES, LINES)], out.at[pl.ds(q * LINES, LINES)], out_sems.at[q]
        )

    @pl.when(flags[0] == 1)
    def ocean():
        for q in range(chunks):
            fetch(q).start()
        table[...] = jnp.zeros(table.shape, F32)
        for line in range(LINES):
            for f in range(flux_count):
                spot = f * LINES + line
                table[spot : spot + 1, line * levels : (line + 1) * levels] = ocean_map[f : f + 1]
        high, low = split_two(table[...])
        wide[:depth] = high
        wide[depth : 2 * depth] = high
        wide[2 * depth :] = low

        def one(q, _):
            start = pl.multiple_of(q * LINES, LINES)
            sea = mask[pl.ds(start, LINES), :] > 0.5
            part = jnp.concatenate(
                [
                    jnp.where(sea, parts[f // share][f % share, pl.ds(start, LINES), :], 0.0)
                    for f in range(flux_count)
                ],
                axis=0,
            )
            rough = part.astype(BF16).astype(F32)
            turned = jnp.concatenate([rough, part - rough, rough], axis=0).T.astype(BF16)
            change = dot_nn(turned, wide[...])
            fetch(q).wait()
            for line in range(LINES):
                held[start + line] += change[:, line * levels : (line + 1) * levels]
            put(q).start()
            return 0

        lax.fori_loop(0, chunks, one, 0, unroll=2)
        for q in range(chunks):
            put(q).wait()


def update(flags, state, parts, mask, ocean_map):
    rows, cols, levels = state.shape
    depth = LINES * ocean_map.shape[0]
    vmem = pl.BlockSpec(memory_space=pltpu.VMEM)
    smem = pl.BlockSpec(memory_space=pltpu.SMEM)
    hbm = pl.BlockSpec(memory_space=pl.ANY)
    return pl.pallas_call(
        functools.partial(update_kernel, len(parts)),
        out_shape=jax.ShapeDtypeStruct(state.shape, F32),
        in_specs=[smem, hbm] + [vmem] * (len(parts) + 2),
        out_specs=hbm,
        input_output_aliases={1: 0},
        scratch_shapes=[
            pltpu.VMEM(state.shape, F32),
            pltpu.VMEM((depth, LINES * levels), F32),
            pltpu.VMEM((3 * depth, LINES * levels), BF16),
            pltpu.SemaphoreType.DMA((rows // LINES,)),
            pltpu.SemaphoreType.DMA((rows // LINES,)),
        ],
        compiler_params=pltpu.CompilerParams(vmem_limit_bytes=24 * MIB),
        cost_estimate=pl.CostEstimate(
            flops=6 * rows * cols * depth * levels,
            bytes_accessed=8 * rows * cols * levels,
            transcendentals=0,
        ),
        name="update",
    )(flags, state, *parts, mask, ocean_map)


def returned_kernel(groups, flags, *refs):
    picked = refs[:groups]
    weight_column, row_line, weights, mask, surface, new_surface, out, total = refs[groups:]
    rows, cols = mask.shape
    weight_count = weights.shape[0]

    @pl.when(flags[0] == 1)
    def ocean():
        out[...] = new_surface[...]

    @pl.when(flags[0] == 0)
    def atmosphere():
        values = jnp.concatenate([p[...] for p in picked], axis=0)
        pair = side_by_side(values)
        which = jnp.broadcast_to(weight_column[...], values.shape)
        total[...] = jnp.zeros(values.shape, F32)

        def one(i, _):
            both = jnp.concatenate([weights[2 * i], weights[2 * i + 1]], axis=0)
            images = dot_nt(pair, jnp.concatenate([both, both], axis=1))
            total[...] += jnp.where(which == 2 * i, images[:, :cols], 0.0) + jnp.where(
                which == 2 * i + 1, images[:, cols:], 0.0
            )
            return 0

        lax.fori_loop(0, weight_count // 2, one, 0, unroll=8)
        spots = lax.broadcasted_iota(jnp.int32, (rows, values.shape[0]), 0)
        chosen = jnp.where(jnp.broadcast_to(row_line[...], spots.shape) == spots, 1.0, 0.0).astype(BF16)
        high, low = split_two(total[...])
        back = dot_nn(chosen, high) + dot_nn(chosen, low)
        out[...] = jnp.where(mask[...] > 0.5, back, surface[...])


def returned(flags, picked, weight_column, row_line, weights, mask, surface, new_surface):
    rows, cols = mask.shape
    entry_total = weight_column.shape[0]
    vmem = pl.BlockSpec(memory_space=pltpu.VMEM)
    smem = pl.BlockSpec(memory_space=pltpu.SMEM)
    return pl.pallas_call(
        functools.partial(returned_kernel, len(picked)),
        out_shape=jax.ShapeDtypeStruct((rows, cols), F32),
        in_specs=[smem] + [vmem] * (len(picked) + 6),
        out_specs=vmem,
        scratch_shapes=[pltpu.VMEM((entry_total, cols), F32)],
        compiler_params=pltpu.CompilerParams(vmem_limit_bytes=16 * MIB),
        name="returned",
    )(flags, *picked, weight_column, row_line, weights, mask, surface, new_surface)


def local(
    state, land_mask, intersection_list, mix_atm, mix_ocn, flux_map, ocean_map, regrid_weights
):
    rows, cols, levels = state.shape
    intersections = intersection_list.shape[2]
    comp_count = lax.axis_size("comp")
    lat_count = lax.axis_size("lat")
    lon_count = lax.axis_size("lon")
    tile_count = lat_count * lon_count
    reach = min(4, lon_count)
    neighbours = 2 * reach
    entry_total = intersections * rows
    capacity = entry_total // neighbours
    comp_index = lax.axis_index("comp")
    lat_index = lax.axis_index("lat")
    tile_index = lat_index * lon_count + lax.axis_index("lon")
    bands = comp_count * lat_count
    ocean_band = (comp_count - 1) * lat_count
    ocean_comp = comp_count - 1
    band = comp_index * lat_count + lat_index
    is_ocean = comp_index == ocean_comp
    upper_valid = (band > 0) & (band != ocean_band)
    lower_valid = (band < bands - 1) & (band != ocean_band - 1)
    flags = jnp.stack([is_ocean, upper_valid, lower_valid, comp_index]).astype(jnp.int32)
    mask = (land_mask == 1).astype(F32)

    def band_shift(value, by, lon_by):
        pairs = []
        for b in range(bands):
            target = b + by
            if 0 <= target < bands and (b >= ocean_band) == (target >= ocean_band):
                for lon in range(lon_count):
                    pairs.append(
                        (b * lon_count + lon, target * lon_count + (lon + lon_by) % lon_count)
                    )
        return lax.ppermute(value, AXES, pairs)

    first_rows, last_rows, sides = take_edges(state)
    up_rows = band_shift(last_rows, 1, 0)
    low_rows = band_shift(first_rows, -1, 0)
    framed = frame_sides(sides, up_rows, low_rows)
    if lon_count == 2:
        left_cols = right_cols = band_shift(framed, 0, 1)
        left_at, right_at = 2, 0
    else:
        left_cols = band_shift(framed[2:], 0, 1)
        right_cols = band_shift(framed[:2], 0, -1)
        left_at, right_at = 0, 0

    entry_list = intersection_list.reshape(entry_total, 3)
    owners = entry_list[:, 0]
    labels = entry_list[:, 2] * rows + entry_list[:, 1]
    offsets = [
        (n // reach * lon_count + n % reach - (reach - 1) // 2) % tile_count
        for n in range(neighbours)
    ]
    distance = (owners - tile_index + tile_count) % tile_count
    hits = distance[:, None] == jnp.array(offsets, jnp.int32)[None, :]
    neighbour_ids = jnp.sum(
        jnp.where(hits, jnp.arange(neighbours, dtype=jnp.int32)[None, :], 0), axis=1
    )
    positions = jnp.arange(entry_total, dtype=jnp.int32)
    earlier = (neighbour_ids[None, :] == neighbour_ids[:, None]) & (
        positions[None, :] < positions[:, None]
    )
    slots = neighbour_ids * capacity + jnp.sum(earlier.astype(jnp.int32), axis=1)
    placing = positions[:, None] == slots[None, :]
    sources = jnp.sum(jnp.where(placing, (positions // intersections)[None, :], 0), axis=1)
    packed_labels = jnp.sum(jnp.where(placing, labels[None, :], 0), axis=1)

    def over_comp(value, shift, last):
        pairs = [
            (c * tile_count + t, (c + shift) % comp_count * tile_count + t)
            for c in range(comp_count if last else comp_count - 1)
            for t in range(tile_count)
        ]
        return lax.ppermute(value, AXES, pairs)

    def over_tiles(value, offset, comps):
        if offset % tile_count == 0:
            return value
        pairs = [
            (c * tile_count + t, c * tile_count + (t + offset) % tile_count)
            for c in range(comps)
            for t in range(tile_count)
        ]
        return lax.ppermute(value, AXES, pairs)

    def with_ocean(value, comp, back):
        pairs = [
            (comp * tile_count + t, ocean_comp * tile_count + t) for t in range(tile_count)
        ]
        if back:
            pairs = [(there, here) for here, there in pairs]
        return lax.ppermute(value, AXES, pairs)

    label_lines = jnp.stack([packed_labels // rows, packed_labels % rows]).astype(BF16)
    label_lines = jnp.pad(label_lines, ((0, LABEL_ROWS - 2), (0, 0)))

    halos = (up_rows, low_rows, left_cols, right_cols, sides)
    moved = advance(
        flags, sources[:, None], label_lines, state, halos, mask, mix_atm, mix_ocn, flux_map.T,
        comp_count, left_at, right_at,
    )
    moved, surface, sea_copy, packed = moved[0], moved[1], moved[2], moved[3:]
    slabs = [packed[0]] + [over_comp(packed[s], s, False) for s in range(1, comp_count)]
    seas = [with_ocean(sea_copy, c, True) for c in range(ocean_comp)] + [sea_copy]
    blocks = regroup(flags, slabs, neighbours)
    blocks = [over_tiles(blocks[n], offsets[n], comp_count) for n in range(neighbours)]
    forcing, shared, hits = regrid(
        flags, ocean_map[:, 0], blocks, seas, regrid_weights, surface, mask
    )
    parts = [shared] + [over_comp(shared, s, True) for s in range(1, comp_count)]
    picks = pick(parts, hits, neighbours)
    new_surface, picked = picks[0], picks[1:]
    arrived = [over_tiles(picked[n], -offsets[n], ocean_comp) for n in range(neighbours)]
    fields = [with_ocean(forcing, c, False) for c in range(ocean_comp)] + [forcing]
    final_state = update(flags, moved, fields, mask, ocean_map)
    weight_column = (packed_labels // rows)[:, None]
    surface_out = returned(
        flags, arrived, weight_column, sources[None, :], regrid_weights, mask, surface, new_surface
    )
    return (final_state, surface_out)


def solution(mesh):
    placed = (
        P(("comp", "lat"), "lon", None),
        P(("comp", "lat"), "lon"),
        P(("comp", "lat"), "lon", None, None),
        P(),
        P(),
        P(),
        P(),
        P(),
    )
    return jax.shard_map(
        local,
        mesh=mesh,
        in_specs=placed,
        out_specs=(P(("comp", "lat"), "lon", None), P(("comp", "lat"), "lon")),
        check_vma=False,
    )
```

```python
import functools

import jax
import jax.numpy as jnp
from jax import lax
from jax.experimental import pallas as pl
from jax.experimental.pallas import tpu as pltpu
from jax.sharding import PartitionSpec as P

SMOOTHING = 0.2
PHYSICS = 0.5
MIB = 1024 * 1024
F32 = jnp.float32
BF16 = jnp.bfloat16
EDGE = 8
CHUNK = 8
AXES = ("comp", "lat", "lon")


def split_two(x):
    high = x.astype(BF16)
    low = (x - high.astype(F32)).astype(BF16)
    return high, low


def side_by_side(x):
    return jnp.concatenate(split_two(x), axis=1)


def dot_nt(a, b):
    return lax.dot_general(a, b, (((1,), (1,)), ((), ())), preferred_element_type=F32)


def dot_nn(a, b):
    return jnp.dot(a, b, preferred_element_type=F32)


def edges_kernel(state, first_rows, last_rows, sides, top, bottom, left, right, sems):
    rows, cols, _ = state.shape
    copies = [
        pltpu.make_async_copy(state.at[pl.ds(0, 2)], top, sems.at[0]),
        pltpu.make_async_copy(state.at[pl.ds(rows - 2, 2)], bottom, sems.at[1]),
        pltpu.make_async_copy(state.at[:, pl.ds(0, EDGE)], left, sems.at[2]),
        pltpu.make_async_copy(state.at[:, pl.ds(cols - EDGE, EDGE)], right, sems.at[3]),
    ]
    for copy in copies:
        copy.start()
    for copy in copies:
        copy.wait()
    first_rows[...] = top[...].astype(BF16)
    last_rows[...] = bottom[...].astype(BF16)
    for i in range(2):
        sides[i] = left[:, i, :]
        sides[2 + i] = right[:, EDGE - 2 + i, :]


def take_edges(state):
    rows, cols, levels = state.shape
    slab = jax.ShapeDtypeStruct((2, cols, levels), BF16)
    side = jax.ShapeDtypeStruct((4, rows, levels), F32)
    vmem = pl.BlockSpec(memory_space=pltpu.VMEM)
    return pl.pallas_call(
        edges_kernel,
        out_shape=(slab, slab, side),
        in_specs=[pl.BlockSpec(memory_space=pltpu.HBM)],
        out_specs=(vmem,) * 3,
        scratch_shapes=[
            pltpu.VMEM((2, cols, levels), F32),
            pltpu.VMEM((2, cols, levels), F32),
            pltpu.VMEM((rows, EDGE, levels), F32),
            pltpu.VMEM((rows, EDGE, levels), F32),
            pltpu.SemaphoreType.DMA((4,)),
        ],
        compiler_params=pltpu.CompilerParams(vmem_limit_bytes=16 * MIB),
        name="edges",
    )(state)


def frame_kernel(sides, up_rows, low_rows, framed):
    _, rows, levels = sides.shape
    cols = up_rows.shape[1]
    framed[...] = jnp.zeros(framed.shape, F32)
    above = up_rows[1].astype(F32)
    below = low_rows[0].astype(F32)
    for i, col in enumerate((0, 1, cols - 2, cols - 1)):
        framed[i, EDGE : EDGE + rows, :] = sides[i]
        framed[i, EDGE - 1 : EDGE, :] = above[col : col + 1, :]
        framed[i, EDGE + rows : EDGE + rows + 1, :] = below[col : col + 1, :]


def frame_sides(sides, up_rows, low_rows):
    count, rows, levels = sides.shape
    vmem = pl.BlockSpec(memory_space=pltpu.VMEM)
    return pl.pallas_call(
        frame_kernel,
        out_shape=jax.ShapeDtypeStruct((count, rows + 2 * EDGE, levels), F32),
        in_specs=[vmem] * 3,
        out_specs=vmem,
        compiler_params=pltpu.CompilerParams(vmem_limit_bytes=16 * MIB),
        name="frame",
    )(sides, up_rows, low_rows)


def advance_kernel(comp_count, left_at, right_at, *refs):
    (flags, source_column, labels, state, up_rows, low_rows, left_in, right_in, own_sides) = refs[:9]
    (mask, mix_atm, mix_ocn, flux_map) = refs[9:13]
    out, surface, sea_copy = refs[13:16]
    packed = refs[16 : 16 + comp_count]
    (values, moved, halo_moved, smooth, pairs, mixed, later_smooth, later_pairs, later_mixed) = refs[
        16 + comp_count : 25 + comp_count
    ]
    (weights, flux_weights, fluxes, staged, top, in_sems, out_sems) = refs[25 + comp_count :]
    left_cols = left_in.at[left_at : left_at + 2]
    right_cols = right_in.at[right_at : right_at + 2]
    first = (smooth, pairs, mixed)
    second = (later_smooth, later_pairs, later_mixed)
    rows, cols, levels = state.shape
    chunks = rows // CHUNK
    inner = pl.ds(EDGE, cols)
    flux_count = flux_map.shape[0]

    def fetch(q):
        return pltpu.make_async_copy(
            state.at[pl.ds(q * CHUNK, CHUNK)],
            values.at[pl.ds(q * CHUNK + 2, CHUNK), inner],
            in_sems.at[q],
        )

    def put(q, slot):
        return pltpu.make_async_copy(
            staged.at[slot], out.at[pl.ds(q * CHUNK, CHUNK)], out_sems.at[slot]
        )

    def begin(q, _):
        fetch(q).start()
        return 0

    lax.fori_loop(0, chunks, begin, 0)
    ocean = flags[0] == 1
    mix = jnp.where(ocean, mix_ocn[...], mix_atm[...])
    mix_high, mix_low = split_two(mix)
    weights[:levels, :levels] = mix_high
    weights[levels:, :levels] = mix_high
    weights[:levels, levels:] = mix_low
    weights[levels:, levels:] = mix_low
    sea_copy[...] = mask[...].astype(BF16)
    map_high, map_low = split_two(flux_map[...])
    flux_weights[...] = jnp.concatenate(
        [
            jnp.concatenate([map_high.astype(F32), map_high.astype(F32)], axis=1),
            jnp.concatenate([map_low.astype(F32), map_low.astype(F32)], axis=1),
        ],
        axis=0,
    ).astype(BF16)
    values[0:2, EDGE : EDGE + cols, :] = up_rows[...].astype(F32)
    values[rows + 2 : rows + 4, EDGE : EDGE + cols, :] = low_rows[...].astype(F32)
    for r, i in ((1, EDGE - 1), (rows + 2, EDGE + rows)):
        values[r, EDGE - 1 : EDGE, :] = left_cols[1, i : i + 1, :]
        values[r, EDGE + cols : EDGE + cols + 1, :] = right_cols[0, i : i + 1, :]

    def side_cells(r, _):
        values[r + 2, EDGE - 1 : EDGE, :] = left_cols[1, pl.ds(r + EDGE, 1), :]
        values[r + 2, EDGE + cols : EDGE + cols + 1, :] = right_cols[0, pl.ds(r + EDGE, 1), :]
        return 0

    lax.fori_loop(0, rows, side_cells, 0, unroll=8)

    def stage(refs, row, total):
        line = SMOOTHING * total
        refs[0][row] = line
        refs[1][row * cols : (row + 1) * cols, :] = side_by_side(line)

    def note_top(q, lines):
        lanes = lax.broadcasted_iota(jnp.int32, (cols, levels), 1)
        kept = lines[0]
        for row in range(1, CHUNK):
            kept = jnp.where(lanes == row, pltpu.roll(lines[row], row, 1), kept)
        turned = pltpu.roll(kept, q * CHUNK, 1)
        top[...] = jnp.where(lanes // CHUNK == q, turned, top[...])

    def mix_rows(refs, count):
        refs[2][: count * cols, :] = dot_nn(refs[1][: count * cols, :], weights[...])

    def finish(refs, row):
        part = refs[2][row * cols : (row + 1) * cols, :]
        return refs[0][row] + PHYSICS * jnp.tanh(part[:, :levels] + part[:, levels:])

    def gather_row(ref, i):
        here = ref[i, EDGE : EDGE + cols, :] + (
            ref[i - 1, EDGE : EDGE + cols, :] + ref[i + 1, EDGE : EDGE + cols, :]
        )
        return here + (
            ref[i, EDGE - 1 : EDGE - 1 + cols, :] + ref[i, EDGE + 1 : EDGE + 1 + cols, :]
        )

    @pl.when(jnp.logical_not(ocean))
    def atmosphere():
        nearest = (left_cols.at[1], right_cols.at[0])
        beyond = (left_cols.at[0], right_cols.at[1])
        within = (own_sides.at[0], own_sides.at[3])
        for s in range(2):
            total = (
                nearest[s][EDGE : EDGE + rows, :]
                + nearest[s][EDGE - 1 : EDGE - 1 + rows, :]
                + nearest[s][EDGE + 1 : EDGE + 1 + rows, :]
            )
            stage(first, s, total + (beyond[s][EDGE : EDGE + rows, :] + within[s][...]))
        mix_rows(first, 2)
        for s in range(2):
            halo_moved[s] = finish(first, s)

        def moved_sides(r, _):
            moved[r + 1, EDGE - 1 : EDGE, :] = halo_moved[0, pl.ds(r, 1), :]
            moved[r + 1, EDGE + cols : EDGE + cols + 1, :] = halo_moved[1, pl.ds(r, 1), :]
            return 0

        lax.fori_loop(0, rows, moved_sides, 0, unroll=8)
        fetch(0).wait()
        fetch(1).wait()
        for row in range(2):
            stage(second, row, gather_row(values, row + 1))
        mix_rows(second, 2)
        moved[0, EDGE : EDGE + cols, :] = finish(second, 0)
        moved[1, EDGE : EDGE + cols, :] = finish(second, 1)

        @pl.when(flags[1] == 0)
        def _():
            moved[0, EDGE : EDGE + cols, :] = jnp.zeros((cols, levels), F32)

        def begin_first(q):
            for row in range(CHUNK):
                stage(first, row, gather_row(values, q * CHUNK + row + 3))
            mix_rows(first, CHUNK)

        def end_first(q):
            for row in range(CHUNK):
                moved[q * CHUNK + row + 2, EDGE : EDGE + cols, :] = finish(first, row)

        def begin_second(q):
            for row in range(CHUNK):
                stage(second, row, gather_row(moved, q * CHUNK + row + 1))

        def end_second(q, slot):
            for row in range(CHUNK):
                line = finish(second, row)
                staged[slot, row] = line
                both = line + moved[q * CHUNK + row + 1, EDGE : EDGE + cols, :]
                later_pairs[row * cols : (row + 1) * cols, :] = side_by_side(both)
            put(q, slot).start()
            note_top(q, [staged[slot, row] for row in range(CHUNK)])
            flux = dot_nt(flux_weights[...], later_pairs[...])
            flux = flux[:flux_count] + flux[flux_count:]
            for row in range(CHUNK):
                r = q * CHUNK + row
                block = PHYSICS * flux[:, row * cols : (row + 1) * cols]
                sea = jnp.broadcast_to(mask[pl.ds(r, 1), :], block.shape)
                block = jnp.where(sea > 0.5, block, 0.0)
                fluxes[pl.ds(pl.multiple_of(r * flux_count, flux_count), flux_count), :] = block

        begin_first(0)
        end_first(0)

        def one_chunk(q, _):
            @pl.when(q + 1 < chunks)
            def _():
                fetch(q + 1).wait()

            slot = (q - 1) % 2

            @pl.when(q >= 3)
            def _():
                put(q - 3, slot).wait()

            begin_first(q)
            begin_second(q - 1)
            end_first(q)
            mix_rows(second, CHUNK)
            end_second(q - 1, slot)
            return 0

        lax.fori_loop(1, chunks, one_chunk, 0)

        @pl.when(flags[2] == 0)
        def _():
            moved[rows + 1, EDGE : EDGE + cols, :] = jnp.zeros((cols, levels), F32)

        last = chunks - 1
        put(last - 2, last % 2).wait()
        begin_second(last)
        mix_rows(second, CHUNK)
        end_second(last, last % 2)
        put(last - 1, (last - 1) % 2).wait()
        put(last, last % 2).wait()
        spots = lax.broadcasted_iota(jnp.int32, (source_column.shape[0], rows), 1)
        placing = jnp.where(source_column[...] == spots, 1.0, 0.0).astype(BF16)
        share = flux_count // comp_count
        for shift in range(comp_count):
            begin_field = lax.rem(flags[3] + shift, comp_count) * share
            for f in range(share):
                field = fluxes[pl.ds(begin_field + f, rows, stride=flux_count), :].astype(BF16)
                packed[shift][: placing.shape[0], f * cols : (f + 1) * cols] = dot_nn(
                    placing, field
                ).astype(BF16)
            packed[shift][placing.shape[0] :, :] = labels[...]
        surface[...] = top[...].T

    @pl.when(ocean)
    def sea_side():
        fetch(0).wait()
        lanes = lax.broadcasted_iota(jnp.int32, (CHUNK, CHUNK * levels), 1) // levels
        lines = lax.broadcasted_iota(jnp.int32, (CHUNK, CHUNK * levels), 0)
        spreader = jnp.where(lanes == lines, 1.0, 0.0).astype(F32)

        def one_chunk(q, _):
            base = q * CHUNK

            @pl.when(q + 1 < chunks)
            def _():
                fetch(q + 1).wait()

            for row in range(CHUNK):
                stage(first, row, gather_row(values, base + row + 2))
            mix_rows(first, CHUNK)
            slot = q % 2

            @pl.when(q >= 2)
            def _():
                put(q - 2, slot).wait()

            sea = dot_nn(mask[pl.ds(pl.multiple_of(base, CHUNK), CHUNK), :].T, spreader)
            for row in range(CHUNK):
                chosen = sea[:, row * levels : (row + 1) * levels] > 0.5
                before = values[base + row + 2, EDGE : EDGE + cols, :]
                staged[slot, row] = jnp.where(chosen, finish(first, row), before)
            put(q, slot).start()
            note_top(q, [staged[slot, row] for row in range(CHUNK)])
            return 0

        lax.fori_loop(0, chunks, one_chunk, 0)
        put(chunks - 2, (chunks - 2) % 2).wait()
        put(chunks - 1, (chunks - 1) % 2).wait()
        surface[...] = top[...].T
        for shift in range(comp_count):
            packed[shift][...] = jnp.zeros(packed[shift].shape, BF16)


def advance(
    flags, source_column, labels, state, halos, mask, mix_atm, mix_ocn, flux_map_t, comp_count, left_at, right_at
):
    rows, cols, levels = state.shape
    fluxes = flux_map_t.shape[0]
    vmem = pl.BlockSpec(memory_space=pltpu.VMEM)
    smem = pl.BlockSpec(memory_space=pltpu.SMEM)
    hbm = pl.BlockSpec(memory_space=pltpu.HBM)
    entry = jax.ShapeDtypeStruct(
        (source_column.shape[0] + labels.shape[0], fluxes // comp_count * cols), BF16
    )
    cells = rows * cols
    return pl.pallas_call(
        functools.partial(advance_kernel, comp_count, left_at, right_at),
        out_shape=(
            jax.ShapeDtypeStruct(state.shape, F32),
            jax.ShapeDtypeStruct((rows, cols), F32),
            jax.ShapeDtypeStruct((rows, cols), BF16),
        )
        + (entry,) * comp_count,
        in_specs=[smem, vmem, vmem, hbm] + [vmem] * (len(halos) + 4),
        out_specs=(hbm,) + (vmem,) * (2 + comp_count),
        scratch_shapes=[
            pltpu.VMEM((rows + 4, cols + 2 * EDGE, levels), F32),
            pltpu.VMEM((rows + 2, cols + 2 * EDGE, levels), F32),
            pltpu.VMEM((2, rows, levels), F32),
            pltpu.VMEM((CHUNK, cols, levels), F32),
            pltpu.VMEM((CHUNK * cols, 2 * levels), BF16),
            pltpu.VMEM((CHUNK * cols, 2 * levels), F32),
            pltpu.VMEM((CHUNK, cols, levels), F32),
            pltpu.VMEM((CHUNK * cols, 2 * levels), BF16),
            pltpu.VMEM((CHUNK * cols, 2 * levels), F32),
            pltpu.VMEM((2 * levels, 2 * levels), BF16),
            pltpu.VMEM((2 * fluxes, 2 * levels), BF16),
            pltpu.VMEM((rows * fluxes, cols), F32),
            pltpu.VMEM((2, CHUNK, cols, levels), F32),
            pltpu.VMEM((cols, levels), F32),
            pltpu.SemaphoreType.DMA((rows // CHUNK,)),
            pltpu.SemaphoreType.DMA((2,)),
        ],
        compiler_params=pltpu.CompilerParams(vmem_limit_bytes=48 * MIB),
        cost_estimate=pl.CostEstimate(
            flops=8 * cells * levels * levels, bytes_accessed=8 * cells * levels, transcendentals=0
        ),
        name="advance",
    )(flags, source_column, labels, state, *halos, mask, mix_atm, mix_ocn, flux_map_t)


BATCH = 8
LABEL_ROWS = 16


def regroup_kernel(count, flags, *refs):
    slabs, blocks = refs[:-count], refs[-count:]
    sources = len(slabs) - 1
    capacity = (blocks[0].shape[0] - LABEL_ROWS) // sources
    size = count * capacity

    def chosen(c, start, stop):
        shift = lax.rem(flags[3] - c + len(slabs), len(slabs))
        value = slabs[0][start:stop, :].astype(F32)
        for s in range(1, len(slabs)):
            value = jnp.where(shift == s, slabs[s][start:stop, :].astype(F32), value)
        return value

    heads = [chosen(c, size, size + LABEL_ROWS) for c in range(sources)]
    lines = [head[i : i + 1] for i in range(2) for head in heads]
    spare = jnp.zeros((LABEL_ROWS - len(lines), heads[0].shape[1]), F32)
    labels = jnp.concatenate(lines + [spare], axis=0).astype(BF16)
    for n in range(count):
        for c in range(sources):
            blocks[n][c * capacity : (c + 1) * capacity, :] = chosen(
                c, n * capacity, (n + 1) * capacity
            ).astype(BF16)
        blocks[n][sources * capacity :, :] = labels


def regroup(flags, slabs, count):
    rows, width = slabs[0].shape
    size = (rows - LABEL_ROWS) // count * (len(slabs) - 1) + LABEL_ROWS
    vmem = pl.BlockSpec(memory_space=pltpu.VMEM)
    return pl.pallas_call(
        functools.partial(regroup_kernel, count),
        out_shape=(jax.ShapeDtypeStruct((size, width), BF16),) * count,
        in_specs=[pl.BlockSpec(memory_space=pltpu.SMEM)] + [vmem] * len(slabs),
        out_specs=(vmem,) * count,
        compiler_params=pltpu.CompilerParams(vmem_limit_bytes=16 * MIB),
        name="regroup",
    )(flags, *slabs)


def regrid_body(count, comp_count, flags, ocean_first, *refs):
    blocks = refs[:count]
    seas = refs[count : count + comp_count]
    weights, surface, mask, forcing, shared, hits, entries, chosen, binned = refs[count + comp_count :]
    sources = comp_count - 1
    rows, cols = mask.shape
    share = forcing.shape[0]
    weight_count = weights.shape[0]
    capacity = (blocks[0].shape[0] - LABEL_ROWS) // sources
    size = count * capacity
    total = sources * size
    width = blocks[0].shape[1]
    for c in range(sources):
        for n in range(count):
            start = c * size + n * capacity
            entries[start : start + capacity, :] = blocks[n][c * capacity : (c + 1) * capacity, :]
    lanes = lax.broadcasted_iota(jnp.int32, (LABEL_ROWS, width), 1) // capacity
    labels = jnp.zeros((LABEL_ROWS, width), F32)
    for n in range(count):
        labels = jnp.where(lanes == n, blocks[n][sources * capacity :, :].astype(F32), labels)
    labels = labels.astype(jnp.int32)
    weight_line = jnp.concatenate([labels[c : c + 1, :size] for c in range(sources)], axis=1)
    target_line = jnp.concatenate(
        [labels[sources + c : sources + c + 1, :size] for c in range(sources)], axis=1
    )
    spots = lax.broadcasted_iota(jnp.int32, (rows, total), 0)
    by_target = jnp.where(target_line == spots, 1.0, 0.0)
    own = by_target[:, :size]
    for c in range(1, sources):
        own = jnp.where(flags[3] == c, by_target[:, c * size : (c + 1) * size], own)
    hits[...] = own.T.astype(BF16)
    by_target = by_target.astype(BF16)
    numbers = lax.broadcasted_iota(jnp.int32, (weight_count, total), 0)
    by_weight = jnp.where(weight_line == numbers, 1.0, 0.0).astype(BF16)
    for g in range(weight_count // BATCH):
        for i in range(BATCH):
            w = g * BATCH + i
            chosen[i * rows : (i + 1) * rows, :] = by_target * by_weight[w : w + 1, :]
        binned[...] = dot_nn(chosen[...], entries[...])
        wide = weights[g * BATCH : (g + 1) * BATCH].reshape(BATCH * cols, cols)
        for f in range(share):
            halves = [
                split_two(binned[i * rows : (i + 1) * rows, f * cols : (f + 1) * cols])
                for i in range(BATCH)
            ]
            part = dot_nn(jnp.concatenate([h for h, _ in halves], axis=1), wide) + dot_nn(
                jnp.concatenate([l for _, l in halves], axis=1), wide
            )
            forcing[f] = part if g == 0 else forcing[f] + part
    change = ocean_first[flags[3] * share] * forcing[0]
    for f in range(1, share):
        change = change + ocean_first[flags[3] * share + f] * forcing[f]
    sea = jnp.where(flags[0] == 1, seas[sources][...].astype(F32), 0.0)
    for c in range(sources):
        sea = sea + jnp.where(flags[3] == c, seas[c][...].astype(F32), 0.0)
    base = jnp.where(flags[0] == 1, surface[...], 0.0)
    shared[...] = base + jnp.where(sea > 0.5, change, 0.0)


def regrid(flags, ocean_first, blocks, seas, weights, surface, mask):
    comp_count = len(seas)
    sources = comp_count - 1
    rows, cols = mask.shape
    count = len(blocks)
    height, width = blocks[0].shape
    size = (height - LABEL_ROWS) // sources * count
    total = size * sources
    share = width // cols
    weight_count = weights.shape[0]
    vmem = pl.BlockSpec(memory_space=pltpu.VMEM)
    smem = pl.BlockSpec(memory_space=pltpu.SMEM)
    return pl.pallas_call(
        functools.partial(regrid_body, count, comp_count),
        out_shape=(
            jax.ShapeDtypeStruct((share, rows, cols), F32),
            jax.ShapeDtypeStruct((rows, cols), F32),
            jax.ShapeDtypeStruct((size, rows), BF16),
        ),
        in_specs=[smem, smem] + [vmem] * (count + comp_count + 3),
        out_specs=(vmem, vmem, vmem),
        scratch_shapes=[
            pltpu.VMEM((total, width), BF16),
            pltpu.VMEM((BATCH * rows, total), BF16),
            pltpu.VMEM((BATCH * rows, width), F32),
        ],
        compiler_params=pltpu.CompilerParams(vmem_limit_bytes=32 * MIB),
        cost_estimate=pl.CostEstimate(
            flops=2 * weight_count * rows * width * (total + 2 * cols),
            bytes_accessed=2 * MIB,
            transcendentals=0,
        ),
        name="regrid",
    )(flags, ocean_first, *blocks, *seas, weights, surface, mask)


def pick_kernel(count, *refs):
    parts = refs[:count]
    hits, surface = refs[count : count + 2]
    picked = refs[count + 2 :]
    now = parts[0][...]
    for part in parts[1:]:
        now = now + part[...]
    surface[...] = now
    pair = jnp.concatenate(split_two(now), axis=0)
    size = picked[0].shape[0]
    for n in range(len(picked)):
        some = hits[n * size : (n + 1) * size, :]
        picked[n][...] = dot_nn(jnp.concatenate([some, some], axis=1), pair)


def pick(parts, hits, neighbours):
    rows, cols = parts[0].shape
    size = hits.shape[0] // neighbours
    vmem = pl.BlockSpec(memory_space=pltpu.VMEM)
    return pl.pallas_call(
        functools.partial(pick_kernel, len(parts)),
        out_shape=(jax.ShapeDtypeStruct((rows, cols), F32),)
        + (jax.ShapeDtypeStruct((size, cols), F32),) * neighbours,
        in_specs=[vmem] * (len(parts) + 1),
        out_specs=(vmem,) * (1 + neighbours),
        compiler_params=pltpu.CompilerParams(vmem_limit_bytes=16 * MIB),
        name="pick",
    )(*parts, hits)


LINES = 8


def update_kernel(groups, flags, state, *refs):
    parts = refs[:groups]
    mask, ocean_map, out, token, held, table, wide, in_sems, out_sems = refs[groups:]
    rows, cols, levels = state.shape
    share = parts[0].shape[0]
    flux_count = groups * share
    chunks = rows // LINES
    depth = LINES * flux_count
    token[...] = jnp.zeros(token.shape, F32)

    def fetch(q):
        return pltpu.make_async_copy(
            state.at[pl.ds(q * LINES, LINES)], held.at[pl.ds(q * LINES, LINES)], in_sems.at[q]
        )

    def put(q):
        return pltpu.make_async_copy(
            held.at[pl.ds(q * LINES, LINES)], out.at[pl.ds(q * LINES, LINES)], out_sems.at[q]
        )

    @pl.when(flags[0] == 1)
    def ocean():
        for q in range(chunks):
            fetch(q).start()
        table[...] = jnp.zeros(table.shape, F32)
        for line in range(LINES):
            for f in range(flux_count):
                spot = f * LINES + line
                table[spot : spot + 1, line * levels : (line + 1) * levels] = ocean_map[f : f + 1]
        high, low = split_two(table[...])
        wide[:depth] = high
        wide[depth : 2 * depth] = high
        wide[2 * depth :] = low

        def one(q, _):
            start = pl.multiple_of(q * LINES, LINES)
            sea = mask[pl.ds(start, LINES), :] > 0.5
            part = jnp.concatenate(
                [
                    jnp.where(sea, parts[f // share][f % share, pl.ds(start, LINES), :], 0.0)
                    for f in range(flux_count)
                ],
                axis=0,
            )
            rough = part.astype(BF16).astype(F32)
            turned = jnp.concatenate([rough, part - rough, rough], axis=0).T.astype(BF16)
            change = dot_nn(turned, wide[...])
            fetch(q).wait()
            for line in range(LINES):
                held[start + line] += change[:, line * levels : (line + 1) * levels]
            put(q).start()
            return 0

        lax.fori_loop(0, chunks, one, 0, unroll=2)
        for q in range(chunks):
            put(q).wait()


def update(flags, state, parts, mask, ocean_map):
    rows, cols, levels = state.shape
    depth = LINES * ocean_map.shape[0]
    vmem = pl.BlockSpec(memory_space=pltpu.VMEM)
    smem = pl.BlockSpec(memory_space=pltpu.SMEM)
    hbm = pl.BlockSpec(memory_space=pltpu.HBM)
    return pl.pallas_call(
        functools.partial(update_kernel, len(parts)),
        out_shape=(
            jax.ShapeDtypeStruct(state.shape, F32),
            jax.ShapeDtypeStruct((EDGE, levels), F32),
        ),
        in_specs=[smem, hbm] + [vmem] * (len(parts) + 2),
        out_specs=(hbm, vmem),
        input_output_aliases={1: 0},
        scratch_shapes=[
            pltpu.VMEM(state.shape, F32),
            pltpu.VMEM((depth, LINES * levels), F32),
            pltpu.VMEM((3 * depth, LINES * levels), BF16),
            pltpu.SemaphoreType.DMA((rows // LINES,)),
            pltpu.SemaphoreType.DMA((rows // LINES,)),
        ],
        compiler_params=pltpu.CompilerParams(vmem_limit_bytes=24 * MIB),
        cost_estimate=pl.CostEstimate(
            flops=6 * rows * cols * depth * levels,
            bytes_accessed=8 * rows * cols * levels,
            transcendentals=0,
        ),
        name="update",
    )(flags, state, *parts, mask, ocean_map)


def returned_kernel(groups, flags, *refs):
    picked = refs[:groups]
    weight_column, row_line, weights, mask, surface, new_surface, token, out, total = refs[groups:]
    rows, cols = mask.shape
    weight_count = weights.shape[0]

    @pl.when(flags[0] == 1)
    def ocean():
        out[...] = new_surface[...]

    @pl.when(flags[0] == 0)
    def atmosphere():
        values = jnp.concatenate([p[...] for p in picked], axis=0)
        pair = side_by_side(values)
        which = jnp.broadcast_to(weight_column[...], values.shape)
        total[...] = jnp.zeros(values.shape, F32)

        def one(i, _):
            both = jnp.concatenate([weights[2 * i], weights[2 * i + 1]], axis=0)
            images = dot_nt(pair, jnp.concatenate([both, both], axis=1))
            total[...] += jnp.where(which == 2 * i, images[:, :cols], 0.0) + jnp.where(
                which == 2 * i + 1, images[:, cols:], 0.0
            )
            return 0

        lax.fori_loop(0, weight_count // 2, one, 0, unroll=8)
        spots = lax.broadcasted_iota(jnp.int32, (rows, values.shape[0]), 0)
        chosen = jnp.where(jnp.broadcast_to(row_line[...], spots.shape) == spots, 1.0, 0.0).astype(BF16)
        high, low = split_two(total[...])
        back = dot_nn(chosen, high) + dot_nn(chosen, low)
        out[...] = jnp.where(mask[...] > 0.5, back, surface[...])


def returned(flags, picked, weight_column, row_line, weights, mask, surface, new_surface, token):
    rows, cols = mask.shape
    entry_total = weight_column.shape[0]
    vmem = pl.BlockSpec(memory_space=pltpu.VMEM)
    smem = pl.BlockSpec(memory_space=pltpu.SMEM)
    return pl.pallas_call(
        functools.partial(returned_kernel, len(picked)),
        out_shape=jax.ShapeDtypeStruct((rows, cols), F32),
        in_specs=[smem] + [vmem] * (len(picked) + 7),
        out_specs=vmem,
        scratch_shapes=[pltpu.VMEM((entry_total, cols), F32)],
        compiler_params=pltpu.CompilerParams(vmem_limit_bytes=16 * MIB),
        name="returned",
    )(flags, *picked, weight_column, row_line, weights, mask, surface, new_surface, token)


def local(
    state, land_mask, intersection_list, mix_atm, mix_ocn, flux_map, ocean_map, regrid_weights
):
    rows, cols, levels = state.shape
    intersections = intersection_list.shape[2]
    comp_count = lax.axis_size("comp")
    lat_count = lax.axis_size("lat")
    lon_count = lax.axis_size("lon")
    tile_count = lat_count * lon_count
    reach = min(4, lon_count)
    neighbours = 2 * reach
    entry_total = intersections * rows
    capacity = entry_total // neighbours
    comp_index = lax.axis_index("comp")
    lat_index = lax.axis_index("lat")
    tile_index = lat_index * lon_count + lax.axis_index("lon")
    bands = comp_count * lat_count
    ocean_band = (comp_count - 1) * lat_count
    ocean_comp = comp_count - 1
    band = comp_index * lat_count + lat_index
    is_ocean = comp_index == ocean_comp
    upper_valid = (band > 0) & (band != ocean_band)
    lower_valid = (band < bands - 1) & (band != ocean_band - 1)
    flags = jnp.stack([is_ocean, upper_valid, lower_valid, comp_index]).astype(jnp.int32)
    mask = (land_mask == 1).astype(F32)

    def band_shift(value, by, lon_by):
        pairs = []
        for b in range(bands):
            target = b + by
            if 0 <= target < bands and (b >= ocean_band) == (target >= ocean_band):
                for lon in range(lon_count):
                    pairs.append(
                        (b * lon_count + lon, target * lon_count + (lon + lon_by) % lon_count)
                    )
        return lax.ppermute(value, AXES, pairs)

    first_rows, last_rows, sides = take_edges(state)
    up_rows = band_shift(last_rows, 1, 0)
    low_rows = band_shift(first_rows, -1, 0)
    framed = frame_sides(sides, up_rows, low_rows)
    if lon_count == 2:
        left_cols = right_cols = band_shift(framed, 0, 1)
        left_at, right_at = 2, 0
    else:
        left_cols = band_shift(framed[2:], 0, 1)
        right_cols = band_shift(framed[:2], 0, -1)
        left_at, right_at = 0, 0

    entry_list = intersection_list.reshape(entry_total, 3)
    owners = entry_list[:, 0]
    labels = entry_list[:, 2] * rows + entry_list[:, 1]
    offsets = [
        (n // reach * lon_count + n % reach - (reach - 1) // 2) % tile_count
        for n in range(neighbours)
    ]
    distance = (owners - tile_index + tile_count) % tile_count
    hits = distance[:, None] == jnp.array(offsets, jnp.int32)[None, :]
    neighbour_ids = jnp.sum(
        jnp.where(hits, jnp.arange(neighbours, dtype=jnp.int32)[None, :], 0), axis=1
    )
    positions = jnp.arange(entry_total, dtype=jnp.int32)
    earlier = (neighbour_ids[None, :] == neighbour_ids[:, None]) & (
        positions[None, :] < positions[:, None]
    )
    slots = neighbour_ids * capacity + jnp.sum(earlier.astype(jnp.int32), axis=1)
    placing = positions[:, None] == slots[None, :]
    sources = jnp.sum(jnp.where(placing, (positions // intersections)[None, :], 0), axis=1)
    packed_labels = jnp.sum(jnp.where(placing, labels[None, :], 0), axis=1)

    def over_comp(value, shift, last):
        pairs = [
            (c * tile_count + t, (c + shift) % comp_count * tile_count + t)
            for c in range(comp_count if last else comp_count - 1)
            for t in range(tile_count)
        ]
        return lax.ppermute(value, AXES, pairs)

    def over_tiles(value, offset, comps):
        if offset % tile_count == 0:
            return value
        pairs = [
            (c * tile_count + t, c * tile_count + (t + offset) % tile_count)
            for c in range(comps)
            for t in range(tile_count)
        ]
        return lax.ppermute(value, AXES, pairs)

    def with_ocean(value, comp, back):
        pairs = [
            (comp * tile_count + t, ocean_comp * tile_count + t) for t in range(tile_count)
        ]
        if back:
            pairs = [(there, here) for here, there in pairs]
        return lax.ppermute(value, AXES, pairs)

    label_lines = jnp.stack([packed_labels // rows, packed_labels % rows]).astype(BF16)
    label_lines = jnp.pad(label_lines, ((0, LABEL_ROWS - 2), (0, 0)))

    halos = (up_rows, low_rows, left_cols, right_cols, sides)
    moved = advance(
        flags, sources[:, None], label_lines, state, halos, mask, mix_atm, mix_ocn, flux_map.T,
        comp_count, left_at, right_at,
    )
    moved, surface, sea_copy, packed = moved[0], moved[1], moved[2], moved[3:]
    slabs = [packed[0]] + [over_comp(packed[s], s, False) for s in range(1, comp_count)]
    seas = [with_ocean(sea_copy, c, True) for c in range(ocean_comp)] + [sea_copy]
    blocks = regroup(flags, slabs, neighbours)
    blocks = [over_tiles(blocks[n], offsets[n], comp_count) for n in range(neighbours)]
    forcing, shared, hits = regrid(
        flags, ocean_map[:, 0], blocks, seas, regrid_weights, surface, mask
    )
    parts = [shared] + [over_comp(shared, s, True) for s in range(1, comp_count)]
    picks = pick(parts, hits, neighbours)
    new_surface, picked = picks[0], picks[1:]
    arrived = [over_tiles(picked[n], -offsets[n], ocean_comp) for n in range(neighbours)]
    fields = [with_ocean(forcing, c, False) for c in range(ocean_comp)] + [forcing]
    final_state, token = update(flags, moved, fields, mask, ocean_map)
    weight_column = (packed_labels // rows)[:, None]
    surface_out = returned(
        flags, arrived, weight_column, sources[None, :], regrid_weights, mask, surface, new_surface,
        token,
    )
    return (final_state, surface_out)


def solution(mesh):
    placed = (
        P(("comp", "lat"), "lon", None),
        P(("comp", "lat"), "lon"),
        P(("comp", "lat"), "lon", None, None),
        P(),
        P(),
        P(),
        P(),
        P(),
    )
    return jax.shard_map(
        local,
        mesh=mesh,
        in_specs=placed,
        out_specs=(P(("comp", "lat"), "lon", None), P(("comp", "lat"), "lon")),
        check_vma=False,
    )
```

```python
import functools

import jax
import jax.numpy as jnp
from jax import lax
from jax.experimental import pallas as pl
from jax.experimental.pallas import tpu as pltpu
from jax.sharding import PartitionSpec as P

SMOOTHING = 0.2
PHYSICS = 0.5
MIB = 1024 * 1024
F32 = jnp.float32
BF16 = jnp.bfloat16
EDGE = 8
STRIP = 16
CHUNK = 8
AXES = ("comp", "lat", "lon")


def split_two(x):
    high = x.astype(BF16)
    low = (x - high.astype(F32)).astype(BF16)
    return high, low


def side_by_side(x):
    return jnp.concatenate(split_two(x), axis=1)


def dot_nt(a, b):
    return lax.dot_general(a, b, (((1,), (1,)), ((), ())), preferred_element_type=F32)


def dot_nn(a, b):
    return jnp.dot(a, b, preferred_element_type=F32)


def edges_kernel(state, first_rows, last_rows, sides, top, bottom, left, right, sems):
    rows, cols, _ = state.shape
    copies = [
        pltpu.make_async_copy(state.at[pl.ds(0, 2)], top, sems.at[0]),
        pltpu.make_async_copy(state.at[pl.ds(rows - 2, 2)], bottom, sems.at[1]),
        pltpu.make_async_copy(state.at[:, pl.ds(0, EDGE)], left, sems.at[2]),
        pltpu.make_async_copy(state.at[:, pl.ds(cols - EDGE, EDGE)], right, sems.at[3]),
    ]
    for copy in copies:
        copy.start()
    for copy in copies:
        copy.wait()
    first_rows[...] = top[...].astype(BF16)
    last_rows[...] = bottom[...].astype(BF16)
    for i in range(2):
        sides[i] = left[:, i, :]
        sides[2 + i] = right[:, EDGE - 2 + i, :]


def take_edges(state):
    rows, cols, levels = state.shape
    slab = jax.ShapeDtypeStruct((2, cols, levels), BF16)
    side = jax.ShapeDtypeStruct((4, rows, levels), F32)
    vmem = pl.BlockSpec(memory_space=pltpu.VMEM)
    return pl.pallas_call(
        edges_kernel,
        out_shape=(slab, slab, side),
        in_specs=[pl.BlockSpec(memory_space=pltpu.HBM)],
        out_specs=(vmem,) * 3,
        scratch_shapes=[
            pltpu.VMEM((2, cols, levels), F32),
            pltpu.VMEM((2, cols, levels), F32),
            pltpu.VMEM((rows, EDGE, levels), F32),
            pltpu.VMEM((rows, EDGE, levels), F32),
            pltpu.SemaphoreType.DMA((4,)),
        ],
        compiler_params=pltpu.CompilerParams(vmem_limit_bytes=50 * MIB),
        name="edges",
    )(state)


def frame_kernel(sides, up_rows, low_rows, framed):
    _, rows, levels = sides.shape
    cols = up_rows.shape[1]
    framed[...] = jnp.zeros(framed.shape, F32)
    above = up_rows[1].astype(F32)
    below = low_rows[0].astype(F32)
    for i, col in enumerate((0, 1, cols - 2, cols - 1)):
        framed[i, EDGE : EDGE + rows, :] = sides[i]
        framed[i, EDGE - 1 : EDGE, :] = above[col : col + 1, :]
        framed[i, EDGE + rows : EDGE + rows + 1, :] = below[col : col + 1, :]


def frame_sides(sides, up_rows, low_rows):
    count, rows, levels = sides.shape
    vmem = pl.BlockSpec(memory_space=pltpu.VMEM)
    return pl.pallas_call(
        frame_kernel,
        out_shape=jax.ShapeDtypeStruct((count, rows + 2 * EDGE, levels), F32),
        in_specs=[vmem] * 3,
        out_specs=vmem,
        compiler_params=pltpu.CompilerParams(vmem_limit_bytes=16 * MIB),
        name="frame",
    )(sides, up_rows, low_rows)


def advance_kernel(comp_count, left_at, right_at, *refs):
    (flags, source_column, labels, state, up_rows, low_rows, left_in, right_in, own_sides) = refs[:9]
    (mask, mix_atm, mix_ocn, flux_map) = refs[9:13]
    out, surface, sea_copy = refs[13:16]
    packed = refs[16]
    (values, moved, halo_moved, smooth, pairs, later_smooth, later_pairs) = refs[17:24]
    (weights, flux_weights, fluxes, staged, top, in_sems, out_sems) = refs[24:]
    left_cols = left_in.at[left_at : left_at + 2]
    right_cols = right_in.at[right_at : right_at + 2]
    first = (smooth, pairs)
    second = (later_smooth, later_pairs)
    rows, cols, levels = state.shape
    chunks = rows // CHUNK
    inner = pl.ds(EDGE, cols)
    flux_count = flux_map.shape[0]

    def fetch(q):
        return pltpu.make_async_copy(
            state.at[pl.ds(q * CHUNK, CHUNK)],
            values.at[pl.ds(q * CHUNK + 2, CHUNK), inner],
            in_sems.at[q],
        )

    def put(q, slot):
        return pltpu.make_async_copy(
            staged.at[slot], out.at[pl.ds(q * CHUNK, CHUNK)], out_sems.at[slot]
        )

    def begin(q, _):
        fetch(q).start()
        return 0

    lax.fori_loop(0, chunks, begin, 0)
    ocean = flags[0] == 1
    mix = jnp.where(ocean, mix_ocn[...], mix_atm[...])
    mix_high, mix_low = split_two(mix)
    weights[:levels, :levels] = mix_high
    weights[levels:, :levels] = mix_high
    weights[:levels, levels:] = mix_low
    weights[levels:, levels:] = mix_low
    sea_copy[...] = mask[...].astype(BF16)
    map_high, map_low = split_two(flux_map[...])
    flux_weights[...] = jnp.concatenate(
        [
            jnp.concatenate([map_high.astype(F32), map_high.astype(F32)], axis=1),
            jnp.concatenate([map_low.astype(F32), map_low.astype(F32)], axis=1),
        ],
        axis=0,
    ).astype(BF16)
    values[0:2, EDGE : EDGE + cols, :] = up_rows[...].astype(F32)
    values[rows + 2 : rows + 4, EDGE : EDGE + cols, :] = low_rows[...].astype(F32)
    for r, i in ((1, EDGE - 1), (rows + 2, EDGE + rows)):
        values[r, EDGE - 1 : EDGE, :] = left_cols[1, i : i + 1, :]
        values[r, EDGE + cols : EDGE + cols + 1, :] = right_cols[0, i : i + 1, :]

    def side_cells(r, _):
        values[r + 2, EDGE - 1 : EDGE, :] = left_cols[1, pl.ds(r + EDGE, 1), :]
        values[r + 2, EDGE + cols : EDGE + cols + 1, :] = right_cols[0, pl.ds(r + EDGE, 1), :]
        return 0

    lax.fori_loop(0, rows, side_cells, 0, unroll=8)

    def stage(refs, row, total):
        line = SMOOTHING * total
        refs[0][row] = line
        refs[1][row * cols : (row + 1) * cols, :] = side_by_side(line)

    def stage_rows(refs, ref, start, count):
        for col in range(0, cols, STRIP):
            left = EDGE + col
            block = ref[pl.ds(start - 1, count + 2), left : left + STRIP, :]
            near = ref[pl.ds(start, count), left - 1 : left - 1 + STRIP, :]
            far = ref[pl.ds(start, count), left + 1 : left + 1 + STRIP, :]
            for row in range(count):
                total = (block[row + 1] + (block[row] + block[row + 2])) + (near[row] + far[row])
                line = SMOOTHING * total
                refs[0][row, col : col + STRIP, :] = line
                spot = row * cols + col
                refs[1][spot : spot + STRIP, :] = side_by_side(line)

    def note_top(q, lines):
        lanes = lax.broadcasted_iota(jnp.int32, (cols, levels), 1)
        kept = lines[0]
        for row in range(1, CHUNK):
            kept = jnp.where(lanes == row, pltpu.roll(lines[row], row, 1), kept)
        turned = pltpu.roll(kept, q * CHUNK, 1)
        top[...] = jnp.where(lanes // CHUNK == q, turned, top[...])

    def mix_rows(refs, count):
        both = dot_nn(refs[1][: count * cols, :], weights[...])
        both = both[:, :levels] + both[:, levels:]
        return [
            refs[0][row] + PHYSICS * jnp.tanh(both[row * cols : (row + 1) * cols, :])
            for row in range(count)
        ]

    @pl.when(jnp.logical_not(ocean))
    def atmosphere():
        nearest = (left_cols.at[1], right_cols.at[0])
        beyond = (left_cols.at[0], right_cols.at[1])
        within = (own_sides.at[0], own_sides.at[3])
        for s in range(2):
            total = (
                nearest[s][EDGE : EDGE + rows, :]
                + nearest[s][EDGE - 1 : EDGE - 1 + rows, :]
                + nearest[s][EDGE + 1 : EDGE + 1 + rows, :]
            )
            stage(first, s, total + (beyond[s][EDGE : EDGE + rows, :] + within[s][...]))
        for s, line in enumerate(mix_rows(first, 2)):
            halo_moved[s] = line

        def moved_sides(r, _):
            moved[r + 1, EDGE - 1 : EDGE, :] = halo_moved[0, pl.ds(r, 1), :]
            moved[r + 1, EDGE + cols : EDGE + cols + 1, :] = halo_moved[1, pl.ds(r, 1), :]
            return 0

        lax.fori_loop(0, rows, moved_sides, 0, unroll=8)
        fetch(0).wait()
        fetch(1).wait()
        stage_rows(second, values, 1, 2)
        for row, line in enumerate(mix_rows(second, 2)):
            moved[row, EDGE : EDGE + cols, :] = line

        @pl.when(flags[1] == 0)
        def _():
            moved[0, EDGE : EDGE + cols, :] = jnp.zeros((cols, levels), F32)

        def begin_first(q):
            stage_rows(first, values, q * CHUNK + 3, CHUNK)

        def end_first(q):
            for row, line in enumerate(mix_rows(first, CHUNK)):
                moved[q * CHUNK + row + 2, EDGE : EDGE + cols, :] = line

        def begin_second(q):
            stage_rows(second, moved, q * CHUNK + 1, CHUNK)

        def end_second(q, slot):
            for row, line in enumerate(mix_rows(second, CHUNK)):
                staged[slot, row] = line
                both = line + moved[q * CHUNK + row + 1, EDGE : EDGE + cols, :]
                later_pairs[row * cols : (row + 1) * cols, :] = side_by_side(both)
            put(q, slot).start()
            note_top(q, [staged[slot, row] for row in range(CHUNK)])
            flux = dot_nt(flux_weights[...], later_pairs[...])
            flux = flux[:flux_count] + flux[flux_count:]
            for row in range(CHUNK):
                r = q * CHUNK + row
                block = PHYSICS * flux[:, row * cols : (row + 1) * cols]
                sea = jnp.broadcast_to(mask[pl.ds(r, 1), :], block.shape)
                block = jnp.where(sea > 0.5, block, 0.0)
                fluxes[pl.ds(pl.multiple_of(r * flux_count, flux_count), flux_count), :] = block

        begin_first(0)
        end_first(0)

        def one_chunk(q, _):
            @pl.when(q + 1 < chunks)
            def _():
                fetch(q + 1).wait()

            slot = (q - 1) % 2

            @pl.when(q >= 3)
            def _():
                put(q - 3, slot).wait()

            begin_first(q)
            begin_second(q - 1)
            end_first(q)
            end_second(q - 1, slot)
            return 0

        lax.fori_loop(1, chunks, one_chunk, 0)

        @pl.when(flags[2] == 0)
        def _():
            moved[rows + 1, EDGE : EDGE + cols, :] = jnp.zeros((cols, levels), F32)

        last = chunks - 1
        put(last - 2, last % 2).wait()
        begin_second(last)
        end_second(last, last % 2)
        put(last - 1, (last - 1) % 2).wait()
        put(last, last % 2).wait()
        spots = lax.broadcasted_iota(jnp.int32, (source_column.shape[0], rows), 1)
        placing = jnp.where(source_column[...] == spots, 1.0, 0.0).astype(BF16)
        share = flux_count // comp_count
        for c in range(comp_count):
            for f in range(share):
                field = fluxes[pl.ds(c * share + f, rows, stride=flux_count), :].astype(BF16)
                packed[c, : placing.shape[0], f * cols : (f + 1) * cols] = dot_nn(
                    placing, field
                ).astype(BF16)
            packed[c, placing.shape[0] :, :] = labels[...]
        surface[...] = top[...].T

    @pl.when(ocean)
    def sea_side():
        fetch(0).wait()
        lanes = lax.broadcasted_iota(jnp.int32, (CHUNK, CHUNK * levels), 1) // levels
        lines = lax.broadcasted_iota(jnp.int32, (CHUNK, CHUNK * levels), 0)
        spreader = jnp.where(lanes == lines, 1.0, 0.0).astype(F32)

        def one_chunk(q, _):
            base = q * CHUNK

            @pl.when(q + 1 < chunks)
            def _():
                fetch(q + 1).wait()

            stage_rows(first, values, base + 2, CHUNK)
            slot = q % 2

            @pl.when(q >= 2)
            def _():
                put(q - 2, slot).wait()

            sea = dot_nn(mask[pl.ds(pl.multiple_of(base, CHUNK), CHUNK), :].T, spreader)
            for row, line in enumerate(mix_rows(first, CHUNK)):
                chosen = sea[:, row * levels : (row + 1) * levels] > 0.5
                before = values[base + row + 2, EDGE : EDGE + cols, :]
                staged[slot, row] = jnp.where(chosen, line, before)
            put(q, slot).start()
            note_top(q, [staged[slot, row] for row in range(CHUNK)])
            return 0

        lax.fori_loop(0, chunks, one_chunk, 0)
        put(chunks - 2, (chunks - 2) % 2).wait()
        put(chunks - 1, (chunks - 1) % 2).wait()
        surface[...] = top[...].T
        packed[...] = jnp.zeros(packed.shape, BF16)


def advance(
    flags, source_column, labels, state, halos, mask, mix_atm, mix_ocn, flux_map_t, comp_count, left_at, right_at
):
    rows, cols, levels = state.shape
    fluxes = flux_map_t.shape[0]
    vmem = pl.BlockSpec(memory_space=pltpu.VMEM)
    smem = pl.BlockSpec(memory_space=pltpu.SMEM)
    hbm = pl.BlockSpec(memory_space=pltpu.HBM)
    entry = jax.ShapeDtypeStruct(
        (comp_count, source_column.shape[0] + labels.shape[0], fluxes // comp_count * cols), BF16
    )
    cells = rows * cols
    return pl.pallas_call(
        functools.partial(advance_kernel, comp_count, left_at, right_at),
        out_shape=(
            jax.ShapeDtypeStruct(state.shape, F32),
            jax.ShapeDtypeStruct((rows, cols), F32),
            jax.ShapeDtypeStruct((rows, cols), BF16),
            entry,
        ),
        in_specs=[smem, vmem, vmem, hbm] + [vmem] * (len(halos) + 4),
        out_specs=(hbm, vmem, vmem, vmem),
        scratch_shapes=[
            pltpu.VMEM((rows + 4, cols + 2 * EDGE, levels), F32),
            pltpu.VMEM((rows + 2, cols + 2 * EDGE, levels), F32),
            pltpu.VMEM((2, rows, levels), F32),
            pltpu.VMEM((CHUNK, cols, levels), F32),
            pltpu.VMEM((CHUNK * cols, 2 * levels), BF16),
            pltpu.VMEM((CHUNK, cols, levels), F32),
            pltpu.VMEM((CHUNK * cols, 2 * levels), BF16),
            pltpu.VMEM((2 * levels, 2 * levels), BF16),
            pltpu.VMEM((2 * fluxes, 2 * levels), BF16),
            pltpu.VMEM((rows * fluxes, cols), F32),
            pltpu.VMEM((2, CHUNK, cols, levels), F32),
            pltpu.VMEM((cols, levels), F32),
            pltpu.SemaphoreType.DMA((rows // CHUNK,)),
            pltpu.SemaphoreType.DMA((2,)),
        ],
        compiler_params=pltpu.CompilerParams(vmem_limit_bytes=48 * MIB),
        cost_estimate=pl.CostEstimate(
            flops=8 * cells * levels * levels, bytes_accessed=8 * cells * levels, transcendentals=0
        ),
        name="advance",
    )(flags, source_column, labels, state, *halos, mask, mix_atm, mix_ocn, flux_map_t)


BATCH = 8
LABEL_ROWS = 16


def regroup_kernel(slabs, *blocks):
    sources = slabs.shape[0] - 1
    capacity = (blocks[0].shape[0] - LABEL_ROWS) // sources
    size = len(blocks) * capacity
    heads = [slabs[c, size : size + LABEL_ROWS, :].astype(F32) for c in range(sources)]
    lines = [head[i : i + 1] for i in range(2) for head in heads]
    spare = jnp.zeros((LABEL_ROWS - len(lines), heads[0].shape[1]), F32)
    labels = jnp.concatenate(lines + [spare], axis=0).astype(BF16)
    for n, block in enumerate(blocks):
        for c in range(sources):
            block[c * capacity : (c + 1) * capacity, :] = slabs[
                c, n * capacity : (n + 1) * capacity, :
            ]
        block[sources * capacity :, :] = labels


def regroup(slabs, count):
    comps, rows, width = slabs.shape
    size = (rows - LABEL_ROWS) // count * (comps - 1) + LABEL_ROWS
    vmem = pl.BlockSpec(memory_space=pltpu.VMEM)
    return pl.pallas_call(
        regroup_kernel,
        out_shape=(jax.ShapeDtypeStruct((size, width), BF16),) * count,
        in_specs=[vmem],
        out_specs=(vmem,) * count,
        compiler_params=pltpu.CompilerParams(vmem_limit_bytes=16 * MIB),
        name="regroup",
    )(slabs)


def regrid_body(count, comp_count, flags, ocean_first, *refs):
    blocks = refs[:count]
    seas = refs[count : count + comp_count]
    weights, surface, mask, forcing, shared, hits, entries, chosen, binned = refs[count + comp_count :]
    sources = comp_count - 1
    rows, cols = mask.shape
    share = forcing.shape[0]
    weight_count = weights.shape[0]
    capacity = (blocks[0].shape[0] - LABEL_ROWS) // sources
    size = count * capacity
    total = sources * size
    width = blocks[0].shape[1]
    for c in range(sources):
        for n in range(count):
            start = c * size + n * capacity
            entries[start : start + capacity, :] = blocks[n][c * capacity : (c + 1) * capacity, :]
    lanes = lax.broadcasted_iota(jnp.int32, (LABEL_ROWS, width), 1) // capacity
    labels = jnp.zeros((LABEL_ROWS, width), F32)
    for n in range(count):
        labels = jnp.where(lanes == n, blocks[n][sources * capacity :, :].astype(F32), labels)
    labels = labels.astype(jnp.int32)
    weight_line = jnp.concatenate([labels[c : c + 1, :size] for c in range(sources)], axis=1)
    target_line = jnp.concatenate(
        [labels[sources + c : sources + c + 1, :size] for c in range(sources)], axis=1
    )
    spots = lax.broadcasted_iota(jnp.int32, (rows, total), 0)
    by_target = jnp.where(target_line == spots, 1.0, 0.0)
    own = by_target[:, :size]
    for c in range(1, sources):
        own = jnp.where(flags[3] == c, by_target[:, c * size : (c + 1) * size], own)
    hits[...] = own.T.astype(BF16)
    by_target = by_target.astype(BF16)
    numbers = lax.broadcasted_iota(jnp.int32, (weight_count, total), 0)
    by_weight = jnp.where(weight_line == numbers, 1.0, 0.0).astype(BF16)
    for g in range(weight_count // BATCH):
        for i in range(BATCH):
            w = g * BATCH + i
            chosen[i * rows : (i + 1) * rows, :] = by_target * by_weight[w : w + 1, :]
        binned[...] = dot_nn(chosen[...], entries[...])
        wide = weights[g * BATCH : (g + 1) * BATCH].reshape(BATCH * cols, cols)
        for f in range(share):
            halves = [
                split_two(binned[i * rows : (i + 1) * rows, f * cols : (f + 1) * cols])
                for i in range(BATCH)
            ]
            part = dot_nn(jnp.concatenate([h for h, _ in halves], axis=1), wide) + dot_nn(
                jnp.concatenate([l for _, l in halves], axis=1), wide
            )
            forcing[f] = part if g == 0 else forcing[f] + part
    change = ocean_first[flags[3] * share] * forcing[0]
    for f in range(1, share):
        change = change + ocean_first[flags[3] * share + f] * forcing[f]
    sea = jnp.where(flags[0] == 1, seas[sources][...].astype(F32), 0.0)
    for c in range(sources):
        sea = sea + jnp.where(flags[3] == c, seas[c][...].astype(F32), 0.0)
    base = jnp.where(flags[0] == 1, surface[...], 0.0)
    value = base + jnp.where(sea > 0.5, change, 0.0)
    for c in range(comp_count):
        shared[c] = value


def regrid(flags, ocean_first, blocks, seas, weights, surface, mask):
    comp_count = len(seas)
    sources = comp_count - 1
    rows, cols = mask.shape
    count = len(blocks)
    height, width = blocks[0].shape
    size = (height - LABEL_ROWS) // sources * count
    total = size * sources
    share = width // cols
    weight_count = weights.shape[0]
    vmem = pl.BlockSpec(memory_space=pltpu.VMEM)
    smem = pl.BlockSpec(memory_space=pltpu.SMEM)
    return pl.pallas_call(
        functools.partial(regrid_body, count, comp_count),
        out_shape=(
            jax.ShapeDtypeStruct((share, rows, cols), F32),
            jax.ShapeDtypeStruct((comp_count, rows, cols), F32),
            jax.ShapeDtypeStruct((size, rows), BF16),
        ),
        in_specs=[smem, smem] + [vmem] * (count + comp_count + 3),
        out_specs=(vmem, vmem, vmem),
        scratch_shapes=[
            pltpu.VMEM((total, width), BF16),
            pltpu.VMEM((BATCH * rows, total), BF16),
            pltpu.VMEM((BATCH * rows, width), F32),
        ],
        compiler_params=pltpu.CompilerParams(vmem_limit_bytes=32 * MIB),
        cost_estimate=pl.CostEstimate(
            flops=2 * weight_count * rows * width * (total + 2 * cols),
            bytes_accessed=2 * MIB,
            transcendentals=0,
        ),
        name="regrid",
    )(flags, ocean_first, *blocks, *seas, weights, surface, mask)


def pick_kernel(parts, hits, surface, *picked):
    now = parts[0]
    for c in range(1, parts.shape[0]):
        now = now + parts[c]
    surface[...] = now
    pair = jnp.concatenate(split_two(now), axis=0)
    size = picked[0].shape[0]
    for n in range(len(picked)):
        some = hits[n * size : (n + 1) * size, :]
        picked[n][...] = dot_nn(jnp.concatenate([some, some], axis=1), pair)


def pick(parts, hits, neighbours):
    _, rows, cols = parts.shape
    size = hits.shape[0] // neighbours
    vmem = pl.BlockSpec(memory_space=pltpu.VMEM)
    return pl.pallas_call(
        pick_kernel,
        out_shape=(jax.ShapeDtypeStruct((rows, cols), F32),)
        + (jax.ShapeDtypeStruct((size, cols), F32),) * neighbours,
        in_specs=[vmem] * 2,
        out_specs=(vmem,) * (1 + neighbours),
        compiler_params=pltpu.CompilerParams(vmem_limit_bytes=16 * MIB),
        name="pick",
    )(parts, hits)


LINES = 8


def update_kernel(groups, flags, state, *refs):
    parts = refs[:groups]
    mask, ocean_map, out, token, held, table, wide, in_sems, out_sems = refs[groups:]
    rows, cols, levels = state.shape
    share = parts[0].shape[0]
    flux_count = groups * share
    chunks = rows // LINES
    depth = LINES * flux_count
    token[...] = jnp.zeros(token.shape, F32)

    def fetch(q):
        return pltpu.make_async_copy(
            state.at[pl.ds(q * LINES, LINES)], held.at[pl.ds(q * LINES, LINES)], in_sems.at[q]
        )

    def put(q):
        return pltpu.make_async_copy(
            held.at[pl.ds(q * LINES, LINES)], out.at[pl.ds(q * LINES, LINES)], out_sems.at[q]
        )

    @pl.when(flags[0] == 1)
    def ocean():
        for q in range(chunks):
            fetch(q).start()
        table[...] = jnp.zeros(table.shape, F32)
        for line in range(LINES):
            for f in range(flux_count):
                spot = f * LINES + line
                table[spot : spot + 1, line * levels : (line + 1) * levels] = ocean_map[f : f + 1]
        high, low = split_two(table[...])
        wide[:depth] = high
        wide[depth : 2 * depth] = high
        wide[2 * depth :] = low

        def one(q, _):
            start = pl.multiple_of(q * LINES, LINES)
            sea = mask[pl.ds(start, LINES), :] > 0.5
            part = jnp.concatenate(
                [
                    jnp.where(sea, parts[f // share][f % share, pl.ds(start, LINES), :], 0.0)
                    for f in range(flux_count)
                ],
                axis=0,
            )
            rough = part.astype(BF16).astype(F32)
            turned = jnp.concatenate([rough, part - rough, rough], axis=0).T.astype(BF16)
            change = dot_nn(turned, wide[...])
            fetch(q).wait()
            for line in range(LINES):
                held[start + line] += change[:, line * levels : (line + 1) * levels]
            put(q).start()
            return 0

        lax.fori_loop(0, chunks, one, 0, unroll=2)
        for q in range(chunks):
            put(q).wait()


def update(flags, state, parts, mask, ocean_map):
    rows, cols, levels = state.shape
    depth = LINES * ocean_map.shape[0]
    vmem = pl.BlockSpec(memory_space=pltpu.VMEM)
    smem = pl.BlockSpec(memory_space=pltpu.SMEM)
    hbm = pl.BlockSpec(memory_space=pltpu.HBM)
    return pl.pallas_call(
        functools.partial(update_kernel, len(parts)),
        out_shape=(
            jax.ShapeDtypeStruct(state.shape, F32),
            jax.ShapeDtypeStruct((EDGE, levels), F32),
        ),
        in_specs=[smem, hbm] + [vmem] * (len(parts) + 2),
        out_specs=(hbm, vmem),
        input_output_aliases={1: 0},
        scratch_shapes=[
            pltpu.VMEM(state.shape, F32),
            pltpu.VMEM((depth, LINES * levels), F32),
            pltpu.VMEM((3 * depth, LINES * levels), BF16),
            pltpu.SemaphoreType.DMA((rows // LINES,)),
            pltpu.SemaphoreType.DMA((rows // LINES,)),
        ],
        compiler_params=pltpu.CompilerParams(vmem_limit_bytes=24 * MIB),
        cost_estimate=pl.CostEstimate(
            flops=6 * rows * cols * depth * levels,
            bytes_accessed=8 * rows * cols * levels,
            transcendentals=0,
        ),
        name="update",
    )(flags, state, *parts, mask, ocean_map)


def returned_kernel(groups, flags, *refs):
    picked = refs[:groups]
    weight_column, row_line, weights, mask, surface, new_surface, token, out, total = refs[groups:]
    rows, cols = mask.shape
    weight_count = weights.shape[0]

    @pl.when(flags[0] == 1)
    def ocean():
        out[...] = new_surface[...]

    @pl.when(flags[0] == 0)
    def atmosphere():
        values = jnp.concatenate([p[...] for p in picked], axis=0)
        pair = side_by_side(values)
        which = jnp.broadcast_to(weight_column[...], values.shape)
        total[...] = jnp.zeros(values.shape, F32)

        def one(i, _):
            both = jnp.concatenate([weights[2 * i], weights[2 * i + 1]], axis=0)
            images = dot_nt(pair, jnp.concatenate([both, both], axis=1))
            total[...] += jnp.where(which == 2 * i, images[:, :cols], 0.0) + jnp.where(
                which == 2 * i + 1, images[:, cols:], 0.0
            )
            return 0

        lax.fori_loop(0, weight_count // 2, one, 0, unroll=8)
        spots = lax.broadcasted_iota(jnp.int32, (rows, values.shape[0]), 0)
        chosen = jnp.where(jnp.broadcast_to(row_line[...], spots.shape) == spots, 1.0, 0.0).astype(BF16)
        high, low = split_two(total[...])
        back = dot_nn(chosen, high) + dot_nn(chosen, low)
        out[...] = jnp.where(mask[...] > 0.5, back, surface[...])


def returned(flags, picked, weight_column, row_line, weights, mask, surface, new_surface, token):
    rows, cols = mask.shape
    entry_total = weight_column.shape[0]
    vmem = pl.BlockSpec(memory_space=pltpu.VMEM)
    smem = pl.BlockSpec(memory_space=pltpu.SMEM)
    return pl.pallas_call(
        functools.partial(returned_kernel, len(picked)),
        out_shape=jax.ShapeDtypeStruct((rows, cols), F32),
        in_specs=[smem] + [vmem] * (len(picked) + 7),
        out_specs=vmem,
        scratch_shapes=[pltpu.VMEM((entry_total, cols), F32)],
        compiler_params=pltpu.CompilerParams(vmem_limit_bytes=16 * MIB),
        name="returned",
    )(flags, *picked, weight_column, row_line, weights, mask, surface, new_surface, token)


def local(
    state, land_mask, intersection_list, mix_atm, mix_ocn, flux_map, ocean_map, regrid_weights
):
    rows, cols, levels = state.shape
    intersections = intersection_list.shape[2]
    comp_count = lax.axis_size("comp")
    lat_count = lax.axis_size("lat")
    lon_count = lax.axis_size("lon")
    tile_count = lat_count * lon_count
    reach = min(4, lon_count)
    neighbours = 2 * reach
    entry_total = intersections * rows
    capacity = entry_total // neighbours
    comp_index = lax.axis_index("comp")
    lat_index = lax.axis_index("lat")
    tile_index = lat_index * lon_count + lax.axis_index("lon")
    bands = comp_count * lat_count
    ocean_band = (comp_count - 1) * lat_count
    ocean_comp = comp_count - 1
    band = comp_index * lat_count + lat_index
    is_ocean = comp_index == ocean_comp
    upper_valid = (band > 0) & (band != ocean_band)
    lower_valid = (band < bands - 1) & (band != ocean_band - 1)
    flags = jnp.stack([is_ocean, upper_valid, lower_valid, comp_index]).astype(jnp.int32)
    mask = (land_mask == 1).astype(F32)

    def band_shift(value, by, lon_by):
        pairs = []
        for b in range(bands):
            target = b + by
            if 0 <= target < bands and (b >= ocean_band) == (target >= ocean_band):
                for lon in range(lon_count):
                    pairs.append(
                        (b * lon_count + lon, target * lon_count + (lon + lon_by) % lon_count)
                    )
        return lax.ppermute(value, AXES, pairs)

    first_rows, last_rows, sides = take_edges(state)
    up_rows = band_shift(last_rows, 1, 0)
    low_rows = band_shift(first_rows, -1, 0)
    framed = frame_sides(sides, up_rows, low_rows)
    if lon_count == 2:
        left_cols = right_cols = band_shift(framed, 0, 1)
        left_at, right_at = 2, 0
    else:
        left_cols = band_shift(framed[2:], 0, 1)
        right_cols = band_shift(framed[:2], 0, -1)
        left_at, right_at = 0, 0

    entry_list = intersection_list.reshape(entry_total, 3)
    owners = entry_list[:, 0]
    labels = entry_list[:, 2] * rows + entry_list[:, 1]
    offsets = [
        (n // reach * lon_count + n % reach - (reach - 1) // 2) % tile_count
        for n in range(neighbours)
    ]
    distance = (owners - tile_index + tile_count) % tile_count
    hits = distance[:, None] == jnp.array(offsets, jnp.int32)[None, :]
    neighbour_ids = jnp.sum(
        jnp.where(hits, jnp.arange(neighbours, dtype=jnp.int32)[None, :], 0), axis=1
    )
    positions = jnp.arange(entry_total, dtype=jnp.int32)
    earlier = (neighbour_ids[None, :] == neighbour_ids[:, None]) & (
        positions[None, :] < positions[:, None]
    )
    slots = neighbour_ids * capacity + jnp.sum(earlier.astype(jnp.int32), axis=1)
    placing = positions[:, None] == slots[None, :]
    sources = jnp.sum(jnp.where(placing, (positions // intersections)[None, :], 0), axis=1)
    packed_labels = jnp.sum(jnp.where(placing, labels[None, :], 0), axis=1)

    def over_comp(value):
        return lax.all_to_all(value, "comp", split_axis=0, concat_axis=0, tiled=True)

    def over_tiles(value, offset, comps):
        if offset % tile_count == 0:
            return value
        pairs = [
            (c * tile_count + t, c * tile_count + (t + offset) % tile_count)
            for c in range(comps)
            for t in range(tile_count)
        ]
        return lax.ppermute(value, AXES, pairs)

    def with_ocean(value, comp, back):
        pairs = [
            (comp * tile_count + t, ocean_comp * tile_count + t) for t in range(tile_count)
        ]
        if back:
            pairs = [(there, here) for here, there in pairs]
        return lax.ppermute(value, AXES, pairs)

    label_lines = jnp.stack([packed_labels // rows, packed_labels % rows]).astype(BF16)
    label_lines = jnp.pad(label_lines, ((0, LABEL_ROWS - 2), (0, 0)))

    halos = (up_rows, low_rows, left_cols, right_cols, sides)
    moved = advance(
        flags, sources[:, None], label_lines, state, halos, mask, mix_atm, mix_ocn, flux_map.T,
        comp_count, left_at, right_at,
    )
    moved, surface, sea_copy, packed = moved
    slabs = over_comp(packed)
    seas = [with_ocean(sea_copy, c, True) for c in range(ocean_comp)] + [sea_copy]
    blocks = regroup(slabs, neighbours)
    blocks = [over_tiles(blocks[n], offsets[n], comp_count) for n in range(neighbours)]
    forcing, shared, hits = regrid(
        flags, ocean_map[:, 0], blocks, seas, regrid_weights, surface, mask
    )
    picks = pick(over_comp(shared), hits, neighbours)
    new_surface, picked = picks[0], picks[1:]
    arrived = [over_tiles(picked[n], -offsets[n], ocean_comp) for n in range(neighbours)]
    fields = [with_ocean(forcing, c, False) for c in range(ocean_comp)] + [forcing]
    final_state, token = update(flags, moved, fields, mask, ocean_map)
    weight_column = (packed_labels // rows)[:, None]
    surface_out = returned(
        flags, arrived, weight_column, sources[None, :], regrid_weights, mask, surface, new_surface,
        token,
    )
    return (final_state, surface_out)


def solution(mesh):
    placed = (
        P(("comp", "lat"), "lon", None),
        P(("comp", "lat"), "lon"),
        P(("comp", "lat"), "lon", None, None),
        P(),
        P(),
        P(),
        P(),
        P(),
    )
    return jax.shard_map(
        local,
        mesh=mesh,
        in_specs=placed,
        out_specs=(P(("comp", "lat"), "lon", None), P(("comp", "lat"), "lon")),
        check_vma=False,
    )
```

```python
import functools

import jax
import jax.numpy as jnp
from jax import lax
from jax.experimental import pallas as pl
from jax.experimental.pallas import tpu as pltpu
from jax.sharding import PartitionSpec as P

SMOOTHING = 0.2
PHYSICS = 0.5
MIB = 1024 * 1024
F32 = jnp.float32
BF16 = jnp.bfloat16
EDGE = 8
STRIP = 16
CHUNK = 8
AXES = ("comp", "lat", "lon")


def split_two(x):
    high = x.astype(BF16)
    low = (x - high.astype(F32)).astype(BF16)
    return high, low


def side_by_side(x):
    return jnp.concatenate(split_two(x), axis=1)


def dot_nt(a, b):
    return lax.dot_general(a, b, (((1,), (1,)), ((), ())), preferred_element_type=F32)


def dot_nn(a, b):
    return jnp.dot(a, b, preferred_element_type=F32)


def edges_kernel(state, first_rows, last_rows, sides, top, bottom, left, right, sems):
    rows, cols, _ = state.shape
    copies = [
        pltpu.make_async_copy(state.at[pl.ds(0, 2)], top, sems.at[0]),
        pltpu.make_async_copy(state.at[pl.ds(rows - 2, 2)], bottom, sems.at[1]),
        pltpu.make_async_copy(state.at[:, pl.ds(0, EDGE)], left, sems.at[2]),
        pltpu.make_async_copy(state.at[:, pl.ds(cols - EDGE, EDGE)], right, sems.at[3]),
    ]
    for copy in copies:
        copy.start()
    for copy in copies:
        copy.wait()
    first_rows[...] = top[...].astype(BF16)
    last_rows[...] = bottom[...].astype(BF16)
    for i in range(2):
        sides[i] = left[:, i, :]
        sides[2 + i] = right[:, EDGE - 2 + i, :]


def take_edges(state):
    rows, cols, levels = state.shape
    slab = jax.ShapeDtypeStruct((2, cols, levels), BF16)
    side = jax.ShapeDtypeStruct((4, rows, levels), F32)
    vmem = pl.BlockSpec(memory_space=pltpu.VMEM)
    return pl.pallas_call(
        edges_kernel,
        out_shape=(slab, slab, side),
        in_specs=[pl.BlockSpec(memory_space=pltpu.HBM)],
        out_specs=(vmem,) * 3,
        scratch_shapes=[
            pltpu.VMEM((2, cols, levels), F32),
            pltpu.VMEM((2, cols, levels), F32),
            pltpu.VMEM((rows, EDGE, levels), F32),
            pltpu.VMEM((rows, EDGE, levels), F32),
            pltpu.SemaphoreType.DMA((4,)),
        ],
        compiler_params=pltpu.CompilerParams(vmem_limit_bytes=50 * MIB),
        name="edges",
    )(state)


def frame_kernel(sides, up_rows, low_rows, framed):
    _, rows, levels = sides.shape
    cols = up_rows.shape[1]
    framed[...] = jnp.zeros(framed.shape, F32)
    above = up_rows[1].astype(F32)
    below = low_rows[0].astype(F32)
    for i, col in enumerate((0, 1, cols - 2, cols - 1)):
        framed[i, EDGE : EDGE + rows, :] = sides[i]
        framed[i, EDGE - 1 : EDGE, :] = above[col : col + 1, :]
        framed[i, EDGE + rows : EDGE + rows + 1, :] = below[col : col + 1, :]


def frame_sides(sides, up_rows, low_rows):
    count, rows, levels = sides.shape
    vmem = pl.BlockSpec(memory_space=pltpu.VMEM)
    return pl.pallas_call(
        frame_kernel,
        out_shape=jax.ShapeDtypeStruct((count, rows + 2 * EDGE, levels), F32),
        in_specs=[vmem] * 3,
        out_specs=vmem,
        compiler_params=pltpu.CompilerParams(vmem_limit_bytes=16 * MIB),
        name="frame",
    )(sides, up_rows, low_rows)


def advance_kernel(comp_count, left_at, right_at, *refs):
    (flags, source_column, labels, state, up_rows, low_rows, left_in, right_in, own_sides) = refs[:9]
    (mask, mix_atm, mix_ocn, flux_map) = refs[9:13]
    out, surface, sea_copy = refs[13:16]
    packed = refs[16]
    (values, moved, halo_moved, smooth, pairs, mixed, later_smooth, later_pairs, later_mixed) = refs[17:26]
    (weights, flux_weights, fluxes, staged, top, in_sems, out_sems) = refs[26:]
    left_cols = left_in.at[left_at : left_at + 2]
    right_cols = right_in.at[right_at : right_at + 2]
    first = (smooth, pairs, mixed)
    second = (later_smooth, later_pairs, later_mixed)
    rows, cols, levels = state.shape
    chunks = rows // CHUNK
    inner = pl.ds(EDGE, cols)
    flux_count = flux_map.shape[0]

    def fetch(q):
        return pltpu.make_async_copy(
            state.at[pl.ds(q * CHUNK, CHUNK)],
            values.at[pl.ds(q * CHUNK + 2, CHUNK), inner],
            in_sems.at[q],
        )

    def put(q, slot):
        return pltpu.make_async_copy(
            staged.at[slot], out.at[pl.ds(q * CHUNK, CHUNK)], out_sems.at[slot]
        )

    def begin(q, _):
        fetch(q).start()
        return 0

    lax.fori_loop(0, chunks, begin, 0)
    ocean = flags[0] == 1
    mix = jnp.where(ocean, mix_ocn[...], mix_atm[...])
    mix_high, mix_low = split_two(mix)
    weights[:levels, :levels] = mix_high
    weights[levels:, :levels] = mix_high
    weights[:levels, levels:] = mix_low
    weights[levels:, levels:] = mix_low
    sea_copy[...] = mask[...].astype(BF16)
    map_high, map_low = split_two(flux_map[...])
    flux_weights[...] = jnp.concatenate(
        [
            jnp.concatenate([map_high.astype(F32), map_high.astype(F32)], axis=1),
            jnp.concatenate([map_low.astype(F32), map_low.astype(F32)], axis=1),
        ],
        axis=0,
    ).astype(BF16)
    values[0:2, EDGE : EDGE + cols, :] = up_rows[...].astype(F32)
    values[rows + 2 : rows + 4, EDGE : EDGE + cols, :] = low_rows[...].astype(F32)
    for r, i in ((1, EDGE - 1), (rows + 2, EDGE + rows)):
        values[r, EDGE - 1 : EDGE, :] = left_cols[1, i : i + 1, :]
        values[r, EDGE + cols : EDGE + cols + 1, :] = right_cols[0, i : i + 1, :]

    def side_cells(r, _):
        values[r + 2, EDGE - 1 : EDGE, :] = left_cols[1, pl.ds(r + EDGE, 1), :]
        values[r + 2, EDGE + cols : EDGE + cols + 1, :] = right_cols[0, pl.ds(r + EDGE, 1), :]
        return 0

    lax.fori_loop(0, rows, side_cells, 0, unroll=8)

    def stage(refs, row, total):
        line = SMOOTHING * total
        refs[0][row] = line
        refs[1][row * cols : (row + 1) * cols, :] = side_by_side(line)

    def stage_rows(refs, ref, start, count):
        for col in range(0, cols, STRIP):
            left = EDGE + col
            block = ref[pl.ds(start - 1, count + 2), left : left + STRIP, :]
            near = ref[pl.ds(start, count), left - 1 : left - 1 + STRIP, :]
            far = ref[pl.ds(start, count), left + 1 : left + 1 + STRIP, :]
            for row in range(count):
                total = (block[row + 1] + (block[row] + block[row + 2])) + (near[row] + far[row])
                line = SMOOTHING * total
                refs[0][row, col : col + STRIP, :] = line
                spot = row * cols + col
                refs[1][spot : spot + STRIP, :] = side_by_side(line)

    def note_top(q, lines):
        lanes = lax.broadcasted_iota(jnp.int32, (cols, levels), 1)
        kept = lines[0]
        for row in range(1, CHUNK):
            kept = jnp.where(lanes == row, pltpu.roll(lines[row], row, 1), kept)
        turned = pltpu.roll(kept, q * CHUNK, 1)
        top[...] = jnp.where(lanes // CHUNK == q, turned, top[...])

    def mix_rows(refs, count):
        refs[2][: count * cols, :] = dot_nn(refs[1][: count * cols, :], weights[...])

    def finish(refs, row):
        part = refs[2][row * cols : (row + 1) * cols, :]
        return refs[0][row] + PHYSICS * jnp.tanh(part[:, :levels] + part[:, levels:])

    @pl.when(jnp.logical_not(ocean))
    def atmosphere():
        nearest = (left_cols.at[1], right_cols.at[0])
        beyond = (left_cols.at[0], right_cols.at[1])
        within = (own_sides.at[0], own_sides.at[3])
        for s in range(2):
            total = (
                nearest[s][EDGE : EDGE + rows, :]
                + nearest[s][EDGE - 1 : EDGE - 1 + rows, :]
                + nearest[s][EDGE + 1 : EDGE + 1 + rows, :]
            )
            stage(first, s, total + (beyond[s][EDGE : EDGE + rows, :] + within[s][...]))
        mix_rows(first, 2)
        for s in range(2):
            halo_moved[s] = finish(first, s)

        def moved_sides(r, _):
            moved[r + 1, EDGE - 1 : EDGE, :] = halo_moved[0, pl.ds(r, 1), :]
            moved[r + 1, EDGE + cols : EDGE + cols + 1, :] = halo_moved[1, pl.ds(r, 1), :]
            return 0

        lax.fori_loop(0, rows, moved_sides, 0, unroll=8)
        fetch(0).wait()
        fetch(1).wait()
        stage_rows(second, values, 1, 2)
        mix_rows(second, 2)
        for row in range(2):
            moved[row, EDGE : EDGE + cols, :] = finish(second, row)

        @pl.when(flags[1] == 0)
        def _():
            moved[0, EDGE : EDGE + cols, :] = jnp.zeros((cols, levels), F32)

        def begin_first(q):
            stage_rows(first, values, q * CHUNK + 3, CHUNK)
            mix_rows(first, CHUNK)

        def end_first(q):
            for row in range(CHUNK):
                moved[q * CHUNK + row + 2, EDGE : EDGE + cols, :] = finish(first, row)

        def begin_second(q):
            stage_rows(second, moved, q * CHUNK + 1, CHUNK)

        def end_second(q, slot):
            for row in range(CHUNK):
                line = finish(second, row)
                staged[slot, row] = line
                both = line + moved[q * CHUNK + row + 1, EDGE : EDGE + cols, :]
                later_pairs[row * cols : (row + 1) * cols, :] = side_by_side(both)
            put(q, slot).start()
            note_top(q, [staged[slot, row] for row in range(CHUNK)])
            flux = dot_nt(flux_weights[...], later_pairs[...])
            flux = flux[:flux_count] + flux[flux_count:]
            for row in range(CHUNK):
                r = q * CHUNK + row
                block = PHYSICS * flux[:, row * cols : (row + 1) * cols]
                sea = jnp.broadcast_to(mask[pl.ds(r, 1), :], block.shape)
                block = jnp.where(sea > 0.5, block, 0.0)
                fluxes[pl.ds(pl.multiple_of(r * flux_count, flux_count), flux_count), :] = block

        begin_first(0)
        end_first(0)

        def one_chunk(q, _):
            @pl.when(q + 1 < chunks)
            def _():
                fetch(q + 1).wait()

            slot = (q - 1) % 2

            @pl.when(q >= 3)
            def _():
                put(q - 3, slot).wait()

            begin_first(q)
            begin_second(q - 1)
            end_first(q)
            mix_rows(second, CHUNK)
            end_second(q - 1, slot)
            return 0

        lax.fori_loop(1, chunks, one_chunk, 0)

        @pl.when(flags[2] == 0)
        def _():
            moved[rows + 1, EDGE : EDGE + cols, :] = jnp.zeros((cols, levels), F32)

        last = chunks - 1
        put(last - 2, last % 2).wait()
        begin_second(last)
        mix_rows(second, CHUNK)
        end_second(last, last % 2)
        put(last - 1, (last - 1) % 2).wait()
        put(last, last % 2).wait()
        spots = lax.broadcasted_iota(jnp.int32, (source_column.shape[0], rows), 1)
        placing = jnp.where(source_column[...] == spots, 1.0, 0.0).astype(BF16)
        share = flux_count // comp_count
        for c in range(comp_count):
            for f in range(share):
                field = fluxes[pl.ds(c * share + f, rows, stride=flux_count), :].astype(BF16)
                packed[c, : placing.shape[0], f * cols : (f + 1) * cols] = dot_nn(
                    placing, field
                ).astype(BF16)
            packed[c, placing.shape[0] :, :] = labels[...]
        surface[...] = top[...].T

    @pl.when(ocean)
    def sea_side():
        fetch(0).wait()
        lanes = lax.broadcasted_iota(jnp.int32, (CHUNK, CHUNK * levels), 1) // levels
        lines = lax.broadcasted_iota(jnp.int32, (CHUNK, CHUNK * levels), 0)
        spreader = jnp.where(lanes == lines, 1.0, 0.0).astype(F32)

        def one_chunk(q, _):
            base = q * CHUNK

            @pl.when(q + 1 < chunks)
            def _():
                fetch(q + 1).wait()

            stage_rows(first, values, base + 2, CHUNK)
            mix_rows(first, CHUNK)
            slot = q % 2

            @pl.when(q >= 2)
            def _():
                put(q - 2, slot).wait()

            sea = dot_nn(mask[pl.ds(pl.multiple_of(base, CHUNK), CHUNK), :].T, spreader)
            for row in range(CHUNK):
                chosen = sea[:, row * levels : (row + 1) * levels] > 0.5
                before = values[base + row + 2, EDGE : EDGE + cols, :]
                staged[slot, row] = jnp.where(chosen, finish(first, row), before)
            put(q, slot).start()
            note_top(q, [staged[slot, row] for row in range(CHUNK)])
            return 0

        lax.fori_loop(0, chunks, one_chunk, 0)
        put(chunks - 2, (chunks - 2) % 2).wait()
        put(chunks - 1, (chunks - 1) % 2).wait()
        surface[...] = top[...].T
        packed[...] = jnp.zeros(packed.shape, BF16)


def advance(
    flags, source_column, labels, state, halos, mask, mix_atm, mix_ocn, flux_map_t, comp_count, left_at, right_at
):
    rows, cols, levels = state.shape
    fluxes = flux_map_t.shape[0]
    vmem = pl.BlockSpec(memory_space=pltpu.VMEM)
    smem = pl.BlockSpec(memory_space=pltpu.SMEM)
    hbm = pl.BlockSpec(memory_space=pltpu.HBM)
    entry = jax.ShapeDtypeStruct(
        (comp_count, source_column.shape[0] + labels.shape[0], fluxes // comp_count * cols), BF16
    )
    cells = rows * cols
    return pl.pallas_call(
        functools.partial(advance_kernel, comp_count, left_at, right_at),
        out_shape=(
            jax.ShapeDtypeStruct(state.shape, F32),
            jax.ShapeDtypeStruct((rows, cols), F32),
            jax.ShapeDtypeStruct((rows, cols), BF16),
            entry,
        ),
        in_specs=[smem, vmem, vmem, hbm] + [vmem] * (len(halos) + 4),
        out_specs=(hbm, vmem, vmem, vmem),
        scratch_shapes=[
            pltpu.VMEM((rows + 4, cols + 2 * EDGE, levels), F32),
            pltpu.VMEM((rows + 2, cols + 2 * EDGE, levels), F32),
            pltpu.VMEM((2, rows, levels), F32),
            pltpu.VMEM((CHUNK, cols, levels), F32),
            pltpu.VMEM((CHUNK * cols, 2 * levels), BF16),
            pltpu.VMEM((CHUNK * cols, 2 * levels), F32),
            pltpu.VMEM((CHUNK, cols, levels), F32),
            pltpu.VMEM((CHUNK * cols, 2 * levels), BF16),
            pltpu.VMEM((CHUNK * cols, 2 * levels), F32),
            pltpu.VMEM((2 * levels, 2 * levels), BF16),
            pltpu.VMEM((2 * fluxes, 2 * levels), BF16),
            pltpu.VMEM((rows * fluxes, cols), F32),
            pltpu.VMEM((2, CHUNK, cols, levels), F32),
            pltpu.VMEM((cols, levels), F32),
            pltpu.SemaphoreType.DMA((rows // CHUNK,)),
            pltpu.SemaphoreType.DMA((2,)),
        ],
        compiler_params=pltpu.CompilerParams(vmem_limit_bytes=48 * MIB),
        cost_estimate=pl.CostEstimate(
            flops=8 * cells * levels * levels, bytes_accessed=8 * cells * levels, transcendentals=0
        ),
        name="advance",
    )(flags, source_column, labels, state, *halos, mask, mix_atm, mix_ocn, flux_map_t)


BATCH = 8
LABEL_ROWS = 16


def regroup_kernel(slabs, *blocks):
    sources = slabs.shape[0] - 1
    capacity = (blocks[0].shape[0] - LABEL_ROWS) // sources
    size = len(blocks) * capacity
    heads = [slabs[c, size : size + LABEL_ROWS, :].astype(F32) for c in range(sources)]
    lines = [head[i : i + 1] for i in range(2) for head in heads]
    spare = jnp.zeros((LABEL_ROWS - len(lines), heads[0].shape[1]), F32)
    labels = jnp.concatenate(lines + [spare], axis=0).astype(BF16)
    for n, block in enumerate(blocks):
        for c in range(sources):
            block[c * capacity : (c + 1) * capacity, :] = slabs[
                c, n * capacity : (n + 1) * capacity, :
            ]
        block[sources * capacity :, :] = labels


def regroup(slabs, count):
    comps, rows, width = slabs.shape
    size = (rows - LABEL_ROWS) // count * (comps - 1) + LABEL_ROWS
    vmem = pl.BlockSpec(memory_space=pltpu.VMEM)
    return pl.pallas_call(
        regroup_kernel,
        out_shape=(jax.ShapeDtypeStruct((size, width), BF16),) * count,
        in_specs=[vmem],
        out_specs=(vmem,) * count,
        compiler_params=pltpu.CompilerParams(vmem_limit_bytes=16 * MIB),
        name="regroup",
    )(slabs)


def regrid_body(count, comp_count, flags, ocean_first, *refs):
    blocks = refs[:count]
    seas = refs[count : count + comp_count]
    weights, surface, mask, shared, hits, entries, chosen, binned = refs[count + comp_count :]
    sources = comp_count - 1
    rows, cols = mask.shape
    share = shared.shape[0] - 1
    weight_count = weights.shape[0]
    capacity = (blocks[0].shape[0] - LABEL_ROWS) // sources
    size = count * capacity
    total = sources * size
    width = blocks[0].shape[1]
    for c in range(sources):
        for n in range(count):
            start = c * size + n * capacity
            entries[start : start + capacity, :] = blocks[n][c * capacity : (c + 1) * capacity, :]
    lanes = lax.broadcasted_iota(jnp.int32, (LABEL_ROWS, width), 1) // capacity
    labels = jnp.zeros((LABEL_ROWS, width), F32)
    for n in range(count):
        labels = jnp.where(lanes == n, blocks[n][sources * capacity :, :].astype(F32), labels)
    labels = labels.astype(jnp.int32)
    weight_line = jnp.concatenate([labels[c : c + 1, :size] for c in range(sources)], axis=1)
    target_line = jnp.concatenate(
        [labels[sources + c : sources + c + 1, :size] for c in range(sources)], axis=1
    )
    spots = lax.broadcasted_iota(jnp.int32, (rows, total), 0)
    by_target = jnp.where(target_line == spots, 1.0, 0.0)
    own = by_target[:, :size]
    for c in range(1, sources):
        own = jnp.where(flags[3] == c, by_target[:, c * size : (c + 1) * size], own)
    hits[...] = own.T.astype(BF16)
    by_target = by_target.astype(BF16)
    numbers = lax.broadcasted_iota(jnp.int32, (weight_count, total), 0)
    by_weight = jnp.where(weight_line == numbers, 1.0, 0.0).astype(BF16)
    for g in range(weight_count // BATCH):
        for i in range(BATCH):
            w = g * BATCH + i
            chosen[i * rows : (i + 1) * rows, :] = by_target * by_weight[w : w + 1, :]
        binned[...] = dot_nn(chosen[...], entries[...])
        wide = weights[g * BATCH : (g + 1) * BATCH].reshape(BATCH * cols, cols)
        for f in range(share):
            halves = [
                split_two(binned[i * rows : (i + 1) * rows, f * cols : (f + 1) * cols])
                for i in range(BATCH)
            ]
            part = dot_nn(jnp.concatenate([h for h, _ in halves], axis=1), wide) + dot_nn(
                jnp.concatenate([l for _, l in halves], axis=1), wide
            )
            shared[f] = part if g == 0 else shared[f] + part
    change = ocean_first[flags[3] * share] * shared[0]
    for f in range(1, share):
        change = change + ocean_first[flags[3] * share + f] * shared[f]
    sea = jnp.where(flags[0] == 1, seas[sources][...].astype(F32), 0.0)
    for c in range(sources):
        sea = sea + jnp.where(flags[3] == c, seas[c][...].astype(F32), 0.0)
    base = jnp.where(flags[0] == 1, surface[...], 0.0)
    shared[share] = base + jnp.where(sea > 0.5, change, 0.0)


def regrid(flags, ocean_first, blocks, seas, weights, surface, mask):
    comp_count = len(seas)
    sources = comp_count - 1
    rows, cols = mask.shape
    count = len(blocks)
    height, width = blocks[0].shape
    size = (height - LABEL_ROWS) // sources * count
    total = size * sources
    share = width // cols
    weight_count = weights.shape[0]
    vmem = pl.BlockSpec(memory_space=pltpu.VMEM)
    smem = pl.BlockSpec(memory_space=pltpu.SMEM)
    return pl.pallas_call(
        functools.partial(regrid_body, count, comp_count),
        out_shape=(
            jax.ShapeDtypeStruct((share + 1, rows, cols), F32),
            jax.ShapeDtypeStruct((size, rows), BF16),
        ),
        in_specs=[smem, smem] + [vmem] * (count + comp_count + 3),
        out_specs=(vmem, vmem),
        scratch_shapes=[
            pltpu.VMEM((total, width), BF16),
            pltpu.VMEM((BATCH * rows, total), BF16),
            pltpu.VMEM((BATCH * rows, width), F32),
        ],
        compiler_params=pltpu.CompilerParams(vmem_limit_bytes=32 * MIB),
        cost_estimate=pl.CostEstimate(
            flops=2 * weight_count * rows * width * (total + 2 * cols),
            bytes_accessed=2 * MIB,
            transcendentals=0,
        ),
        name="regrid",
    )(flags, ocean_first, *blocks, *seas, weights, surface, mask)


def pick_kernel(count, *refs):
    parts = refs[:count]
    hits, surface = refs[count : count + 2]
    picked = refs[count + 2 :]
    share = parts[0].shape[0] - 1
    now = parts[0][share]
    for part in parts[1:]:
        now = now + part[share]
    surface[...] = now
    pair = jnp.concatenate(split_two(now), axis=0)
    size = picked[0].shape[0]
    for n in range(len(picked)):
        some = hits[n * size : (n + 1) * size, :]
        picked[n][...] = dot_nn(jnp.concatenate([some, some], axis=1), pair)


def pick(parts, hits, neighbours):
    _, rows, cols = parts[0].shape
    size = hits.shape[0] // neighbours
    vmem = pl.BlockSpec(memory_space=pltpu.VMEM)
    return pl.pallas_call(
        functools.partial(pick_kernel, len(parts)),
        out_shape=(jax.ShapeDtypeStruct((rows, cols), F32),)
        + (jax.ShapeDtypeStruct((size, cols), F32),) * neighbours,
        in_specs=[vmem] * (len(parts) + 1),
        out_specs=(vmem,) * (1 + neighbours),
        compiler_params=pltpu.CompilerParams(vmem_limit_bytes=16 * MIB),
        name="pick",
    )(*parts, hits)


LINES = 8


def update_kernel(groups, flags, state, *refs):
    parts = refs[:groups]
    mask, ocean_map, out, token, held, table, wide, in_sems, out_sems = refs[groups:]
    rows, cols, levels = state.shape
    share = parts[0].shape[0] - 1
    flux_count = groups * share
    chunks = rows // LINES
    depth = LINES * flux_count
    token[...] = jnp.zeros(token.shape, F32)

    def fetch(q):
        return pltpu.make_async_copy(
            state.at[pl.ds(q * LINES, LINES)], held.at[pl.ds(q * LINES, LINES)], in_sems.at[q]
        )

    def put(q):
        return pltpu.make_async_copy(
            held.at[pl.ds(q * LINES, LINES)], out.at[pl.ds(q * LINES, LINES)], out_sems.at[q]
        )

    @pl.when(flags[0] == 1)
    def ocean():
        for q in range(chunks):
            fetch(q).start()
        table[...] = jnp.zeros(table.shape, F32)
        for line in range(LINES):
            for f in range(flux_count):
                spot = f * LINES + line
                table[spot : spot + 1, line * levels : (line + 1) * levels] = ocean_map[f : f + 1]
        high, low = split_two(table[...])
        wide[:depth] = high
        wide[depth : 2 * depth] = high
        wide[2 * depth :] = low

        def one(q, _):
            start = pl.multiple_of(q * LINES, LINES)
            sea = mask[pl.ds(start, LINES), :] > 0.5
            part = jnp.concatenate(
                [
                    jnp.where(sea, parts[f // share][f % share, pl.ds(start, LINES), :], 0.0)
                    for f in range(flux_count)
                ],
                axis=0,
            )
            rough = part.astype(BF16).astype(F32)
            turned = jnp.concatenate([rough, part - rough, rough], axis=0).T.astype(BF16)
            change = dot_nn(turned, wide[...])
            fetch(q).wait()
            for line in range(LINES):
                held[start + line] += change[:, line * levels : (line + 1) * levels]
            put(q).start()
            return 0

        lax.fori_loop(0, chunks, one, 0, unroll=2)
        for q in range(chunks):
            put(q).wait()


def update(flags, state, parts, mask, ocean_map):
    rows, cols, levels = state.shape
    depth = LINES * ocean_map.shape[0]
    vmem = pl.BlockSpec(memory_space=pltpu.VMEM)
    smem = pl.BlockSpec(memory_space=pltpu.SMEM)
    hbm = pl.BlockSpec(memory_space=pltpu.HBM)
    return pl.pallas_call(
        functools.partial(update_kernel, len(parts)),
        out_shape=(
            jax.ShapeDtypeStruct(state.shape, F32),
            jax.ShapeDtypeStruct((EDGE, levels), F32),
        ),
        in_specs=[smem, hbm] + [vmem] * (len(parts) + 2),
        out_specs=(hbm, vmem),
        input_output_aliases={1: 0},
        scratch_shapes=[
            pltpu.VMEM(state.shape, F32),
            pltpu.VMEM((depth, LINES * levels), F32),
            pltpu.VMEM((3 * depth, LINES * levels), BF16),
            pltpu.SemaphoreType.DMA((rows // LINES,)),
            pltpu.SemaphoreType.DMA((rows // LINES,)),
        ],
        compiler_params=pltpu.CompilerParams(vmem_limit_bytes=24 * MIB),
        cost_estimate=pl.CostEstimate(
            flops=6 * rows * cols * depth * levels,
            bytes_accessed=8 * rows * cols * levels,
            transcendentals=0,
        ),
        name="update",
    )(flags, state, *parts, mask, ocean_map)


def returned_kernel(groups, flags, *refs):
    picked = refs[:groups]
    weight_column, row_line, weights, mask, surface, new_surface, token, out, total = refs[groups:]
    rows, cols = mask.shape
    weight_count = weights.shape[0]

    @pl.when(flags[0] == 1)
    def ocean():
        out[...] = new_surface[...]

    @pl.when(flags[0] == 0)
    def atmosphere():
        values = jnp.concatenate([p[...] for p in picked], axis=0)
        pair = side_by_side(values)
        which = jnp.broadcast_to(weight_column[...], values.shape)
        total[...] = jnp.zeros(values.shape, F32)

        def one(i, _):
            both = jnp.concatenate([weights[2 * i], weights[2 * i + 1]], axis=0)
            images = dot_nt(pair, jnp.concatenate([both, both], axis=1))
            total[...] += jnp.where(which == 2 * i, images[:, :cols], 0.0) + jnp.where(
                which == 2 * i + 1, images[:, cols:], 0.0
            )
            return 0

        lax.fori_loop(0, weight_count // 2, one, 0, unroll=8)
        spots = lax.broadcasted_iota(jnp.int32, (rows, values.shape[0]), 0)
        chosen = jnp.where(jnp.broadcast_to(row_line[...], spots.shape) == spots, 1.0, 0.0).astype(BF16)
        high, low = split_two(total[...])
        back = dot_nn(chosen, high) + dot_nn(chosen, low)
        out[...] = jnp.where(mask[...] > 0.5, back, surface[...])


def returned(flags, picked, weight_column, row_line, weights, mask, surface, new_surface, token):
    rows, cols = mask.shape
    entry_total = weight_column.shape[0]
    vmem = pl.BlockSpec(memory_space=pltpu.VMEM)
    smem = pl.BlockSpec(memory_space=pltpu.SMEM)
    return pl.pallas_call(
        functools.partial(returned_kernel, len(picked)),
        out_shape=jax.ShapeDtypeStruct((rows, cols), F32),
        in_specs=[smem] + [vmem] * (len(picked) + 7),
        out_specs=vmem,
        scratch_shapes=[pltpu.VMEM((entry_total, cols), F32)],
        compiler_params=pltpu.CompilerParams(vmem_limit_bytes=16 * MIB),
        name="returned",
    )(flags, *picked, weight_column, row_line, weights, mask, surface, new_surface, token)


def local(
    state, land_mask, intersection_list, mix_atm, mix_ocn, flux_map, ocean_map, regrid_weights
):
    rows, cols, levels = state.shape
    intersections = intersection_list.shape[2]
    comp_count = lax.axis_size("comp")
    lat_count = lax.axis_size("lat")
    lon_count = lax.axis_size("lon")
    tile_count = lat_count * lon_count
    reach = min(4, lon_count)
    neighbours = 2 * reach
    entry_total = intersections * rows
    capacity = entry_total // neighbours
    comp_index = lax.axis_index("comp")
    lat_index = lax.axis_index("lat")
    tile_index = lat_index * lon_count + lax.axis_index("lon")
    bands = comp_count * lat_count
    ocean_band = (comp_count - 1) * lat_count
    ocean_comp = comp_count - 1
    band = comp_index * lat_count + lat_index
    is_ocean = comp_index == ocean_comp
    upper_valid = (band > 0) & (band != ocean_band)
    lower_valid = (band < bands - 1) & (band != ocean_band - 1)
    flags = jnp.stack([is_ocean, upper_valid, lower_valid, comp_index]).astype(jnp.int32)
    mask = (land_mask == 1).astype(F32)

    def band_shift(value, by, lon_by):
        pairs = []
        for b in range(bands):
            target = b + by
            if 0 <= target < bands and (b >= ocean_band) == (target >= ocean_band):
                for lon in range(lon_count):
                    pairs.append(
                        (b * lon_count + lon, target * lon_count + (lon + lon_by) % lon_count)
                    )
        return lax.ppermute(value, AXES, pairs)

    first_rows, last_rows, sides = take_edges(state)
    up_rows = band_shift(last_rows, 1, 0)
    low_rows = band_shift(first_rows, -1, 0)
    framed = frame_sides(sides, up_rows, low_rows)
    if lon_count == 2:
        left_cols = right_cols = band_shift(framed, 0, 1)
        left_at, right_at = 2, 0
    else:
        left_cols = band_shift(framed[2:], 0, 1)
        right_cols = band_shift(framed[:2], 0, -1)
        left_at, right_at = 0, 0

    entry_list = intersection_list.reshape(entry_total, 3)
    owners = entry_list[:, 0]
    labels = entry_list[:, 2] * rows + entry_list[:, 1]
    offsets = [
        (n // reach * lon_count + n % reach - (reach - 1) // 2) % tile_count
        for n in range(neighbours)
    ]
    distance = (owners - tile_index + tile_count) % tile_count
    hits = distance[:, None] == jnp.array(offsets, jnp.int32)[None, :]
    neighbour_ids = jnp.sum(
        jnp.where(hits, jnp.arange(neighbours, dtype=jnp.int32)[None, :], 0), axis=1
    )
    positions = jnp.arange(entry_total, dtype=jnp.int32)
    earlier = (neighbour_ids[None, :] == neighbour_ids[:, None]) & (
        positions[None, :] < positions[:, None]
    )
    slots = neighbour_ids * capacity + jnp.sum(earlier.astype(jnp.int32), axis=1)
    placing = positions[:, None] == slots[None, :]
    sources = jnp.sum(jnp.where(placing, (positions // intersections)[None, :], 0), axis=1)
    packed_labels = jnp.sum(jnp.where(placing, labels[None, :], 0), axis=1)

    def over_comp(value):
        return lax.all_to_all(value, "comp", split_axis=0, concat_axis=0, tiled=True)

    def shifted_comp(value, shift):
        pairs = [
            (c * tile_count + t, (c + shift) % comp_count * tile_count + t)
            for c in range(comp_count)
            for t in range(tile_count)
        ]
        return lax.ppermute(value, AXES, pairs)

    def over_tiles(value, offset, comps):
        if offset % tile_count == 0:
            return value
        pairs = [
            (c * tile_count + t, c * tile_count + (t + offset) % tile_count)
            for c in range(comps)
            for t in range(tile_count)
        ]
        return lax.ppermute(value, AXES, pairs)

    def from_ocean(value, comp):
        pairs = [
            (ocean_comp * tile_count + t, comp * tile_count + t) for t in range(tile_count)
        ]
        return lax.ppermute(value, AXES, pairs)

    label_lines = jnp.stack([packed_labels // rows, packed_labels % rows]).astype(BF16)
    label_lines = jnp.pad(label_lines, ((0, LABEL_ROWS - 2), (0, 0)))

    halos = (up_rows, low_rows, left_cols, right_cols, sides)
    moved = advance(
        flags, sources[:, None], label_lines, state, halos, mask, mix_atm, mix_ocn, flux_map.T,
        comp_count, left_at, right_at,
    )
    moved, surface, sea_copy, packed = moved
    slabs = over_comp(packed)
    seas = [from_ocean(sea_copy, c) for c in range(ocean_comp)] + [sea_copy]
    blocks = regroup(slabs, neighbours)
    blocks = [over_tiles(blocks[n], offsets[n], comp_count) for n in range(neighbours)]
    shared, hits = regrid(
        flags, ocean_map[:, 0], blocks, seas, regrid_weights, surface, mask
    )
    parts = [shared] + [shifted_comp(shared, s) for s in range(1, comp_count)]
    picks = pick(parts, hits, neighbours)
    new_surface, picked = picks[0], picks[1:]
    arrived = [over_tiles(picked[n], -offsets[n], ocean_comp) for n in range(neighbours)]
    fields = parts[:0:-1] + parts[:1]
    final_state, token = update(flags, moved, fields, mask, ocean_map)
    weight_column = (packed_labels // rows)[:, None]
    surface_out = returned(
        flags, arrived, weight_column, sources[None, :], regrid_weights, mask, surface, new_surface,
        token,
    )
    return (final_state, surface_out)


def solution(mesh):
    placed = (
        P(("comp", "lat"), "lon", None),
        P(("comp", "lat"), "lon"),
        P(("comp", "lat"), "lon", None, None),
        P(),
        P(),
        P(),
        P(),
        P(),
    )
    return jax.shard_map(
        local,
        mesh=mesh,
        in_specs=placed,
        out_specs=(P(("comp", "lat"), "lon", None), P(("comp", "lat"), "lon")),
        check_vma=False,
    )
```

```python
import functools

import jax
import jax.numpy as jnp
from jax import lax
from jax.experimental import pallas as pl
from jax.experimental.pallas import tpu as pltpu
from jax.sharding import PartitionSpec as P

SMOOTHING = 0.2
PHYSICS = 0.5
MIB = 1024 * 1024
F32 = jnp.float32
BF16 = jnp.bfloat16
EDGE = 8
AHEAD = 4
CHUNK = 8
AXES = ("comp", "lat", "lon")


def split_two(x):
    high = x.astype(BF16)
    low = (x - high.astype(F32)).astype(BF16)
    return high, low


def side_by_side(x):
    return jnp.concatenate(split_two(x), axis=1)


def dot_nt(a, b):
    return lax.dot_general(a, b, (((1,), (1,)), ((), ())), preferred_element_type=F32)


def dot_nn(a, b):
    return jnp.dot(a, b, preferred_element_type=F32)


def edges_kernel(state, first_rows, last_rows, sides, top, bottom, left, right, sems):
    rows, cols, _ = state.shape
    copies = [
        pltpu.make_async_copy(state.at[pl.ds(0, 2)], top, sems.at[0]),
        pltpu.make_async_copy(state.at[pl.ds(rows - 2, 2)], bottom, sems.at[1]),
        pltpu.make_async_copy(state.at[:, pl.ds(0, EDGE)], left, sems.at[2]),
        pltpu.make_async_copy(state.at[:, pl.ds(cols - EDGE, EDGE)], right, sems.at[3]),
    ]
    for copy in copies:
        copy.start()
    for copy in copies:
        copy.wait()
    first_rows[...] = top[...].astype(BF16)
    last_rows[...] = bottom[...].astype(BF16)
    for i in range(2):
        sides[i] = left[:, i, :]
        sides[2 + i] = right[:, EDGE - 2 + i, :]


def take_edges(state):
    rows, cols, levels = state.shape
    slab = jax.ShapeDtypeStruct((2, cols, levels), BF16)
    side = jax.ShapeDtypeStruct((4, rows, levels), F32)
    vmem = pl.BlockSpec(memory_space=pltpu.VMEM)
    return pl.pallas_call(
        edges_kernel,
        out_shape=(slab, slab, side),
        in_specs=[pl.BlockSpec(memory_space=pltpu.HBM)],
        out_specs=(vmem,) * 3,
        scratch_shapes=[
            pltpu.VMEM((2, cols, levels), F32),
            pltpu.VMEM((2, cols, levels), F32),
            pltpu.VMEM((rows, EDGE, levels), F32),
            pltpu.VMEM((rows, EDGE, levels), F32),
            pltpu.SemaphoreType.DMA((4,)),
        ],
        compiler_params=pltpu.CompilerParams(vmem_limit_bytes=50 * MIB),
        name="edges",
    )(state)


def frame_kernel(sides, up_rows, low_rows, framed):
    _, rows, levels = sides.shape
    cols = up_rows.shape[1]
    framed[...] = jnp.zeros(framed.shape, F32)
    above = up_rows[1].astype(F32)
    below = low_rows[0].astype(F32)
    for i, col in enumerate((0, 1, cols - 2, cols - 1)):
        framed[i, EDGE : EDGE + rows, :] = sides[i]
        framed[i, EDGE - 1 : EDGE, :] = above[col : col + 1, :]
        framed[i, EDGE + rows : EDGE + rows + 1, :] = below[col : col + 1, :]


def frame_sides(sides, up_rows, low_rows):
    count, rows, levels = sides.shape
    vmem = pl.BlockSpec(memory_space=pltpu.VMEM)
    return pl.pallas_call(
        frame_kernel,
        out_shape=jax.ShapeDtypeStruct((count, rows + 2 * EDGE, levels), F32),
        in_specs=[vmem] * 3,
        out_specs=vmem,
        compiler_params=pltpu.CompilerParams(vmem_limit_bytes=16 * MIB),
        name="frame",
    )(sides, up_rows, low_rows)


def advance_kernel(comp_count, left_at, right_at, *refs):
    (flags, source_column, labels, state, up_rows, low_rows, left_in, right_in, own_sides) = refs[:9]
    (mask, mix_atm, mix_ocn, flux_map) = refs[9:13]
    out, surface, sea_copy = refs[13:16]
    packed = refs[16]
    (values, moved, halo_moved, smooth, pairs, mixed, later_smooth, later_pairs, later_mixed) = refs[17:26]
    (weights, flux_weights, fluxes, staged, top, in_sems, out_sems) = refs[26:]
    left_cols = left_in.at[left_at : left_at + 2]
    right_cols = right_in.at[right_at : right_at + 2]
    first = (smooth, pairs, mixed)
    second = (later_smooth, later_pairs, later_mixed)
    rows, cols, levels = state.shape
    chunks = rows // CHUNK
    inner = pl.ds(EDGE, cols)
    flux_count = flux_map.shape[0]

    def fetch(q):
        return pltpu.make_async_copy(
            state.at[pl.ds(q * CHUNK, CHUNK)],
            values.at[pl.ds(q * CHUNK + 2, CHUNK), inner],
            in_sems.at[q],
        )

    def put(q, slot):
        return pltpu.make_async_copy(
            staged.at[slot], out.at[pl.ds(q * CHUNK, CHUNK)], out_sems.at[slot]
        )

    def begin(q, _):
        fetch(q).start()
        return 0

    lax.fori_loop(0, AHEAD, begin, 0)
    ocean = flags[0] == 1
    mix = jnp.where(ocean, mix_ocn[...], mix_atm[...])
    mix_high, mix_low = split_two(mix)
    weights[:levels, :levels] = mix_high
    weights[levels:, :levels] = mix_high
    weights[:levels, levels:] = mix_low
    weights[levels:, levels:] = mix_low
    sea_copy[...] = mask[...].astype(BF16)
    map_high, map_low = split_two(flux_map[...])
    flux_weights[...] = jnp.concatenate(
        [
            jnp.concatenate([map_high.astype(F32), map_high.astype(F32)], axis=1),
            jnp.concatenate([map_low.astype(F32), map_low.astype(F32)], axis=1),
        ],
        axis=0,
    ).astype(BF16)
    values[0:2, EDGE : EDGE + cols, :] = up_rows[...].astype(F32)
    values[rows + 2 : rows + 4, EDGE : EDGE + cols, :] = low_rows[...].astype(F32)
    for r, i in ((1, EDGE - 1), (rows + 2, EDGE + rows)):
        values[r, EDGE - 1 : EDGE, :] = left_cols[1, i : i + 1, :]
        values[r, EDGE + cols : EDGE + cols + 1, :] = right_cols[0, i : i + 1, :]

    def side_cells(start, count):
        for row in range(count):
            values[start + row + 2, EDGE - 1 : EDGE, :] = left_cols[1, pl.ds(start + row + EDGE, 1), :]
            values[start + row + 2, EDGE + cols : EDGE + cols + 1, :] = right_cols[
                0, pl.ds(start + row + EDGE, 1), :
            ]

    def moved_sides(start, count):
        for row in range(count):
            moved[start + row + 1, EDGE - 1 : EDGE, :] = halo_moved[0, pl.ds(start + row, 1), :]
            moved[start + row + 1, EDGE + cols : EDGE + cols + 1, :] = halo_moved[
                1, pl.ds(start + row, 1), :
            ]

    def stage(refs, row, total):
        line = SMOOTHING * total
        refs[0][row] = line
        refs[1][row * cols : (row + 1) * cols, :] = side_by_side(line)

    def stage_rows(refs, ref, start, count):
        for row in range(count):
            i = start + row
            here = ref[i, EDGE : EDGE + cols, :] + (
                ref[i - 1, EDGE : EDGE + cols, :] + ref[i + 1, EDGE : EDGE + cols, :]
            )
            near = ref[i, EDGE - 1 : EDGE - 1 + cols, :] + ref[i, EDGE + 1 : EDGE + 1 + cols, :]
            stage(refs, row, here + near)

    def note_top(q, lines):
        lanes = lax.broadcasted_iota(jnp.int32, (cols, levels), 1)
        kept = lines[0]
        for row in range(1, CHUNK):
            kept = jnp.where(lanes == row, pltpu.roll(lines[row], row, 1), kept)
        turned = pltpu.roll(kept, q * CHUNK, 1)
        top[...] = jnp.where(lanes // CHUNK == q, turned, top[...])

    def mix_rows(refs, count):
        refs[2][: count * cols, :] = dot_nn(refs[1][: count * cols, :], weights[...])

    def finish(refs, row):
        part = refs[2][row * cols : (row + 1) * cols, :]
        return refs[0][row] + PHYSICS * jnp.tanh(part[:, :levels] + part[:, levels:])

    @pl.when(jnp.logical_not(ocean))
    def atmosphere():
        nearest = (left_cols.at[1], right_cols.at[0])
        beyond = (left_cols.at[0], right_cols.at[1])
        within = (own_sides.at[0], own_sides.at[3])
        for s in range(2):
            total = (
                nearest[s][EDGE : EDGE + rows, :]
                + nearest[s][EDGE - 1 : EDGE - 1 + rows, :]
                + nearest[s][EDGE + 1 : EDGE + 1 + rows, :]
            )
            stage(first, s, total + (beyond[s][EDGE : EDGE + rows, :] + within[s][...]))
        mix_rows(first, 2)
        for s in range(2):
            halo_moved[s] = finish(first, s)

        side_cells(0, 1)
        fetch(0).wait()
        fetch(1).wait()
        stage_rows(second, values, 1, 2)
        mix_rows(second, 2)
        for row in range(2):
            moved[row, EDGE : EDGE + cols, :] = finish(second, row)

        @pl.when(flags[1] == 0)
        def _():
            moved[0, EDGE : EDGE + cols, :] = jnp.zeros((cols, levels), F32)

        def begin_first(q):
            side_cells(jnp.minimum(q * CHUNK + 1, rows - CHUNK), CHUNK)
            stage_rows(first, values, q * CHUNK + 3, CHUNK)
            mix_rows(first, CHUNK)

        def end_first(q):
            for row in range(CHUNK):
                moved[q * CHUNK + row + 2, EDGE : EDGE + cols, :] = finish(first, row)

        def begin_second(q):
            moved_sides(q * CHUNK, CHUNK)
            stage_rows(second, moved, q * CHUNK + 1, CHUNK)

        def end_second(q, slot):
            for row in range(CHUNK):
                line = finish(second, row)
                staged[slot, row] = line
                both = line + moved[q * CHUNK + row + 1, EDGE : EDGE + cols, :]
                later_pairs[row * cols : (row + 1) * cols, :] = side_by_side(both)
            put(q, slot).start()
            note_top(q, [staged[slot, row] for row in range(CHUNK)])
            flux = dot_nt(flux_weights[...], later_pairs[...])
            flux = flux[:flux_count] + flux[flux_count:]
            for row in range(CHUNK):
                r = q * CHUNK + row
                block = PHYSICS * flux[:, row * cols : (row + 1) * cols]
                sea = jnp.broadcast_to(mask[pl.ds(r, 1), :], block.shape)
                block = jnp.where(sea > 0.5, block, 0.0)
                fluxes[pl.ds(pl.multiple_of(r * flux_count, flux_count), flux_count), :] = block

        fetch(AHEAD).start()
        begin_first(0)
        end_first(0)

        def one_chunk(q, _):
            @pl.when(q + 1 < chunks)
            def _():
                fetch(q + 1).wait()

            @pl.when(q + AHEAD < chunks)
            def _():
                fetch(q + AHEAD).start()

            slot = (q - 1) % 2

            @pl.when(q >= 3)
            def _():
                put(q - 3, slot).wait()

            begin_first(q)
            begin_second(q - 1)
            end_first(q)
            mix_rows(second, CHUNK)
            end_second(q - 1, slot)
            return 0

        lax.fori_loop(1, chunks, one_chunk, 0)

        @pl.when(flags[2] == 0)
        def _():
            moved[rows + 1, EDGE : EDGE + cols, :] = jnp.zeros((cols, levels), F32)

        last = chunks - 1
        put(last - 2, last % 2).wait()
        begin_second(last)
        mix_rows(second, CHUNK)
        end_second(last, last % 2)
        spots = lax.broadcasted_iota(jnp.int32, (source_column.shape[0], rows), 1)
        placing = jnp.where(source_column[...] == spots, 1.0, 0.0).astype(BF16)
        share = flux_count // comp_count
        for c in range(comp_count):
            for f in range(share):
                field = fluxes[pl.ds(c * share + f, rows, stride=flux_count), :].astype(BF16)
                packed[c, : placing.shape[0], f * cols : (f + 1) * cols] = dot_nn(
                    placing, field
                ).astype(BF16)
            packed[c, placing.shape[0] :, :] = labels[...]
        put(last - 1, (last - 1) % 2).wait()
        put(last, last % 2).wait()
        surface[...] = top[...].T

    @pl.when(ocean)
    def sea_side():
        fetch(0).wait()
        lanes = lax.broadcasted_iota(jnp.int32, (CHUNK, CHUNK * levels), 1) // levels
        lines = lax.broadcasted_iota(jnp.int32, (CHUNK, CHUNK * levels), 0)
        spreader = jnp.where(lanes == lines, 1.0, 0.0).astype(F32)

        def one_chunk(q, _):
            base = q * CHUNK

            @pl.when(q + 1 < chunks)
            def _():
                fetch(q + 1).wait()

            @pl.when(q + AHEAD < chunks)
            def _():
                fetch(q + AHEAD).start()

            side_cells(base, CHUNK)
            stage_rows(first, values, base + 2, CHUNK)
            mix_rows(first, CHUNK)
            slot = q % 2

            @pl.when(q >= 2)
            def _():
                put(q - 2, slot).wait()

            sea = dot_nn(mask[pl.ds(pl.multiple_of(base, CHUNK), CHUNK), :].T, spreader)
            for row in range(CHUNK):
                chosen = sea[:, row * levels : (row + 1) * levels] > 0.5
                before = values[base + row + 2, EDGE : EDGE + cols, :]
                staged[slot, row] = jnp.where(chosen, finish(first, row), before)
            put(q, slot).start()
            note_top(q, [staged[slot, row] for row in range(CHUNK)])
            return 0

        lax.fori_loop(0, chunks, one_chunk, 0)
        put(chunks - 2, (chunks - 2) % 2).wait()
        put(chunks - 1, (chunks - 1) % 2).wait()
        surface[...] = top[...].T
        packed[...] = jnp.zeros(packed.shape, BF16)


def advance(
    flags, source_column, labels, state, halos, mask, mix_atm, mix_ocn, flux_map_t, comp_count, left_at, right_at
):
    rows, cols, levels = state.shape
    fluxes = flux_map_t.shape[0]
    vmem = pl.BlockSpec(memory_space=pltpu.VMEM)
    smem = pl.BlockSpec(memory_space=pltpu.SMEM)
    hbm = pl.BlockSpec(memory_space=pltpu.HBM)
    entry = jax.ShapeDtypeStruct(
        (comp_count, source_column.shape[0] + labels.shape[0], fluxes // comp_count * cols), BF16
    )
    cells = rows * cols
    return pl.pallas_call(
        functools.partial(advance_kernel, comp_count, left_at, right_at),
        out_shape=(
            jax.ShapeDtypeStruct(state.shape, F32),
            jax.ShapeDtypeStruct((rows, cols), F32),
            jax.ShapeDtypeStruct((rows, cols), BF16),
            entry,
        ),
        in_specs=[smem, vmem, vmem, hbm] + [vmem] * (len(halos) + 4),
        out_specs=(hbm, vmem, vmem, vmem),
        scratch_shapes=[
            pltpu.VMEM((rows + 4, cols + 2 * EDGE, levels), F32),
            pltpu.VMEM((rows + 2, cols + 2 * EDGE, levels), F32),
            pltpu.VMEM((2, rows, levels), F32),
            pltpu.VMEM((CHUNK, cols, levels), F32),
            pltpu.VMEM((CHUNK * cols, 2 * levels), BF16),
            pltpu.VMEM((CHUNK * cols, 2 * levels), F32),
            pltpu.VMEM((CHUNK, cols, levels), F32),
            pltpu.VMEM((CHUNK * cols, 2 * levels), BF16),
            pltpu.VMEM((CHUNK * cols, 2 * levels), F32),
            pltpu.VMEM((2 * levels, 2 * levels), BF16),
            pltpu.VMEM((2 * fluxes, 2 * levels), BF16),
            pltpu.VMEM((rows * fluxes, cols), F32),
            pltpu.VMEM((2, CHUNK, cols, levels), F32),
            pltpu.VMEM((cols, levels), F32),
            pltpu.SemaphoreType.DMA((rows // CHUNK,)),
            pltpu.SemaphoreType.DMA((2,)),
        ],
        compiler_params=pltpu.CompilerParams(vmem_limit_bytes=48 * MIB),
        cost_estimate=pl.CostEstimate(
            flops=8 * cells * levels * levels, bytes_accessed=8 * cells * levels, transcendentals=0
        ),
        name="advance",
    )(flags, source_column, labels, state, *halos, mask, mix_atm, mix_ocn, flux_map_t)


BATCH = 8
LABEL_ROWS = 16


def regroup_kernel(slabs, *blocks):
    sources = slabs.shape[0] - 1
    capacity = (blocks[0].shape[0] - LABEL_ROWS) // sources
    size = len(blocks) * capacity
    heads = [slabs[c, size : size + LABEL_ROWS, :].astype(F32) for c in range(sources)]
    lines = [head[i : i + 1] for i in range(2) for head in heads]
    spare = jnp.zeros((LABEL_ROWS - len(lines), heads[0].shape[1]), F32)
    labels = jnp.concatenate(lines + [spare], axis=0).astype(BF16)
    for n, block in enumerate(blocks):
        for c in range(sources):
            block[c * capacity : (c + 1) * capacity, :] = slabs[
                c, n * capacity : (n + 1) * capacity, :
            ]
        block[sources * capacity :, :] = labels


def regroup(slabs, count):
    comps, rows, width = slabs.shape
    size = (rows - LABEL_ROWS) // count * (comps - 1) + LABEL_ROWS
    vmem = pl.BlockSpec(memory_space=pltpu.VMEM)
    return pl.pallas_call(
        regroup_kernel,
        out_shape=(jax.ShapeDtypeStruct((size, width), BF16),) * count,
        in_specs=[vmem],
        out_specs=(vmem,) * count,
        compiler_params=pltpu.CompilerParams(vmem_limit_bytes=16 * MIB),
        name="regroup",
    )(slabs)


def regrid_body(count, comp_count, flags, ocean_first, *refs):
    blocks = refs[:count]
    seas = refs[count : count + comp_count]
    weights, surface, mask, forcing, shared, hits, entries, chosen, binned = refs[count + comp_count :]
    sources = comp_count - 1
    rows, cols = mask.shape
    share = forcing.shape[0]
    weight_count = weights.shape[0]
    capacity = (blocks[0].shape[0] - LABEL_ROWS) // sources
    size = count * capacity
    total = sources * size
    width = blocks[0].shape[1]
    for c in range(sources):
        for n in range(count):
            start = c * size + n * capacity
            entries[start : start + capacity, :] = blocks[n][c * capacity : (c + 1) * capacity, :]
    lanes = lax.broadcasted_iota(jnp.int32, (LABEL_ROWS, width), 1) // capacity
    labels = jnp.zeros((LABEL_ROWS, width), F32)
    for n in range(count):
        labels = jnp.where(lanes == n, blocks[n][sources * capacity :, :].astype(F32), labels)
    labels = labels.astype(jnp.int32)
    weight_line = jnp.concatenate([labels[c : c + 1, :size] for c in range(sources)], axis=1)
    target_line = jnp.concatenate(
        [labels[sources + c : sources + c + 1, :size] for c in range(sources)], axis=1
    )
    spots = lax.broadcasted_iota(jnp.int32, (rows, total), 0)
    by_target = jnp.where(target_line == spots, 1.0, 0.0)
    own = by_target[:, :size]
    for c in range(1, sources):
        own = jnp.where(flags[3] == c, by_target[:, c * size : (c + 1) * size], own)
    hits[...] = own.T.astype(BF16)
    by_target = by_target.astype(BF16)
    numbers = lax.broadcasted_iota(jnp.int32, (weight_count, total), 0)
    by_weight = jnp.where(weight_line == numbers, 1.0, 0.0).astype(BF16)
    for g in range(weight_count // BATCH):
        for i in range(BATCH):
            w = g * BATCH + i
            chosen[i * rows : (i + 1) * rows, :] = by_target * by_weight[w : w + 1, :]
        binned[...] = dot_nn(chosen[...], entries[...])
        wide = weights[g * BATCH : (g + 1) * BATCH].reshape(BATCH * cols, cols)
        halves = [
            [
                split_two(binned[i * rows : (i + 1) * rows, f * cols : (f + 1) * cols])
                for i in range(BATCH)
            ]
            for f in range(share)
        ]
        stacked = jnp.concatenate(
            [
                jnp.concatenate([half[k] for half in halves[f]], axis=1)
                for k in range(2)
                for f in range(share)
            ],
            axis=0,
        )
        product = dot_nn(stacked, wide)
        for f in range(share):
            part = product[f * rows : (f + 1) * rows] + product[
                (share + f) * rows : (share + f + 1) * rows
            ]
            forcing[f] = part if g == 0 else forcing[f] + part
    change = ocean_first[flags[3] * share] * forcing[0]
    for f in range(1, share):
        change = change + ocean_first[flags[3] * share + f] * forcing[f]
    sea = jnp.where(flags[0] == 1, seas[sources][...].astype(F32), 0.0)
    for c in range(sources):
        sea = sea + jnp.where(flags[3] == c, seas[c][...].astype(F32), 0.0)
    base = jnp.where(flags[0] == 1, surface[...], 0.0)
    shared[...] = base + jnp.where(sea > 0.5, change, 0.0)


def regrid(flags, ocean_first, blocks, seas, weights, surface, mask):
    comp_count = len(seas)
    sources = comp_count - 1
    rows, cols = mask.shape
    count = len(blocks)
    height, width = blocks[0].shape
    size = (height - LABEL_ROWS) // sources * count
    total = size * sources
    share = width // cols
    weight_count = weights.shape[0]
    vmem = pl.BlockSpec(memory_space=pltpu.VMEM)
    smem = pl.BlockSpec(memory_space=pltpu.SMEM)
    return pl.pallas_call(
        functools.partial(regrid_body, count, comp_count),
        out_shape=(
            jax.ShapeDtypeStruct((share, rows, cols), F32),
            jax.ShapeDtypeStruct((rows, cols), F32),
            jax.ShapeDtypeStruct((size, rows), BF16),
        ),
        in_specs=[smem, smem] + [vmem] * (count + comp_count + 3),
        out_specs=(vmem, vmem, vmem),
        scratch_shapes=[
            pltpu.VMEM((total, width), BF16),
            pltpu.VMEM((BATCH * rows, total), BF16),
            pltpu.VMEM((BATCH * rows, width), F32),
        ],
        compiler_params=pltpu.CompilerParams(vmem_limit_bytes=32 * MIB),
        cost_estimate=pl.CostEstimate(
            flops=2 * weight_count * rows * width * (total + 2 * cols),
            bytes_accessed=2 * MIB,
            transcendentals=0,
        ),
        name="regrid",
    )(flags, ocean_first, *blocks, *seas, weights, surface, mask)


def pick_kernel(count, *refs):
    parts = refs[:count]
    hits, surface = refs[count : count + 2]
    picked = refs[count + 2 :]
    now = parts[0][...]
    for part in parts[1:]:
        now = now + part[...]
    surface[...] = now
    pair = jnp.concatenate(split_two(now), axis=0)
    size = picked[0].shape[0]
    for n in range(len(picked)):
        some = hits[n * size : (n + 1) * size, :]
        picked[n][...] = dot_nn(jnp.concatenate([some, some], axis=1), pair)


def pick(parts, hits, neighbours):
    rows, cols = parts[0].shape
    size = hits.shape[0] // neighbours
    vmem = pl.BlockSpec(memory_space=pltpu.VMEM)
    return pl.pallas_call(
        functools.partial(pick_kernel, len(parts)),
        out_shape=(jax.ShapeDtypeStruct((rows, cols), F32),)
        + (jax.ShapeDtypeStruct((size, cols), F32),) * neighbours,
        in_specs=[vmem] * (len(parts) + 1),
        out_specs=(vmem,) * (1 + neighbours),
        compiler_params=pltpu.CompilerParams(vmem_limit_bytes=16 * MIB),
        name="pick",
    )(*parts, hits)


LINES = 8


def update_kernel(groups, flags, state, *refs):
    parts = refs[:groups]
    mask, ocean_map, out, token, held, table, wide, in_sems, out_sems = refs[groups:]
    rows, cols, levels = state.shape
    share = parts[0].shape[0]
    flux_count = groups * share
    chunks = rows // LINES
    depth = LINES * flux_count
    token[...] = jnp.zeros(token.shape, F32)

    def fetch(q):
        return pltpu.make_async_copy(
            state.at[pl.ds(q * LINES, LINES)], held.at[pl.ds(q * LINES, LINES)], in_sems.at[q]
        )

    def put(q):
        return pltpu.make_async_copy(
            held.at[pl.ds(q * LINES, LINES)], out.at[pl.ds(q * LINES, LINES)], out_sems.at[q]
        )

    @pl.when(flags[0] == 1)
    def ocean():
        for q in range(chunks):
            fetch(q).start()
        table[...] = jnp.zeros(table.shape, F32)
        for line in range(LINES):
            for f in range(flux_count):
                spot = f * LINES + line
                table[spot : spot + 1, line * levels : (line + 1) * levels] = ocean_map[f : f + 1]
        high, low = split_two(table[...])
        wide[:depth] = high
        wide[depth : 2 * depth] = high
        wide[2 * depth :] = low

        def one(q, _):
            start = pl.multiple_of(q * LINES, LINES)
            sea = mask[pl.ds(start, LINES), :] > 0.5
            part = jnp.concatenate(
                [
                    jnp.where(sea, parts[f // share][f % share, pl.ds(start, LINES), :], 0.0)
                    for f in range(flux_count)
                ],
                axis=0,
            )
            rough = part.astype(BF16).astype(F32)
            turned = jnp.concatenate([rough, part - rough, rough], axis=0).T.astype(BF16)
            change = dot_nn(turned, wide[...])
            fetch(q).wait()
            for line in range(LINES):
                held[start + line] += change[:, line * levels : (line + 1) * levels]
            put(q).start()
            return 0

        lax.fori_loop(0, chunks, one, 0, unroll=2)
        for q in range(chunks):
            put(q).wait()


def update(flags, state, parts, mask, ocean_map):
    rows, cols, levels = state.shape
    depth = LINES * ocean_map.shape[0]
    vmem = pl.BlockSpec(memory_space=pltpu.VMEM)
    smem = pl.BlockSpec(memory_space=pltpu.SMEM)
    hbm = pl.BlockSpec(memory_space=pltpu.HBM)
    return pl.pallas_call(
        functools.partial(update_kernel, len(parts)),
        out_shape=(
            jax.ShapeDtypeStruct(state.shape, F32),
            jax.ShapeDtypeStruct((EDGE, levels), F32),
        ),
        in_specs=[smem, hbm] + [vmem] * (len(parts) + 2),
        out_specs=(hbm, vmem),
        input_output_aliases={1: 0},
        scratch_shapes=[
            pltpu.VMEM(state.shape, F32),
            pltpu.VMEM((depth, LINES * levels), F32),
            pltpu.VMEM((3 * depth, LINES * levels), BF16),
            pltpu.SemaphoreType.DMA((rows // LINES,)),
            pltpu.SemaphoreType.DMA((rows // LINES,)),
        ],
        compiler_params=pltpu.CompilerParams(vmem_limit_bytes=24 * MIB),
        cost_estimate=pl.CostEstimate(
            flops=6 * rows * cols * depth * levels,
            bytes_accessed=8 * rows * cols * levels,
            transcendentals=0,
        ),
        name="update",
    )(flags, state, *parts, mask, ocean_map)


def returned_kernel(groups, flags, *refs):
    picked = refs[:groups]
    weight_column, row_line, weights, mask, surface, new_surface, token, out, total = refs[groups:]
    rows, cols = mask.shape
    weight_count = weights.shape[0]

    @pl.when(flags[0] == 1)
    def ocean():
        out[...] = new_surface[...]

    @pl.when(flags[0] == 0)
    def atmosphere():
        values = jnp.concatenate([p[...] for p in picked], axis=0)
        pair = side_by_side(values)
        which = jnp.broadcast_to(weight_column[...], values.shape)
        total[...] = jnp.zeros(values.shape, F32)

        def one(i, _):
            both = jnp.concatenate([weights[2 * i], weights[2 * i + 1]], axis=0)
            images = dot_nt(pair, jnp.concatenate([both, both], axis=1))
            total[...] += jnp.where(which == 2 * i, images[:, :cols], 0.0) + jnp.where(
                which == 2 * i + 1, images[:, cols:], 0.0
            )
            return 0

        lax.fori_loop(0, weight_count // 2, one, 0, unroll=8)
        spots = lax.broadcasted_iota(jnp.int32, (rows, values.shape[0]), 0)
        chosen = jnp.where(jnp.broadcast_to(row_line[...], spots.shape) == spots, 1.0, 0.0).astype(BF16)
        high, low = split_two(total[...])
        back = dot_nn(chosen, high) + dot_nn(chosen, low)
        out[...] = jnp.where(mask[...] > 0.5, back, surface[...])


def returned(flags, picked, weight_column, row_line, weights, mask, surface, new_surface, token):
    rows, cols = mask.shape
    entry_total = weight_column.shape[0]
    vmem = pl.BlockSpec(memory_space=pltpu.VMEM)
    smem = pl.BlockSpec(memory_space=pltpu.SMEM)
    return pl.pallas_call(
        functools.partial(returned_kernel, len(picked)),
        out_shape=jax.ShapeDtypeStruct((rows, cols), F32),
        in_specs=[smem] + [vmem] * (len(picked) + 7),
        out_specs=vmem,
        scratch_shapes=[pltpu.VMEM((entry_total, cols), F32)],
        compiler_params=pltpu.CompilerParams(vmem_limit_bytes=16 * MIB),
        name="returned",
    )(flags, *picked, weight_column, row_line, weights, mask, surface, new_surface, token)


def local(
    state, land_mask, intersection_list, mix_atm, mix_ocn, flux_map, ocean_map, regrid_weights
):
    rows, cols, levels = state.shape
    intersections = intersection_list.shape[2]
    comp_count = lax.axis_size("comp")
    lat_count = lax.axis_size("lat")
    lon_count = lax.axis_size("lon")
    tile_count = lat_count * lon_count
    reach = min(4, lon_count)
    neighbours = 2 * reach
    entry_total = intersections * rows
    capacity = entry_total // neighbours
    comp_index = lax.axis_index("comp")
    lat_index = lax.axis_index("lat")
    tile_index = lat_index * lon_count + lax.axis_index("lon")
    bands = comp_count * lat_count
    ocean_band = (comp_count - 1) * lat_count
    ocean_comp = comp_count - 1
    band = comp_index * lat_count + lat_index
    is_ocean = comp_index == ocean_comp
    upper_valid = (band > 0) & (band != ocean_band)
    lower_valid = (band < bands - 1) & (band != ocean_band - 1)
    flags = jnp.stack([is_ocean, upper_valid, lower_valid, comp_index]).astype(jnp.int32)
    mask = (land_mask == 1).astype(F32)

    def band_shift(value, by, lon_by):
        pairs = []
        for b in range(bands):
            target = b + by
            if 0 <= target < bands and (b >= ocean_band) == (target >= ocean_band):
                for lon in range(lon_count):
                    pairs.append(
                        (b * lon_count + lon, target * lon_count + (lon + lon_by) % lon_count)
                    )
        return lax.ppermute(value, AXES, pairs)

    first_rows, last_rows, sides = take_edges(state)
    up_rows = band_shift(last_rows, 1, 0)
    low_rows = band_shift(first_rows, -1, 0)
    framed = frame_sides(sides, up_rows, low_rows)
    if lon_count == 2:
        left_cols = right_cols = band_shift(framed, 0, 1)
        left_at, right_at = 2, 0
    else:
        left_cols = band_shift(framed[2:], 0, 1)
        right_cols = band_shift(framed[:2], 0, -1)
        left_at, right_at = 0, 0

    entry_list = intersection_list.reshape(entry_total, 3)
    owners = entry_list[:, 0]
    labels = entry_list[:, 2] * rows + entry_list[:, 1]
    offsets = [
        (n // reach * lon_count + n % reach - (reach - 1) // 2) % tile_count
        for n in range(neighbours)
    ]
    distance = (owners - tile_index + tile_count) % tile_count
    hits = distance[:, None] == jnp.array(offsets, jnp.int32)[None, :]
    neighbour_ids = jnp.sum(
        jnp.where(hits, jnp.arange(neighbours, dtype=jnp.int32)[None, :], 0), axis=1
    )
    positions = jnp.arange(entry_total, dtype=jnp.int32)
    earlier = (neighbour_ids[None, :] == neighbour_ids[:, None]) & (
        positions[None, :] < positions[:, None]
    )
    slots = neighbour_ids * capacity + jnp.sum(earlier.astype(jnp.int32), axis=1)
    placing = positions[:, None] == slots[None, :]
    sources = jnp.sum(jnp.where(placing, (positions // intersections)[None, :], 0), axis=1)
    packed_labels = jnp.sum(jnp.where(placing, labels[None, :], 0), axis=1)

    def over_comp(value):
        return lax.all_to_all(value, "comp", split_axis=0, concat_axis=0, tiled=True)

    def shifted_comp(value, shift):
        pairs = [
            (c * tile_count + t, (c + shift) % comp_count * tile_count + t)
            for c in range(comp_count)
            for t in range(tile_count)
        ]
        return lax.ppermute(value, AXES, pairs)

    def over_tiles(value, offset, comps):
        if offset % tile_count == 0:
            return value
        pairs = [
            (c * tile_count + t, c * tile_count + (t + offset) % tile_count)
            for c in range(comps)
            for t in range(tile_count)
        ]
        return lax.ppermute(value, AXES, pairs)

    def from_ocean(value, comp):
        pairs = [
            (ocean_comp * tile_count + t, comp * tile_count + t) for t in range(tile_count)
        ]
        return lax.ppermute(value, AXES, pairs)

    def to_ocean(value, comp):
        pairs = [
            (comp * tile_count + t, ocean_comp * tile_count + t) for t in range(tile_count)
        ]
        return lax.ppermute(value, AXES, pairs)

    label_lines = jnp.stack([packed_labels // rows, packed_labels % rows]).astype(BF16)
    label_lines = jnp.pad(label_lines, ((0, LABEL_ROWS - 2), (0, 0)))

    halos = (up_rows, low_rows, left_cols, right_cols, sides)
    moved = advance(
        flags, sources[:, None], label_lines, state, halos, mask, mix_atm, mix_ocn, flux_map.T,
        comp_count, left_at, right_at,
    )
    moved, surface, sea_copy, packed = moved
    slabs = over_comp(packed)
    seas = [from_ocean(sea_copy, c) for c in range(ocean_comp)] + [sea_copy]
    blocks = regroup(slabs, neighbours)
    blocks = [over_tiles(blocks[n], offsets[n], comp_count) for n in range(neighbours)]
    forcing, shared, hits = regrid(
        flags, ocean_map[:, 0], blocks, seas, regrid_weights, surface, mask
    )
    parts = [shared] + [shifted_comp(shared, s) for s in range(1, comp_count)]
    parts[1], forcing = lax.optimization_barrier((parts[1], forcing))
    picks = pick(parts, hits, neighbours)
    new_surface, picked = picks[0], picks[1:]
    arrived = [over_tiles(picked[n], -offsets[n], ocean_comp) for n in range(neighbours)]
    fields = [to_ocean(forcing, c) for c in range(ocean_comp)] + [forcing]
    final_state, token = update(flags, moved, fields, mask, ocean_map)
    weight_column = (packed_labels // rows)[:, None]
    surface_out = returned(
        flags, arrived, weight_column, sources[None, :], regrid_weights, mask, surface, new_surface,
        token,
    )
    return (final_state, surface_out)


def solution(mesh):
    placed = (
        P(("comp", "lat"), "lon", None),
        P(("comp", "lat"), "lon"),
        P(("comp", "lat"), "lon", None, None),
        P(),
        P(),
        P(),
        P(),
        P(),
    )
    return jax.shard_map(
        local,
        mesh=mesh,
        in_specs=placed,
        out_specs=(P(("comp", "lat"), "lon", None), P(("comp", "lat"), "lon")),
        check_vma=False,
    )
```

```python
import functools

import jax
import jax.numpy as jnp
from jax import lax
from jax.experimental import pallas as pl
from jax.experimental.pallas import tpu as pltpu
from jax.sharding import PartitionSpec as P

SMOOTHING = 0.2
PHYSICS = 0.5
MIB = 1024 * 1024
F32 = jnp.float32
BF16 = jnp.bfloat16
EDGE = 8
AHEAD = 4
CHUNK = 8
AXES = ("comp", "lat", "lon")


def split_two(x):
    high = x.astype(BF16)
    low = (x - high.astype(F32)).astype(BF16)
    return high, low


def side_by_side(x):
    return jnp.concatenate(split_two(x), axis=1)


def dot_nt(a, b):
    return lax.dot_general(a, b, (((1,), (1,)), ((), ())), preferred_element_type=F32)


def dot_nn(a, b):
    return jnp.dot(a, b, preferred_element_type=F32)


def edges_kernel(state, first_rows, last_rows, sides, top, bottom, left, right, sems):
    rows, cols, _ = state.shape
    copies = [
        pltpu.make_async_copy(state.at[pl.ds(0, 2)], top, sems.at[0]),
        pltpu.make_async_copy(state.at[pl.ds(rows - 2, 2)], bottom, sems.at[1]),
        pltpu.make_async_copy(state.at[:, pl.ds(0, EDGE)], left, sems.at[2]),
        pltpu.make_async_copy(state.at[:, pl.ds(cols - EDGE, EDGE)], right, sems.at[3]),
    ]
    for copy in copies:
        copy.start()
    for copy in copies:
        copy.wait()
    first_rows[...] = top[...].astype(BF16)
    last_rows[...] = bottom[...].astype(BF16)
    for i in range(2):
        sides[i] = left[:, i, :]
        sides[2 + i] = right[:, EDGE - 2 + i, :]


def take_edges(state):
    rows, cols, levels = state.shape
    slab = jax.ShapeDtypeStruct((2, cols, levels), BF16)
    side = jax.ShapeDtypeStruct((4, rows, levels), F32)
    vmem = pl.BlockSpec(memory_space=pltpu.VMEM)
    return pl.pallas_call(
        edges_kernel,
        out_shape=(slab, slab, side),
        in_specs=[pl.BlockSpec(memory_space=pltpu.HBM)],
        out_specs=(vmem,) * 3,
        scratch_shapes=[
            pltpu.VMEM((2, cols, levels), F32),
            pltpu.VMEM((2, cols, levels), F32),
            pltpu.VMEM((rows, EDGE, levels), F32),
            pltpu.VMEM((rows, EDGE, levels), F32),
            pltpu.SemaphoreType.DMA((4,)),
        ],
        compiler_params=pltpu.CompilerParams(vmem_limit_bytes=50 * MIB),
        name="edges",
    )(state)


def frame_kernel(sides, up_rows, low_rows, framed):
    _, rows, levels = sides.shape
    cols = up_rows.shape[1]
    framed[...] = jnp.zeros(framed.shape, F32)
    above = up_rows[1].astype(F32)
    below = low_rows[0].astype(F32)
    for i, col in enumerate((0, 1, cols - 2, cols - 1)):
        framed[i, EDGE : EDGE + rows, :] = sides[i]
        framed[i, EDGE - 1 : EDGE, :] = above[col : col + 1, :]
        framed[i, EDGE + rows : EDGE + rows + 1, :] = below[col : col + 1, :]


def frame_sides(sides, up_rows, low_rows):
    count, rows, levels = sides.shape
    vmem = pl.BlockSpec(memory_space=pltpu.VMEM)
    return pl.pallas_call(
        frame_kernel,
        out_shape=jax.ShapeDtypeStruct((count, rows + 2 * EDGE, levels), F32),
        in_specs=[vmem] * 3,
        out_specs=vmem,
        compiler_params=pltpu.CompilerParams(vmem_limit_bytes=16 * MIB),
        name="frame",
    )(sides, up_rows, low_rows)


def advance_kernel(comp_count, left_at, right_at, *refs):
    (flags, ocean_first, source_column, labels, state, up_rows, low_rows, left_in, right_in) = refs[:9]
    (own_sides, mask, mix_atm, mix_ocn, flux_map) = refs[9:14]
    out, surface, packed = refs[14:17]
    phi = refs[17:-16]
    (values, moved, halo_moved, smooth, pairs, mixed, later_smooth, later_pairs, later_mixed) = refs[-16:-7]
    (weights, flux_weights, fluxes, staged, top, in_sems, out_sems) = refs[-7:]
    left_cols = left_in.at[left_at : left_at + 2]
    right_cols = right_in.at[right_at : right_at + 2]
    first = (smooth, pairs, mixed)
    second = (later_smooth, later_pairs, later_mixed)
    rows, cols, levels = state.shape
    chunks = rows // CHUNK
    inner = pl.ds(EDGE, cols)
    flux_count = flux_map.shape[0]

    def fetch(q):
        return pltpu.make_async_copy(
            state.at[pl.ds(q * CHUNK, CHUNK)],
            values.at[pl.ds(q * CHUNK + 2, CHUNK), inner],
            in_sems.at[q],
        )

    def put(q, slot):
        return pltpu.make_async_copy(
            staged.at[slot], out.at[pl.ds(q * CHUNK, CHUNK)], out_sems.at[slot]
        )

    def begin(q, _):
        fetch(q).start()
        return 0

    lax.fori_loop(0, AHEAD, begin, 0)
    ocean = flags[0] == 1
    mix = jnp.where(ocean, mix_ocn[...], mix_atm[...])
    mix_high, mix_low = split_two(mix)
    weights[:levels, :levels] = mix_high
    weights[levels:, :levels] = mix_high
    weights[:levels, levels:] = mix_low
    weights[levels:, levels:] = mix_low
    map_high, map_low = split_two(flux_map[...])
    flux_weights[...] = jnp.concatenate(
        [
            jnp.concatenate([map_high.astype(F32), map_high.astype(F32)], axis=1),
            jnp.concatenate([map_low.astype(F32), map_low.astype(F32)], axis=1),
        ],
        axis=0,
    ).astype(BF16)
    values[0:2, EDGE : EDGE + cols, :] = up_rows[...].astype(F32)
    values[rows + 2 : rows + 4, EDGE : EDGE + cols, :] = low_rows[...].astype(F32)
    for r, i in ((1, EDGE - 1), (rows + 2, EDGE + rows)):
        values[r, EDGE - 1 : EDGE, :] = left_cols[1, i : i + 1, :]
        values[r, EDGE + cols : EDGE + cols + 1, :] = right_cols[0, i : i + 1, :]

    def side_cells(start, count):
        for row in range(count):
            values[start + row + 2, EDGE - 1 : EDGE, :] = left_cols[1, pl.ds(start + row + EDGE, 1), :]
            values[start + row + 2, EDGE + cols : EDGE + cols + 1, :] = right_cols[
                0, pl.ds(start + row + EDGE, 1), :
            ]

    def moved_sides(start, count):
        for row in range(count):
            moved[start + row + 1, EDGE - 1 : EDGE, :] = halo_moved[0, pl.ds(start + row, 1), :]
            moved[start + row + 1, EDGE + cols : EDGE + cols + 1, :] = halo_moved[
                1, pl.ds(start + row, 1), :
            ]

    def stage(refs, row, total):
        line = SMOOTHING * total
        refs[0][row] = line
        refs[1][row * cols : (row + 1) * cols, :] = side_by_side(line)

    def stage_rows(refs, ref, start, count):
        for row in range(count):
            i = start + row
            here = ref[i, EDGE : EDGE + cols, :] + (
                ref[i - 1, EDGE : EDGE + cols, :] + ref[i + 1, EDGE : EDGE + cols, :]
            )
            near = ref[i, EDGE - 1 : EDGE - 1 + cols, :] + ref[i, EDGE + 1 : EDGE + 1 + cols, :]
            stage(refs, row, here + near)

    def note_top(q, lines):
        lanes = lax.broadcasted_iota(jnp.int32, (cols, levels), 1)
        kept = lines[0]
        for row in range(1, CHUNK):
            kept = jnp.where(lanes == row, pltpu.roll(lines[row], row, 1), kept)
        turned = pltpu.roll(kept, q * CHUNK, 1)
        top[...] = jnp.where(lanes // CHUNK == q, turned, top[...])

    def mix_rows(refs, count):
        refs[2][: count * cols, :] = dot_nn(refs[1][: count * cols, :], weights[...])

    def finish(refs, row):
        part = refs[2][row * cols : (row + 1) * cols, :]
        return refs[0][row] + PHYSICS * jnp.tanh(part[:, :levels] + part[:, levels:])

    @pl.when(jnp.logical_not(ocean))
    def atmosphere():
        nearest = (left_cols.at[1], right_cols.at[0])
        beyond = (left_cols.at[0], right_cols.at[1])
        within = (own_sides.at[0], own_sides.at[3])
        for s in range(2):
            total = (
                nearest[s][EDGE : EDGE + rows, :]
                + nearest[s][EDGE - 1 : EDGE - 1 + rows, :]
                + nearest[s][EDGE + 1 : EDGE + 1 + rows, :]
            )
            stage(first, s, total + (beyond[s][EDGE : EDGE + rows, :] + within[s][...]))
        mix_rows(first, 2)
        for s in range(2):
            halo_moved[s] = finish(first, s)

        side_cells(0, 1)
        fetch(0).wait()
        fetch(1).wait()
        stage_rows(second, values, 1, 2)
        mix_rows(second, 2)
        for row in range(2):
            moved[row, EDGE : EDGE + cols, :] = finish(second, row)

        @pl.when(flags[1] == 0)
        def _():
            moved[0, EDGE : EDGE + cols, :] = jnp.zeros((cols, levels), F32)

        def begin_first(q):
            side_cells(jnp.minimum(q * CHUNK + 1, rows - CHUNK), CHUNK)
            stage_rows(first, values, q * CHUNK + 3, CHUNK)
            mix_rows(first, CHUNK)

        def end_first(q):
            for row in range(CHUNK):
                moved[q * CHUNK + row + 2, EDGE : EDGE + cols, :] = finish(first, row)

        def begin_second(q):
            moved_sides(q * CHUNK, CHUNK)
            stage_rows(second, moved, q * CHUNK + 1, CHUNK)

        def end_second(q, slot):
            for row in range(CHUNK):
                line = finish(second, row)
                staged[slot, row] = line
                both = line + moved[q * CHUNK + row + 1, EDGE : EDGE + cols, :]
                later_pairs[row * cols : (row + 1) * cols, :] = side_by_side(both)
            put(q, slot).start()
            note_top(q, [staged[slot, row] for row in range(CHUNK)])
            flux = dot_nt(flux_weights[...], later_pairs[...])
            flux = flux[:flux_count] + flux[flux_count:]
            for row in range(CHUNK):
                r = q * CHUNK + row
                block = PHYSICS * flux[:, row * cols : (row + 1) * cols]
                sea = jnp.broadcast_to(mask[pl.ds(r, 1), :], block.shape)
                block = jnp.where(sea > 0.5, block, 0.0)
                fluxes[pl.ds(pl.multiple_of(r * flux_count, flux_count), flux_count), :] = block

        fetch(AHEAD).start()
        begin_first(0)
        end_first(0)

        def one_chunk(q, _):
            @pl.when(q + 1 < chunks)
            def _():
                fetch(q + 1).wait()

            @pl.when(q + AHEAD < chunks)
            def _():
                fetch(q + AHEAD).start()

            slot = (q - 1) % 2

            @pl.when(q >= 3)
            def _():
                put(q - 3, slot).wait()

            begin_first(q)
            begin_second(q - 1)
            end_first(q)
            mix_rows(second, CHUNK)
            end_second(q - 1, slot)
            return 0

        lax.fori_loop(1, chunks, one_chunk, 0)

        @pl.when(flags[2] == 0)
        def _():
            moved[rows + 1, EDGE : EDGE + cols, :] = jnp.zeros((cols, levels), F32)

        last = chunks - 1
        put(last - 2, last % 2).wait()
        begin_second(last)
        mix_rows(second, CHUNK)
        end_second(last, last % 2)
        spots = lax.broadcasted_iota(jnp.int32, (source_column.shape[0], rows), 1)
        placing = jnp.where(source_column[...] == spots, 1.0, 0.0).astype(BF16)
        share = flux_count // comp_count
        size = placing.shape[0]
        total = jnp.zeros((size, cols), F32)
        for c in range(comp_count):
            for f in range(share):
                index = c * share + f
                field = fluxes[pl.ds(index, rows, stride=flux_count), :].astype(BF16)
                value = dot_nn(placing, field)
                packed[c, :size, f * cols : (f + 1) * cols] = value.astype(BF16)
                total = total + ocean_first[index] * value
            packed[c, size:, :] = labels[...]
        total = side_by_side(total)
        capacity = size // len(phi)
        for n, block in enumerate(phi):
            block[:capacity, :] = total[n * capacity : (n + 1) * capacity, :]
            block[capacity:, :] = labels[...]
        put(last - 1, (last - 1) % 2).wait()
        put(last, last % 2).wait()
        surface[...] = top[...].T

    @pl.when(ocean)
    def sea_side():
        fetch(0).wait()
        lanes = lax.broadcasted_iota(jnp.int32, (CHUNK, CHUNK * levels), 1) // levels
        lines = lax.broadcasted_iota(jnp.int32, (CHUNK, CHUNK * levels), 0)
        spreader = jnp.where(lanes == lines, 1.0, 0.0).astype(F32)

        def one_chunk(q, _):
            base = q * CHUNK

            @pl.when(q + 1 < chunks)
            def _():
                fetch(q + 1).wait()

            @pl.when(q + AHEAD < chunks)
            def _():
                fetch(q + AHEAD).start()

            side_cells(base, CHUNK)
            stage_rows(first, values, base + 2, CHUNK)
            mix_rows(first, CHUNK)
            slot = q % 2

            @pl.when(q >= 2)
            def _():
                put(q - 2, slot).wait()

            sea = dot_nn(mask[pl.ds(pl.multiple_of(base, CHUNK), CHUNK), :].T, spreader)
            for row in range(CHUNK):
                chosen = sea[:, row * levels : (row + 1) * levels] > 0.5
                before = values[base + row + 2, EDGE : EDGE + cols, :]
                staged[slot, row] = jnp.where(chosen, finish(first, row), before)
            put(q, slot).start()
            note_top(q, [staged[slot, row] for row in range(CHUNK)])
            return 0

        lax.fori_loop(0, chunks, one_chunk, 0)
        put(chunks - 2, (chunks - 2) % 2).wait()
        put(chunks - 1, (chunks - 1) % 2).wait()
        surface[...] = top[...].T
        packed[...] = jnp.zeros(packed.shape, BF16)
        for block in phi:
            block[...] = jnp.zeros(block.shape, BF16)


def advance(
    flags, ocean_first, source_column, labels, state, halos, mask, mix_atm, mix_ocn, flux_map_t,
    comp_count, neighbours, left_at, right_at,
):
    rows, cols, levels = state.shape
    fluxes = flux_map_t.shape[0]
    vmem = pl.BlockSpec(memory_space=pltpu.VMEM)
    smem = pl.BlockSpec(memory_space=pltpu.SMEM)
    hbm = pl.BlockSpec(memory_space=pltpu.HBM)
    entry = jax.ShapeDtypeStruct(
        (comp_count, source_column.shape[0] + labels.shape[0], fluxes // comp_count * cols), BF16
    )
    block = jax.ShapeDtypeStruct(
        (source_column.shape[0] // neighbours + labels.shape[0], 2 * cols), BF16
    )
    cells = rows * cols
    return pl.pallas_call(
        functools.partial(advance_kernel, comp_count, left_at, right_at),
        out_shape=(
            jax.ShapeDtypeStruct(state.shape, F32),
            jax.ShapeDtypeStruct((rows, cols), F32),
            entry,
        )
        + (block,) * neighbours,
        in_specs=[smem, smem, vmem, vmem, hbm] + [vmem] * (len(halos) + 4),
        out_specs=(hbm, vmem, vmem) + (vmem,) * neighbours,
        scratch_shapes=[
            pltpu.VMEM((rows + 4, cols + 2 * EDGE, levels), F32),
            pltpu.VMEM((rows + 2, cols + 2 * EDGE, levels), F32),
            pltpu.VMEM((2, rows, levels), F32),
            pltpu.VMEM((CHUNK, cols, levels), F32),
            pltpu.VMEM((CHUNK * cols, 2 * levels), BF16),
            pltpu.VMEM((CHUNK * cols, 2 * levels), F32),
            pltpu.VMEM((CHUNK, cols, levels), F32),
            pltpu.VMEM((CHUNK * cols, 2 * levels), BF16),
            pltpu.VMEM((CHUNK * cols, 2 * levels), F32),
            pltpu.VMEM((2 * levels, 2 * levels), BF16),
            pltpu.VMEM((2 * fluxes, 2 * levels), BF16),
            pltpu.VMEM((rows * fluxes, cols), F32),
            pltpu.VMEM((2, CHUNK, cols, levels), F32),
            pltpu.VMEM((cols, levels), F32),
            pltpu.SemaphoreType.DMA((rows // CHUNK,)),
            pltpu.SemaphoreType.DMA((2,)),
        ],
        compiler_params=pltpu.CompilerParams(vmem_limit_bytes=48 * MIB),
        cost_estimate=pl.CostEstimate(
            flops=8 * cells * levels * levels, bytes_accessed=8 * cells * levels, transcendentals=0
        ),
        name="advance",
    )(flags, ocean_first, source_column, labels, state, *halos, mask, mix_atm, mix_ocn, flux_map_t)


BATCH = 8
LABEL_ROWS = 16


def regroup_kernel(slabs, *blocks):
    sources = slabs.shape[0] - 1
    capacity = (blocks[0].shape[0] - LABEL_ROWS) // sources
    size = len(blocks) * capacity
    heads = [slabs[c, size : size + LABEL_ROWS, :].astype(F32) for c in range(sources)]
    lines = [head[i : i + 1] for i in range(2) for head in heads]
    spare = jnp.zeros((LABEL_ROWS - len(lines), heads[0].shape[1]), F32)
    labels = jnp.concatenate(lines + [spare], axis=0).astype(BF16)
    for n, block in enumerate(blocks):
        for c in range(sources):
            block[c * capacity : (c + 1) * capacity, :] = slabs[
                c, n * capacity : (n + 1) * capacity, :
            ]
        block[sources * capacity :, :] = labels


def regroup(slabs, count):
    comps, rows, width = slabs.shape
    size = (rows - LABEL_ROWS) // count * (comps - 1) + LABEL_ROWS
    vmem = pl.BlockSpec(memory_space=pltpu.VMEM)
    return pl.pallas_call(
        regroup_kernel,
        out_shape=(jax.ShapeDtypeStruct((size, width), BF16),) * count,
        in_specs=[vmem],
        out_specs=(vmem,) * count,
        compiler_params=pltpu.CompilerParams(vmem_limit_bytes=16 * MIB),
        name="regroup",
    )(slabs)


def label_lines_of(blocks, start, lines):
    width = blocks[0].shape[1]
    capacity = width // len(blocks)
    lanes = lax.broadcasted_iota(jnp.int32, (LABEL_ROWS, width), 1) // capacity
    labels = jnp.zeros((LABEL_ROWS, width), F32)
    for n, block in enumerate(blocks):
        labels = jnp.where(lanes == n, block[start:, :].astype(F32), labels)
    labels = labels.astype(jnp.int32)
    join = lambda first: jnp.concatenate([labels[first + c : first + c + 1] for c in range(lines)], axis=1)
    return join(0), join(lines)


def selectors(weight_line, target_line, weight_count, rows):
    total = target_line.shape[1]
    spots = lax.broadcasted_iota(jnp.int32, (rows, total), 0)
    by_target = jnp.where(target_line == spots, 1.0, 0.0)
    numbers = lax.broadcasted_iota(jnp.int32, (weight_count, total), 0)
    by_weight = jnp.where(weight_line == numbers, 1.0, 0.0).astype(BF16)
    return by_target, by_weight


def project_kernel(count, flags, *refs):
    blocks = refs[:count]
    weights, surface, mask, shared, hits, entries, chosen = refs[count:]
    rows, cols = mask.shape
    weight_count = weights.shape[0]
    capacity = blocks[0].shape[0] - LABEL_ROWS
    for n in range(count):
        entries[n * capacity : (n + 1) * capacity, :] = blocks[n][:capacity, :]
    weight_line, target_line = label_lines_of(blocks, capacity, 1)
    by_target, by_weight = selectors(weight_line, target_line, weight_count, rows)
    hits[...] = by_target.T.astype(BF16)
    by_target = by_target.astype(BF16)
    change = jnp.zeros((rows, cols), F32)
    for g in range(weight_count // BATCH):
        for i in range(BATCH):
            w = g * BATCH + i
            chosen[i * rows : (i + 1) * rows, :] = by_target * by_weight[w : w + 1, :]
        both = dot_nn(chosen[...], entries[...])
        both = both[:, :cols] + both[:, cols:]
        wide = weights[g * BATCH : (g + 1) * BATCH].reshape(BATCH * cols, cols)
        halves = [split_two(both[i * rows : (i + 1) * rows, :]) for i in range(BATCH)]
        stacked = jnp.concatenate(
            [jnp.concatenate([half[k] for half in halves], axis=1) for k in range(2)], axis=0
        )
        product = dot_nn(stacked, wide)
        change = change + (product[:rows] + product[rows:])
    shared[0] = jnp.where(flags[0] == 1, surface[...], change)
    shared[1] = mask[...]


def project(flags, blocks, weights, surface, mask):
    rows, cols = mask.shape
    count = len(blocks)
    height, width = blocks[0].shape
    total = count * (height - LABEL_ROWS)
    vmem = pl.BlockSpec(memory_space=pltpu.VMEM)
    smem = pl.BlockSpec(memory_space=pltpu.SMEM)
    return pl.pallas_call(
        functools.partial(project_kernel, count),
        out_shape=(
            jax.ShapeDtypeStruct((2, rows, cols), F32),
            jax.ShapeDtypeStruct((total, rows), BF16),
        ),
        in_specs=[smem] + [vmem] * (count + 3),
        out_specs=(vmem, vmem),
        scratch_shapes=[
            pltpu.VMEM((total, width), BF16),
            pltpu.VMEM((BATCH * rows, total), BF16),
        ],
        compiler_params=pltpu.CompilerParams(vmem_limit_bytes=32 * MIB),
        cost_estimate=pl.CostEstimate(
            flops=2 * weights.shape[0] * rows * (width * total + 2 * cols * cols),
            bytes_accessed=2 * MIB,
            transcendentals=0,
        ),
        name="project",
    )(flags, *blocks, weights, surface, mask)


def regrid_kernel(sources, *refs):
    blocks = refs[:-5]
    weights, forcing, entries, chosen, binned = refs[-5:]
    share, rows, cols = forcing.shape
    weight_count = weights.shape[0]
    count = len(blocks)
    capacity = (blocks[0].shape[0] - LABEL_ROWS) // sources
    size = count * capacity
    for c in range(sources):
        for n in range(count):
            start = c * size + n * capacity
            entries[start : start + capacity, :] = blocks[n][c * capacity : (c + 1) * capacity, :]
    weight_line, target_line = label_lines_of(blocks, sources * capacity, sources)
    by_target, by_weight = selectors(weight_line, target_line, weight_count, rows)
    by_target = by_target.astype(BF16)
    for g in range(weight_count // BATCH):
        for i in range(BATCH):
            w = g * BATCH + i
            chosen[i * rows : (i + 1) * rows, :] = by_target * by_weight[w : w + 1, :]
        binned[...] = dot_nn(chosen[...], entries[...])
        wide = weights[g * BATCH : (g + 1) * BATCH].reshape(BATCH * cols, cols)
        halves = [
            [
                split_two(binned[i * rows : (i + 1) * rows, f * cols : (f + 1) * cols])
                for i in range(BATCH)
            ]
            for f in range(share)
        ]
        stacked = jnp.concatenate(
            [
                jnp.concatenate([half[k] for half in halves[f]], axis=1)
                for k in range(2)
                for f in range(share)
            ],
            axis=0,
        )
        product = dot_nn(stacked, wide)
        for f in range(share):
            part = product[f * rows : (f + 1) * rows] + product[
                (share + f) * rows : (share + f + 1) * rows
            ]
            forcing[f] = part if g == 0 else forcing[f] + part


def regrid(blocks, comp_count, weights, rows):
    sources = comp_count - 1
    weight_count, cols, _ = weights.shape
    height, width = blocks[0].shape
    total = (height - LABEL_ROWS) * len(blocks)
    share = width // cols
    vmem = pl.BlockSpec(memory_space=pltpu.VMEM)
    return pl.pallas_call(
        functools.partial(regrid_kernel, sources),
        out_shape=jax.ShapeDtypeStruct((share, rows, cols), F32),
        in_specs=[vmem] * (len(blocks) + 1),
        out_specs=vmem,
        scratch_shapes=[
            pltpu.VMEM((total, width), BF16),
            pltpu.VMEM((BATCH * rows, total), BF16),
            pltpu.VMEM((BATCH * rows, width), F32),
        ],
        compiler_params=pltpu.CompilerParams(vmem_limit_bytes=32 * MIB),
        cost_estimate=pl.CostEstimate(
            flops=2 * weight_count * rows * width * (total + 2 * cols),
            bytes_accessed=2 * MIB,
            transcendentals=0,
        ),
        name="regrid",
    )(*blocks, weights)


def pick_kernel(count, flags, *refs):
    parts = refs[:count]
    hits, surface = refs[count : count + 2]
    picked = refs[count + 2 :]
    from_ocean = lax.rem(flags[3] + 1, count)
    base = jnp.zeros(surface.shape, F32)
    sea = base
    change = base
    for shift in range(count):
        is_base = from_ocean == shift
        base = base + jnp.where(is_base, parts[shift][0], 0.0)
        sea = sea + jnp.where(is_base, parts[shift][1], 0.0)
        change = change + jnp.where(is_base, 0.0, parts[shift][0])
    now = base + jnp.where(sea > 0.5, change, 0.0)
    surface[...] = now
    pair = jnp.concatenate(split_two(now), axis=0)
    size = picked[0].shape[0]
    for n in range(len(picked)):
        some = hits[n * size : (n + 1) * size, :]
        picked[n][...] = dot_nn(jnp.concatenate([some, some], axis=1), pair)


def pick(flags, parts, hits, neighbours):
    _, rows, cols = parts[0].shape
    size = hits.shape[0] // neighbours
    vmem = pl.BlockSpec(memory_space=pltpu.VMEM)
    return pl.pallas_call(
        functools.partial(pick_kernel, len(parts)),
        out_shape=(jax.ShapeDtypeStruct((rows, cols), F32),)
        + (jax.ShapeDtypeStruct((size, cols), F32),) * neighbours,
        in_specs=[pl.BlockSpec(memory_space=pltpu.SMEM)] + [vmem] * (len(parts) + 1),
        out_specs=(vmem,) * (1 + neighbours),
        compiler_params=pltpu.CompilerParams(vmem_limit_bytes=16 * MIB),
        name="pick",
    )(flags, *parts, hits)


LINES = 8


def update_kernel(groups, flags, state, *refs):
    parts = refs[:groups]
    mask, ocean_map, out, token, held, table, wide, in_sems, out_sems = refs[groups:]
    rows, cols, levels = state.shape
    share = parts[0].shape[0]
    flux_count = groups * share
    chunks = rows // LINES
    depth = LINES * flux_count
    token[...] = jnp.zeros(token.shape, F32)

    def fetch(q):
        return pltpu.make_async_copy(
            state.at[pl.ds(q * LINES, LINES)], held.at[pl.ds(q * LINES, LINES)], in_sems.at[q]
        )

    def put(q):
        return pltpu.make_async_copy(
            held.at[pl.ds(q * LINES, LINES)], out.at[pl.ds(q * LINES, LINES)], out_sems.at[q]
        )

    @pl.when(flags[0] == 1)
    def ocean():
        for q in range(chunks):
            fetch(q).start()
        table[...] = jnp.zeros(table.shape, F32)
        for line in range(LINES):
            for f in range(flux_count):
                spot = f * LINES + line
                table[spot : spot + 1, line * levels : (line + 1) * levels] = ocean_map[f : f + 1]
        high, low = split_two(table[...])
        wide[:depth] = high
        wide[depth : 2 * depth] = high
        wide[2 * depth :] = low

        def one(q, _):
            start = pl.multiple_of(q * LINES, LINES)
            sea = mask[pl.ds(start, LINES), :] > 0.5
            part = jnp.concatenate(
                [
                    jnp.where(sea, parts[f // share][f % share, pl.ds(start, LINES), :], 0.0)
                    for f in range(flux_count)
                ],
                axis=0,
            )
            rough = part.astype(BF16).astype(F32)
            turned = jnp.concatenate([rough, part - rough, rough], axis=0).T.astype(BF16)
            change = dot_nn(turned, wide[...])
            fetch(q).wait()
            for line in range(LINES):
                held[start + line] += change[:, line * levels : (line + 1) * levels]
            put(q).start()
            return 0

        lax.fori_loop(0, chunks, one, 0, unroll=2)
        for q in range(chunks):
            put(q).wait()


def update(flags, state, parts, mask, ocean_map):
    rows, cols, levels = state.shape
    depth = LINES * ocean_map.shape[0]
    vmem = pl.BlockSpec(memory_space=pltpu.VMEM)
    smem = pl.BlockSpec(memory_space=pltpu.SMEM)
    hbm = pl.BlockSpec(memory_space=pltpu.HBM)
    return pl.pallas_call(
        functools.partial(update_kernel, len(parts)),
        out_shape=(
            jax.ShapeDtypeStruct(state.shape, F32),
            jax.ShapeDtypeStruct((EDGE, levels), F32),
        ),
        in_specs=[smem, hbm] + [vmem] * (len(parts) + 2),
        out_specs=(hbm, vmem),
        input_output_aliases={1: 0},
        scratch_shapes=[
            pltpu.VMEM(state.shape, F32),
            pltpu.VMEM((depth, LINES * levels), F32),
            pltpu.VMEM((3 * depth, LINES * levels), BF16),
            pltpu.SemaphoreType.DMA((rows // LINES,)),
            pltpu.SemaphoreType.DMA((rows // LINES,)),
        ],
        compiler_params=pltpu.CompilerParams(vmem_limit_bytes=24 * MIB),
        cost_estimate=pl.CostEstimate(
            flops=6 * rows * cols * depth * levels,
            bytes_accessed=8 * rows * cols * levels,
            transcendentals=0,
        ),
        name="update",
    )(flags, state, *parts, mask, ocean_map)


def returned_kernel(groups, flags, *refs):
    picked = refs[:groups]
    weight_column, row_line, weights, mask, surface, new_surface, token, out, total = refs[groups:]
    rows, cols = mask.shape
    weight_count = weights.shape[0]

    @pl.when(flags[0] == 1)
    def ocean():
        out[...] = new_surface[...]

    @pl.when(flags[0] == 0)
    def atmosphere():
        values = jnp.concatenate([p[...] for p in picked], axis=0)
        pair = side_by_side(values)
        which = jnp.broadcast_to(weight_column[...], values.shape)
        total[...] = jnp.zeros(values.shape, F32)

        def one(i, _):
            both = jnp.concatenate([weights[2 * i], weights[2 * i + 1]], axis=0)
            images = dot_nt(pair, jnp.concatenate([both, both], axis=1))
            total[...] += jnp.where(which == 2 * i, images[:, :cols], 0.0) + jnp.where(
                which == 2 * i + 1, images[:, cols:], 0.0
            )
            return 0

        lax.fori_loop(0, weight_count // 2, one, 0, unroll=8)
        spots = lax.broadcasted_iota(jnp.int32, (rows, values.shape[0]), 0)
        chosen = jnp.where(jnp.broadcast_to(row_line[...], spots.shape) == spots, 1.0, 0.0).astype(BF16)
        high, low = split_two(total[...])
        back = dot_nn(chosen, high) + dot_nn(chosen, low)
        out[...] = jnp.where(mask[...] > 0.5, back, surface[...])


def returned(flags, picked, weight_column, row_line, weights, mask, surface, new_surface, token):
    rows, cols = mask.shape
    entry_total = weight_column.shape[0]
    vmem = pl.BlockSpec(memory_space=pltpu.VMEM)
    smem = pl.BlockSpec(memory_space=pltpu.SMEM)
    return pl.pallas_call(
        functools.partial(returned_kernel, len(picked)),
        out_shape=jax.ShapeDtypeStruct((rows, cols), F32),
        in_specs=[smem] + [vmem] * (len(picked) + 7),
        out_specs=vmem,
        scratch_shapes=[pltpu.VMEM((entry_total, cols), F32)],
        compiler_params=pltpu.CompilerParams(vmem_limit_bytes=16 * MIB),
        name="returned",
    )(flags, *picked, weight_column, row_line, weights, mask, surface, new_surface, token)


def local(
    state, land_mask, intersection_list, mix_atm, mix_ocn, flux_map, ocean_map, regrid_weights
):
    rows, cols, levels = state.shape
    intersections = intersection_list.shape[2]
    comp_count = lax.axis_size("comp")
    lat_count = lax.axis_size("lat")
    lon_count = lax.axis_size("lon")
    tile_count = lat_count * lon_count
    reach = min(4, lon_count)
    neighbours = 2 * reach
    entry_total = intersections * rows
    capacity = entry_total // neighbours
    comp_index = lax.axis_index("comp")
    lat_index = lax.axis_index("lat")
    tile_index = lat_index * lon_count + lax.axis_index("lon")
    bands = comp_count * lat_count
    ocean_band = (comp_count - 1) * lat_count
    ocean_comp = comp_count - 1
    band = comp_index * lat_count + lat_index
    is_ocean = comp_index == ocean_comp
    upper_valid = (band > 0) & (band != ocean_band)
    lower_valid = (band < bands - 1) & (band != ocean_band - 1)
    flags = jnp.stack([is_ocean, upper_valid, lower_valid, comp_index]).astype(jnp.int32)
    mask = (land_mask == 1).astype(F32)

    def band_shift(value, by, lon_by):
        pairs = []
        for b in range(bands):
            target = b + by
            if 0 <= target < bands and (b >= ocean_band) == (target >= ocean_band):
                for lon in range(lon_count):
                    pairs.append(
                        (b * lon_count + lon, target * lon_count + (lon + lon_by) % lon_count)
                    )
        return lax.ppermute(value, AXES, pairs)

    first_rows, last_rows, sides = take_edges(state)
    up_rows = band_shift(last_rows, 1, 0)
    low_rows = band_shift(first_rows, -1, 0)
    framed = frame_sides(sides, up_rows, low_rows)
    if lon_count == 2:
        left_cols = right_cols = band_shift(framed, 0, 1)
        left_at, right_at = 2, 0
    else:
        left_cols = band_shift(framed[2:], 0, 1)
        right_cols = band_shift(framed[:2], 0, -1)
        left_at, right_at = 0, 0

    entry_list = intersection_list.reshape(entry_total, 3)
    owners = entry_list[:, 0]
    labels = entry_list[:, 2] * rows + entry_list[:, 1]
    offsets = [
        (n // reach * lon_count + n % reach - (reach - 1) // 2) % tile_count
        for n in range(neighbours)
    ]
    distance = (owners - tile_index + tile_count) % tile_count
    hits = distance[:, None] == jnp.array(offsets, jnp.int32)[None, :]
    neighbour_ids = jnp.sum(
        jnp.where(hits, jnp.arange(neighbours, dtype=jnp.int32)[None, :], 0), axis=1
    )
    positions = jnp.arange(entry_total, dtype=jnp.int32)
    earlier = (neighbour_ids[None, :] == neighbour_ids[:, None]) & (
        positions[None, :] < positions[:, None]
    )
    slots = neighbour_ids * capacity + jnp.sum(earlier.astype(jnp.int32), axis=1)
    placing = positions[:, None] == slots[None, :]
    sources = jnp.sum(jnp.where(placing, (positions // intersections)[None, :], 0), axis=1)
    packed_labels = jnp.sum(jnp.where(placing, labels[None, :], 0), axis=1)

    def over_comp(value):
        return lax.all_to_all(value, "comp", split_axis=0, concat_axis=0, tiled=True)

    def shifted_comp(value, shift):
        pairs = [
            (c * tile_count + t, (c + shift) % comp_count * tile_count + t)
            for c in range(comp_count)
            for t in range(tile_count)
        ]
        return lax.ppermute(value, AXES, pairs)

    def over_tiles(value, offset, comps):
        if offset % tile_count == 0:
            return value
        pairs = [
            (c * tile_count + t, c * tile_count + (t + offset) % tile_count)
            for c in range(comps)
            for t in range(tile_count)
        ]
        return lax.ppermute(value, AXES, pairs)

    def to_ocean(value, comp):
        pairs = [
            (comp * tile_count + t, ocean_comp * tile_count + t) for t in range(tile_count)
        ]
        return lax.ppermute(value, AXES, pairs)

    label_lines = jnp.stack([packed_labels // rows, packed_labels % rows]).astype(BF16)
    label_lines = jnp.pad(label_lines, ((0, LABEL_ROWS - 2), (0, 0)))

    halos = (up_rows, low_rows, left_cols, right_cols, sides)
    moved = advance(
        flags, ocean_map[:, 0], sources[:, None], label_lines, state, halos, mask, mix_atm, mix_ocn,
        flux_map.T, comp_count, neighbours, left_at, right_at,
    )
    moved, surface, packed, phi = moved[0], moved[1], moved[2], moved[3:]
    phi = [over_tiles(phi[n], offsets[n], ocean_comp) for n in range(neighbours)]
    phi[1], packed = lax.optimization_barrier((phi[1], packed))
    shared, hits = project(flags, phi, regrid_weights, surface, mask)
    parts = [shared] + [shifted_comp(shared, s) for s in range(1, comp_count)]
    picks = pick(flags, parts, hits, neighbours)
    blocks = regroup(over_comp(packed), neighbours)
    blocks = [over_tiles(blocks[n], offsets[n], comp_count) for n in range(neighbours)]
    forcing = regrid(blocks, comp_count, regrid_weights, rows)
    new_surface, picked = picks[0], picks[1:]
    arrived = [over_tiles(picked[n], -offsets[n], ocean_comp) for n in range(neighbours)]
    fields = [to_ocean(forcing, c) for c in range(ocean_comp)] + [forcing]
    final_state, token = update(flags, moved, fields, mask, ocean_map)
    weight_column = (packed_labels // rows)[:, None]
    surface_out = returned(
        flags, arrived, weight_column, sources[None, :], regrid_weights, mask, surface, new_surface,
        token,
    )
    return (final_state, surface_out)


def solution(mesh):
    placed = (
        P(("comp", "lat"), "lon", None),
        P(("comp", "lat"), "lon"),
        P(("comp", "lat"), "lon", None, None),
        P(),
        P(),
        P(),
        P(),
        P(),
    )
    return jax.shard_map(
        local,
        mesh=mesh,
        in_specs=placed,
        out_specs=(P(("comp", "lat"), "lon", None), P(("comp", "lat"), "lon")),
        check_vma=False,
    )
```

```python
import functools

import jax
import jax.numpy as jnp
from jax import lax
from jax.experimental import pallas as pl
from jax.experimental.pallas import tpu as pltpu
from jax.sharding import PartitionSpec as P

SMOOTHING = 0.2
PHYSICS = 0.5
MIB = 1024 * 1024
F32 = jnp.float32
BF16 = jnp.bfloat16
EDGE = 8
AHEAD = 4
CHUNK = 8
AXES = ("comp", "lat", "lon")


def split_two(x):
    high = x.astype(BF16)
    low = (x - high.astype(F32)).astype(BF16)
    return high, low


def side_by_side(x):
    return jnp.concatenate(split_two(x), axis=1)


def dot_nt(a, b):
    return lax.dot_general(a, b, (((1,), (1,)), ((), ())), preferred_element_type=F32)


def dot_nn(a, b):
    return jnp.dot(a, b, preferred_element_type=F32)


def edges_kernel(state, first_rows, last_rows, sides, top, bottom, left, right, sems):
    rows, cols, _ = state.shape
    copies = [
        pltpu.make_async_copy(state.at[pl.ds(0, 2)], top, sems.at[0]),
        pltpu.make_async_copy(state.at[pl.ds(rows - 2, 2)], bottom, sems.at[1]),
        pltpu.make_async_copy(state.at[:, pl.ds(0, EDGE)], left, sems.at[2]),
        pltpu.make_async_copy(state.at[:, pl.ds(cols - EDGE, EDGE)], right, sems.at[3]),
    ]
    for copy in copies:
        copy.start()
    for copy in copies:
        copy.wait()
    first_rows[...] = top[...].astype(BF16)
    last_rows[...] = bottom[...].astype(BF16)
    for i in range(2):
        sides[i] = left[:, i, :]
        sides[2 + i] = right[:, EDGE - 2 + i, :]


def take_edges(state):
    rows, cols, levels = state.shape
    slab = jax.ShapeDtypeStruct((2, cols, levels), BF16)
    side = jax.ShapeDtypeStruct((4, rows, levels), F32)
    vmem = pl.BlockSpec(memory_space=pltpu.VMEM)
    return pl.pallas_call(
        edges_kernel,
        out_shape=(slab, slab, side),
        in_specs=[pl.BlockSpec(memory_space=pltpu.HBM)],
        out_specs=(vmem,) * 3,
        scratch_shapes=[
            pltpu.VMEM((2, cols, levels), F32),
            pltpu.VMEM((2, cols, levels), F32),
            pltpu.VMEM((rows, EDGE, levels), F32),
            pltpu.VMEM((rows, EDGE, levels), F32),
            pltpu.SemaphoreType.DMA((4,)),
        ],
        compiler_params=pltpu.CompilerParams(vmem_limit_bytes=50 * MIB),
        name="edges",
    )(state)


def frame_kernel(sides, up_rows, low_rows, framed):
    _, rows, levels = sides.shape
    cols = up_rows.shape[1]
    framed[...] = jnp.zeros(framed.shape, F32)
    above = up_rows[1].astype(F32)
    below = low_rows[0].astype(F32)
    for i, col in enumerate((0, 1, cols - 2, cols - 1)):
        framed[i, EDGE : EDGE + rows, :] = sides[i]
        framed[i, EDGE - 1 : EDGE, :] = above[col : col + 1, :]
        framed[i, EDGE + rows : EDGE + rows + 1, :] = below[col : col + 1, :]


def frame_sides(sides, up_rows, low_rows):
    count, rows, levels = sides.shape
    vmem = pl.BlockSpec(memory_space=pltpu.VMEM)
    return pl.pallas_call(
        frame_kernel,
        out_shape=jax.ShapeDtypeStruct((count, rows + 2 * EDGE, levels), F32),
        in_specs=[vmem] * 3,
        out_specs=vmem,
        compiler_params=pltpu.CompilerParams(vmem_limit_bytes=16 * MIB),
        name="frame",
    )(sides, up_rows, low_rows)


def advance_kernel(comp_count, left_at, right_at, *refs):
    (flags, ocean_first, source_column, labels, state, up_rows, low_rows, left_in, right_in) = refs[:9]
    (own_sides, mask, mix_atm, mix_ocn, flux_map) = refs[9:14]
    out, surface, packed = refs[14:17]
    phi = refs[17:-16]
    (values, moved, halo_moved, smooth, pairs, mixed, later_smooth, later_pairs, later_mixed) = refs[-16:-7]
    (weights, flux_weights, fluxes, staged, top, in_sems, out_sems) = refs[-7:]
    left_cols = left_in.at[left_at : left_at + 2]
    right_cols = right_in.at[right_at : right_at + 2]
    first = (smooth, pairs, mixed)
    second = (later_smooth, later_pairs, later_mixed)
    rows, cols, levels = state.shape
    chunks = rows // CHUNK
    inner = pl.ds(EDGE, cols)
    flux_count = flux_map.shape[0]

    def fetch(q):
        return pltpu.make_async_copy(
            state.at[pl.ds(q * CHUNK, CHUNK)],
            values.at[pl.ds(q * CHUNK + 2, CHUNK), inner],
            in_sems.at[q],
        )

    def put(q, slot):
        return pltpu.make_async_copy(
            staged.at[slot], out.at[pl.ds(q * CHUNK, CHUNK)], out_sems.at[slot]
        )

    def begin(q, _):
        fetch(q).start()
        return 0

    lax.fori_loop(0, AHEAD, begin, 0)
    ocean = flags[0] == 1
    mix = jnp.where(ocean, mix_ocn[...], mix_atm[...])
    mix_high, mix_low = split_two(mix)
    weights[:levels, :levels] = mix_high
    weights[levels:, :levels] = mix_high
    weights[:levels, levels:] = mix_low
    weights[levels:, levels:] = mix_low
    map_high, map_low = split_two(flux_map[...])
    flux_weights[...] = jnp.concatenate(
        [
            jnp.concatenate([map_high.astype(F32), map_high.astype(F32)], axis=1),
            jnp.concatenate([map_low.astype(F32), map_low.astype(F32)], axis=1),
        ],
        axis=0,
    ).astype(BF16)
    values[0:2, EDGE : EDGE + cols, :] = up_rows[...].astype(F32)
    values[rows + 2 : rows + 4, EDGE : EDGE + cols, :] = low_rows[...].astype(F32)
    for r, i in ((1, EDGE - 1), (rows + 2, EDGE + rows)):
        values[r, EDGE - 1 : EDGE, :] = left_cols[1, i : i + 1, :]
        values[r, EDGE + cols : EDGE + cols + 1, :] = right_cols[0, i : i + 1, :]

    def side_cells(start, count):
        for row in range(count):
            values[start + row + 2, EDGE - 1 : EDGE, :] = left_cols[1, pl.ds(start + row + EDGE, 1), :]
            values[start + row + 2, EDGE + cols : EDGE + cols + 1, :] = right_cols[
                0, pl.ds(start + row + EDGE, 1), :
            ]

    def moved_sides(start, count):
        for row in range(count):
            moved[start + row + 1, EDGE - 1 : EDGE, :] = halo_moved[0, pl.ds(start + row, 1), :]
            moved[start + row + 1, EDGE + cols : EDGE + cols + 1, :] = halo_moved[
                1, pl.ds(start + row, 1), :
            ]

    def stage(refs, row, total):
        line = SMOOTHING * total
        refs[0][row] = line
        refs[1][row * cols : (row + 1) * cols, :] = side_by_side(line)

    def stage_rows(refs, ref, start, count):
        for row in range(count):
            i = start + row
            here = ref[i, EDGE : EDGE + cols, :] + (
                ref[i - 1, EDGE : EDGE + cols, :] + ref[i + 1, EDGE : EDGE + cols, :]
            )
            near = ref[i, EDGE - 1 : EDGE - 1 + cols, :] + ref[i, EDGE + 1 : EDGE + 1 + cols, :]
            stage(refs, row, here + near)

    def note_top(q, lines):
        lanes = lax.broadcasted_iota(jnp.int32, (cols, levels), 1)
        kept = lines[0]
        for row in range(1, CHUNK):
            kept = jnp.where(lanes == row, pltpu.roll(lines[row], row, 1), kept)
        turned = pltpu.roll(kept, q * CHUNK, 1)
        top[...] = jnp.where(lanes // CHUNK == q, turned, top[...])

    def mix_rows(refs, count):
        refs[2][: count * cols, :] = dot_nn(refs[1][: count * cols, :], weights[...])

    def finish(refs, row):
        part = refs[2][row * cols : (row + 1) * cols, :]
        return refs[0][row] + PHYSICS * jnp.tanh(part[:, :levels] + part[:, levels:])

    @pl.when(jnp.logical_not(ocean))
    def atmosphere():
        nearest = (left_cols.at[1], right_cols.at[0])
        beyond = (left_cols.at[0], right_cols.at[1])
        within = (own_sides.at[0], own_sides.at[3])
        for s in range(2):
            total = (
                nearest[s][EDGE : EDGE + rows, :]
                + nearest[s][EDGE - 1 : EDGE - 1 + rows, :]
                + nearest[s][EDGE + 1 : EDGE + 1 + rows, :]
            )
            stage(first, s, total + (beyond[s][EDGE : EDGE + rows, :] + within[s][...]))
        mix_rows(first, 2)
        for s in range(2):
            halo_moved[s] = finish(first, s)

        side_cells(0, 1)
        fetch(0).wait()
        fetch(1).wait()
        stage_rows(second, values, 1, 2)
        mix_rows(second, 2)
        for row in range(2):
            moved[row, EDGE : EDGE + cols, :] = finish(second, row)

        @pl.when(flags[1] == 0)
        def _():
            moved[0, EDGE : EDGE + cols, :] = jnp.zeros((cols, levels), F32)

        def begin_first(q):
            side_cells(jnp.minimum(q * CHUNK + 1, rows - CHUNK), CHUNK)
            stage_rows(first, values, q * CHUNK + 3, CHUNK)
            mix_rows(first, CHUNK)

        def end_first(q):
            for row in range(CHUNK):
                moved[q * CHUNK + row + 2, EDGE : EDGE + cols, :] = finish(first, row)

        def begin_second(q):
            moved_sides(q * CHUNK, CHUNK)
            stage_rows(second, moved, q * CHUNK + 1, CHUNK)

        def end_second(q, slot):
            for row in range(CHUNK):
                line = finish(second, row)
                staged[slot, row] = line
                both = line + moved[q * CHUNK + row + 1, EDGE : EDGE + cols, :]
                later_pairs[row * cols : (row + 1) * cols, :] = side_by_side(both)
            put(q, slot).start()
            note_top(q, [staged[slot, row] for row in range(CHUNK)])
            flux = dot_nt(flux_weights[...], later_pairs[...])
            flux = flux[:flux_count] + flux[flux_count:]
            for row in range(CHUNK):
                r = q * CHUNK + row
                block = PHYSICS * flux[:, row * cols : (row + 1) * cols]
                sea = jnp.broadcast_to(mask[pl.ds(r, 1), :], block.shape)
                block = jnp.where(sea > 0.5, block, 0.0)
                fluxes[pl.ds(pl.multiple_of(r * flux_count, flux_count), flux_count), :] = block

        fetch(AHEAD).start()
        begin_first(0)
        end_first(0)

        def one_chunk(q, _):
            @pl.when(q + 1 < chunks)
            def _():
                fetch(q + 1).wait()

            @pl.when(q + AHEAD < chunks)
            def _():
                fetch(q + AHEAD).start()

            slot = (q - 1) % 2

            @pl.when(q >= 3)
            def _():
                put(q - 3, slot).wait()

            begin_first(q)
            begin_second(q - 1)
            end_first(q)
            mix_rows(second, CHUNK)
            end_second(q - 1, slot)
            return 0

        lax.fori_loop(1, chunks, one_chunk, 0)

        @pl.when(flags[2] == 0)
        def _():
            moved[rows + 1, EDGE : EDGE + cols, :] = jnp.zeros((cols, levels), F32)

        last = chunks - 1
        put(last - 2, last % 2).wait()
        begin_second(last)
        mix_rows(second, CHUNK)
        end_second(last, last % 2)
        spots = lax.broadcasted_iota(jnp.int32, (source_column.shape[0], rows), 1)
        placing = jnp.where(source_column[...] == spots, 1.0, 0.0).astype(BF16)
        share = flux_count // comp_count
        size = placing.shape[0]
        total = jnp.zeros((size, cols), F32)
        for c in range(comp_count):
            for f in range(share):
                index = c * share + f
                field = fluxes[pl.ds(index, rows, stride=flux_count), :].astype(BF16)
                value = dot_nn(placing, field)
                packed[c, :size, f * cols : (f + 1) * cols] = value.astype(BF16)
                total = total + ocean_first[index] * value
            packed[c, size:, :] = labels[...]
        total = side_by_side(total)
        capacity = size // len(phi)
        for n, block in enumerate(phi):
            block[:capacity, :] = total[n * capacity : (n + 1) * capacity, :]
            block[capacity:, :] = labels[...]
        put(last - 1, (last - 1) % 2).wait()
        put(last, last % 2).wait()
        surface[...] = top[...].T

    @pl.when(ocean)
    def sea_side():
        fetch(0).wait()
        lanes = lax.broadcasted_iota(jnp.int32, (CHUNK, CHUNK * levels), 1) // levels
        lines = lax.broadcasted_iota(jnp.int32, (CHUNK, CHUNK * levels), 0)
        spreader = jnp.where(lanes == lines, 1.0, 0.0).astype(F32)

        def one_chunk(q, _):
            base = q * CHUNK

            @pl.when(q + 1 < chunks)
            def _():
                fetch(q + 1).wait()

            @pl.when(q + AHEAD < chunks)
            def _():
                fetch(q + AHEAD).start()

            side_cells(base, CHUNK)
            stage_rows(first, values, base + 2, CHUNK)
            mix_rows(first, CHUNK)
            slot = q % 2

            @pl.when(q >= 2)
            def _():
                put(q - 2, slot).wait()

            sea = dot_nn(mask[pl.ds(pl.multiple_of(base, CHUNK), CHUNK), :].T, spreader)
            for row in range(CHUNK):
                chosen = sea[:, row * levels : (row + 1) * levels] > 0.5
                before = values[base + row + 2, EDGE : EDGE + cols, :]
                staged[slot, row] = jnp.where(chosen, finish(first, row), before)
            put(q, slot).start()
            note_top(q, [staged[slot, row] for row in range(CHUNK)])
            return 0

        lax.fori_loop(0, chunks, one_chunk, 0)
        put(chunks - 2, (chunks - 2) % 2).wait()
        put(chunks - 1, (chunks - 1) % 2).wait()
        surface[...] = top[...].T
        packed[...] = jnp.zeros(packed.shape, BF16)
        for block in phi:
            block[...] = jnp.zeros(block.shape, BF16)


def advance(
    flags, ocean_first, source_column, labels, state, halos, mask, mix_atm, mix_ocn, flux_map_t,
    comp_count, neighbours, left_at, right_at,
):
    rows, cols, levels = state.shape
    fluxes = flux_map_t.shape[0]
    vmem = pl.BlockSpec(memory_space=pltpu.VMEM)
    smem = pl.BlockSpec(memory_space=pltpu.SMEM)
    hbm = pl.BlockSpec(memory_space=pltpu.HBM)
    entry = jax.ShapeDtypeStruct(
        (comp_count, source_column.shape[0] + labels.shape[0], fluxes // comp_count * cols), BF16
    )
    block = jax.ShapeDtypeStruct(
        (source_column.shape[0] // neighbours + labels.shape[0], 2 * cols), BF16
    )
    cells = rows * cols
    return pl.pallas_call(
        functools.partial(advance_kernel, comp_count, left_at, right_at),
        out_shape=(
            jax.ShapeDtypeStruct(state.shape, F32),
            jax.ShapeDtypeStruct((rows, cols), F32),
            entry,
        )
        + (block,) * neighbours,
        in_specs=[smem, smem, vmem, vmem, hbm] + [vmem] * (len(halos) + 4),
        out_specs=(hbm, vmem, vmem) + (vmem,) * neighbours,
        scratch_shapes=[
            pltpu.VMEM((rows + 4, cols + 2 * EDGE, levels), F32),
            pltpu.VMEM((rows + 2, cols + 2 * EDGE, levels), F32),
            pltpu.VMEM((2, rows, levels), F32),
            pltpu.VMEM((CHUNK, cols, levels), F32),
            pltpu.VMEM((CHUNK * cols, 2 * levels), BF16),
            pltpu.VMEM((CHUNK * cols, 2 * levels), F32),
            pltpu.VMEM((CHUNK, cols, levels), F32),
            pltpu.VMEM((CHUNK * cols, 2 * levels), BF16),
            pltpu.VMEM((CHUNK * cols, 2 * levels), F32),
            pltpu.VMEM((2 * levels, 2 * levels), BF16),
            pltpu.VMEM((2 * fluxes, 2 * levels), BF16),
            pltpu.VMEM((rows * fluxes, cols), F32),
            pltpu.VMEM((2, CHUNK, cols, levels), F32),
            pltpu.VMEM((cols, levels), F32),
            pltpu.SemaphoreType.DMA((rows // CHUNK,)),
            pltpu.SemaphoreType.DMA((2,)),
        ],
        compiler_params=pltpu.CompilerParams(vmem_limit_bytes=48 * MIB),
        cost_estimate=pl.CostEstimate(
            flops=8 * cells * levels * levels, bytes_accessed=8 * cells * levels, transcendentals=0
        ),
        name="advance",
    )(flags, ocean_first, source_column, labels, state, *halos, mask, mix_atm, mix_ocn, flux_map_t)


BATCH = 8
LABEL_ROWS = 16


def regroup_kernel(slabs, *blocks):
    sources = slabs.shape[0] - 1
    capacity = (blocks[0].shape[0] - LABEL_ROWS) // sources
    size = len(blocks) * capacity
    heads = [slabs[c, size : size + LABEL_ROWS, :].astype(F32) for c in range(sources)]
    lines = [head[i : i + 1] for i in range(2) for head in heads]
    spare = jnp.zeros((LABEL_ROWS - len(lines), heads[0].shape[1]), F32)
    labels = jnp.concatenate(lines + [spare], axis=0).astype(BF16)
    for n, block in enumerate(blocks):
        for c in range(sources):
            block[c * capacity : (c + 1) * capacity, :] = slabs[
                c, n * capacity : (n + 1) * capacity, :
            ]
        block[sources * capacity :, :] = labels


def regroup(slabs, count):
    comps, rows, width = slabs.shape
    size = (rows - LABEL_ROWS) // count * (comps - 1) + LABEL_ROWS
    vmem = pl.BlockSpec(memory_space=pltpu.VMEM)
    return pl.pallas_call(
        regroup_kernel,
        out_shape=(jax.ShapeDtypeStruct((size, width), BF16),) * count,
        in_specs=[vmem],
        out_specs=(vmem,) * count,
        compiler_params=pltpu.CompilerParams(vmem_limit_bytes=16 * MIB),
        name="regroup",
    )(slabs)


def label_lines_of(blocks, start, lines):
    width = blocks[0].shape[1]
    capacity = width // len(blocks)
    lanes = lax.broadcasted_iota(jnp.int32, (LABEL_ROWS, width), 1) // capacity
    labels = jnp.zeros((LABEL_ROWS, width), F32)
    for n, block in enumerate(blocks):
        labels = jnp.where(lanes == n, block[start:, :].astype(F32), labels)
    labels = labels.astype(jnp.int32)
    join = lambda first: jnp.concatenate([labels[first + c : first + c + 1] for c in range(lines)], axis=1)
    return join(0), join(lines)


def selectors(weight_line, target_line, weight_count, rows):
    total = target_line.shape[1]
    spots = lax.broadcasted_iota(jnp.int32, (rows, total), 0)
    by_target = jnp.where(target_line == spots, 1.0, 0.0)
    numbers = lax.broadcasted_iota(jnp.int32, (weight_count, total), 0)
    by_weight = jnp.where(weight_line == numbers, 1.0, 0.0).astype(BF16)
    return by_target, by_weight


def project_kernel(count, flags, *refs):
    blocks = refs[:count]
    weights, surface, mask, shared, hits, entries, chosen = refs[count:]
    rows, cols = mask.shape
    weight_count = weights.shape[0]
    capacity = blocks[0].shape[0] - LABEL_ROWS
    for n in range(count):
        entries[n * capacity : (n + 1) * capacity, :] = blocks[n][:capacity, :]
    weight_line, target_line = label_lines_of(blocks, capacity, 1)
    by_target, by_weight = selectors(weight_line, target_line, weight_count, rows)
    hits[...] = by_target.T.astype(BF16)
    by_target = by_target.astype(BF16)
    change = jnp.zeros((rows, cols), F32)
    for g in range(weight_count // BATCH):
        for i in range(BATCH):
            w = g * BATCH + i
            chosen[i * rows : (i + 1) * rows, :] = by_target * by_weight[w : w + 1, :]
        both = dot_nn(chosen[...], entries[...])
        both = both[:, :cols] + both[:, cols:]
        wide = weights[g * BATCH : (g + 1) * BATCH].reshape(BATCH * cols, cols)
        halves = [split_two(both[i * rows : (i + 1) * rows, :]) for i in range(BATCH)]
        stacked = jnp.concatenate(
            [jnp.concatenate([half[k] for half in halves], axis=1) for k in range(2)], axis=0
        )
        product = dot_nn(stacked, wide)
        change = change + (product[:rows] + product[rows:])
    shared[0] = jnp.where(flags[0] == 1, surface[...], change)
    shared[1] = mask[...]


def project(flags, blocks, weights, surface, mask):
    rows, cols = mask.shape
    count = len(blocks)
    height, width = blocks[0].shape
    total = count * (height - LABEL_ROWS)
    vmem = pl.BlockSpec(memory_space=pltpu.VMEM)
    smem = pl.BlockSpec(memory_space=pltpu.SMEM)
    return pl.pallas_call(
        functools.partial(project_kernel, count),
        out_shape=(
            jax.ShapeDtypeStruct((2, rows, cols), F32),
            jax.ShapeDtypeStruct((total, rows), BF16),
        ),
        in_specs=[smem] + [vmem] * (count + 3),
        out_specs=(vmem, vmem),
        scratch_shapes=[
            pltpu.VMEM((total, width), BF16),
            pltpu.VMEM((BATCH * rows, total), BF16),
        ],
        compiler_params=pltpu.CompilerParams(vmem_limit_bytes=32 * MIB),
        cost_estimate=pl.CostEstimate(
            flops=2 * weights.shape[0] * rows * (width * total + 2 * cols * cols),
            bytes_accessed=2 * MIB,
            transcendentals=0,
        ),
        name="project",
    )(flags, *blocks, weights, surface, mask)


def regrid_kernel(sources, *refs):
    blocks = refs[:-5]
    weights, forcing, entries, chosen, binned = refs[-5:]
    share, rows, cols = forcing.shape
    weight_count = weights.shape[0]
    count = len(blocks)
    capacity = (blocks[0].shape[0] - LABEL_ROWS) // sources
    size = count * capacity
    for c in range(sources):
        for n in range(count):
            start = c * size + n * capacity
            entries[start : start + capacity, :] = blocks[n][c * capacity : (c + 1) * capacity, :]
    weight_line, target_line = label_lines_of(blocks, sources * capacity, sources)
    by_target, by_weight = selectors(weight_line, target_line, weight_count, rows)
    by_target = by_target.astype(BF16)
    for g in range(weight_count // BATCH):
        for i in range(BATCH):
            w = g * BATCH + i
            chosen[i * rows : (i + 1) * rows, :] = by_target * by_weight[w : w + 1, :]
        binned[...] = dot_nn(chosen[...], entries[...])
        wide = weights[g * BATCH : (g + 1) * BATCH].reshape(BATCH * cols, cols)
        halves = [
            [
                split_two(binned[i * rows : (i + 1) * rows, f * cols : (f + 1) * cols])
                for i in range(BATCH)
            ]
            for f in range(share)
        ]
        stacked = jnp.concatenate(
            [
                jnp.concatenate([half[k] for half in halves[f]], axis=1)
                for k in range(2)
                for f in range(share)
            ],
            axis=0,
        )
        product = dot_nn(stacked, wide)
        for f in range(share):
            part = product[f * rows : (f + 1) * rows] + product[
                (share + f) * rows : (share + f + 1) * rows
            ]
            forcing[f] = part if g == 0 else forcing[f] + part


def regrid(blocks, comp_count, weights, rows):
    sources = comp_count - 1
    weight_count, cols, _ = weights.shape
    height, width = blocks[0].shape
    total = (height - LABEL_ROWS) * len(blocks)
    share = width // cols
    vmem = pl.BlockSpec(memory_space=pltpu.VMEM)
    return pl.pallas_call(
        functools.partial(regrid_kernel, sources),
        out_shape=jax.ShapeDtypeStruct((share, rows, cols), F32),
        in_specs=[vmem] * (len(blocks) + 1),
        out_specs=vmem,
        scratch_shapes=[
            pltpu.VMEM((total, width), BF16),
            pltpu.VMEM((BATCH * rows, total), BF16),
            pltpu.VMEM((BATCH * rows, width), F32),
        ],
        compiler_params=pltpu.CompilerParams(vmem_limit_bytes=32 * MIB),
        cost_estimate=pl.CostEstimate(
            flops=2 * weight_count * rows * width * (total + 2 * cols),
            bytes_accessed=2 * MIB,
            transcendentals=0,
        ),
        name="regrid",
    )(*blocks, weights)


def pick_kernel(count, flags, *refs):
    parts = refs[:count]
    hits, surface = refs[count : count + 2]
    picked = refs[count + 2 :]
    from_ocean = lax.rem(flags[3] + 1, count)
    base = jnp.zeros(surface.shape, F32)
    sea = base
    change = base
    for shift in range(count):
        is_base = from_ocean == shift
        base = base + jnp.where(is_base, parts[shift][0], 0.0)
        sea = sea + jnp.where(is_base, parts[shift][1], 0.0)
        change = change + jnp.where(is_base, 0.0, parts[shift][0])
    now = base + jnp.where(sea > 0.5, change, 0.0)
    surface[...] = now
    pair = jnp.concatenate(split_two(now), axis=0)
    size = picked[0].shape[0]
    for n in range(len(picked)):
        some = hits[n * size : (n + 1) * size, :]
        picked[n][...] = dot_nn(jnp.concatenate([some, some], axis=1), pair)


def pick(flags, parts, hits, neighbours):
    _, rows, cols = parts[0].shape
    size = hits.shape[0] // neighbours
    vmem = pl.BlockSpec(memory_space=pltpu.VMEM)
    return pl.pallas_call(
        functools.partial(pick_kernel, len(parts)),
        out_shape=(jax.ShapeDtypeStruct((rows, cols), F32),)
        + (jax.ShapeDtypeStruct((size, cols), F32),) * neighbours,
        in_specs=[pl.BlockSpec(memory_space=pltpu.SMEM)] + [vmem] * (len(parts) + 1),
        out_specs=(vmem,) * (1 + neighbours),
        compiler_params=pltpu.CompilerParams(vmem_limit_bytes=16 * MIB),
        name="pick",
    )(flags, *parts, hits)


LINES = 8


def update_kernel(groups, flags, state, *refs):
    parts = refs[:groups]
    mask, ocean_map, out, token, held, table, wide, in_sems, out_sems = refs[groups:]
    rows, cols, levels = state.shape
    share = parts[0].shape[0]
    flux_count = groups * share
    chunks = rows // LINES
    depth = LINES * flux_count
    token[...] = jnp.zeros(token.shape, F32)

    def fetch(q):
        return pltpu.make_async_copy(
            state.at[pl.ds(q * LINES, LINES)], held.at[pl.ds(q * LINES, LINES)], in_sems.at[q]
        )

    def put(q):
        return pltpu.make_async_copy(
            held.at[pl.ds(q * LINES, LINES)], out.at[pl.ds(q * LINES, LINES)], out_sems.at[q]
        )

    @pl.when(flags[0] == 1)
    def ocean():
        for q in range(chunks):
            fetch(q).start()
        table[...] = jnp.zeros(table.shape, F32)
        for line in range(LINES):
            for f in range(flux_count):
                spot = f * LINES + line
                table[spot : spot + 1, line * levels : (line + 1) * levels] = ocean_map[f : f + 1]
        high, low = split_two(table[...])
        wide[:depth] = high
        wide[depth : 2 * depth] = high
        wide[2 * depth :] = low

        def one(q, _):
            start = pl.multiple_of(q * LINES, LINES)
            sea = mask[pl.ds(start, LINES), :] > 0.5
            part = jnp.concatenate(
                [
                    jnp.where(sea, parts[f // share][f % share, pl.ds(start, LINES), :], 0.0)
                    for f in range(flux_count)
                ],
                axis=0,
            )
            rough = part.astype(BF16).astype(F32)
            turned = jnp.concatenate([rough, part - rough, rough], axis=0).T.astype(BF16)
            change = dot_nn(turned, wide[...])
            fetch(q).wait()
            for line in range(LINES):
                held[start + line] += change[:, line * levels : (line + 1) * levels]
            put(q).start()
            return 0

        lax.fori_loop(0, chunks, one, 0, unroll=2)
        for q in range(chunks):
            put(q).wait()


def update(flags, state, parts, mask, ocean_map):
    rows, cols, levels = state.shape
    depth = LINES * ocean_map.shape[0]
    vmem = pl.BlockSpec(memory_space=pltpu.VMEM)
    smem = pl.BlockSpec(memory_space=pltpu.SMEM)
    hbm = pl.BlockSpec(memory_space=pltpu.HBM)
    return pl.pallas_call(
        functools.partial(update_kernel, len(parts)),
        out_shape=(
            jax.ShapeDtypeStruct(state.shape, F32),
            jax.ShapeDtypeStruct((EDGE, levels), F32),
        ),
        in_specs=[smem, hbm] + [vmem] * (len(parts) + 2),
        out_specs=(hbm, vmem),
        input_output_aliases={1: 0},
        scratch_shapes=[
            pltpu.VMEM(state.shape, F32),
            pltpu.VMEM((depth, LINES * levels), F32),
            pltpu.VMEM((3 * depth, LINES * levels), BF16),
            pltpu.SemaphoreType.DMA((rows // LINES,)),
            pltpu.SemaphoreType.DMA((rows // LINES,)),
        ],
        compiler_params=pltpu.CompilerParams(vmem_limit_bytes=24 * MIB),
        cost_estimate=pl.CostEstimate(
            flops=6 * rows * cols * depth * levels,
            bytes_accessed=8 * rows * cols * levels,
            transcendentals=0,
        ),
        name="update",
    )(flags, state, *parts, mask, ocean_map)


def returned_kernel(groups, flags, *refs):
    picked = refs[:groups]
    weight_column, row_line, weights, mask, surface, new_surface, token, out, total = refs[groups:]
    rows, cols = mask.shape
    weight_count = weights.shape[0]

    @pl.when(flags[0] == 1)
    def ocean():
        out[...] = new_surface[...]

    @pl.when(flags[0] == 0)
    def atmosphere():
        values = jnp.concatenate([p[...] for p in picked], axis=0)
        pair = side_by_side(values)
        which = jnp.broadcast_to(weight_column[...], values.shape)
        total[...] = jnp.zeros(values.shape, F32)

        def one(i, _):
            both = jnp.concatenate([weights[2 * i], weights[2 * i + 1]], axis=0)
            images = dot_nt(pair, jnp.concatenate([both, both], axis=1))
            total[...] += jnp.where(which == 2 * i, images[:, :cols], 0.0) + jnp.where(
                which == 2 * i + 1, images[:, cols:], 0.0
            )
            return 0

        lax.fori_loop(0, weight_count // 2, one, 0, unroll=8)
        spots = lax.broadcasted_iota(jnp.int32, (rows, values.shape[0]), 0)
        chosen = jnp.where(jnp.broadcast_to(row_line[...], spots.shape) == spots, 1.0, 0.0).astype(BF16)
        high, low = split_two(total[...])
        back = dot_nn(chosen, high) + dot_nn(chosen, low)
        out[...] = jnp.where(mask[...] > 0.5, back, surface[...])


def returned(flags, picked, weight_column, row_line, weights, mask, surface, new_surface, token):
    rows, cols = mask.shape
    entry_total = weight_column.shape[0]
    vmem = pl.BlockSpec(memory_space=pltpu.VMEM)
    smem = pl.BlockSpec(memory_space=pltpu.SMEM)
    return pl.pallas_call(
        functools.partial(returned_kernel, len(picked)),
        out_shape=jax.ShapeDtypeStruct((rows, cols), F32),
        in_specs=[smem] + [vmem] * (len(picked) + 7),
        out_specs=vmem,
        scratch_shapes=[pltpu.VMEM((entry_total, cols), F32)],
        compiler_params=pltpu.CompilerParams(vmem_limit_bytes=16 * MIB),
        name="returned",
    )(flags, *picked, weight_column, row_line, weights, mask, surface, new_surface, token)


def local(
    state, land_mask, intersection_list, mix_atm, mix_ocn, flux_map, ocean_map, regrid_weights
):
    rows, cols, levels = state.shape
    intersections = intersection_list.shape[2]
    comp_count = lax.axis_size("comp")
    lat_count = lax.axis_size("lat")
    lon_count = lax.axis_size("lon")
    tile_count = lat_count * lon_count
    reach = min(4, lon_count)
    neighbours = 2 * reach
    entry_total = intersections * rows
    capacity = entry_total // neighbours
    comp_index = lax.axis_index("comp")
    lat_index = lax.axis_index("lat")
    tile_index = lat_index * lon_count + lax.axis_index("lon")
    bands = comp_count * lat_count
    ocean_band = (comp_count - 1) * lat_count
    ocean_comp = comp_count - 1
    band = comp_index * lat_count + lat_index
    is_ocean = comp_index == ocean_comp
    upper_valid = (band > 0) & (band != ocean_band)
    lower_valid = (band < bands - 1) & (band != ocean_band - 1)
    flags = jnp.stack([is_ocean, upper_valid, lower_valid, comp_index]).astype(jnp.int32)
    mask = (land_mask == 1).astype(F32)

    def band_shift(value, by, lon_by):
        pairs = []
        for b in range(bands):
            target = b + by
            if 0 <= target < bands and (b >= ocean_band) == (target >= ocean_band):
                for lon in range(lon_count):
                    pairs.append(
                        (b * lon_count + lon, target * lon_count + (lon + lon_by) % lon_count)
                    )
        return lax.ppermute(value, AXES, pairs)

    first_rows, last_rows, sides = take_edges(state)
    up_rows = band_shift(last_rows, 1, 0)
    low_rows = band_shift(first_rows, -1, 0)
    framed = frame_sides(sides, up_rows, low_rows)
    if lon_count == 2:
        left_cols = right_cols = band_shift(framed, 0, 1)
        left_at, right_at = 2, 0
    else:
        left_cols = band_shift(framed[2:], 0, 1)
        right_cols = band_shift(framed[:2], 0, -1)
        left_at, right_at = 0, 0

    entry_list = intersection_list.reshape(entry_total, 3)
    owners = entry_list[:, 0]
    labels = entry_list[:, 2] * rows + entry_list[:, 1]
    offsets = [
        (n // reach * lon_count + n % reach - (reach - 1) // 2) % tile_count
        for n in range(neighbours)
    ]
    distance = (owners - tile_index + tile_count) % tile_count
    hits = distance[:, None] == jnp.array(offsets, jnp.int32)[None, :]
    neighbour_ids = jnp.sum(
        jnp.where(hits, jnp.arange(neighbours, dtype=jnp.int32)[None, :], 0), axis=1
    )
    positions = jnp.arange(entry_total, dtype=jnp.int32)
    earlier = (neighbour_ids[None, :] == neighbour_ids[:, None]) & (
        positions[None, :] < positions[:, None]
    )
    slots = neighbour_ids * capacity + jnp.sum(earlier.astype(jnp.int32), axis=1)
    placing = positions[:, None] == slots[None, :]
    sources = jnp.sum(jnp.where(placing, (positions // intersections)[None, :], 0), axis=1)
    packed_labels = jnp.sum(jnp.where(placing, labels[None, :], 0), axis=1)

    def over_comp(value):
        return lax.all_to_all(value, "comp", split_axis=0, concat_axis=0, tiled=True)

    def shifted_comp(value, shift):
        pairs = [
            (c * tile_count + t, (c + shift) % comp_count * tile_count + t)
            for c in range(comp_count)
            for t in range(tile_count)
        ]
        return lax.ppermute(value, AXES, pairs)

    def over_tiles(value, offset, comps):
        if offset % tile_count == 0:
            return value
        pairs = [
            (c * tile_count + t, c * tile_count + (t + offset) % tile_count)
            for c in range(comps)
            for t in range(tile_count)
        ]
        return lax.ppermute(value, AXES, pairs)

    def to_ocean(value, comp):
        pairs = [
            (comp * tile_count + t, ocean_comp * tile_count + t) for t in range(tile_count)
        ]
        return lax.ppermute(value, AXES, pairs)

    label_lines = jnp.stack([packed_labels // rows, packed_labels % rows]).astype(BF16)
    label_lines = jnp.pad(label_lines, ((0, LABEL_ROWS - 2), (0, 0)))

    halos = (up_rows, low_rows, left_cols, right_cols, sides)
    moved = advance(
        flags, ocean_map[:, 0], sources[:, None], label_lines, state, halos, mask, mix_atm, mix_ocn,
        flux_map.T, comp_count, neighbours, left_at, right_at,
    )
    moved, surface, packed, phi = moved[0], moved[1], moved[2], moved[3:]
    phi = [over_tiles(phi[n], offsets[n], ocean_comp) for n in range(neighbours)]
    shared, hits = project(flags, phi, regrid_weights, surface, mask)
    slabs, shared = lax.optimization_barrier((over_comp(packed), shared))
    parts = [shared] + [shifted_comp(shared, s) for s in range(1, comp_count)]
    picks = pick(flags, parts, hits, neighbours)
    blocks = regroup(slabs, neighbours)
    blocks = [over_tiles(blocks[n], offsets[n], comp_count) for n in range(neighbours)]
    forcing = regrid(blocks, comp_count, regrid_weights, rows)
    new_surface, picked = picks[0], picks[1:]
    arrived = [over_tiles(picked[n], -offsets[n], ocean_comp) for n in range(neighbours)]
    fields = [to_ocean(forcing, c) for c in range(ocean_comp)] + [forcing]
    final_state, token = update(flags, moved, fields, mask, ocean_map)
    weight_column = (packed_labels // rows)[:, None]
    surface_out = returned(
        flags, arrived, weight_column, sources[None, :], regrid_weights, mask, surface, new_surface,
        token,
    )
    return (final_state, surface_out)


def solution(mesh):
    placed = (
        P(("comp", "lat"), "lon", None),
        P(("comp", "lat"), "lon"),
        P(("comp", "lat"), "lon", None, None),
        P(),
        P(),
        P(),
        P(),
        P(),
    )
    return jax.shard_map(
        local,
        mesh=mesh,
        in_specs=placed,
        out_specs=(P(("comp", "lat"), "lon", None), P(("comp", "lat"), "lon")),
        check_vma=False,
    )
```

```python
import functools

import jax
import jax.numpy as jnp
from jax import lax
from jax.experimental import pallas as pl
from jax.experimental.pallas import tpu as pltpu
from jax.sharding import PartitionSpec as P

SMOOTHING = 0.2
PHYSICS = 0.5
MIB = 1024 * 1024
F32 = jnp.float32
BF16 = jnp.bfloat16
EDGE = 8
AHEAD = 4
CHUNK = 8
AXES = ("comp", "lat", "lon")


def split_two(x):
    high = x.astype(BF16)
    low = (x - high.astype(F32)).astype(BF16)
    return high, low


def side_by_side(x):
    return jnp.concatenate(split_two(x), axis=1)


def dot_nt(a, b):
    return lax.dot_general(a, b, (((1,), (1,)), ((), ())), preferred_element_type=F32)


def dot_nn(a, b):
    return jnp.dot(a, b, preferred_element_type=F32)


def edges_kernel(state, first_rows, last_rows, sides, top, bottom, left, right, sems):
    rows, cols, _ = state.shape
    copies = [
        pltpu.make_async_copy(state.at[pl.ds(0, 2)], top, sems.at[0]),
        pltpu.make_async_copy(state.at[pl.ds(rows - 2, 2)], bottom, sems.at[1]),
        pltpu.make_async_copy(state.at[:, pl.ds(0, EDGE)], left, sems.at[2]),
        pltpu.make_async_copy(state.at[:, pl.ds(cols - EDGE, EDGE)], right, sems.at[3]),
    ]
    for copy in copies:
        copy.start()
    for copy in copies:
        copy.wait()
    first_rows[...] = top[...].astype(BF16)
    last_rows[...] = bottom[...].astype(BF16)
    for i in range(2):
        sides[i] = left[:, i, :]
        sides[2 + i] = right[:, EDGE - 2 + i, :]


def take_edges(state):
    rows, cols, levels = state.shape
    slab = jax.ShapeDtypeStruct((2, cols, levels), BF16)
    side = jax.ShapeDtypeStruct((4, rows, levels), F32)
    vmem = pl.BlockSpec(memory_space=pltpu.VMEM)
    return pl.pallas_call(
        edges_kernel,
        out_shape=(slab, slab, side),
        in_specs=[pl.BlockSpec(memory_space=pltpu.HBM)],
        out_specs=(vmem,) * 3,
        scratch_shapes=[
            pltpu.VMEM((2, cols, levels), F32),
            pltpu.VMEM((2, cols, levels), F32),
            pltpu.VMEM((rows, EDGE, levels), F32),
            pltpu.VMEM((rows, EDGE, levels), F32),
            pltpu.SemaphoreType.DMA((4,)),
        ],
        compiler_params=pltpu.CompilerParams(vmem_limit_bytes=50 * MIB),
        name="edges",
    )(state)


def frame_kernel(sides, up_rows, low_rows, framed):
    _, rows, levels = sides.shape
    cols = up_rows.shape[1]
    framed[...] = jnp.zeros(framed.shape, F32)
    above = up_rows[1].astype(F32)
    below = low_rows[0].astype(F32)
    for i, col in enumerate((0, 1, cols - 2, cols - 1)):
        framed[i, EDGE : EDGE + rows, :] = sides[i]
        framed[i, EDGE - 1 : EDGE, :] = above[col : col + 1, :]
        framed[i, EDGE + rows : EDGE + rows + 1, :] = below[col : col + 1, :]


def frame_sides(sides, up_rows, low_rows):
    count, rows, levels = sides.shape
    vmem = pl.BlockSpec(memory_space=pltpu.VMEM)
    return pl.pallas_call(
        frame_kernel,
        out_shape=jax.ShapeDtypeStruct((count, rows + 2 * EDGE, levels), F32),
        in_specs=[vmem] * 3,
        out_specs=vmem,
        compiler_params=pltpu.CompilerParams(vmem_limit_bytes=16 * MIB),
        name="frame",
    )(sides, up_rows, low_rows)


def advance_kernel(comp_count, left_at, right_at, *refs):
    (flags, source_column, labels, state, up_rows, low_rows, left_in, right_in, own_sides) = refs[:9]
    (mask, mix_atm, mix_ocn, flux_map) = refs[9:13]
    out, surface, sea_copy = refs[13:16]
    packed = refs[16]
    (values, moved, halo_moved, smooth, pairs, mixed, later_smooth, later_pairs, later_mixed) = refs[17:26]
    (weights, flux_weights, flux_pairs, fluxes, staged, top, in_sems, out_sems) = refs[26:]
    left_cols = left_in.at[left_at : left_at + 2]
    right_cols = right_in.at[right_at : right_at + 2]
    first = (smooth, pairs, mixed)
    second = (later_smooth, later_pairs, later_mixed)
    rows, cols, levels = state.shape
    chunks = rows // CHUNK
    inner = pl.ds(EDGE, cols)
    flux_count = flux_map.shape[0]

    def fetch(q):
        return pltpu.make_async_copy(
            state.at[pl.ds(q * CHUNK, CHUNK)],
            values.at[pl.ds(q * CHUNK + 2, CHUNK), inner],
            in_sems.at[q],
        )

    def put(q, slot):
        return pltpu.make_async_copy(
            staged.at[slot], out.at[pl.ds(q * CHUNK, CHUNK)], out_sems.at[slot]
        )

    def begin(q, _):
        fetch(q).start()
        return 0

    lax.fori_loop(0, AHEAD, begin, 0)
    ocean = flags[0] == 1
    mix = jnp.where(ocean, mix_ocn[...], mix_atm[...])
    mix_high, mix_low = split_two(mix)
    weights[:levels, :levels] = mix_high
    weights[levels:, :levels] = mix_high
    weights[:levels, levels:] = mix_low
    weights[levels:, levels:] = mix_low
    sea_copy[...] = mask[...].astype(BF16)
    map_high, map_low = split_two(flux_map[...])
    flux_weights[...] = jnp.concatenate(
        [
            jnp.concatenate([map_high.astype(F32), map_high.astype(F32)], axis=1),
            jnp.concatenate([map_low.astype(F32), map_low.astype(F32)], axis=1),
        ],
        axis=0,
    ).astype(BF16)
    values[0:2, EDGE : EDGE + cols, :] = up_rows[...].astype(F32)
    values[rows + 2 : rows + 4, EDGE : EDGE + cols, :] = low_rows[...].astype(F32)
    for r, i in ((1, EDGE - 1), (rows + 2, EDGE + rows)):
        values[r, EDGE - 1 : EDGE, :] = left_cols[1, i : i + 1, :]
        values[r, EDGE + cols : EDGE + cols + 1, :] = right_cols[0, i : i + 1, :]

    def side_cells(start, count):
        for row in range(count):
            values[start + row + 2, EDGE - 1 : EDGE, :] = left_cols[1, pl.ds(start + row + EDGE, 1), :]
            values[start + row + 2, EDGE + cols : EDGE + cols + 1, :] = right_cols[
                0, pl.ds(start + row + EDGE, 1), :
            ]

    def moved_sides(start, count):
        for row in range(count):
            moved[start + row + 1, EDGE - 1 : EDGE, :] = halo_moved[0, pl.ds(start + row, 1), :]
            moved[start + row + 1, EDGE + cols : EDGE + cols + 1, :] = halo_moved[
                1, pl.ds(start + row, 1), :
            ]

    def stage(refs, row, total):
        line = SMOOTHING * total
        refs[0][row] = line
        refs[1][row * cols : (row + 1) * cols, :] = side_by_side(line)

    def stage_rows(refs, ref, start, count):
        for row in range(count):
            i = start + row
            here = ref[i, EDGE : EDGE + cols, :] + (
                ref[i - 1, EDGE : EDGE + cols, :] + ref[i + 1, EDGE : EDGE + cols, :]
            )
            near = ref[i, EDGE - 1 : EDGE - 1 + cols, :] + ref[i, EDGE + 1 : EDGE + 1 + cols, :]
            stage(refs, row, here + near)

    def note_top(q, lines):
        lanes = lax.broadcasted_iota(jnp.int32, (cols, levels), 1)
        kept = lines[0]
        for row in range(1, CHUNK):
            kept = jnp.where(lanes == row, pltpu.roll(lines[row], row, 1), kept)
        turned = pltpu.roll(kept, q * CHUNK, 1)
        top[...] = jnp.where(lanes // CHUNK == q, turned, top[...])

    def mix_rows(refs, count):
        refs[2][: count * cols, :] = dot_nn(refs[1][: count * cols, :], weights[...])

    def finish(refs, row):
        part = refs[2][row * cols : (row + 1) * cols, :]
        return refs[0][row] + PHYSICS * jnp.tanh(part[:, :levels] + part[:, levels:])

    @pl.when(jnp.logical_not(ocean))
    def atmosphere():
        nearest = (left_cols.at[1], right_cols.at[0])
        beyond = (left_cols.at[0], right_cols.at[1])
        within = (own_sides.at[0], own_sides.at[3])
        for s in range(2):
            total = (
                nearest[s][EDGE : EDGE + rows, :]
                + nearest[s][EDGE - 1 : EDGE - 1 + rows, :]
                + nearest[s][EDGE + 1 : EDGE + 1 + rows, :]
            )
            stage(first, s, total + (beyond[s][EDGE : EDGE + rows, :] + within[s][...]))
        mix_rows(first, 2)
        for s in range(2):
            halo_moved[s] = finish(first, s)

        side_cells(0, 1)
        fetch(0).wait()
        fetch(1).wait()
        stage_rows(second, values, 1, 2)
        mix_rows(second, 2)
        for row in range(2):
            moved[row, EDGE : EDGE + cols, :] = finish(second, row)

        @pl.when(flags[1] == 0)
        def _():
            moved[0, EDGE : EDGE + cols, :] = jnp.zeros((cols, levels), F32)

        def begin_first(q):
            side_cells(jnp.minimum(q * CHUNK + 1, rows - CHUNK), CHUNK)
            stage_rows(first, values, q * CHUNK + 3, CHUNK)
            mix_rows(first, CHUNK)

        def end_first(q):
            for row in range(CHUNK):
                moved[q * CHUNK + row + 2, EDGE : EDGE + cols, :] = finish(first, row)

        def begin_second(q):
            moved_sides(q * CHUNK, CHUNK)
            stage_rows(second, moved, q * CHUNK + 1, CHUNK)

        def end_second(q, slot):
            for row in range(CHUNK):
                line = finish(second, row)
                staged[slot, row] = line
                both = line + moved[q * CHUNK + row + 1, EDGE : EDGE + cols, :]
                flux_pairs[row * cols : (row + 1) * cols, :] = side_by_side(both)
            put(q, slot).start()
            note_top(q, [staged[slot, row] for row in range(CHUNK)])

        def sum_fluxes(q):
            flux = dot_nt(flux_weights[...], flux_pairs[...])
            flux = flux[:flux_count] + flux[flux_count:]
            for row in range(CHUNK):
                r = q * CHUNK + row
                block = PHYSICS * flux[:, row * cols : (row + 1) * cols]
                sea = jnp.broadcast_to(mask[pl.ds(r, 1), :], block.shape)
                block = jnp.where(sea > 0.5, block, 0.0)
                fluxes[pl.ds(pl.multiple_of(r * flux_count, flux_count), flux_count), :] = block

        fetch(AHEAD).start()
        flux_pairs[...] = jnp.zeros(flux_pairs.shape, BF16)
        begin_first(0)
        end_first(0)

        def one_chunk(q, _):
            @pl.when(q + 1 < chunks)
            def _():
                fetch(q + 1).wait()

            @pl.when(q + AHEAD < chunks)
            def _():
                fetch(q + AHEAD).start()

            slot = (q - 1) % 2

            @pl.when(q >= 3)
            def _():
                put(q - 3, slot).wait()

            sum_fluxes(jnp.maximum(q - 2, 0))
            begin_first(q)
            begin_second(q - 1)
            mix_rows(second, CHUNK)
            end_first(q)
            end_second(q - 1, slot)
            return 0

        lax.fori_loop(1, chunks, one_chunk, 0)

        @pl.when(flags[2] == 0)
        def _():
            moved[rows + 1, EDGE : EDGE + cols, :] = jnp.zeros((cols, levels), F32)

        last = chunks - 1
        put(last - 2, last % 2).wait()
        sum_fluxes(last - 1)
        begin_second(last)
        mix_rows(second, CHUNK)
        end_second(last, last % 2)
        sum_fluxes(last)
        spots = lax.broadcasted_iota(jnp.int32, (source_column.shape[0], rows), 1)
        placing = jnp.where(source_column[...] == spots, 1.0, 0.0).astype(BF16)
        share = flux_count // comp_count
        for c in range(comp_count):
            for f in range(share):
                field = fluxes[pl.ds(c * share + f, rows, stride=flux_count), :].astype(BF16)
                packed[c, : placing.shape[0], f * cols : (f + 1) * cols] = dot_nn(
                    placing, field
                ).astype(BF16)
            packed[c, placing.shape[0] :, :] = labels[...]
        put(last - 1, (last - 1) % 2).wait()
        put(last, last % 2).wait()
        surface[...] = top[...].T

    @pl.when(ocean)
    def sea_side():
        fetch(0).wait()
        lanes = lax.broadcasted_iota(jnp.int32, (CHUNK, CHUNK * levels), 1) // levels
        lines = lax.broadcasted_iota(jnp.int32, (CHUNK, CHUNK * levels), 0)
        spreader = jnp.where(lanes == lines, 1.0, 0.0).astype(F32)

        def one_chunk(q, _):
            base = q * CHUNK

            @pl.when(q + 1 < chunks)
            def _():
                fetch(q + 1).wait()

            @pl.when(q + AHEAD < chunks)
            def _():
                fetch(q + AHEAD).start()

            side_cells(base, CHUNK)
            stage_rows(first, values, base + 2, CHUNK)
            mix_rows(first, CHUNK)
            slot = q % 2

            @pl.when(q >= 2)
            def _():
                put(q - 2, slot).wait()

            sea = dot_nn(mask[pl.ds(pl.multiple_of(base, CHUNK), CHUNK), :].T, spreader)
            for row in range(CHUNK):
                chosen = sea[:, row * levels : (row + 1) * levels] > 0.5
                before = values[base + row + 2, EDGE : EDGE + cols, :]
                staged[slot, row] = jnp.where(chosen, finish(first, row), before)
            put(q, slot).start()
            note_top(q, [staged[slot, row] for row in range(CHUNK)])
            return 0

        lax.fori_loop(0, chunks, one_chunk, 0)
        put(chunks - 2, (chunks - 2) % 2).wait()
        put(chunks - 1, (chunks - 1) % 2).wait()
        surface[...] = top[...].T
        packed[...] = jnp.zeros(packed.shape, BF16)


def advance(
    flags, source_column, labels, state, halos, mask, mix_atm, mix_ocn, flux_map_t, comp_count, left_at, right_at
):
    rows, cols, levels = state.shape
    fluxes = flux_map_t.shape[0]
    vmem = pl.BlockSpec(memory_space=pltpu.VMEM)
    smem = pl.BlockSpec(memory_space=pltpu.SMEM)
    hbm = pl.BlockSpec(memory_space=pltpu.HBM)
    entry = jax.ShapeDtypeStruct(
        (comp_count, source_column.shape[0] + labels.shape[0], fluxes // comp_count * cols), BF16
    )
    cells = rows * cols
    return pl.pallas_call(
        functools.partial(advance_kernel, comp_count, left_at, right_at),
        out_shape=(
            jax.ShapeDtypeStruct(state.shape, F32),
            jax.ShapeDtypeStruct((rows, cols), F32),
            jax.ShapeDtypeStruct((rows, cols), BF16),
            entry,
        ),
        in_specs=[smem, vmem, vmem, hbm] + [vmem] * (len(halos) + 4),
        out_specs=(hbm, vmem, vmem, vmem),
        scratch_shapes=[
            pltpu.VMEM((rows + 4, cols + 2 * EDGE, levels), F32),
            pltpu.VMEM((rows + 2, cols + 2 * EDGE, levels), F32),
            pltpu.VMEM((2, rows, levels), F32),
            pltpu.VMEM((CHUNK, cols, levels), F32),
            pltpu.VMEM((CHUNK * cols, 2 * levels), BF16),
            pltpu.VMEM((CHUNK * cols, 2 * levels), F32),
            pltpu.VMEM((CHUNK, cols, levels), F32),
            pltpu.VMEM((CHUNK * cols, 2 * levels), BF16),
            pltpu.VMEM((CHUNK * cols, 2 * levels), F32),
            pltpu.VMEM((2 * levels, 2 * levels), BF16),
            pltpu.VMEM((2 * fluxes, 2 * levels), BF16),
            pltpu.VMEM((CHUNK * cols, 2 * levels), BF16),
            pltpu.VMEM((rows * fluxes, cols), F32),
            pltpu.VMEM((2, CHUNK, cols, levels), F32),
            pltpu.VMEM((cols, levels), F32),
            pltpu.SemaphoreType.DMA((rows // CHUNK,)),
            pltpu.SemaphoreType.DMA((2,)),
        ],
        compiler_params=pltpu.CompilerParams(vmem_limit_bytes=48 * MIB),
        cost_estimate=pl.CostEstimate(
            flops=8 * cells * levels * levels, bytes_accessed=8 * cells * levels, transcendentals=0
        ),
        name="advance",
    )(flags, source_column, labels, state, *halos, mask, mix_atm, mix_ocn, flux_map_t)


BATCH = 8
LABEL_ROWS = 16


def regroup_kernel(slabs, *blocks):
    sources = slabs.shape[0] - 1
    capacity = (blocks[0].shape[0] - LABEL_ROWS) // sources
    size = len(blocks) * capacity
    heads = [slabs[c, size : size + LABEL_ROWS, :].astype(F32) for c in range(sources)]
    lines = [head[i : i + 1] for i in range(2) for head in heads]
    spare = jnp.zeros((LABEL_ROWS - len(lines), heads[0].shape[1]), F32)
    labels = jnp.concatenate(lines + [spare], axis=0).astype(BF16)
    for n, block in enumerate(blocks):
        for c in range(sources):
            block[c * capacity : (c + 1) * capacity, :] = slabs[
                c, n * capacity : (n + 1) * capacity, :
            ]
        block[sources * capacity :, :] = labels


def regroup(slabs, count):
    comps, rows, width = slabs.shape
    size = (rows - LABEL_ROWS) // count * (comps - 1) + LABEL_ROWS
    vmem = pl.BlockSpec(memory_space=pltpu.VMEM)
    return pl.pallas_call(
        regroup_kernel,
        out_shape=(jax.ShapeDtypeStruct((size, width), BF16),) * count,
        in_specs=[vmem],
        out_specs=(vmem,) * count,
        compiler_params=pltpu.CompilerParams(vmem_limit_bytes=16 * MIB),
        name="regroup",
    )(slabs)


def regrid_body(count, comp_count, flags, ocean_first, *refs):
    blocks = refs[:count]
    seas = refs[count : count + comp_count]
    weights, surface, mask, forcing, shared, hits, entries, chosen, binned = refs[count + comp_count :]
    sources = comp_count - 1
    rows, cols = mask.shape
    share = forcing.shape[0]
    weight_count = weights.shape[0]
    capacity = (blocks[0].shape[0] - LABEL_ROWS) // sources
    size = count * capacity
    total = sources * size
    width = blocks[0].shape[1]
    for c in range(sources):
        for n in range(count):
            start = c * size + n * capacity
            entries[start : start + capacity, :] = blocks[n][c * capacity : (c + 1) * capacity, :]
    lanes = lax.broadcasted_iota(jnp.int32, (LABEL_ROWS, width), 1) // capacity
    labels = jnp.zeros((LABEL_ROWS, width), F32)
    for n in range(count):
        labels = jnp.where(lanes == n, blocks[n][sources * capacity :, :].astype(F32), labels)
    labels = labels.astype(jnp.int32)
    weight_line = jnp.concatenate([labels[c : c + 1, :size] for c in range(sources)], axis=1)
    target_line = jnp.concatenate(
        [labels[sources + c : sources + c + 1, :size] for c in range(sources)], axis=1
    )
    spots = lax.broadcasted_iota(jnp.int32, (rows, total), 0)
    by_target = jnp.where(target_line == spots, 1.0, 0.0)
    own = by_target[:, :size]
    for c in range(1, sources):
        own = jnp.where(flags[3] == c, by_target[:, c * size : (c + 1) * size], own)
    hits[...] = own.T.astype(BF16)
    by_target = by_target.astype(BF16)
    numbers = lax.broadcasted_iota(jnp.int32, (weight_count, total), 0)
    by_weight = jnp.where(weight_line == numbers, 1.0, 0.0).astype(BF16)
    for g in range(weight_count // BATCH):
        for i in range(BATCH):
            w = g * BATCH + i
            chosen[i * rows : (i + 1) * rows, :] = by_target * by_weight[w : w + 1, :]
        binned[...] = dot_nn(chosen[...], entries[...])
        wide = weights[g * BATCH : (g + 1) * BATCH].reshape(BATCH * cols, cols)
        halves = [
            [
                split_two(binned[i * rows : (i + 1) * rows, f * cols : (f + 1) * cols])
                for i in range(BATCH)
            ]
            for f in range(share)
        ]
        stacked = jnp.concatenate(
            [
                jnp.concatenate([half[k] for half in halves[f]], axis=1)
                for k in range(2)
                for f in range(share)
            ],
            axis=0,
        )
        product = dot_nn(stacked, wide)
        for f in range(share):
            part = product[f * rows : (f + 1) * rows] + product[
                (share + f) * rows : (share + f + 1) * rows
            ]
            forcing[f] = part if g == 0 else forcing[f] + part
    change = ocean_first[flags[3] * share] * forcing[0]
    for f in range(1, share):
        change = change + ocean_first[flags[3] * share + f] * forcing[f]
    sea = jnp.where(flags[0] == 1, seas[sources][...].astype(F32), 0.0)
    for c in range(sources):
        sea = sea + jnp.where(flags[3] == c, seas[c][...].astype(F32), 0.0)
    base = jnp.where(flags[0] == 1, surface[...], 0.0)
    shared[...] = base + jnp.where(sea > 0.5, change, 0.0)


def regrid(flags, ocean_first, blocks, seas, weights, surface, mask):
    comp_count = len(seas)
    sources = comp_count - 1
    rows, cols = mask.shape
    count = len(blocks)
    height, width = blocks[0].shape
    size = (height - LABEL_ROWS) // sources * count
    total = size * sources
    share = width // cols
    weight_count = weights.shape[0]
    vmem = pl.BlockSpec(memory_space=pltpu.VMEM)
    smem = pl.BlockSpec(memory_space=pltpu.SMEM)
    return pl.pallas_call(
        functools.partial(regrid_body, count, comp_count),
        out_shape=(
            jax.ShapeDtypeStruct((share, rows, cols), F32),
            jax.ShapeDtypeStruct((rows, cols), F32),
            jax.ShapeDtypeStruct((size, rows), BF16),
        ),
        in_specs=[smem, smem] + [vmem] * (count + comp_count + 3),
        out_specs=(vmem, vmem, vmem),
        scratch_shapes=[
            pltpu.VMEM((total, width), BF16),
            pltpu.VMEM((BATCH * rows, total), BF16),
            pltpu.VMEM((BATCH * rows, width), F32),
        ],
        compiler_params=pltpu.CompilerParams(vmem_limit_bytes=32 * MIB),
        cost_estimate=pl.CostEstimate(
            flops=2 * weight_count * rows * width * (total + 2 * cols),
            bytes_accessed=2 * MIB,
            transcendentals=0,
        ),
        name="regrid",
    )(flags, ocean_first, *blocks, *seas, weights, surface, mask)


def pick_kernel(count, *refs):
    parts = refs[:count]
    hits, surface = refs[count : count + 2]
    picked = refs[count + 2 :]
    now = parts[0][...]
    for part in parts[1:]:
        now = now + part[...]
    surface[...] = now
    pair = jnp.concatenate(split_two(now), axis=0)
    size = picked[0].shape[0]
    for n in range(len(picked)):
        some = hits[n * size : (n + 1) * size, :]
        picked[n][...] = dot_nn(jnp.concatenate([some, some], axis=1), pair)


def pick(parts, hits, neighbours):
    rows, cols = parts[0].shape
    size = hits.shape[0] // neighbours
    vmem = pl.BlockSpec(memory_space=pltpu.VMEM)
    return pl.pallas_call(
        functools.partial(pick_kernel, len(parts)),
        out_shape=(jax.ShapeDtypeStruct((rows, cols), F32),)
        + (jax.ShapeDtypeStruct((size, cols), F32),) * neighbours,
        in_specs=[vmem] * (len(parts) + 1),
        out_specs=(vmem,) * (1 + neighbours),
        compiler_params=pltpu.CompilerParams(vmem_limit_bytes=16 * MIB),
        name="pick",
    )(*parts, hits)


LINES = 8


def update_kernel(groups, flags, state, *refs):
    parts = refs[:groups]
    mask, ocean_map, out, token, held, table, wide, in_sems, out_sems = refs[groups:]
    rows, cols, levels = state.shape
    share = parts[0].shape[0]
    flux_count = groups * share
    chunks = rows // LINES
    depth = LINES * flux_count
    token[...] = jnp.zeros(token.shape, F32)

    def fetch(q):
        return pltpu.make_async_copy(
            state.at[pl.ds(q * LINES, LINES)], held.at[pl.ds(q * LINES, LINES)], in_sems.at[q]
        )

    def put(q):
        return pltpu.make_async_copy(
            held.at[pl.ds(q * LINES, LINES)], out.at[pl.ds(q * LINES, LINES)], out_sems.at[q]
        )

    @pl.when(flags[0] == 1)
    def ocean():
        for q in range(chunks):
            fetch(q).start()
        table[...] = jnp.zeros(table.shape, F32)
        for line in range(LINES):
            for f in range(flux_count):
                spot = f * LINES + line
                table[spot : spot + 1, line * levels : (line + 1) * levels] = ocean_map[f : f + 1]
        high, low = split_two(table[...])
        wide[:depth] = high
        wide[depth : 2 * depth] = high
        wide[2 * depth :] = low

        def one(q, _):
            start = pl.multiple_of(q * LINES, LINES)
            sea = mask[pl.ds(start, LINES), :] > 0.5
            part = jnp.concatenate(
                [
                    jnp.where(sea, parts[f // share][f % share, pl.ds(start, LINES), :], 0.0)
                    for f in range(flux_count)
                ],
                axis=0,
            )
            rough = part.astype(BF16).astype(F32)
            turned = jnp.concatenate([rough, part - rough, rough], axis=0).T.astype(BF16)
            change = dot_nn(turned, wide[...])
            fetch(q).wait()
            for line in range(LINES):
                held[start + line] += change[:, line * levels : (line + 1) * levels]
            put(q).start()
            return 0

        lax.fori_loop(0, chunks, one, 0, unroll=2)
        for q in range(chunks):
            put(q).wait()


def update(flags, state, parts, mask, ocean_map):
    rows, cols, levels = state.shape
    depth = LINES * ocean_map.shape[0]
    vmem = pl.BlockSpec(memory_space=pltpu.VMEM)
    smem = pl.BlockSpec(memory_space=pltpu.SMEM)
    hbm = pl.BlockSpec(memory_space=pltpu.HBM)
    return pl.pallas_call(
        functools.partial(update_kernel, len(parts)),
        out_shape=(
            jax.ShapeDtypeStruct(state.shape, F32),
            jax.ShapeDtypeStruct((EDGE, levels), F32),
        ),
        in_specs=[smem, hbm] + [vmem] * (len(parts) + 2),
        out_specs=(hbm, vmem),
        input_output_aliases={1: 0},
        scratch_shapes=[
            pltpu.VMEM(state.shape, F32),
            pltpu.VMEM((depth, LINES * levels), F32),
            pltpu.VMEM((3 * depth, LINES * levels), BF16),
            pltpu.SemaphoreType.DMA((rows // LINES,)),
            pltpu.SemaphoreType.DMA((rows // LINES,)),
        ],
        compiler_params=pltpu.CompilerParams(vmem_limit_bytes=24 * MIB),
        cost_estimate=pl.CostEstimate(
            flops=6 * rows * cols * depth * levels,
            bytes_accessed=8 * rows * cols * levels,
            transcendentals=0,
        ),
        name="update",
    )(flags, state, *parts, mask, ocean_map)


def returned_kernel(groups, flags, *refs):
    picked = refs[:groups]
    weight_column, row_line, weights, mask, surface, new_surface, token, out, total = refs[groups:]
    rows, cols = mask.shape
    weight_count = weights.shape[0]

    @pl.when(flags[0] == 1)
    def ocean():
        out[...] = new_surface[...]

    @pl.when(flags[0] == 0)
    def atmosphere():
        values = jnp.concatenate([p[...] for p in picked], axis=0)
        pair = side_by_side(values)
        which = jnp.broadcast_to(weight_column[...], values.shape)
        total[...] = jnp.zeros(values.shape, F32)

        def one(i, _):
            both = jnp.concatenate([weights[2 * i], weights[2 * i + 1]], axis=0)
            images = dot_nt(pair, jnp.concatenate([both, both], axis=1))
            total[...] += jnp.where(which == 2 * i, images[:, :cols], 0.0) + jnp.where(
                which == 2 * i + 1, images[:, cols:], 0.0
            )
            return 0

        lax.fori_loop(0, weight_count // 2, one, 0, unroll=8)
        spots = lax.broadcasted_iota(jnp.int32, (rows, values.shape[0]), 0)
        chosen = jnp.where(jnp.broadcast_to(row_line[...], spots.shape) == spots, 1.0, 0.0).astype(BF16)
        high, low = split_two(total[...])
        back = dot_nn(chosen, high) + dot_nn(chosen, low)
        out[...] = jnp.where(mask[...] > 0.5, back, surface[...])


def returned(flags, picked, weight_column, row_line, weights, mask, surface, new_surface, token):
    rows, cols = mask.shape
    entry_total = weight_column.shape[0]
    vmem = pl.BlockSpec(memory_space=pltpu.VMEM)
    smem = pl.BlockSpec(memory_space=pltpu.SMEM)
    return pl.pallas_call(
        functools.partial(returned_kernel, len(picked)),
        out_shape=jax.ShapeDtypeStruct((rows, cols), F32),
        in_specs=[smem] + [vmem] * (len(picked) + 7),
        out_specs=vmem,
        scratch_shapes=[pltpu.VMEM((entry_total, cols), F32)],
        compiler_params=pltpu.CompilerParams(vmem_limit_bytes=16 * MIB),
        name="returned",
    )(flags, *picked, weight_column, row_line, weights, mask, surface, new_surface, token)


def local(
    state, land_mask, intersection_list, mix_atm, mix_ocn, flux_map, ocean_map, regrid_weights
):
    rows, cols, levels = state.shape
    intersections = intersection_list.shape[2]
    comp_count = lax.axis_size("comp")
    lat_count = lax.axis_size("lat")
    lon_count = lax.axis_size("lon")
    tile_count = lat_count * lon_count
    reach = min(4, lon_count)
    neighbours = 2 * reach
    entry_total = intersections * rows
    capacity = entry_total // neighbours
    comp_index = lax.axis_index("comp")
    lat_index = lax.axis_index("lat")
    tile_index = lat_index * lon_count + lax.axis_index("lon")
    bands = comp_count * lat_count
    ocean_band = (comp_count - 1) * lat_count
    ocean_comp = comp_count - 1
    band = comp_index * lat_count + lat_index
    is_ocean = comp_index == ocean_comp
    upper_valid = (band > 0) & (band != ocean_band)
    lower_valid = (band < bands - 1) & (band != ocean_band - 1)
    flags = jnp.stack([is_ocean, upper_valid, lower_valid, comp_index]).astype(jnp.int32)
    mask = (land_mask == 1).astype(F32)

    def band_shift(value, by, lon_by):
        pairs = []
        for b in range(bands):
            target = b + by
            if 0 <= target < bands and (b >= ocean_band) == (target >= ocean_band):
                for lon in range(lon_count):
                    pairs.append(
                        (b * lon_count + lon, target * lon_count + (lon + lon_by) % lon_count)
                    )
        return lax.ppermute(value, AXES, pairs)

    first_rows, last_rows, sides = take_edges(state)
    up_rows = band_shift(last_rows, 1, 0)
    low_rows = band_shift(first_rows, -1, 0)
    framed = frame_sides(sides, up_rows, low_rows)
    if lon_count == 2:
        left_cols = right_cols = band_shift(framed, 0, 1)
        left_at, right_at = 2, 0
    else:
        left_cols = band_shift(framed[2:], 0, 1)
        right_cols = band_shift(framed[:2], 0, -1)
        left_at, right_at = 0, 0

    entry_list = intersection_list.reshape(entry_total, 3)
    owners = entry_list[:, 0]
    labels = entry_list[:, 2] * rows + entry_list[:, 1]
    offsets = [
        (n // reach * lon_count + n % reach - (reach - 1) // 2) % tile_count
        for n in range(neighbours)
    ]
    distance = (owners - tile_index + tile_count) % tile_count
    hits = distance[:, None] == jnp.array(offsets, jnp.int32)[None, :]
    neighbour_ids = jnp.sum(
        jnp.where(hits, jnp.arange(neighbours, dtype=jnp.int32)[None, :], 0), axis=1
    )
    positions = jnp.arange(entry_total, dtype=jnp.int32)
    earlier = (neighbour_ids[None, :] == neighbour_ids[:, None]) & (
        positions[None, :] < positions[:, None]
    )
    slots = neighbour_ids * capacity + jnp.sum(earlier.astype(jnp.int32), axis=1)
    placing = positions[:, None] == slots[None, :]
    sources = jnp.sum(jnp.where(placing, (positions // intersections)[None, :], 0), axis=1)
    packed_labels = jnp.sum(jnp.where(placing, labels[None, :], 0), axis=1)

    def over_comp(value):
        return lax.all_to_all(value, "comp", split_axis=0, concat_axis=0, tiled=True)

    def shifted_comp(value, shift):
        pairs = [
            (c * tile_count + t, (c + shift) % comp_count * tile_count + t)
            for c in range(comp_count)
            for t in range(tile_count)
        ]
        return lax.ppermute(value, AXES, pairs)

    def over_tiles(value, offset, comps):
        if offset % tile_count == 0:
            return value
        pairs = [
            (c * tile_count + t, c * tile_count + (t + offset) % tile_count)
            for c in range(comps)
            for t in range(tile_count)
        ]
        return lax.ppermute(value, AXES, pairs)

    def from_ocean(value, comp):
        pairs = [
            (ocean_comp * tile_count + t, comp * tile_count + t) for t in range(tile_count)
        ]
        return lax.ppermute(value, AXES, pairs)

    def to_ocean(value, comp):
        pairs = [
            (comp * tile_count + t, ocean_comp * tile_count + t) for t in range(tile_count)
        ]
        return lax.ppermute(value, AXES, pairs)

    label_lines = jnp.stack([packed_labels // rows, packed_labels % rows]).astype(BF16)
    label_lines = jnp.pad(label_lines, ((0, LABEL_ROWS - 2), (0, 0)))

    halos = (up_rows, low_rows, left_cols, right_cols, sides)
    moved = advance(
        flags, sources[:, None], label_lines, state, halos, mask, mix_atm, mix_ocn, flux_map.T,
        comp_count, left_at, right_at,
    )
    moved, surface, sea_copy, packed = moved
    slabs = over_comp(packed)
    seas = [from_ocean(sea_copy, c) for c in range(ocean_comp)] + [sea_copy]
    blocks = regroup(slabs, neighbours)
    blocks = [over_tiles(blocks[n], offsets[n], comp_count) for n in range(neighbours)]
    forcing, shared, hits = regrid(
        flags, ocean_map[:, 0], blocks, seas, regrid_weights, surface, mask
    )
    parts = [shared] + [shifted_comp(shared, s) for s in range(1, comp_count)]
    parts[1], forcing = lax.optimization_barrier((parts[1], forcing))
    picks = pick(parts, hits, neighbours)
    new_surface, picked = picks[0], picks[1:]
    arrived = [over_tiles(picked[n], -offsets[n], ocean_comp) for n in range(neighbours)]
    fields = [to_ocean(forcing, c) for c in range(ocean_comp)] + [forcing]
    final_state, token = update(flags, moved, fields, mask, ocean_map)
    weight_column = (packed_labels // rows)[:, None]
    surface_out = returned(
        flags, arrived, weight_column, sources[None, :], regrid_weights, mask, surface, new_surface,
        token,
    )
    return (final_state, surface_out)


def solution(mesh):
    placed = (
        P(("comp", "lat"), "lon", None),
        P(("comp", "lat"), "lon"),
        P(("comp", "lat"), "lon", None, None),
        P(),
        P(),
        P(),
        P(),
        P(),
    )
    return jax.shard_map(
        local,
        mesh=mesh,
        in_specs=placed,
        out_specs=(P(("comp", "lat"), "lon", None), P(("comp", "lat"), "lon")),
        check_vma=False,
    )
```

```python
import functools

import jax
import jax.numpy as jnp
from jax import lax
from jax.experimental import pallas as pl
from jax.experimental.pallas import tpu as pltpu
from jax.sharding import PartitionSpec as P

SMOOTHING = 0.2
PHYSICS = 0.5
MIB = 1024 * 1024
F32 = jnp.float32
BF16 = jnp.bfloat16
EDGE = 8
LINES = 8
AHEAD = 4
CHUNK = 8
AXES = ("comp", "lat", "lon")


def split_two(x):
    high = x.astype(BF16)
    low = (x - high.astype(F32)).astype(BF16)
    return high, low


def side_by_side(x):
    return jnp.concatenate(split_two(x), axis=1)


def dot_nt(a, b):
    return lax.dot_general(a, b, (((1,), (1,)), ((), ())), preferred_element_type=F32)


def dot_nn(a, b):
    return jnp.dot(a, b, preferred_element_type=F32)


def edges_kernel(state, first_rows, last_rows, sides, top, bottom, left, right, sems):
    rows, cols, _ = state.shape
    copies = [
        pltpu.make_async_copy(state.at[pl.ds(0, 2)], top, sems.at[0]),
        pltpu.make_async_copy(state.at[pl.ds(rows - 2, 2)], bottom, sems.at[1]),
        pltpu.make_async_copy(state.at[:, pl.ds(0, EDGE)], left, sems.at[2]),
        pltpu.make_async_copy(state.at[:, pl.ds(cols - EDGE, EDGE)], right, sems.at[3]),
    ]
    for copy in copies:
        copy.start()
    for copy in copies:
        copy.wait()
    first_rows[...] = top[...].astype(BF16)
    last_rows[...] = bottom[...].astype(BF16)
    for i in range(2):
        sides[i] = left[:, i, :]
        sides[2 + i] = right[:, EDGE - 2 + i, :]


def take_edges(state):
    rows, cols, levels = state.shape
    slab = jax.ShapeDtypeStruct((2, cols, levels), BF16)
    side = jax.ShapeDtypeStruct((4, rows, levels), F32)
    vmem = pl.BlockSpec(memory_space=pltpu.VMEM)
    return pl.pallas_call(
        edges_kernel,
        out_shape=(slab, slab, side),
        in_specs=[pl.BlockSpec(memory_space=pltpu.HBM)],
        out_specs=(vmem,) * 3,
        scratch_shapes=[
            pltpu.VMEM((2, cols, levels), F32),
            pltpu.VMEM((2, cols, levels), F32),
            pltpu.VMEM((rows, EDGE, levels), F32),
            pltpu.VMEM((rows, EDGE, levels), F32),
            pltpu.SemaphoreType.DMA((4,)),
        ],
        compiler_params=pltpu.CompilerParams(vmem_limit_bytes=50 * MIB),
        name="edges",
    )(state)


def frame_kernel(sides, up_rows, low_rows, framed):
    _, rows, levels = sides.shape
    cols = up_rows.shape[1]
    framed[...] = jnp.zeros(framed.shape, F32)
    above = up_rows[1].astype(F32)
    below = low_rows[0].astype(F32)
    for i, col in enumerate((0, 1, cols - 2, cols - 1)):
        framed[i, EDGE : EDGE + rows, :] = sides[i]
        framed[i, EDGE - 1 : EDGE, :] = above[col : col + 1, :]
        framed[i, EDGE + rows : EDGE + rows + 1, :] = below[col : col + 1, :]


def frame_sides(sides, up_rows, low_rows):
    count, rows, levels = sides.shape
    vmem = pl.BlockSpec(memory_space=pltpu.VMEM)
    return pl.pallas_call(
        frame_kernel,
        out_shape=jax.ShapeDtypeStruct((count, rows + 2 * EDGE, levels), F32),
        in_specs=[vmem] * 3,
        out_specs=vmem,
        compiler_params=pltpu.CompilerParams(vmem_limit_bytes=16 * MIB),
        name="frame",
    )(sides, up_rows, low_rows)


def advance_kernel(comp_count, left_at, right_at, *refs):
    (flags, source_column, labels, state, up_rows, low_rows, left_in, right_in, own_sides) = refs[:9]
    (mask, mix_atm, mix_ocn, flux_map, ocean_map) = refs[9:14]
    out, surface, sea_copy, packed, wide = refs[14:19]
    (values, moved, halo_moved, smooth, pairs, mixed, later_smooth, later_pairs, later_mixed) = refs[19:28]
    (weights, flux_weights, flux_pairs, fluxes, staged, top, table, in_sems, out_sems) = refs[28:]
    left_cols = left_in.at[left_at : left_at + 2]
    right_cols = right_in.at[right_at : right_at + 2]
    first = (smooth, pairs, mixed)
    second = (later_smooth, later_pairs, later_mixed)
    rows, cols, levels = state.shape
    chunks = rows // CHUNK
    inner = pl.ds(EDGE, cols)
    flux_count = flux_map.shape[0]

    def fetch(q):
        return pltpu.make_async_copy(
            state.at[pl.ds(q * CHUNK, CHUNK)],
            values.at[pl.ds(q * CHUNK + 2, CHUNK), inner],
            in_sems.at[q],
        )

    def put(q, slot):
        return pltpu.make_async_copy(
            staged.at[slot], out.at[pl.ds(q * CHUNK, CHUNK)], out_sems.at[slot]
        )

    def begin(q, _):
        fetch(q).start()
        return 0

    lax.fori_loop(0, AHEAD, begin, 0)
    ocean = flags[0] == 1
    mix = jnp.where(ocean, mix_ocn[...], mix_atm[...])
    mix_high, mix_low = split_two(mix)
    weights[:levels, :levels] = mix_high
    weights[levels:, :levels] = mix_high
    weights[:levels, levels:] = mix_low
    weights[levels:, levels:] = mix_low
    sea_copy[...] = mask[...].astype(BF16)
    map_high, map_low = split_two(flux_map[...])
    flux_weights[...] = jnp.concatenate(
        [
            jnp.concatenate([map_high.astype(F32), map_high.astype(F32)], axis=1),
            jnp.concatenate([map_low.astype(F32), map_low.astype(F32)], axis=1),
        ],
        axis=0,
    ).astype(BF16)
    values[0:2, EDGE : EDGE + cols, :] = up_rows[...].astype(F32)
    values[rows + 2 : rows + 4, EDGE : EDGE + cols, :] = low_rows[...].astype(F32)
    for r, i in ((1, EDGE - 1), (rows + 2, EDGE + rows)):
        values[r, EDGE - 1 : EDGE, :] = left_cols[1, i : i + 1, :]
        values[r, EDGE + cols : EDGE + cols + 1, :] = right_cols[0, i : i + 1, :]

    def side_cells(start, count):
        for row in range(count):
            values[start + row + 2, EDGE - 1 : EDGE, :] = left_cols[1, pl.ds(start + row + EDGE, 1), :]
            values[start + row + 2, EDGE + cols : EDGE + cols + 1, :] = right_cols[
                0, pl.ds(start + row + EDGE, 1), :
            ]

    def moved_sides(start, count):
        for row in range(count):
            moved[start + row + 1, EDGE - 1 : EDGE, :] = halo_moved[0, pl.ds(start + row, 1), :]
            moved[start + row + 1, EDGE + cols : EDGE + cols + 1, :] = halo_moved[
                1, pl.ds(start + row, 1), :
            ]

    def stage(refs, row, total):
        line = SMOOTHING * total
        refs[0][row] = line
        refs[1][row * cols : (row + 1) * cols, :] = side_by_side(line)

    def stage_rows(refs, ref, start, count):
        for row in range(count):
            i = start + row
            here = ref[i, EDGE : EDGE + cols, :] + (
                ref[i - 1, EDGE : EDGE + cols, :] + ref[i + 1, EDGE : EDGE + cols, :]
            )
            near = ref[i, EDGE - 1 : EDGE - 1 + cols, :] + ref[i, EDGE + 1 : EDGE + 1 + cols, :]
            stage(refs, row, here + near)

    def note_top(q, lines):
        lanes = lax.broadcasted_iota(jnp.int32, (cols, levels), 1)
        kept = lines[0]
        for row in range(1, CHUNK):
            kept = jnp.where(lanes == row, pltpu.roll(lines[row], row, 1), kept)
        turned = pltpu.roll(kept, q * CHUNK, 1)
        top[...] = jnp.where(lanes // CHUNK == q, turned, top[...])

    def mix_rows(refs, count):
        refs[2][: count * cols, :] = dot_nn(refs[1][: count * cols, :], weights[...])

    def finish(refs, row):
        part = refs[2][row * cols : (row + 1) * cols, :]
        return refs[0][row] + PHYSICS * jnp.tanh(part[:, :levels] + part[:, levels:])

    @pl.when(jnp.logical_not(ocean))
    def atmosphere():
        nearest = (left_cols.at[1], right_cols.at[0])
        beyond = (left_cols.at[0], right_cols.at[1])
        within = (own_sides.at[0], own_sides.at[3])
        for s in range(2):
            total = (
                nearest[s][EDGE : EDGE + rows, :]
                + nearest[s][EDGE - 1 : EDGE - 1 + rows, :]
                + nearest[s][EDGE + 1 : EDGE + 1 + rows, :]
            )
            stage(first, s, total + (beyond[s][EDGE : EDGE + rows, :] + within[s][...]))
        mix_rows(first, 2)
        for s in range(2):
            halo_moved[s] = finish(first, s)

        side_cells(0, 1)
        fetch(0).wait()
        fetch(1).wait()
        stage_rows(second, values, 1, 2)
        mix_rows(second, 2)
        for row in range(2):
            moved[row, EDGE : EDGE + cols, :] = finish(second, row)

        @pl.when(flags[1] == 0)
        def _():
            moved[0, EDGE : EDGE + cols, :] = jnp.zeros((cols, levels), F32)

        def begin_first(q):
            side_cells(jnp.minimum(q * CHUNK + 1, rows - CHUNK), CHUNK)
            stage_rows(first, values, q * CHUNK + 3, CHUNK)
            mix_rows(first, CHUNK)

        def end_first(q):
            for row in range(CHUNK):
                moved[q * CHUNK + row + 2, EDGE : EDGE + cols, :] = finish(first, row)

        def begin_second(q):
            moved_sides(q * CHUNK, CHUNK)
            stage_rows(second, moved, q * CHUNK + 1, CHUNK)

        def end_second(q, slot):
            for row in range(CHUNK):
                line = finish(second, row)
                staged[slot, row] = line
                both = line + moved[q * CHUNK + row + 1, EDGE : EDGE + cols, :]
                flux_pairs[row * cols : (row + 1) * cols, :] = side_by_side(both)
            put(q, slot).start()

        def sum_fluxes(q):
            note_top(q, [staged[q % 2, row] for row in range(CHUNK)])
            flux = dot_nt(flux_weights[...], flux_pairs[...])
            flux = flux[:flux_count] + flux[flux_count:]
            for row in range(CHUNK):
                r = q * CHUNK + row
                block = PHYSICS * flux[:, row * cols : (row + 1) * cols]
                sea = jnp.broadcast_to(mask[pl.ds(r, 1), :], block.shape)
                block = jnp.where(sea > 0.5, block, 0.0)
                fluxes[pl.ds(pl.multiple_of(r * flux_count, flux_count), flux_count), :] = block

        fetch(AHEAD).start()
        flux_pairs[...] = jnp.zeros(flux_pairs.shape, BF16)
        staged[0] = jnp.zeros(staged.shape[1:], F32)
        begin_first(0)
        end_first(0)

        def one_chunk(q, _):
            @pl.when(q + 1 < chunks)
            def _():
                fetch(q + 1).wait()

            @pl.when(q + AHEAD < chunks)
            def _():
                fetch(q + AHEAD).start()

            slot = (q - 1) % 2

            @pl.when(q >= 3)
            def _():
                put(q - 3, slot).wait()

            sum_fluxes(jnp.maximum(q - 2, 0))
            begin_first(q)
            begin_second(q - 1)
            mix_rows(second, CHUNK)
            end_first(q)
            end_second(q - 1, slot)
            return 0

        lax.fori_loop(1, chunks, one_chunk, 0)

        @pl.when(flags[2] == 0)
        def _():
            moved[rows + 1, EDGE : EDGE + cols, :] = jnp.zeros((cols, levels), F32)

        last = chunks - 1
        put(last - 2, last % 2).wait()
        sum_fluxes(last - 1)
        begin_second(last)
        mix_rows(second, CHUNK)
        end_second(last, last % 2)
        sum_fluxes(last)
        spots = lax.broadcasted_iota(jnp.int32, (source_column.shape[0], rows), 1)
        placing = jnp.where(source_column[...] == spots, 1.0, 0.0).astype(BF16)
        share = flux_count // comp_count
        for c in range(comp_count):
            for f in range(share):
                field = fluxes[pl.ds(c * share + f, rows, stride=flux_count), :].astype(BF16)
                packed[c, : placing.shape[0], f * cols : (f + 1) * cols] = dot_nn(
                    placing, field
                ).astype(BF16)
            packed[c, placing.shape[0] :, :] = labels[...]
        put(last - 1, (last - 1) % 2).wait()
        put(last, last % 2).wait()
        surface[...] = top[...].T

    @pl.when(ocean)
    def sea_side():
        fetch(0).wait()
        lanes = lax.broadcasted_iota(jnp.int32, (CHUNK, CHUNK * levels), 1) // levels
        lines = lax.broadcasted_iota(jnp.int32, (CHUNK, CHUNK * levels), 0)
        spreader = jnp.where(lanes == lines, 1.0, 0.0).astype(F32)

        def one_chunk(q, _):
            base = q * CHUNK

            @pl.when(q + 1 < chunks)
            def _():
                fetch(q + 1).wait()

            @pl.when(q + AHEAD < chunks)
            def _():
                fetch(q + AHEAD).start()

            side_cells(base, CHUNK)
            stage_rows(first, values, base + 2, CHUNK)
            mix_rows(first, CHUNK)
            slot = q % 2

            @pl.when(q >= 2)
            def _():
                put(q - 2, slot).wait()

            sea = dot_nn(mask[pl.ds(pl.multiple_of(base, CHUNK), CHUNK), :].T, spreader)
            for row in range(CHUNK):
                chosen = sea[:, row * levels : (row + 1) * levels] > 0.5
                before = values[base + row + 2, EDGE : EDGE + cols, :]
                staged[slot, row] = jnp.where(chosen, finish(first, row), before)
            put(q, slot).start()
            note_top(q, [staged[slot, row] for row in range(CHUNK)])
            return 0

        lax.fori_loop(0, chunks, one_chunk, 0)
        put(chunks - 2, (chunks - 2) % 2).wait()
        put(chunks - 1, (chunks - 1) % 2).wait()
        surface[...] = top[...].T
        packed[...] = jnp.zeros(packed.shape, BF16)
        table[...] = jnp.zeros(table.shape, F32)
        for line in range(LINES):
            for f in range(flux_count):
                spot = f * LINES + line
                table[spot : spot + 1, line * levels : (line + 1) * levels] = ocean_map[f : f + 1]
        high, low = split_two(table[...])
        depth = table.shape[0]
        wide[:depth] = high
        wide[depth : 2 * depth] = high
        wide[2 * depth :] = low


def advance(
    flags, source_column, labels, state, halos, mask, mix_atm, mix_ocn, flux_map_t, ocean_map,
    comp_count, left_at, right_at,
):
    rows, cols, levels = state.shape
    fluxes = flux_map_t.shape[0]
    vmem = pl.BlockSpec(memory_space=pltpu.VMEM)
    smem = pl.BlockSpec(memory_space=pltpu.SMEM)
    hbm = pl.BlockSpec(memory_space=pltpu.HBM)
    entry = jax.ShapeDtypeStruct(
        (comp_count, source_column.shape[0] + labels.shape[0], fluxes // comp_count * cols), BF16
    )
    cells = rows * cols
    return pl.pallas_call(
        functools.partial(advance_kernel, comp_count, left_at, right_at),
        out_shape=(
            jax.ShapeDtypeStruct(state.shape, F32),
            jax.ShapeDtypeStruct((rows, cols), F32),
            jax.ShapeDtypeStruct((rows, cols), BF16),
            entry,
            jax.ShapeDtypeStruct((3 * LINES * fluxes, LINES * levels), BF16),
        ),
        in_specs=[smem, vmem, vmem, hbm] + [vmem] * (len(halos) + 5),
        out_specs=(hbm, vmem, vmem, vmem, vmem),
        scratch_shapes=[
            pltpu.VMEM((rows + 4, cols + 2 * EDGE, levels), F32),
            pltpu.VMEM((rows + 2, cols + 2 * EDGE, levels), F32),
            pltpu.VMEM((2, rows, levels), F32),
            pltpu.VMEM((CHUNK, cols, levels), F32),
            pltpu.VMEM((CHUNK * cols, 2 * levels), BF16),
            pltpu.VMEM((CHUNK * cols, 2 * levels), F32),
            pltpu.VMEM((CHUNK, cols, levels), F32),
            pltpu.VMEM((CHUNK * cols, 2 * levels), BF16),
            pltpu.VMEM((CHUNK * cols, 2 * levels), F32),
            pltpu.VMEM((2 * levels, 2 * levels), BF16),
            pltpu.VMEM((2 * fluxes, 2 * levels), BF16),
            pltpu.VMEM((CHUNK * cols, 2 * levels), BF16),
            pltpu.VMEM((rows * fluxes, cols), F32),
            pltpu.VMEM((2, CHUNK, cols, levels), F32),
            pltpu.VMEM((cols, levels), F32),
            pltpu.VMEM((LINES * fluxes, LINES * levels), F32),
            pltpu.SemaphoreType.DMA((rows // CHUNK,)),
            pltpu.SemaphoreType.DMA((2,)),
        ],
        compiler_params=pltpu.CompilerParams(vmem_limit_bytes=48 * MIB),
        cost_estimate=pl.CostEstimate(
            flops=8 * cells * levels * levels, bytes_accessed=8 * cells * levels, transcendentals=0
        ),
        name="advance",
    )(flags, source_column, labels, state, *halos, mask, mix_atm, mix_ocn, flux_map_t, ocean_map)


BATCH = 8
LABEL_ROWS = 16


def regroup_kernel(slabs, *blocks):
    sources = slabs.shape[0] - 1
    capacity = (blocks[0].shape[0] - LABEL_ROWS) // sources
    size = len(blocks) * capacity
    heads = [slabs[c, size : size + LABEL_ROWS, :].astype(F32) for c in range(sources)]
    lines = [head[i : i + 1] for i in range(2) for head in heads]
    spare = jnp.zeros((LABEL_ROWS - len(lines), heads[0].shape[1]), F32)
    labels = jnp.concatenate(lines + [spare], axis=0).astype(BF16)
    for n, block in enumerate(blocks):
        for c in range(sources):
            block[c * capacity : (c + 1) * capacity, :] = slabs[
                c, n * capacity : (n + 1) * capacity, :
            ]
        block[sources * capacity :, :] = labels


def regroup(slabs, count):
    comps, rows, width = slabs.shape
    size = (rows - LABEL_ROWS) // count * (comps - 1) + LABEL_ROWS
    vmem = pl.BlockSpec(memory_space=pltpu.VMEM)
    return pl.pallas_call(
        regroup_kernel,
        out_shape=(jax.ShapeDtypeStruct((size, width), BF16),) * count,
        in_specs=[vmem],
        out_specs=(vmem,) * count,
        compiler_params=pltpu.CompilerParams(vmem_limit_bytes=16 * MIB),
        name="regroup",
    )(slabs)


def regrid_body(count, comp_count, flags, ocean_first, *refs):
    blocks = refs[:count]
    seas = refs[count : count + comp_count]
    weights, surface, mask, forcing, shared, hits, entries, chosen, binned = refs[count + comp_count :]
    sources = comp_count - 1
    rows, cols = mask.shape
    share = forcing.shape[0]
    weight_count = weights.shape[0]
    capacity = (blocks[0].shape[0] - LABEL_ROWS) // sources
    size = count * capacity
    total = sources * size
    width = blocks[0].shape[1]
    for c in range(sources):
        for n in range(count):
            start = c * size + n * capacity
            entries[start : start + capacity, :] = blocks[n][c * capacity : (c + 1) * capacity, :]
    lanes = lax.broadcasted_iota(jnp.int32, (LABEL_ROWS, width), 1) // capacity
    labels = jnp.zeros((LABEL_ROWS, width), F32)
    for n in range(count):
        labels = jnp.where(lanes == n, blocks[n][sources * capacity :, :].astype(F32), labels)
    labels = labels.astype(jnp.int32)
    weight_line = jnp.concatenate([labels[c : c + 1, :size] for c in range(sources)], axis=1)
    target_line = jnp.concatenate(
        [labels[sources + c : sources + c + 1, :size] for c in range(sources)], axis=1
    )
    spots = lax.broadcasted_iota(jnp.int32, (rows, total), 0)
    by_target = jnp.where(target_line == spots, 1.0, 0.0)
    own = by_target[:, :size]
    for c in range(1, sources):
        own = jnp.where(flags[3] == c, by_target[:, c * size : (c + 1) * size], own)
    hits[...] = own.T.astype(BF16)
    by_target = by_target.astype(BF16)
    numbers = lax.broadcasted_iota(jnp.int32, (weight_count, total), 0)
    by_weight = jnp.where(weight_line == numbers, 1.0, 0.0).astype(BF16)
    for g in range(weight_count // BATCH):
        for i in range(BATCH):
            w = g * BATCH + i
            chosen[i * rows : (i + 1) * rows, :] = by_target * by_weight[w : w + 1, :]
        binned[...] = dot_nn(chosen[...], entries[...])
        wide = weights[g * BATCH : (g + 1) * BATCH].reshape(BATCH * cols, cols)
        halves = [
            [
                split_two(binned[i * rows : (i + 1) * rows, f * cols : (f + 1) * cols])
                for i in range(BATCH)
            ]
            for f in range(share)
        ]
        stacked = jnp.concatenate(
            [
                jnp.concatenate([half[k] for half in halves[f]], axis=1)
                for k in range(2)
                for f in range(share)
            ],
            axis=0,
        )
        product = dot_nn(stacked, wide)
        for f in range(share):
            part = product[f * rows : (f + 1) * rows] + product[
                (share + f) * rows : (share + f + 1) * rows
            ]
            forcing[f] = part if g == 0 else forcing[f] + part
    change = ocean_first[flags[3] * share] * forcing[0]
    for f in range(1, share):
        change = change + ocean_first[flags[3] * share + f] * forcing[f]
    sea = jnp.where(flags[0] == 1, seas[sources][...].astype(F32), 0.0)
    for c in range(sources):
        sea = sea + jnp.where(flags[3] == c, seas[c][...].astype(F32), 0.0)
    base = jnp.where(flags[0] == 1, surface[...], 0.0)
    shared[...] = base + jnp.where(sea > 0.5, change, 0.0)


def regrid(flags, ocean_first, blocks, seas, weights, surface, mask):
    comp_count = len(seas)
    sources = comp_count - 1
    rows, cols = mask.shape
    count = len(blocks)
    height, width = blocks[0].shape
    size = (height - LABEL_ROWS) // sources * count
    total = size * sources
    share = width // cols
    weight_count = weights.shape[0]
    vmem = pl.BlockSpec(memory_space=pltpu.VMEM)
    smem = pl.BlockSpec(memory_space=pltpu.SMEM)
    return pl.pallas_call(
        functools.partial(regrid_body, count, comp_count),
        out_shape=(
            jax.ShapeDtypeStruct((share, rows, cols), F32),
            jax.ShapeDtypeStruct((rows, cols), F32),
            jax.ShapeDtypeStruct((size, rows), BF16),
        ),
        in_specs=[smem, smem] + [vmem] * (count + comp_count + 3),
        out_specs=(vmem, vmem, vmem),
        scratch_shapes=[
            pltpu.VMEM((total, width), BF16),
            pltpu.VMEM((BATCH * rows, total), BF16),
            pltpu.VMEM((BATCH * rows, width), F32),
        ],
        compiler_params=pltpu.CompilerParams(vmem_limit_bytes=32 * MIB),
        cost_estimate=pl.CostEstimate(
            flops=2 * weight_count * rows * width * (total + 2 * cols),
            bytes_accessed=2 * MIB,
            transcendentals=0,
        ),
        name="regrid",
    )(flags, ocean_first, *blocks, *seas, weights, surface, mask)


def pick_kernel(count, *refs):
    parts = refs[:count]
    hits, surface = refs[count : count + 2]
    picked = refs[count + 2 :]
    now = parts[0][...]
    for part in parts[1:]:
        now = now + part[...]
    surface[...] = now
    pair = jnp.concatenate(split_two(now), axis=0)
    size = picked[0].shape[0]
    for n in range(len(picked)):
        some = hits[n * size : (n + 1) * size, :]
        picked[n][...] = dot_nn(jnp.concatenate([some, some], axis=1), pair)


def pick(parts, hits, neighbours):
    rows, cols = parts[0].shape
    size = hits.shape[0] // neighbours
    vmem = pl.BlockSpec(memory_space=pltpu.VMEM)
    return pl.pallas_call(
        functools.partial(pick_kernel, len(parts)),
        out_shape=(jax.ShapeDtypeStruct((rows, cols), F32),)
        + (jax.ShapeDtypeStruct((size, cols), F32),) * neighbours,
        in_specs=[vmem] * (len(parts) + 1),
        out_specs=(vmem,) * (1 + neighbours),
        compiler_params=pltpu.CompilerParams(vmem_limit_bytes=16 * MIB),
        name="pick",
    )(*parts, hits)


def update_kernel(groups, flags, state, *refs):
    parts = refs[:groups]
    mask, wide, out, token, held, in_sems, out_sems = refs[groups:]
    rows, cols, levels = state.shape
    share = parts[0].shape[0]
    flux_count = groups * share
    chunks = rows // LINES
    token[...] = jnp.zeros(token.shape, F32)

    def fetch(q):
        return pltpu.make_async_copy(
            state.at[pl.ds(q * LINES, LINES)], held.at[pl.ds(q * LINES, LINES)], in_sems.at[q]
        )

    def put(q):
        return pltpu.make_async_copy(
            held.at[pl.ds(q * LINES, LINES)], out.at[pl.ds(q * LINES, LINES)], out_sems.at[q]
        )

    @pl.when(flags[0] == 1)
    def ocean():
        for q in range(chunks):
            fetch(q).start()
        def one(q, _):
            start = pl.multiple_of(q * LINES, LINES)
            sea = mask[pl.ds(start, LINES), :] > 0.5
            part = jnp.concatenate(
                [
                    jnp.where(sea, parts[f // share][f % share, pl.ds(start, LINES), :], 0.0)
                    for f in range(flux_count)
                ],
                axis=0,
            )
            rough = part.astype(BF16).astype(F32)
            turned = jnp.concatenate([rough, part - rough, rough], axis=0).T.astype(BF16)
            change = dot_nn(turned, wide[...])
            fetch(q).wait()
            for line in range(LINES):
                held[start + line] += change[:, line * levels : (line + 1) * levels]
            put(q).start()
            return 0

        lax.fori_loop(0, chunks, one, 0, unroll=2)
        for q in range(chunks):
            put(q).wait()


def update(flags, state, parts, mask, wide):
    rows, cols, levels = state.shape
    depth = wide.shape[0] // 3
    vmem = pl.BlockSpec(memory_space=pltpu.VMEM)
    smem = pl.BlockSpec(memory_space=pltpu.SMEM)
    hbm = pl.BlockSpec(memory_space=pltpu.HBM)
    return pl.pallas_call(
        functools.partial(update_kernel, len(parts)),
        out_shape=(
            jax.ShapeDtypeStruct(state.shape, F32),
            jax.ShapeDtypeStruct((EDGE, levels), F32),
        ),
        in_specs=[smem, hbm] + [vmem] * (len(parts) + 2),
        out_specs=(hbm, vmem),
        input_output_aliases={1: 0},
        scratch_shapes=[
            pltpu.VMEM(state.shape, F32),
            pltpu.SemaphoreType.DMA((rows // LINES,)),
            pltpu.SemaphoreType.DMA((rows // LINES,)),
        ],
        compiler_params=pltpu.CompilerParams(vmem_limit_bytes=24 * MIB),
        cost_estimate=pl.CostEstimate(
            flops=6 * rows * cols * depth * levels,
            bytes_accessed=8 * rows * cols * levels,
            transcendentals=0,
        ),
        name="update",
    )(flags, state, *parts, mask, wide)


def returned_kernel(groups, flags, *refs):
    picked = refs[:groups]
    weight_line, row_line, weights, mask, surface, new_surface, token, out, total = refs[groups:]
    rows, cols = mask.shape
    weight_count = weights.shape[0]

    @pl.when(flags[0] == 1)
    def ocean():
        out[...] = new_surface[...]

    @pl.when(flags[0] == 0)
    def atmosphere():
        values = jnp.concatenate([p[...] for p in picked], axis=0)
        turned = values.T
        pair = jnp.concatenate(split_two(turned), axis=0)
        total[...] = jnp.zeros(turned.shape, F32)

        def one(i, _):
            block = weights[pl.ds(4 * i, 4)].reshape(4 * cols, cols)
            images = dot_nn(jnp.concatenate([block, block], axis=1), pair)
            some = total[...]
            for j in range(4):
                chosen = weight_line[...] == 4 * i + j
                some = some + jnp.where(chosen, images[j * cols : (j + 1) * cols, :], 0.0)
            total[...] = some
            return 0

        lax.fori_loop(0, weight_count // 4, one, 0, unroll=2)
        spots = lax.broadcasted_iota(jnp.int32, (rows, values.shape[0]), 0)
        chosen = jnp.where(jnp.broadcast_to(row_line[...], spots.shape) == spots, 1.0, 0.0).astype(BF16)
        high, low = split_two(total[...])
        back = dot_nt(chosen, high) + dot_nt(chosen, low)
        out[...] = jnp.where(mask[...] > 0.5, back, surface[...])


def returned(flags, picked, weight_line, row_line, weights, mask, surface, new_surface, token):
    rows, cols = mask.shape
    entry_total = weight_line.shape[1]
    vmem = pl.BlockSpec(memory_space=pltpu.VMEM)
    smem = pl.BlockSpec(memory_space=pltpu.SMEM)
    return pl.pallas_call(
        functools.partial(returned_kernel, len(picked)),
        out_shape=jax.ShapeDtypeStruct((rows, cols), F32),
        in_specs=[smem] + [vmem] * (len(picked) + 7),
        out_specs=vmem,
        scratch_shapes=[pltpu.VMEM((cols, entry_total), F32)],
        compiler_params=pltpu.CompilerParams(vmem_limit_bytes=16 * MIB),
        name="returned",
    )(flags, *picked, weight_line, row_line, weights, mask, surface, new_surface, token)


def local(
    state, land_mask, intersection_list, mix_atm, mix_ocn, flux_map, ocean_map, regrid_weights
):
    rows, cols, levels = state.shape
    intersections = intersection_list.shape[2]
    comp_count = lax.axis_size("comp")
    lat_count = lax.axis_size("lat")
    lon_count = lax.axis_size("lon")
    tile_count = lat_count * lon_count
    reach = min(4, lon_count)
    neighbours = 2 * reach
    entry_total = intersections * rows
    capacity = entry_total // neighbours
    comp_index = lax.axis_index("comp")
    lat_index = lax.axis_index("lat")
    tile_index = lat_index * lon_count + lax.axis_index("lon")
    bands = comp_count * lat_count
    ocean_band = (comp_count - 1) * lat_count
    ocean_comp = comp_count - 1
    band = comp_index * lat_count + lat_index
    is_ocean = comp_index == ocean_comp
    upper_valid = (band > 0) & (band != ocean_band)
    lower_valid = (band < bands - 1) & (band != ocean_band - 1)
    flags = jnp.stack([is_ocean, upper_valid, lower_valid, comp_index]).astype(jnp.int32)
    mask = (land_mask == 1).astype(F32)

    def band_shift(value, by, lon_by):
        pairs = []
        for b in range(bands):
            target = b + by
            if 0 <= target < bands and (b >= ocean_band) == (target >= ocean_band):
                for lon in range(lon_count):
                    pairs.append(
                        (b * lon_count + lon, target * lon_count + (lon + lon_by) % lon_count)
                    )
        return lax.ppermute(value, AXES, pairs)

    first_rows, last_rows, sides = take_edges(state)
    up_rows = band_shift(last_rows, 1, 0)
    low_rows = band_shift(first_rows, -1, 0)
    framed = frame_sides(sides, up_rows, low_rows)
    if lon_count == 2:
        left_cols = right_cols = band_shift(framed, 0, 1)
        left_at, right_at = 2, 0
    else:
        left_cols = band_shift(framed[2:], 0, 1)
        right_cols = band_shift(framed[:2], 0, -1)
        left_at, right_at = 0, 0

    entry_list = intersection_list.reshape(entry_total, 3)
    owners = entry_list[:, 0]
    labels = entry_list[:, 2] * rows + entry_list[:, 1]
    offsets = [
        (n // reach * lon_count + n % reach - (reach - 1) // 2) % tile_count
        for n in range(neighbours)
    ]
    distance = (owners - tile_index + tile_count) % tile_count
    hits = distance[:, None] == jnp.array(offsets, jnp.int32)[None, :]
    neighbour_ids = jnp.sum(
        jnp.where(hits, jnp.arange(neighbours, dtype=jnp.int32)[None, :], 0), axis=1
    )
    positions = jnp.arange(entry_total, dtype=jnp.int32)
    earlier = (neighbour_ids[None, :] == neighbour_ids[:, None]) & (
        positions[None, :] < positions[:, None]
    )
    slots = neighbour_ids * capacity + jnp.sum(earlier.astype(jnp.int32), axis=1)
    placing = positions[:, None] == slots[None, :]
    sources = jnp.sum(jnp.where(placing, (positions // intersections)[None, :], 0), axis=1)
    packed_labels = jnp.sum(jnp.where(placing, labels[None, :], 0), axis=1)

    def over_comp(value):
        return lax.all_to_all(value, "comp", split_axis=0, concat_axis=0, tiled=True)

    def shifted_comp(value, shift):
        pairs = [
            (c * tile_count + t, (c + shift) % comp_count * tile_count + t)
            for c in range(comp_count)
            for t in range(tile_count)
        ]
        return lax.ppermute(value, AXES, pairs)

    def over_tiles(value, offset, comps):
        if offset % tile_count == 0:
            return value
        pairs = [
            (c * tile_count + t, c * tile_count + (t + offset) % tile_count)
            for c in range(comps)
            for t in range(tile_count)
        ]
        return lax.ppermute(value, AXES, pairs)

    def from_ocean(value, comp):
        pairs = [
            (ocean_comp * tile_count + t, comp * tile_count + t) for t in range(tile_count)
        ]
        return lax.ppermute(value, AXES, pairs)

    def to_ocean(value, comp):
        pairs = [
            (comp * tile_count + t, ocean_comp * tile_count + t) for t in range(tile_count)
        ]
        return lax.ppermute(value, AXES, pairs)

    label_lines = jnp.stack([packed_labels // rows, packed_labels % rows]).astype(BF16)
    label_lines = jnp.pad(label_lines, ((0, LABEL_ROWS - 2), (0, 0)))

    halos = (up_rows, low_rows, left_cols, right_cols, sides)
    moved = advance(
        flags, sources[:, None], label_lines, state, halos, mask, mix_atm, mix_ocn, flux_map.T,
        ocean_map, comp_count, left_at, right_at,
    )
    moved, surface, sea_copy, packed, wide = moved
    slabs = over_comp(packed)
    seas = [from_ocean(sea_copy, c) for c in range(ocean_comp)] + [sea_copy]
    blocks = regroup(slabs, neighbours)
    blocks = [over_tiles(blocks[n], offsets[n], comp_count) for n in range(neighbours)]
    forcing, shared, hits = regrid(
        flags, ocean_map[:, 0], blocks, seas, regrid_weights, surface, mask
    )
    parts = [shared] + [shifted_comp(shared, s) for s in range(1, comp_count)]
    parts[1], forcing = lax.optimization_barrier((parts[1], forcing))
    picks = pick(parts, hits, neighbours)
    new_surface, picked = picks[0], picks[1:]
    arrived = [over_tiles(picked[n], -offsets[n], ocean_comp) for n in range(neighbours)]
    fields = [to_ocean(forcing, c) for c in range(ocean_comp)] + [forcing]
    final_state, token = update(flags, moved, fields, mask, wide)
    weight_line = (packed_labels // rows)[None, :]
    surface_out = returned(
        flags, arrived, weight_line, sources[None, :], regrid_weights, mask, surface, new_surface,
        token,
    )
    return (final_state, surface_out)


def solution(mesh):
    placed = (
        P(("comp", "lat"), "lon", None),
        P(("comp", "lat"), "lon"),
        P(("comp", "lat"), "lon", None, None),
        P(),
        P(),
        P(),
        P(),
        P(),
    )
    return jax.shard_map(
        local,
        mesh=mesh,
        in_specs=placed,
        out_specs=(P(("comp", "lat"), "lon", None), P(("comp", "lat"), "lon")),
        check_vma=False,
    )
```

```python
import functools

import jax
import jax.numpy as jnp
from jax import lax
from jax.experimental import pallas as pl
from jax.experimental.pallas import tpu as pltpu
from jax.sharding import PartitionSpec as P

SMOOTHING = 0.2
PHYSICS = 0.5
MIB = 1024 * 1024
F32 = jnp.float32
BF16 = jnp.bfloat16
EDGE = 8
AHEAD = 4
CHUNK = 8
AXES = ("comp", "lat", "lon")


def split_two(x):
    high = x.astype(BF16)
    low = (x - high.astype(F32)).astype(BF16)
    return high, low


def side_by_side(x):
    return jnp.concatenate(split_two(x), axis=1)


def dot_nt(a, b):
    return lax.dot_general(a, b, (((1,), (1,)), ((), ())), preferred_element_type=F32)


def dot_nn(a, b):
    return jnp.dot(a, b, preferred_element_type=F32)


def edges_kernel(state, first_rows, last_rows, sides, top, bottom, left, right, sems):
    rows, cols, _ = state.shape
    copies = [
        pltpu.make_async_copy(state.at[pl.ds(0, 2)], top, sems.at[0]),
        pltpu.make_async_copy(state.at[pl.ds(rows - 2, 2)], bottom, sems.at[1]),
        pltpu.make_async_copy(state.at[:, pl.ds(0, EDGE)], left, sems.at[2]),
        pltpu.make_async_copy(state.at[:, pl.ds(cols - EDGE, EDGE)], right, sems.at[3]),
    ]
    for copy in copies:
        copy.start()
    for copy in copies:
        copy.wait()
    first_rows[...] = top[...].astype(BF16)
    last_rows[...] = bottom[...].astype(BF16)
    for i in range(2):
        sides[i] = left[:, i, :]
        sides[2 + i] = right[:, EDGE - 2 + i, :]


def take_edges(state):
    rows, cols, levels = state.shape
    slab = jax.ShapeDtypeStruct((2, cols, levels), BF16)
    side = jax.ShapeDtypeStruct((4, rows, levels), F32)
    vmem = pl.BlockSpec(memory_space=pltpu.VMEM)
    return pl.pallas_call(
        edges_kernel,
        out_shape=(slab, slab, side),
        in_specs=[pl.BlockSpec(memory_space=pltpu.HBM)],
        out_specs=(vmem,) * 3,
        scratch_shapes=[
            pltpu.VMEM((2, cols, levels), F32),
            pltpu.VMEM((2, cols, levels), F32),
            pltpu.VMEM((rows, EDGE, levels), F32),
            pltpu.VMEM((rows, EDGE, levels), F32),
            pltpu.SemaphoreType.DMA((4,)),
        ],
        compiler_params=pltpu.CompilerParams(vmem_limit_bytes=50 * MIB),
        name="edges",
    )(state)


def frame_kernel(sides, up_rows, low_rows, framed):
    _, rows, levels = sides.shape
    cols = up_rows.shape[1]
    framed[...] = jnp.zeros(framed.shape, F32)
    above = up_rows[1].astype(F32)
    below = low_rows[0].astype(F32)
    for i, col in enumerate((0, 1, cols - 2, cols - 1)):
        framed[i, EDGE : EDGE + rows, :] = sides[i]
        framed[i, EDGE - 1 : EDGE, :] = above[col : col + 1, :]
        framed[i, EDGE + rows : EDGE + rows + 1, :] = below[col : col + 1, :]


def frame_sides(sides, up_rows, low_rows):
    count, rows, levels = sides.shape
    vmem = pl.BlockSpec(memory_space=pltpu.VMEM)
    return pl.pallas_call(
        frame_kernel,
        out_shape=jax.ShapeDtypeStruct((count, rows + 2 * EDGE, levels), F32),
        in_specs=[vmem] * 3,
        out_specs=vmem,
        compiler_params=pltpu.CompilerParams(vmem_limit_bytes=16 * MIB),
        name="frame",
    )(sides, up_rows, low_rows)


def advance_kernel(comp_count, left_at, right_at, *refs):
    (flags, labels, state, up_rows, low_rows, left_in, right_in, own_sides) = refs[:8]
    (mask, mix_atm, mix_ocn, flux_map) = refs[8:12]
    out, surface, sea_copy, packed = refs[12:16]
    (values, moved, halo_moved, smooth, pairs, mixed, later_smooth, later_pairs, later_mixed) = refs[16:25]
    (weights, flux_weights, flux_pairs, fluxes, staged, top, in_sems, out_sems) = refs[25:]
    left_cols = left_in.at[left_at : left_at + 2]
    right_cols = right_in.at[right_at : right_at + 2]
    first = (smooth, pairs, mixed)
    second = (later_smooth, later_pairs, later_mixed)
    rows, cols, levels = state.shape
    chunks = rows // CHUNK
    inner = pl.ds(EDGE, cols)
    flux_count = flux_map.shape[0]

    def fetch(q):
        return pltpu.make_async_copy(
            state.at[pl.ds(q * CHUNK, CHUNK)],
            values.at[pl.ds(q * CHUNK + 2, CHUNK), inner],
            in_sems.at[q],
        )

    def put(q, slot):
        return pltpu.make_async_copy(
            staged.at[slot], out.at[pl.ds(q * CHUNK, CHUNK)], out_sems.at[slot]
        )

    def begin(q, _):
        fetch(q).start()
        return 0

    lax.fori_loop(0, AHEAD, begin, 0)
    ocean = flags[0] == 1
    mix = jnp.where(ocean, mix_ocn[...], mix_atm[...])
    mix_high, mix_low = split_two(mix)
    weights[:levels, :levels] = mix_high
    weights[levels:, :levels] = mix_high
    weights[:levels, levels:] = mix_low
    weights[levels:, levels:] = mix_low
    sea_copy[...] = mask[...].astype(BF16)
    map_high, map_low = split_two(flux_map[...])
    flux_weights[...] = jnp.concatenate(
        [
            jnp.concatenate([map_high.astype(F32), map_high.astype(F32)], axis=1),
            jnp.concatenate([map_low.astype(F32), map_low.astype(F32)], axis=1),
        ],
        axis=0,
    ).astype(BF16)
    values[0:2, EDGE : EDGE + cols, :] = up_rows[...].astype(F32)
    values[rows + 2 : rows + 4, EDGE : EDGE + cols, :] = low_rows[...].astype(F32)
    for r, i in ((1, EDGE - 1), (rows + 2, EDGE + rows)):
        values[r, EDGE - 1 : EDGE, :] = left_cols[1, i : i + 1, :]
        values[r, EDGE + cols : EDGE + cols + 1, :] = right_cols[0, i : i + 1, :]

    def side_cells(start, count):
        for row in range(count):
            values[start + row + 2, EDGE - 1 : EDGE, :] = left_cols[1, pl.ds(start + row + EDGE, 1), :]
            values[start + row + 2, EDGE + cols : EDGE + cols + 1, :] = right_cols[
                0, pl.ds(start + row + EDGE, 1), :
            ]

    def moved_sides(start, count):
        for row in range(count):
            moved[start + row + 1, EDGE - 1 : EDGE, :] = halo_moved[0, pl.ds(start + row, 1), :]
            moved[start + row + 1, EDGE + cols : EDGE + cols + 1, :] = halo_moved[
                1, pl.ds(start + row, 1), :
            ]

    def stage(refs, row, total):
        line = SMOOTHING * total
        refs[0][row] = line
        refs[1][row * cols : (row + 1) * cols, :] = side_by_side(line)

    def stage_rows(refs, ref, start, count):
        for row in range(count):
            i = start + row
            here = ref[i, EDGE : EDGE + cols, :] + (
                ref[i - 1, EDGE : EDGE + cols, :] + ref[i + 1, EDGE : EDGE + cols, :]
            )
            near = ref[i, EDGE - 1 : EDGE - 1 + cols, :] + ref[i, EDGE + 1 : EDGE + 1 + cols, :]
            stage(refs, row, here + near)

    def note_top(q, lines):
        lanes = lax.broadcasted_iota(jnp.int32, (cols, levels), 1)
        kept = lines[0]
        for row in range(1, CHUNK):
            kept = jnp.where(lanes == row, pltpu.roll(lines[row], row, 1), kept)
        turned = pltpu.roll(kept, q * CHUNK, 1)
        top[...] = jnp.where(lanes // CHUNK == q, turned, top[...])

    def mix_rows(refs, count):
        refs[2][: count * cols, :] = dot_nn(refs[1][: count * cols, :], weights[...])

    def finish(refs, row):
        part = refs[2][row * cols : (row + 1) * cols, :]
        return refs[0][row] + PHYSICS * jnp.tanh(part[:, :levels] + part[:, levels:])

    @pl.when(jnp.logical_not(ocean))
    def atmosphere():
        nearest = (left_cols.at[1], right_cols.at[0])
        beyond = (left_cols.at[0], right_cols.at[1])
        within = (own_sides.at[0], own_sides.at[3])
        for s in range(2):
            total = (
                nearest[s][EDGE : EDGE + rows, :]
                + nearest[s][EDGE - 1 : EDGE - 1 + rows, :]
                + nearest[s][EDGE + 1 : EDGE + 1 + rows, :]
            )
            stage(first, s, total + (beyond[s][EDGE : EDGE + rows, :] + within[s][...]))
        mix_rows(first, 2)
        for s in range(2):
            halo_moved[s] = finish(first, s)

        side_cells(0, 1)
        fetch(0).wait()
        fetch(1).wait()
        stage_rows(second, values, 1, 2)
        mix_rows(second, 2)
        for row in range(2):
            moved[row, EDGE : EDGE + cols, :] = finish(second, row)

        @pl.when(flags[1] == 0)
        def _():
            moved[0, EDGE : EDGE + cols, :] = jnp.zeros((cols, levels), F32)

        def begin_first(q):
            side_cells(jnp.minimum(q * CHUNK + 1, rows - CHUNK), CHUNK)
            stage_rows(first, values, q * CHUNK + 3, CHUNK)
            mix_rows(first, CHUNK)

        def end_first(q):
            for row in range(CHUNK):
                moved[q * CHUNK + row + 2, EDGE : EDGE + cols, :] = finish(first, row)

        def begin_second(q):
            moved_sides(q * CHUNK, CHUNK)
            stage_rows(second, moved, q * CHUNK + 1, CHUNK)

        def end_second(q, slot):
            for row in range(CHUNK):
                line = finish(second, row)
                staged[slot, row] = line
                both = line + moved[q * CHUNK + row + 1, EDGE : EDGE + cols, :]
                flux_pairs[row * cols : (row + 1) * cols, :] = side_by_side(both)
            put(q, slot).start()
            note_top(q, [staged[slot, row] for row in range(CHUNK)])

        def sum_fluxes(q):
            flux = dot_nt(flux_weights[...], flux_pairs[...])
            flux = flux[:flux_count] + flux[flux_count:]
            for row in range(CHUNK):
                r = q * CHUNK + row
                block = PHYSICS * flux[:, row * cols : (row + 1) * cols]
                sea = jnp.broadcast_to(mask[pl.ds(r, 1), :], block.shape)
                block = jnp.where(sea > 0.5, block, 0.0)
                fluxes[pl.ds(pl.multiple_of(r * flux_count, flux_count), flux_count), :] = block

        fetch(AHEAD).start()
        flux_pairs[...] = jnp.zeros(flux_pairs.shape, BF16)
        begin_first(0)
        end_first(0)

        def one_chunk(q, _):
            @pl.when(q + 1 < chunks)
            def _():
                fetch(q + 1).wait()

            @pl.when(q + AHEAD < chunks)
            def _():
                fetch(q + AHEAD).start()

            slot = (q - 1) % 2

            @pl.when(q >= 3)
            def _():
                put(q - 3, slot).wait()

            sum_fluxes(jnp.maximum(q - 2, 0))
            begin_first(q)
            begin_second(q - 1)
            mix_rows(second, CHUNK)
            end_first(q)
            end_second(q - 1, slot)
            return 0

        lax.fori_loop(1, chunks, one_chunk, 0)

        @pl.when(flags[2] == 0)
        def _():
            moved[rows + 1, EDGE : EDGE + cols, :] = jnp.zeros((cols, levels), F32)

        last = chunks - 1
        put(last - 2, last % 2).wait()
        sum_fluxes(last - 1)
        begin_second(last)
        mix_rows(second, CHUNK)
        end_second(last, last % 2)
        sum_fluxes(last)
        share = flux_count // comp_count
        for c in range(comp_count):
            for f in range(share):
                field = fluxes[pl.ds(c * share + f, rows, stride=flux_count), :]
                packed[c, :rows, f * cols : (f + 1) * cols] = field.astype(BF16)
            packed[c, rows:, :] = labels[...]
        put(last - 1, (last - 1) % 2).wait()
        put(last, last % 2).wait()
        surface[...] = top[...].T

    @pl.when(ocean)
    def sea_side():
        fetch(0).wait()
        lanes = lax.broadcasted_iota(jnp.int32, (CHUNK, CHUNK * levels), 1) // levels
        lines = lax.broadcasted_iota(jnp.int32, (CHUNK, CHUNK * levels), 0)
        spreader = jnp.where(lanes == lines, 1.0, 0.0).astype(F32)

        def one_chunk(q, _):
            base = q * CHUNK

            @pl.when(q + 1 < chunks)
            def _():
                fetch(q + 1).wait()

            @pl.when(q + AHEAD < chunks)
            def _():
                fetch(q + AHEAD).start()

            side_cells(base, CHUNK)
            stage_rows(first, values, base + 2, CHUNK)
            mix_rows(first, CHUNK)
            slot = q % 2

            @pl.when(q >= 2)
            def _():
                put(q - 2, slot).wait()

            sea = dot_nn(mask[pl.ds(pl.multiple_of(base, CHUNK), CHUNK), :].T, spreader)
            for row in range(CHUNK):
                chosen = sea[:, row * levels : (row + 1) * levels] > 0.5
                before = values[base + row + 2, EDGE : EDGE + cols, :]
                staged[slot, row] = jnp.where(chosen, finish(first, row), before)
            put(q, slot).start()
            note_top(q, [staged[slot, row] for row in range(CHUNK)])
            return 0

        lax.fori_loop(0, chunks, one_chunk, 0)
        put(chunks - 2, (chunks - 2) % 2).wait()
        put(chunks - 1, (chunks - 1) % 2).wait()
        surface[...] = top[...].T
        packed[...] = jnp.zeros(packed.shape, BF16)


def advance(
    flags, labels, state, halos, mask, mix_atm, mix_ocn, flux_map_t, comp_count, left_at, right_at
):
    rows, cols, levels = state.shape
    fluxes = flux_map_t.shape[0]
    vmem = pl.BlockSpec(memory_space=pltpu.VMEM)
    smem = pl.BlockSpec(memory_space=pltpu.SMEM)
    hbm = pl.BlockSpec(memory_space=pltpu.HBM)
    entry = jax.ShapeDtypeStruct(
        (comp_count, rows + labels.shape[0], fluxes // comp_count * cols), BF16
    )
    cells = rows * cols
    return pl.pallas_call(
        functools.partial(advance_kernel, comp_count, left_at, right_at),
        out_shape=(
            jax.ShapeDtypeStruct(state.shape, F32),
            jax.ShapeDtypeStruct((rows, cols), F32),
            jax.ShapeDtypeStruct((rows, cols), BF16),
            entry,
        ),
        in_specs=[smem, vmem, hbm] + [vmem] * (len(halos) + 4),
        out_specs=(hbm, vmem, vmem, vmem),
        scratch_shapes=[
            pltpu.VMEM((rows + 4, cols + 2 * EDGE, levels), F32),
            pltpu.VMEM((rows + 2, cols + 2 * EDGE, levels), F32),
            pltpu.VMEM((2, rows, levels), F32),
            pltpu.VMEM((CHUNK, cols, levels), F32),
            pltpu.VMEM((CHUNK * cols, 2 * levels), BF16),
            pltpu.VMEM((CHUNK * cols, 2 * levels), F32),
            pltpu.VMEM((CHUNK, cols, levels), F32),
            pltpu.VMEM((CHUNK * cols, 2 * levels), BF16),
            pltpu.VMEM((CHUNK * cols, 2 * levels), F32),
            pltpu.VMEM((2 * levels, 2 * levels), BF16),
            pltpu.VMEM((2 * fluxes, 2 * levels), BF16),
            pltpu.VMEM((CHUNK * cols, 2 * levels), BF16),
            pltpu.VMEM((rows * fluxes, cols), F32),
            pltpu.VMEM((2, CHUNK, cols, levels), F32),
            pltpu.VMEM((cols, levels), F32),
            pltpu.SemaphoreType.DMA((rows // CHUNK,)),
            pltpu.SemaphoreType.DMA((2,)),
        ],
        compiler_params=pltpu.CompilerParams(vmem_limit_bytes=48 * MIB),
        cost_estimate=pl.CostEstimate(
            flops=8 * cells * levels * levels, bytes_accessed=8 * cells * levels, transcendentals=0
        ),
        name="advance",
    )(flags, labels, state, *halos, mask, mix_atm, mix_ocn, flux_map_t)


BATCH = 8
LABEL_ROWS = 16


def regroup_kernel(slabs, *blocks):
    sources = slabs.shape[0] - 1
    capacity = (blocks[0].shape[0] - LABEL_ROWS) // sources
    rows = slabs.shape[1] - LABEL_ROWS
    size = len(blocks) * capacity
    heads = [slabs[c, rows:, :].astype(F32) for c in range(sources)]
    lines = [head[i : i + 1] for i in range(2) for head in heads]
    spare = jnp.zeros((LABEL_ROWS - len(lines), heads[0].shape[1]), F32)
    labels = jnp.concatenate(lines + [spare], axis=0).astype(BF16)
    spots = lax.broadcasted_iota(jnp.int32, (rows, size), 0).astype(F32)
    for c in range(sources):
        placing = jnp.where(heads[c][2:3, :size] == spots, 1.0, 0.0).T.astype(BF16)
        packed = dot_nn(placing, slabs[c, :rows, :]).astype(BF16)
        for n, block in enumerate(blocks):
            block[c * capacity : (c + 1) * capacity, :] = packed[n * capacity : (n + 1) * capacity, :]
    for block in blocks:
        block[sources * capacity :, :] = labels


def regroup(slabs, count, entry_total):
    comps, rows, width = slabs.shape
    size = entry_total // count * (comps - 1) + LABEL_ROWS
    vmem = pl.BlockSpec(memory_space=pltpu.VMEM)
    return pl.pallas_call(
        regroup_kernel,
        out_shape=(jax.ShapeDtypeStruct((size, width), BF16),) * count,
        in_specs=[vmem],
        out_specs=(vmem,) * count,
        compiler_params=pltpu.CompilerParams(vmem_limit_bytes=16 * MIB),
        name="regroup",
    )(slabs)


def regrid_body(count, comp_count, flags, ocean_first, *refs):
    blocks = refs[:count]
    seas = refs[count : count + comp_count]
    weights, surface, mask, forcing, shared, hits, entries, chosen, binned = refs[count + comp_count :]
    sources = comp_count - 1
    rows, cols = mask.shape
    share = forcing.shape[0]
    weight_count = weights.shape[0]
    capacity = (blocks[0].shape[0] - LABEL_ROWS) // sources
    size = count * capacity
    total = sources * size
    width = blocks[0].shape[1]
    for c in range(sources):
        for n in range(count):
            start = c * size + n * capacity
            entries[start : start + capacity, :] = blocks[n][c * capacity : (c + 1) * capacity, :]
    lanes = lax.broadcasted_iota(jnp.int32, (LABEL_ROWS, width), 1) // capacity
    labels = jnp.zeros((LABEL_ROWS, width), F32)
    for n in range(count):
        labels = jnp.where(lanes == n, blocks[n][sources * capacity :, :].astype(F32), labels)
    labels = labels.astype(jnp.int32)
    weight_line = jnp.concatenate([labels[c : c + 1, :size] for c in range(sources)], axis=1)
    target_line = jnp.concatenate(
        [labels[sources + c : sources + c + 1, :size] for c in range(sources)], axis=1
    )
    spots = lax.broadcasted_iota(jnp.int32, (rows, total), 0)
    by_target = jnp.where(target_line == spots, 1.0, 0.0)
    own = by_target[:, :size]
    for c in range(1, sources):
        own = jnp.where(flags[3] == c, by_target[:, c * size : (c + 1) * size], own)
    hits[...] = own.T.astype(BF16)
    by_target = by_target.astype(BF16)
    numbers = lax.broadcasted_iota(jnp.int32, (weight_count, total), 0)
    by_weight = jnp.where(weight_line == numbers, 1.0, 0.0).astype(BF16)
    for g in range(weight_count // BATCH):
        for i in range(BATCH):
            w = g * BATCH + i
            chosen[i * rows : (i + 1) * rows, :] = by_target * by_weight[w : w + 1, :]
        binned[...] = dot_nn(chosen[...], entries[...])
        wide = weights[g * BATCH : (g + 1) * BATCH].reshape(BATCH * cols, cols)
        halves = [
            [
                split_two(binned[i * rows : (i + 1) * rows, f * cols : (f + 1) * cols])
                for i in range(BATCH)
            ]
            for f in range(share)
        ]
        stacked = jnp.concatenate(
            [
                jnp.concatenate([half[k] for half in halves[f]], axis=1)
                for k in range(2)
                for f in range(share)
            ],
            axis=0,
        )
        product = dot_nn(stacked, wide)
        for f in range(share):
            part = product[f * rows : (f + 1) * rows] + product[
                (share + f) * rows : (share + f + 1) * rows
            ]
            forcing[f] = part if g == 0 else forcing[f] + part
    change = ocean_first[flags[3] * share] * forcing[0]
    for f in range(1, share):
        change = change + ocean_first[flags[3] * share + f] * forcing[f]
    sea = jnp.where(flags[0] == 1, seas[sources][...].astype(F32), 0.0)
    for c in range(sources):
        sea = sea + jnp.where(flags[3] == c, seas[c][...].astype(F32), 0.0)
    base = jnp.where(flags[0] == 1, surface[...], 0.0)
    shared[...] = base + jnp.where(sea > 0.5, change, 0.0)


def regrid(flags, ocean_first, blocks, seas, weights, surface, mask):
    comp_count = len(seas)
    sources = comp_count - 1
    rows, cols = mask.shape
    count = len(blocks)
    height, width = blocks[0].shape
    size = (height - LABEL_ROWS) // sources * count
    total = size * sources
    share = width // cols
    weight_count = weights.shape[0]
    vmem = pl.BlockSpec(memory_space=pltpu.VMEM)
    smem = pl.BlockSpec(memory_space=pltpu.SMEM)
    return pl.pallas_call(
        functools.partial(regrid_body, count, comp_count),
        out_shape=(
            jax.ShapeDtypeStruct((share, rows, cols), F32),
            jax.ShapeDtypeStruct((rows, cols), F32),
            jax.ShapeDtypeStruct((size, rows), BF16),
        ),
        in_specs=[smem, smem] + [vmem] * (count + comp_count + 3),
        out_specs=(vmem, vmem, vmem),
        scratch_shapes=[
            pltpu.VMEM((total, width), BF16),
            pltpu.VMEM((BATCH * rows, total), BF16),
            pltpu.VMEM((BATCH * rows, width), F32),
        ],
        compiler_params=pltpu.CompilerParams(vmem_limit_bytes=32 * MIB),
        cost_estimate=pl.CostEstimate(
            flops=2 * weight_count * rows * width * (total + 2 * cols),
            bytes_accessed=2 * MIB,
            transcendentals=0,
        ),
        name="regrid",
    )(flags, ocean_first, *blocks, *seas, weights, surface, mask)


def pick_kernel(count, *refs):
    parts = refs[:count]
    hits, surface = refs[count : count + 2]
    picked = refs[count + 2 :]
    now = parts[0][...]
    for part in parts[1:]:
        now = now + part[...]
    surface[...] = now
    pair = jnp.concatenate(split_two(now), axis=0)
    size = picked[0].shape[0]
    for n in range(len(picked)):
        some = hits[n * size : (n + 1) * size, :]
        picked[n][...] = dot_nn(jnp.concatenate([some, some], axis=1), pair)


def pick(parts, hits, neighbours):
    rows, cols = parts[0].shape
    size = hits.shape[0] // neighbours
    vmem = pl.BlockSpec(memory_space=pltpu.VMEM)
    return pl.pallas_call(
        functools.partial(pick_kernel, len(parts)),
        out_shape=(jax.ShapeDtypeStruct((rows, cols), F32),)
        + (jax.ShapeDtypeStruct((size, cols), F32),) * neighbours,
        in_specs=[vmem] * (len(parts) + 1),
        out_specs=(vmem,) * (1 + neighbours),
        compiler_params=pltpu.CompilerParams(vmem_limit_bytes=16 * MIB),
        name="pick",
    )(*parts, hits)


LINES = 8


def update_kernel(groups, flags, state, *refs):
    parts = refs[:groups]
    mask, ocean_map, out, token, held, table, wide, in_sems, out_sems = refs[groups:]
    rows, cols, levels = state.shape
    share = parts[0].shape[0]
    flux_count = groups * share
    chunks = rows // LINES
    depth = LINES * flux_count
    token[...] = jnp.zeros(token.shape, F32)

    def fetch(q):
        return pltpu.make_async_copy(
            state.at[pl.ds(q * LINES, LINES)], held.at[pl.ds(q * LINES, LINES)], in_sems.at[q]
        )

    def put(q):
        return pltpu.make_async_copy(
            held.at[pl.ds(q * LINES, LINES)], out.at[pl.ds(q * LINES, LINES)], out_sems.at[q]
        )

    @pl.when(flags[0] == 1)
    def ocean():
        for q in range(chunks):
            fetch(q).start()
        table[...] = jnp.zeros(table.shape, F32)
        for line in range(LINES):
            for f in range(flux_count):
                spot = f * LINES + line
                table[spot : spot + 1, line * levels : (line + 1) * levels] = ocean_map[f : f + 1]
        high, low = split_two(table[...])
        wide[:depth] = high
        wide[depth : 2 * depth] = high
        wide[2 * depth :] = low

        def one(q, _):
            start = pl.multiple_of(q * LINES, LINES)
            sea = mask[pl.ds(start, LINES), :] > 0.5
            part = jnp.concatenate(
                [
                    jnp.where(sea, parts[f // share][f % share, pl.ds(start, LINES), :], 0.0)
                    for f in range(flux_count)
                ],
                axis=0,
            )
            rough = part.astype(BF16).astype(F32)
            turned = jnp.concatenate([rough, part - rough, rough], axis=0).T.astype(BF16)
            change = dot_nn(turned, wide[...])
            fetch(q).wait()
            for line in range(LINES):
                held[start + line] += change[:, line * levels : (line + 1) * levels]
            put(q).start()
            return 0

        lax.fori_loop(0, chunks, one, 0, unroll=2)
        for q in range(chunks):
            put(q).wait()


def update(flags, state, parts, mask, ocean_map):
    rows, cols, levels = state.shape
    depth = LINES * ocean_map.shape[0]
    vmem = pl.BlockSpec(memory_space=pltpu.VMEM)
    smem = pl.BlockSpec(memory_space=pltpu.SMEM)
    hbm = pl.BlockSpec(memory_space=pltpu.HBM)
    return pl.pallas_call(
        functools.partial(update_kernel, len(parts)),
        out_shape=(
            jax.ShapeDtypeStruct(state.shape, F32),
            jax.ShapeDtypeStruct((EDGE, levels), F32),
        ),
        in_specs=[smem, hbm] + [vmem] * (len(parts) + 2),
        out_specs=(hbm, vmem),
        input_output_aliases={1: 0},
        scratch_shapes=[
            pltpu.VMEM(state.shape, F32),
            pltpu.VMEM((depth, LINES * levels), F32),
            pltpu.VMEM((3 * depth, LINES * levels), BF16),
            pltpu.SemaphoreType.DMA((rows // LINES,)),
            pltpu.SemaphoreType.DMA((rows // LINES,)),
        ],
        compiler_params=pltpu.CompilerParams(vmem_limit_bytes=24 * MIB),
        cost_estimate=pl.CostEstimate(
            flops=6 * rows * cols * depth * levels,
            bytes_accessed=8 * rows * cols * levels,
            transcendentals=0,
        ),
        name="update",
    )(flags, state, *parts, mask, ocean_map)


def returned_kernel(groups, flags, *refs):
    picked = refs[:groups]
    weight_column, row_line, weights, mask, surface, new_surface, token, out, total = refs[groups:]
    rows, cols = mask.shape
    weight_count = weights.shape[0]

    @pl.when(flags[0] == 1)
    def ocean():
        out[...] = new_surface[...]

    @pl.when(flags[0] == 0)
    def atmosphere():
        values = jnp.concatenate([p[...] for p in picked], axis=0)
        pair = side_by_side(values)
        which = jnp.broadcast_to(weight_column[...], values.shape)
        total[...] = jnp.zeros(values.shape, F32)

        def one(i, _):
            both = jnp.concatenate([weights[2 * i], weights[2 * i + 1]], axis=0)
            images = dot_nt(pair, jnp.concatenate([both, both], axis=1))
            total[...] += jnp.where(which == 2 * i, images[:, :cols], 0.0) + jnp.where(
                which == 2 * i + 1, images[:, cols:], 0.0
            )
            return 0

        lax.fori_loop(0, weight_count // 2, one, 0, unroll=8)
        spots = lax.broadcasted_iota(jnp.int32, (rows, values.shape[0]), 0)
        chosen = jnp.where(jnp.broadcast_to(row_line[...], spots.shape) == spots, 1.0, 0.0).astype(BF16)
        high, low = split_two(total[...])
        back = dot_nn(chosen, high) + dot_nn(chosen, low)
        out[...] = jnp.where(mask[...] > 0.5, back, surface[...])


def returned(flags, picked, weight_column, row_line, weights, mask, surface, new_surface, token):
    rows, cols = mask.shape
    entry_total = weight_column.shape[0]
    vmem = pl.BlockSpec(memory_space=pltpu.VMEM)
    smem = pl.BlockSpec(memory_space=pltpu.SMEM)
    return pl.pallas_call(
        functools.partial(returned_kernel, len(picked)),
        out_shape=jax.ShapeDtypeStruct((rows, cols), F32),
        in_specs=[smem] + [vmem] * (len(picked) + 7),
        out_specs=vmem,
        scratch_shapes=[pltpu.VMEM((entry_total, cols), F32)],
        compiler_params=pltpu.CompilerParams(vmem_limit_bytes=16 * MIB),
        name="returned",
    )(flags, *picked, weight_column, row_line, weights, mask, surface, new_surface, token)


def local(
    state, land_mask, intersection_list, mix_atm, mix_ocn, flux_map, ocean_map, regrid_weights
):
    rows, cols, levels = state.shape
    intersections = intersection_list.shape[2]
    comp_count = lax.axis_size("comp")
    lat_count = lax.axis_size("lat")
    lon_count = lax.axis_size("lon")
    tile_count = lat_count * lon_count
    reach = min(4, lon_count)
    neighbours = 2 * reach
    entry_total = intersections * rows
    capacity = entry_total // neighbours
    comp_index = lax.axis_index("comp")
    lat_index = lax.axis_index("lat")
    tile_index = lat_index * lon_count + lax.axis_index("lon")
    bands = comp_count * lat_count
    ocean_band = (comp_count - 1) * lat_count
    ocean_comp = comp_count - 1
    band = comp_index * lat_count + lat_index
    is_ocean = comp_index == ocean_comp
    upper_valid = (band > 0) & (band != ocean_band)
    lower_valid = (band < bands - 1) & (band != ocean_band - 1)
    flags = jnp.stack([is_ocean, upper_valid, lower_valid, comp_index]).astype(jnp.int32)
    mask = (land_mask == 1).astype(F32)

    def band_shift(value, by, lon_by):
        pairs = []
        for b in range(bands):
            target = b + by
            if 0 <= target < bands and (b >= ocean_band) == (target >= ocean_band):
                for lon in range(lon_count):
                    pairs.append(
                        (b * lon_count + lon, target * lon_count + (lon + lon_by) % lon_count)
                    )
        return lax.ppermute(value, AXES, pairs)

    first_rows, last_rows, sides = take_edges(state)
    up_rows = band_shift(last_rows, 1, 0)
    low_rows = band_shift(first_rows, -1, 0)
    framed = frame_sides(sides, up_rows, low_rows)
    if lon_count == 2:
        left_cols = right_cols = band_shift(framed, 0, 1)
        left_at, right_at = 2, 0
    else:
        left_cols = band_shift(framed[2:], 0, 1)
        right_cols = band_shift(framed[:2], 0, -1)
        left_at, right_at = 0, 0

    entry_list = intersection_list.reshape(entry_total, 3)
    owners = entry_list[:, 0]
    labels = entry_list[:, 2] * rows + entry_list[:, 1]
    offsets = [
        (n // reach * lon_count + n % reach - (reach - 1) // 2) % tile_count
        for n in range(neighbours)
    ]
    distance = (owners - tile_index + tile_count) % tile_count
    hits = distance[:, None] == jnp.array(offsets, jnp.int32)[None, :]
    neighbour_ids = jnp.sum(
        jnp.where(hits, jnp.arange(neighbours, dtype=jnp.int32)[None, :], 0), axis=1
    )
    positions = jnp.arange(entry_total, dtype=jnp.int32)
    earlier = (neighbour_ids[None, :] == neighbour_ids[:, None]) & (
        positions[None, :] < positions[:, None]
    )
    slots = neighbour_ids * capacity + jnp.sum(earlier.astype(jnp.int32), axis=1)
    placing = positions[:, None] == slots[None, :]
    sources = jnp.sum(jnp.where(placing, (positions // intersections)[None, :], 0), axis=1)
    packed_labels = jnp.sum(jnp.where(placing, labels[None, :], 0), axis=1)

    def over_comp(value):
        return lax.all_to_all(value, "comp", split_axis=0, concat_axis=0, tiled=True)

    def shifted_comp(value, shift):
        pairs = [
            (c * tile_count + t, (c + shift) % comp_count * tile_count + t)
            for c in range(comp_count)
            for t in range(tile_count)
        ]
        return lax.ppermute(value, AXES, pairs)

    def over_tiles(value, offset, comps):
        if offset % tile_count == 0:
            return value
        pairs = [
            (c * tile_count + t, c * tile_count + (t + offset) % tile_count)
            for c in range(comps)
            for t in range(tile_count)
        ]
        return lax.ppermute(value, AXES, pairs)

    def from_ocean(value, comp):
        pairs = [
            (ocean_comp * tile_count + t, comp * tile_count + t) for t in range(tile_count)
        ]
        return lax.ppermute(value, AXES, pairs)

    def to_ocean(value, comp):
        pairs = [
            (comp * tile_count + t, ocean_comp * tile_count + t) for t in range(tile_count)
        ]
        return lax.ppermute(value, AXES, pairs)

    label_lines = jnp.stack([packed_labels // rows, packed_labels % rows, sources]).astype(BF16)
    label_lines = jnp.pad(label_lines, ((0, LABEL_ROWS - 3), (0, 0)))

    halos = (up_rows, low_rows, left_cols, right_cols, sides)
    moved = advance(
        flags, label_lines, state, halos, mask, mix_atm, mix_ocn, flux_map.T,
        comp_count, left_at, right_at,
    )
    moved, surface, sea_copy, packed = moved
    slabs = over_comp(packed)
    seas = [from_ocean(sea_copy, c) for c in range(ocean_comp)] + [sea_copy]
    blocks = regroup(slabs, neighbours, entry_total)
    blocks = [over_tiles(blocks[n], offsets[n], comp_count) for n in range(neighbours)]
    forcing, shared, hits = regrid(
        flags, ocean_map[:, 0], blocks, seas, regrid_weights, surface, mask
    )
    parts = [shared] + [shifted_comp(shared, s) for s in range(1, comp_count)]
    parts[1], forcing = lax.optimization_barrier((parts[1], forcing))
    picks = pick(parts, hits, neighbours)
    new_surface, picked = picks[0], picks[1:]
    arrived = [over_tiles(picked[n], -offsets[n], ocean_comp) for n in range(neighbours)]
    fields = [to_ocean(forcing, c) for c in range(ocean_comp)] + [forcing]
    final_state, token = update(flags, moved, fields, mask, ocean_map)
    weight_column = (packed_labels // rows)[:, None]
    surface_out = returned(
        flags, arrived, weight_column, sources[None, :], regrid_weights, mask, surface, new_surface,
        token,
    )
    return (final_state, surface_out)


def solution(mesh):
    placed = (
        P(("comp", "lat"), "lon", None),
        P(("comp", "lat"), "lon"),
        P(("comp", "lat"), "lon", None, None),
        P(),
        P(),
        P(),
        P(),
        P(),
    )
    return jax.shard_map(
        local,
        mesh=mesh,
        in_specs=placed,
        out_specs=(P(("comp", "lat"), "lon", None), P(("comp", "lat"), "lon")),
        check_vma=False,
    )
```

```python
import functools

import jax
import jax.numpy as jnp
from jax import lax
from jax.experimental import pallas as pl
from jax.experimental.pallas import tpu as pltpu
from jax.sharding import PartitionSpec as P

SMOOTHING = 0.2
PHYSICS = 0.5
MIB = 1024 * 1024
F32 = jnp.float32
BF16 = jnp.bfloat16
EDGE = 8
AHEAD = 4
CHUNK = 8
AXES = ("comp", "lat", "lon")


def split_two(x):
    high = x.astype(BF16)
    low = (x - high.astype(F32)).astype(BF16)
    return high, low


def side_by_side(x):
    return jnp.concatenate(split_two(x), axis=1)


def dot_nt(a, b):
    return lax.dot_general(a, b, (((1,), (1,)), ((), ())), preferred_element_type=F32)


def dot_nn(a, b):
    return jnp.dot(a, b, preferred_element_type=F32)


def edges_kernel(state, first_rows, last_rows, sides, top, bottom, left, right, sems):
    rows, cols, _ = state.shape
    copies = [
        pltpu.make_async_copy(state.at[pl.ds(0, 2)], top, sems.at[0]),
        pltpu.make_async_copy(state.at[pl.ds(rows - 2, 2)], bottom, sems.at[1]),
        pltpu.make_async_copy(state.at[:, pl.ds(0, EDGE)], left, sems.at[2]),
        pltpu.make_async_copy(state.at[:, pl.ds(cols - EDGE, EDGE)], right, sems.at[3]),
    ]
    for copy in copies:
        copy.start()
    for copy in copies:
        copy.wait()
    first_rows[...] = top[...].astype(BF16)
    last_rows[...] = bottom[...].astype(BF16)
    for i in range(2):
        sides[i] = left[:, i, :]
        sides[2 + i] = right[:, EDGE - 2 + i, :]


def take_edges(state):
    rows, cols, levels = state.shape
    slab = jax.ShapeDtypeStruct((2, cols, levels), BF16)
    side = jax.ShapeDtypeStruct((4, rows, levels), F32)
    vmem = pl.BlockSpec(memory_space=pltpu.VMEM)
    return pl.pallas_call(
        edges_kernel,
        out_shape=(slab, slab, side),
        in_specs=[pl.BlockSpec(memory_space=pltpu.HBM)],
        out_specs=(vmem,) * 3,
        scratch_shapes=[
            pltpu.VMEM((2, cols, levels), F32),
            pltpu.VMEM((2, cols, levels), F32),
            pltpu.VMEM((rows, EDGE, levels), F32),
            pltpu.VMEM((rows, EDGE, levels), F32),
            pltpu.SemaphoreType.DMA((4,)),
        ],
        compiler_params=pltpu.CompilerParams(vmem_limit_bytes=50 * MIB),
        name="edges",
    )(state)


def frame_kernel(sides, up_rows, low_rows, framed):
    _, rows, levels = sides.shape
    cols = up_rows.shape[1]
    framed[...] = jnp.zeros(framed.shape, F32)
    above = up_rows[1].astype(F32)
    below = low_rows[0].astype(F32)
    for i, col in enumerate((0, 1, cols - 2, cols - 1)):
        framed[i, EDGE : EDGE + rows, :] = sides[i]
        framed[i, EDGE - 1 : EDGE, :] = above[col : col + 1, :]
        framed[i, EDGE + rows : EDGE + rows + 1, :] = below[col : col + 1, :]


def frame_sides(sides, up_rows, low_rows):
    count, rows, levels = sides.shape
    vmem = pl.BlockSpec(memory_space=pltpu.VMEM)
    return pl.pallas_call(
        frame_kernel,
        out_shape=jax.ShapeDtypeStruct((count, rows + 2 * EDGE, levels), F32),
        in_specs=[vmem] * 3,
        out_specs=vmem,
        compiler_params=pltpu.CompilerParams(vmem_limit_bytes=16 * MIB),
        name="frame",
    )(sides, up_rows, low_rows)


def advance_kernel(comp_count, left_at, right_at, *refs):
    (flags, labels, state, up_rows, low_rows, left_in, right_in, own_sides) = refs[:8]
    (mask, mix_atm, mix_ocn, flux_map) = refs[8:12]
    out, surface, sea_copy, packed = refs[12:16]
    (values, moved, halo_moved, pairs, mixed, later_pairs, later_mixed) = refs[16:23]
    (weights, flux_weights, flux_pairs, fluxes, staged, top, in_sems, out_sems) = refs[23:]
    left_cols = left_in.at[left_at : left_at + 2]
    right_cols = right_in.at[right_at : right_at + 2]
    first = (pairs, mixed)
    second = (later_pairs, later_mixed)
    rows, cols, levels = state.shape
    chunks = rows // CHUNK
    inner = pl.ds(EDGE, cols)
    flux_count = flux_map.shape[0]

    def fetch(q):
        return pltpu.make_async_copy(
            state.at[pl.ds(q * CHUNK, CHUNK)],
            values.at[pl.ds(q * CHUNK + 2, CHUNK), inner],
            in_sems.at[q],
        )

    def put(q, slot):
        return pltpu.make_async_copy(
            staged.at[slot], out.at[pl.ds(q * CHUNK, CHUNK)], out_sems.at[slot]
        )

    def begin(q, _):
        fetch(q).start()
        return 0

    lax.fori_loop(0, AHEAD, begin, 0)
    ocean = flags[0] == 1
    mix = jnp.where(ocean, mix_ocn[...], mix_atm[...])
    mix_high, mix_low = split_two(mix)
    weights[:levels, :levels] = mix_high
    weights[levels:, :levels] = mix_high
    weights[:levels, levels:] = mix_low
    weights[levels:, levels:] = mix_low
    sea_copy[...] = mask[...].astype(BF16)
    map_high, map_low = split_two(flux_map[...])
    flux_weights[...] = jnp.concatenate(
        [
            jnp.concatenate([map_high.astype(F32), map_high.astype(F32)], axis=1),
            jnp.concatenate([map_low.astype(F32), map_low.astype(F32)], axis=1),
        ],
        axis=0,
    ).astype(BF16)
    values[0:2, EDGE : EDGE + cols, :] = up_rows[...].astype(F32)
    values[rows + 2 : rows + 4, EDGE : EDGE + cols, :] = low_rows[...].astype(F32)
    for r, i in ((1, EDGE - 1), (rows + 2, EDGE + rows)):
        values[r, EDGE - 1 : EDGE, :] = left_cols[1, i : i + 1, :]
        values[r, EDGE + cols : EDGE + cols + 1, :] = right_cols[0, i : i + 1, :]

    def side_cells(start, count):
        for row in range(count):
            values[start + row + 2, EDGE - 1 : EDGE, :] = left_cols[1, pl.ds(start + row + EDGE, 1), :]
            values[start + row + 2, EDGE + cols : EDGE + cols + 1, :] = right_cols[
                0, pl.ds(start + row + EDGE, 1), :
            ]

    def moved_sides(start, count):
        for row in range(count):
            moved[start + row + 1, EDGE - 1 : EDGE, :] = halo_moved[0, pl.ds(start + row, 1), :]
            moved[start + row + 1, EDGE + cols : EDGE + cols + 1, :] = halo_moved[
                1, pl.ds(start + row, 1), :
            ]

    def stage(refs, row, total):
        line = SMOOTHING * total
        refs[0][row * cols : (row + 1) * cols, :] = side_by_side(line)

    def stage_rows(refs, ref, start, count):
        for row in range(count):
            i = start + row
            here = ref[i, EDGE : EDGE + cols, :] + (
                ref[i - 1, EDGE : EDGE + cols, :] + ref[i + 1, EDGE : EDGE + cols, :]
            )
            near = ref[i, EDGE - 1 : EDGE - 1 + cols, :] + ref[i, EDGE + 1 : EDGE + 1 + cols, :]
            stage(refs, row, here + near)

    def note_top(q, lines):
        lanes = lax.broadcasted_iota(jnp.int32, (cols, levels), 1)
        kept = lines[0]
        for row in range(1, CHUNK):
            kept = jnp.where(lanes == row, pltpu.roll(lines[row], row, 1), kept)
        turned = pltpu.roll(kept, q * CHUNK, 1)
        top[...] = jnp.where(lanes // CHUNK == q, turned, top[...])

    def mix_rows(refs, count):
        refs[1][: count * cols, :] = dot_nn(refs[0][: count * cols, :], weights[...])

    def finish(refs, row):
        part = refs[1][row * cols : (row + 1) * cols, :]
        pair = refs[0][row * cols : (row + 1) * cols, :].astype(F32)
        change = PHYSICS * jnp.tanh(part[:, :levels] + part[:, levels:])
        return (pair[:, :levels] + pair[:, levels:]) + change

    @pl.when(jnp.logical_not(ocean))
    def atmosphere():
        nearest = (left_cols.at[1], right_cols.at[0])
        beyond = (left_cols.at[0], right_cols.at[1])
        within = (own_sides.at[0], own_sides.at[3])
        for s in range(2):
            total = (
                nearest[s][EDGE : EDGE + rows, :]
                + nearest[s][EDGE - 1 : EDGE - 1 + rows, :]
                + nearest[s][EDGE + 1 : EDGE + 1 + rows, :]
            )
            stage(first, s, total + (beyond[s][EDGE : EDGE + rows, :] + within[s][...]))
        mix_rows(first, 2)
        for s in range(2):
            halo_moved[s] = finish(first, s)

        side_cells(0, 1)
        fetch(0).wait()
        fetch(1).wait()
        stage_rows(second, values, 1, 2)
        mix_rows(second, 2)
        for row in range(2):
            moved[row, EDGE : EDGE + cols, :] = finish(second, row)

        @pl.when(flags[1] == 0)
        def _():
            moved[0, EDGE : EDGE + cols, :] = jnp.zeros((cols, levels), F32)

        def begin_first(q):
            side_cells(jnp.minimum(q * CHUNK + 1, rows - CHUNK), CHUNK)
            stage_rows(first, values, q * CHUNK + 3, CHUNK)
            mix_rows(first, CHUNK)

        def end_first(q):
            for row in range(CHUNK):
                moved[q * CHUNK + row + 2, EDGE : EDGE + cols, :] = finish(first, row)

        def begin_second(q):
            moved_sides(q * CHUNK, CHUNK)
            stage_rows(second, moved, q * CHUNK + 1, CHUNK)

        def end_second(q, slot):
            for row in range(CHUNK):
                line = finish(second, row)
                staged[slot, row] = line
                both = line + moved[q * CHUNK + row + 1, EDGE : EDGE + cols, :]
                flux_pairs[row * cols : (row + 1) * cols, :] = side_by_side(both)
            put(q, slot).start()
            note_top(q, [staged[slot, row] for row in range(CHUNK)])

        def sum_fluxes(q):
            flux = dot_nt(flux_weights[...], flux_pairs[...])
            flux = flux[:flux_count] + flux[flux_count:]
            for row in range(CHUNK):
                r = q * CHUNK + row
                block = PHYSICS * flux[:, row * cols : (row + 1) * cols]
                sea = jnp.broadcast_to(mask[pl.ds(r, 1), :], block.shape)
                block = jnp.where(sea > 0.5, block, 0.0)
                fluxes[pl.ds(pl.multiple_of(r * flux_count, flux_count), flux_count), :] = block

        fetch(AHEAD).start()
        flux_pairs[...] = jnp.zeros(flux_pairs.shape, BF16)
        begin_first(0)
        end_first(0)

        def one_chunk(q, _):
            @pl.when(q + 1 < chunks)
            def _():
                fetch(q + 1).wait()

            @pl.when(q + AHEAD < chunks)
            def _():
                fetch(q + AHEAD).start()

            slot = (q - 1) % 2

            @pl.when(q >= 3)
            def _():
                put(q - 3, slot).wait()

            sum_fluxes(jnp.maximum(q - 2, 0))
            begin_first(q)
            begin_second(q - 1)
            mix_rows(second, CHUNK)
            end_first(q)
            end_second(q - 1, slot)
            return 0

        lax.fori_loop(1, chunks, one_chunk, 0)

        @pl.when(flags[2] == 0)
        def _():
            moved[rows + 1, EDGE : EDGE + cols, :] = jnp.zeros((cols, levels), F32)

        last = chunks - 1
        put(last - 2, last % 2).wait()
        sum_fluxes(last - 1)
        begin_second(last)
        mix_rows(second, CHUNK)
        end_second(last, last % 2)
        sum_fluxes(last)
        share = flux_count // comp_count
        for c in range(comp_count):
            for f in range(share):
                field = fluxes[pl.ds(c * share + f, rows, stride=flux_count), :]
                packed[c, :rows, f * cols : (f + 1) * cols] = field.astype(BF16)
            packed[c, rows:, :] = labels[...]
        put(last - 1, (last - 1) % 2).wait()
        put(last, last % 2).wait()
        surface[...] = top[...].T

    @pl.when(ocean)
    def sea_side():
        fetch(0).wait()
        lanes = lax.broadcasted_iota(jnp.int32, (CHUNK, CHUNK * levels), 1) // levels
        lines = lax.broadcasted_iota(jnp.int32, (CHUNK, CHUNK * levels), 0)
        spreader = jnp.where(lanes == lines, 1.0, 0.0).astype(F32)

        def one_chunk(q, _):
            base = q * CHUNK

            @pl.when(q + 1 < chunks)
            def _():
                fetch(q + 1).wait()

            @pl.when(q + AHEAD < chunks)
            def _():
                fetch(q + AHEAD).start()

            side_cells(base, CHUNK)
            stage_rows(first, values, base + 2, CHUNK)
            mix_rows(first, CHUNK)
            slot = q % 2

            @pl.when(q >= 2)
            def _():
                put(q - 2, slot).wait()

            sea = dot_nn(mask[pl.ds(pl.multiple_of(base, CHUNK), CHUNK), :].T, spreader)
            for row in range(CHUNK):
                chosen = sea[:, row * levels : (row + 1) * levels] > 0.5
                before = values[base + row + 2, EDGE : EDGE + cols, :]
                staged[slot, row] = jnp.where(chosen, finish(first, row), before)
            put(q, slot).start()
            note_top(q, [staged[slot, row] for row in range(CHUNK)])
            return 0

        lax.fori_loop(0, chunks, one_chunk, 0)
        put(chunks - 2, (chunks - 2) % 2).wait()
        put(chunks - 1, (chunks - 1) % 2).wait()
        surface[...] = top[...].T
        packed[...] = jnp.zeros(packed.shape, BF16)


def advance(
    flags, labels, state, halos, mask, mix_atm, mix_ocn, flux_map_t, comp_count, left_at, right_at
):
    rows, cols, levels = state.shape
    fluxes = flux_map_t.shape[0]
    vmem = pl.BlockSpec(memory_space=pltpu.VMEM)
    smem = pl.BlockSpec(memory_space=pltpu.SMEM)
    hbm = pl.BlockSpec(memory_space=pltpu.HBM)
    entry = jax.ShapeDtypeStruct(
        (comp_count, rows + labels.shape[0], fluxes // comp_count * cols), BF16
    )
    cells = rows * cols
    return pl.pallas_call(
        functools.partial(advance_kernel, comp_count, left_at, right_at),
        out_shape=(
            jax.ShapeDtypeStruct(state.shape, F32),
            jax.ShapeDtypeStruct((rows, cols), F32),
            jax.ShapeDtypeStruct((rows, cols), BF16),
            entry,
        ),
        in_specs=[smem, vmem, hbm] + [vmem] * (len(halos) + 4),
        out_specs=(hbm, vmem, vmem, vmem),
        scratch_shapes=[
            pltpu.VMEM((rows + 4, cols + 2 * EDGE, levels), F32),
            pltpu.VMEM((rows + 2, cols + 2 * EDGE, levels), F32),
            pltpu.VMEM((2, rows, levels), F32),
            pltpu.VMEM((CHUNK * cols, 2 * levels), BF16),
            pltpu.VMEM((CHUNK * cols, 2 * levels), F32),
            pltpu.VMEM((CHUNK * cols, 2 * levels), BF16),
            pltpu.VMEM((CHUNK * cols, 2 * levels), F32),
            pltpu.VMEM((2 * levels, 2 * levels), BF16),
            pltpu.VMEM((2 * fluxes, 2 * levels), BF16),
            pltpu.VMEM((CHUNK * cols, 2 * levels), BF16),
            pltpu.VMEM((rows * fluxes, cols), F32),
            pltpu.VMEM((2, CHUNK, cols, levels), F32),
            pltpu.VMEM((cols, levels), F32),
            pltpu.SemaphoreType.DMA((rows // CHUNK,)),
            pltpu.SemaphoreType.DMA((2,)),
        ],
        compiler_params=pltpu.CompilerParams(vmem_limit_bytes=48 * MIB),
        cost_estimate=pl.CostEstimate(
            flops=8 * cells * levels * levels, bytes_accessed=8 * cells * levels, transcendentals=0
        ),
        name="advance",
    )(flags, labels, state, *halos, mask, mix_atm, mix_ocn, flux_map_t)


BATCH = 8
LABEL_ROWS = 16


def regroup_kernel(slabs, *blocks):
    sources = slabs.shape[0] - 1
    capacity = (blocks[0].shape[0] - LABEL_ROWS) // sources
    rows = slabs.shape[1] - LABEL_ROWS
    size = len(blocks) * capacity
    heads = [slabs[c, rows:, :].astype(F32) for c in range(sources)]
    lines = [head[i : i + 1] for i in range(2) for head in heads]
    spare = jnp.zeros((LABEL_ROWS - len(lines), heads[0].shape[1]), F32)
    labels = jnp.concatenate(lines + [spare], axis=0).astype(BF16)
    spots = lax.broadcasted_iota(jnp.int32, (rows, size), 0).astype(F32)
    for c in range(sources):
        placing = jnp.where(heads[c][2:3, :size] == spots, 1.0, 0.0).T.astype(BF16)
        packed = dot_nn(placing, slabs[c, :rows, :]).astype(BF16)
        for n, block in enumerate(blocks):
            block[c * capacity : (c + 1) * capacity, :] = packed[n * capacity : (n + 1) * capacity, :]
    for block in blocks:
        block[sources * capacity :, :] = labels


def regroup(slabs, count, entry_total):
    comps, rows, width = slabs.shape
    size = entry_total // count * (comps - 1) + LABEL_ROWS
    vmem = pl.BlockSpec(memory_space=pltpu.VMEM)
    return pl.pallas_call(
        regroup_kernel,
        out_shape=(jax.ShapeDtypeStruct((size, width), BF16),) * count,
        in_specs=[vmem],
        out_specs=(vmem,) * count,
        compiler_params=pltpu.CompilerParams(vmem_limit_bytes=16 * MIB),
        name="regroup",
    )(slabs)


def regrid_body(count, comp_count, flags, ocean_first, *refs):
    blocks = refs[:count]
    seas = refs[count : count + comp_count]
    weights, surface, mask, forcing, shared, hits, entries, chosen, binned = refs[count + comp_count :]
    sources = comp_count - 1
    rows, cols = mask.shape
    share = forcing.shape[0]
    weight_count = weights.shape[0]
    capacity = (blocks[0].shape[0] - LABEL_ROWS) // sources
    size = count * capacity
    total = sources * size
    width = blocks[0].shape[1]
    for c in range(sources):
        for n in range(count):
            start = c * size + n * capacity
            entries[start : start + capacity, :] = blocks[n][c * capacity : (c + 1) * capacity, :]
    lanes = lax.broadcasted_iota(jnp.int32, (LABEL_ROWS, width), 1) // capacity
    labels = jnp.zeros((LABEL_ROWS, width), F32)
    for n in range(count):
        labels = jnp.where(lanes == n, blocks[n][sources * capacity :, :].astype(F32), labels)
    labels = labels.astype(jnp.int32)
    weight_line = jnp.concatenate([labels[c : c + 1, :size] for c in range(sources)], axis=1)
    target_line = jnp.concatenate(
        [labels[sources + c : sources + c + 1, :size] for c in range(sources)], axis=1
    )
    spots = lax.broadcasted_iota(jnp.int32, (rows, total), 0)
    by_target = jnp.where(target_line == spots, 1.0, 0.0)
    own = by_target[:, :size]
    for c in range(1, sources):
        own = jnp.where(flags[3] == c, by_target[:, c * size : (c + 1) * size], own)
    hits[...] = own.T.astype(BF16)
    by_target = by_target.astype(BF16)
    numbers = lax.broadcasted_iota(jnp.int32, (weight_count, total), 0)
    by_weight = jnp.where(weight_line == numbers, 1.0, 0.0).astype(BF16)
    for g in range(weight_count // BATCH):
        for i in range(BATCH):
            w = g * BATCH + i
            chosen[i * rows : (i + 1) * rows, :] = by_target * by_weight[w : w + 1, :]
        binned[...] = dot_nn(chosen[...], entries[...])
        wide = weights[g * BATCH : (g + 1) * BATCH].reshape(BATCH * cols, cols)
        halves = [
            [
                split_two(binned[i * rows : (i + 1) * rows, f * cols : (f + 1) * cols])
                for i in range(BATCH)
            ]
            for f in range(share)
        ]
        stacked = jnp.concatenate(
            [
                jnp.concatenate([half[k] for half in halves[f]], axis=1)
                for k in range(2)
                for f in range(share)
            ],
            axis=0,
        )
        product = dot_nn(stacked, wide)
        for f in range(share):
            part = product[f * rows : (f + 1) * rows] + product[
                (share + f) * rows : (share + f + 1) * rows
            ]
            forcing[f] = part if g == 0 else forcing[f] + part
    change = ocean_first[flags[3] * share] * forcing[0]
    for f in range(1, share):
        change = change + ocean_first[flags[3] * share + f] * forcing[f]
    sea = jnp.where(flags[0] == 1, seas[sources][...].astype(F32), 0.0)
    for c in range(sources):
        sea = sea + jnp.where(flags[3] == c, seas[c][...].astype(F32), 0.0)
    base = jnp.where(flags[0] == 1, surface[...], 0.0)
    shared[...] = base + jnp.where(sea > 0.5, change, 0.0)


def regrid(flags, ocean_first, blocks, seas, weights, surface, mask):
    comp_count = len(seas)
    sources = comp_count - 1
    rows, cols = mask.shape
    count = len(blocks)
    height, width = blocks[0].shape
    size = (height - LABEL_ROWS) // sources * count
    total = size * sources
    share = width // cols
    weight_count = weights.shape[0]
    vmem = pl.BlockSpec(memory_space=pltpu.VMEM)
    smem = pl.BlockSpec(memory_space=pltpu.SMEM)
    return pl.pallas_call(
        functools.partial(regrid_body, count, comp_count),
        out_shape=(
            jax.ShapeDtypeStruct((share, rows, cols), F32),
            jax.ShapeDtypeStruct((rows, cols), F32),
            jax.ShapeDtypeStruct((size, rows), BF16),
        ),
        in_specs=[smem, smem] + [vmem] * (count + comp_count + 3),
        out_specs=(vmem, vmem, vmem),
        scratch_shapes=[
            pltpu.VMEM((total, width), BF16),
            pltpu.VMEM((BATCH * rows, total), BF16),
            pltpu.VMEM((BATCH * rows, width), F32),
        ],
        compiler_params=pltpu.CompilerParams(vmem_limit_bytes=32 * MIB),
        cost_estimate=pl.CostEstimate(
            flops=2 * weight_count * rows * width * (total + 2 * cols),
            bytes_accessed=2 * MIB,
            transcendentals=0,
        ),
        name="regrid",
    )(flags, ocean_first, *blocks, *seas, weights, surface, mask)


def pick_kernel(count, *refs):
    parts = refs[:count]
    hits, surface = refs[count : count + 2]
    picked = refs[count + 2 :]
    now = parts[0][...]
    for part in parts[1:]:
        now = now + part[...]
    surface[...] = now
    pair = jnp.concatenate(split_two(now), axis=0)
    size = picked[0].shape[0]
    for n in range(len(picked)):
        some = hits[n * size : (n + 1) * size, :]
        picked[n][...] = dot_nn(jnp.concatenate([some, some], axis=1), pair)


def pick(parts, hits, neighbours):
    rows, cols = parts[0].shape
    size = hits.shape[0] // neighbours
    vmem = pl.BlockSpec(memory_space=pltpu.VMEM)
    return pl.pallas_call(
        functools.partial(pick_kernel, len(parts)),
        out_shape=(jax.ShapeDtypeStruct((rows, cols), F32),)
        + (jax.ShapeDtypeStruct((size, cols), F32),) * neighbours,
        in_specs=[vmem] * (len(parts) + 1),
        out_specs=(vmem,) * (1 + neighbours),
        compiler_params=pltpu.CompilerParams(vmem_limit_bytes=16 * MIB),
        name="pick",
    )(*parts, hits)


LINES = 8


def update_kernel(groups, flags, state, *refs):
    parts = refs[:groups]
    mask, ocean_map, out, token, held, table, wide, in_sems, out_sems = refs[groups:]
    rows, cols, levels = state.shape
    share = parts[0].shape[0]
    flux_count = groups * share
    chunks = rows // LINES
    depth = LINES * flux_count
    token[...] = jnp.zeros(token.shape, F32)

    def fetch(q):
        return pltpu.make_async_copy(
            state.at[pl.ds(q * LINES, LINES)], held.at[pl.ds(q * LINES, LINES)], in_sems.at[q]
        )

    def put(q):
        return pltpu.make_async_copy(
            held.at[pl.ds(q * LINES, LINES)], out.at[pl.ds(q * LINES, LINES)], out_sems.at[q]
        )

    @pl.when(flags[0] == 1)
    def ocean():
        for q in range(chunks):
            fetch(q).start()
        table[...] = jnp.zeros(table.shape, F32)
        for line in range(LINES):
            for f in range(flux_count):
                spot = f * LINES + line
                table[spot : spot + 1, line * levels : (line + 1) * levels] = ocean_map[f : f + 1]
        high, low = split_two(table[...])
        wide[:depth] = high
        wide[depth : 2 * depth] = high
        wide[2 * depth :] = low

        def one(q, _):
            start = pl.multiple_of(q * LINES, LINES)
            sea = mask[pl.ds(start, LINES), :] > 0.5
            part = jnp.concatenate(
                [
                    jnp.where(sea, parts[f // share][f % share, pl.ds(start, LINES), :], 0.0)
                    for f in range(flux_count)
                ],
                axis=0,
            )
            rough = part.astype(BF16).astype(F32)
            turned = jnp.concatenate([rough, part - rough, rough], axis=0).T.astype(BF16)
            change = dot_nn(turned, wide[...])
            fetch(q).wait()
            for line in range(LINES):
                held[start + line] += change[:, line * levels : (line + 1) * levels]
            put(q).start()
            return 0

        lax.fori_loop(0, chunks, one, 0, unroll=2)
        for q in range(chunks):
            put(q).wait()


def update(flags, state, parts, mask, ocean_map):
    rows, cols, levels = state.shape
    depth = LINES * ocean_map.shape[0]
    vmem = pl.BlockSpec(memory_space=pltpu.VMEM)
    smem = pl.BlockSpec(memory_space=pltpu.SMEM)
    hbm = pl.BlockSpec(memory_space=pltpu.HBM)
    return pl.pallas_call(
        functools.partial(update_kernel, len(parts)),
        out_shape=(
            jax.ShapeDtypeStruct(state.shape, F32),
            jax.ShapeDtypeStruct((EDGE, levels), F32),
        ),
        in_specs=[smem, hbm] + [vmem] * (len(parts) + 2),
        out_specs=(hbm, vmem),
        input_output_aliases={1: 0},
        scratch_shapes=[
            pltpu.VMEM(state.shape, F32),
            pltpu.VMEM((depth, LINES * levels), F32),
            pltpu.VMEM((3 * depth, LINES * levels), BF16),
            pltpu.SemaphoreType.DMA((rows // LINES,)),
            pltpu.SemaphoreType.DMA((rows // LINES,)),
        ],
        compiler_params=pltpu.CompilerParams(vmem_limit_bytes=24 * MIB),
        cost_estimate=pl.CostEstimate(
            flops=6 * rows * cols * depth * levels,
            bytes_accessed=8 * rows * cols * levels,
            transcendentals=0,
        ),
        name="update",
    )(flags, state, *parts, mask, ocean_map)


def returned_kernel(groups, flags, *refs):
    picked = refs[:groups]
    weight_column, row_line, weights, mask, surface, new_surface, token, out, total = refs[groups:]
    rows, cols = mask.shape
    weight_count = weights.shape[0]

    @pl.when(flags[0] == 1)
    def ocean():
        out[...] = new_surface[...]

    @pl.when(flags[0] == 0)
    def atmosphere():
        values = jnp.concatenate([p[...] for p in picked], axis=0)
        pair = side_by_side(values)
        which = jnp.broadcast_to(weight_column[...], values.shape)
        total[...] = jnp.zeros(values.shape, F32)

        def one(i, _):
            both = jnp.concatenate([weights[2 * i], weights[2 * i + 1]], axis=0)
            images = dot_nt(pair, jnp.concatenate([both, both], axis=1))
            total[...] += jnp.where(which == 2 * i, images[:, :cols], 0.0) + jnp.where(
                which == 2 * i + 1, images[:, cols:], 0.0
            )
            return 0

        lax.fori_loop(0, weight_count // 2, one, 0, unroll=8)
        spots = lax.broadcasted_iota(jnp.int32, (rows, values.shape[0]), 0)
        chosen = jnp.where(jnp.broadcast_to(row_line[...], spots.shape) == spots, 1.0, 0.0).astype(BF16)
        high, low = split_two(total[...])
        back = dot_nn(chosen, high) + dot_nn(chosen, low)
        out[...] = jnp.where(mask[...] > 0.5, back, surface[...])


def returned(flags, picked, weight_column, row_line, weights, mask, surface, new_surface, token):
    rows, cols = mask.shape
    entry_total = weight_column.shape[0]
    vmem = pl.BlockSpec(memory_space=pltpu.VMEM)
    smem = pl.BlockSpec(memory_space=pltpu.SMEM)
    return pl.pallas_call(
        functools.partial(returned_kernel, len(picked)),
        out_shape=jax.ShapeDtypeStruct((rows, cols), F32),
        in_specs=[smem] + [vmem] * (len(picked) + 7),
        out_specs=vmem,
        scratch_shapes=[pltpu.VMEM((entry_total, cols), F32)],
        compiler_params=pltpu.CompilerParams(vmem_limit_bytes=16 * MIB),
        name="returned",
    )(flags, *picked, weight_column, row_line, weights, mask, surface, new_surface, token)


def local(
    state, land_mask, intersection_list, mix_atm, mix_ocn, flux_map, ocean_map, regrid_weights
):
    rows, cols, levels = state.shape
    intersections = intersection_list.shape[2]
    comp_count = lax.axis_size("comp")
    lat_count = lax.axis_size("lat")
    lon_count = lax.axis_size("lon")
    tile_count = lat_count * lon_count
    reach = min(4, lon_count)
    neighbours = 2 * reach
    entry_total = intersections * rows
    capacity = entry_total // neighbours
    comp_index = lax.axis_index("comp")
    lat_index = lax.axis_index("lat")
    tile_index = lat_index * lon_count + lax.axis_index("lon")
    bands = comp_count * lat_count
    ocean_band = (comp_count - 1) * lat_count
    ocean_comp = comp_count - 1
    band = comp_index * lat_count + lat_index
    is_ocean = comp_index == ocean_comp
    upper_valid = (band > 0) & (band != ocean_band)
    lower_valid = (band < bands - 1) & (band != ocean_band - 1)
    flags = jnp.stack([is_ocean, upper_valid, lower_valid, comp_index]).astype(jnp.int32)
    mask = (land_mask == 1).astype(F32)

    def band_shift(value, by, lon_by):
        pairs = []
        for b in range(bands):
            target = b + by
            if 0 <= target < bands and (b >= ocean_band) == (target >= ocean_band):
                for lon in range(lon_count):
                    pairs.append(
                        (b * lon_count + lon, target * lon_count + (lon + lon_by) % lon_count)
                    )
        return lax.ppermute(value, AXES, pairs)

    first_rows, last_rows, sides = take_edges(state)
    up_rows = band_shift(last_rows, 1, 0)
    low_rows = band_shift(first_rows, -1, 0)
    framed = frame_sides(sides, up_rows, low_rows)
    if lon_count == 2:
        left_cols = right_cols = band_shift(framed, 0, 1)
        left_at, right_at = 2, 0
    else:
        left_cols = band_shift(framed[2:], 0, 1)
        right_cols = band_shift(framed[:2], 0, -1)
        left_at, right_at = 0, 0

    entry_list = intersection_list.reshape(entry_total, 3)
    owners = entry_list[:, 0]
    labels = entry_list[:, 2] * rows + entry_list[:, 1]
    offsets = [
        (n // reach * lon_count + n % reach - (reach - 1) // 2) % tile_count
        for n in range(neighbours)
    ]
    distance = (owners - tile_index + tile_count) % tile_count
    hits = distance[:, None] == jnp.array(offsets, jnp.int32)[None, :]
    neighbour_ids = jnp.sum(
        jnp.where(hits, jnp.arange(neighbours, dtype=jnp.int32)[None, :], 0), axis=1
    )
    positions = jnp.arange(entry_total, dtype=jnp.int32)
    earlier = (neighbour_ids[None, :] == neighbour_ids[:, None]) & (
        positions[None, :] < positions[:, None]
    )
    slots = neighbour_ids * capacity + jnp.sum(earlier.astype(jnp.int32), axis=1)
    placing = positions[:, None] == slots[None, :]
    sources = jnp.sum(jnp.where(placing, (positions // intersections)[None, :], 0), axis=1)
    packed_labels = jnp.sum(jnp.where(placing, labels[None, :], 0), axis=1)

    def over_comp(value):
        return lax.all_to_all(value, "comp", split_axis=0, concat_axis=0, tiled=True)

    def shifted_comp(value, shift):
        pairs = [
            (c * tile_count + t, (c + shift) % comp_count * tile_count + t)
            for c in range(comp_count)
            for t in range(tile_count)
        ]
        return lax.ppermute(value, AXES, pairs)

    def over_tiles(value, offset, comps):
        if offset % tile_count == 0:
            return value
        pairs = [
            (c * tile_count + t, c * tile_count + (t + offset) % tile_count)
            for c in range(comps)
            for t in range(tile_count)
        ]
        return lax.ppermute(value, AXES, pairs)

    def from_ocean(value, comp):
        pairs = [
            (ocean_comp * tile_count + t, comp * tile_count + t) for t in range(tile_count)
        ]
        return lax.ppermute(value, AXES, pairs)

    def to_ocean(value, comp):
        pairs = [
            (comp * tile_count + t, ocean_comp * tile_count + t) for t in range(tile_count)
        ]
        return lax.ppermute(value, AXES, pairs)

    label_lines = jnp.stack([packed_labels // rows, packed_labels % rows, sources]).astype(BF16)
    label_lines = jnp.pad(label_lines, ((0, LABEL_ROWS - 3), (0, 0)))

    halos = (up_rows, low_rows, left_cols, right_cols, sides)
    moved = advance(
        flags, label_lines, state, halos, mask, mix_atm, mix_ocn, flux_map.T,
        comp_count, left_at, right_at,
    )
    moved, surface, sea_copy, packed = moved
    slabs = over_comp(packed)
    seas = [from_ocean(sea_copy, c) for c in range(ocean_comp)] + [sea_copy]
    blocks = regroup(slabs, neighbours, entry_total)
    blocks = [over_tiles(blocks[n], offsets[n], comp_count) for n in range(neighbours)]
    forcing, shared, hits = regrid(
        flags, ocean_map[:, 0], blocks, seas, regrid_weights, surface, mask
    )
    parts = [shared] + [shifted_comp(shared, s) for s in range(1, comp_count)]
    parts[1], forcing = lax.optimization_barrier((parts[1], forcing))
    picks = pick(parts, hits, neighbours)
    new_surface, picked = picks[0], picks[1:]
    arrived = [over_tiles(picked[n], -offsets[n], ocean_comp) for n in range(neighbours)]
    fields = [to_ocean(forcing, c) for c in range(ocean_comp)] + [forcing]
    final_state, token = update(flags, moved, fields, mask, ocean_map)
    weight_column = (packed_labels // rows)[:, None]
    surface_out = returned(
        flags, arrived, weight_column, sources[None, :], regrid_weights, mask, surface, new_surface,
        token,
    )
    return (final_state, surface_out)


def solution(mesh):
    placed = (
        P(("comp", "lat"), "lon", None),
        P(("comp", "lat"), "lon"),
        P(("comp", "lat"), "lon", None, None),
        P(),
        P(),
        P(),
        P(),
        P(),
    )
    return jax.shard_map(
        local,
        mesh=mesh,
        in_specs=placed,
        out_specs=(P(("comp", "lat"), "lon", None), P(("comp", "lat"), "lon")),
        check_vma=False,
    )
```

```python
import functools

import jax
import jax.numpy as jnp
from jax import lax
from jax.experimental import pallas as pl
from jax.experimental.pallas import tpu as pltpu
from jax.sharding import PartitionSpec as P

SMOOTHING = 0.2
PHYSICS = 0.5
MIB = 1024 * 1024
F32 = jnp.float32
BF16 = jnp.bfloat16
EDGE = 8
AHEAD = 4
CHUNK = 8
AXES = ("comp", "lat", "lon")


def split_two(x):
    high = x.astype(BF16)
    low = (x - high.astype(F32)).astype(BF16)
    return high, low


def side_by_side(x):
    return jnp.concatenate(split_two(x), axis=1)


def dot_nt(a, b):
    return lax.dot_general(a, b, (((1,), (1,)), ((), ())), preferred_element_type=F32)


def dot_nn(a, b):
    return jnp.dot(a, b, preferred_element_type=F32)


def edges_kernel(state, first_rows, last_rows, sides, top, bottom, left, right, sems):
    rows, cols, _ = state.shape
    copies = [
        pltpu.make_async_copy(state.at[pl.ds(0, 2)], top, sems.at[0]),
        pltpu.make_async_copy(state.at[pl.ds(rows - 2, 2)], bottom, sems.at[1]),
        pltpu.make_async_copy(state.at[:, pl.ds(0, EDGE)], left, sems.at[2]),
        pltpu.make_async_copy(state.at[:, pl.ds(cols - EDGE, EDGE)], right, sems.at[3]),
    ]
    for copy in copies:
        copy.start()
    for copy in copies:
        copy.wait()
    first_rows[...] = top[...].astype(BF16)
    last_rows[...] = bottom[...].astype(BF16)
    for i in range(2):
        sides[i] = left[:, i, :]
        sides[2 + i] = right[:, EDGE - 2 + i, :]


def take_edges(state):
    rows, cols, levels = state.shape
    slab = jax.ShapeDtypeStruct((2, cols, levels), BF16)
    side = jax.ShapeDtypeStruct((4, rows, levels), F32)
    vmem = pl.BlockSpec(memory_space=pltpu.VMEM)
    return pl.pallas_call(
        edges_kernel,
        out_shape=(slab, slab, side),
        in_specs=[pl.BlockSpec(memory_space=pltpu.HBM)],
        out_specs=(vmem,) * 3,
        scratch_shapes=[
            pltpu.VMEM((2, cols, levels), F32),
            pltpu.VMEM((2, cols, levels), F32),
            pltpu.VMEM((rows, EDGE, levels), F32),
            pltpu.VMEM((rows, EDGE, levels), F32),
            pltpu.SemaphoreType.DMA((4,)),
        ],
        compiler_params=pltpu.CompilerParams(vmem_limit_bytes=50 * MIB),
        name="edges",
    )(state)


def frame_kernel(sides, up_rows, low_rows, framed):
    _, rows, levels = sides.shape
    cols = up_rows.shape[1]
    framed[...] = jnp.zeros(framed.shape, F32)
    above = up_rows[1].astype(F32)
    below = low_rows[0].astype(F32)
    for i, col in enumerate((0, 1, cols - 2, cols - 1)):
        framed[i, EDGE : EDGE + rows, :] = sides[i]
        framed[i, EDGE - 1 : EDGE, :] = above[col : col + 1, :]
        framed[i, EDGE + rows : EDGE + rows + 1, :] = below[col : col + 1, :]


def frame_sides(sides, up_rows, low_rows):
    count, rows, levels = sides.shape
    vmem = pl.BlockSpec(memory_space=pltpu.VMEM)
    return pl.pallas_call(
        frame_kernel,
        out_shape=jax.ShapeDtypeStruct((count, rows + 2 * EDGE, levels), F32),
        in_specs=[vmem] * 3,
        out_specs=vmem,
        compiler_params=pltpu.CompilerParams(vmem_limit_bytes=16 * MIB),
        name="frame",
    )(sides, up_rows, low_rows)


def advance_kernel(comp_count, left_at, right_at, *refs):
    (flags, labels, state, up_rows, low_rows, left_in, right_in, own_sides) = refs[:8]
    (mask, mix_atm, mix_ocn, flux_map) = refs[8:12]
    out, surface, sea_copy, packed = refs[12:16]
    (values, moved, halo_moved, smooth, pairs, mixed, later_smooth, later_pairs, later_mixed) = refs[16:25]
    (weights, flux_weights, flux_pairs, fluxes, staged, top, in_sems, out_sems) = refs[25:]
    left_cols = left_in.at[left_at : left_at + 2]
    right_cols = right_in.at[right_at : right_at + 2]
    first = (smooth, pairs, mixed)
    second = (later_smooth, later_pairs, later_mixed)
    rows, cols, levels = state.shape
    chunks = rows // CHUNK
    inner = pl.ds(EDGE, cols)
    flux_count = flux_map.shape[0]

    def fetch(q):
        return pltpu.make_async_copy(
            state.at[pl.ds(q * CHUNK, CHUNK)],
            values.at[pl.ds(q * CHUNK + 2, CHUNK), inner],
            in_sems.at[q],
        )

    def put(q, slot):
        return pltpu.make_async_copy(
            staged.at[slot], out.at[pl.ds(q * CHUNK, CHUNK)], out_sems.at[slot]
        )

    def begin(q, _):
        fetch(q).start()
        return 0

    lax.fori_loop(0, AHEAD, begin, 0)
    ocean = flags[0] == 1
    mix = jnp.where(ocean, mix_ocn[...], mix_atm[...])
    mix_high, mix_low = split_two(mix)
    weights[:levels, :levels] = mix_high
    weights[levels:, :levels] = mix_high
    weights[:levels, levels:] = mix_low
    weights[levels:, levels:] = mix_low
    sea_copy[...] = mask[...].astype(BF16)
    map_high, map_low = split_two(flux_map[...])
    flux_weights[...] = jnp.concatenate(
        [
            jnp.concatenate([map_high.astype(F32), map_high.astype(F32)], axis=1),
            jnp.concatenate([map_low.astype(F32), map_low.astype(F32)], axis=1),
        ],
        axis=0,
    ).astype(BF16)
    values[0:2, EDGE : EDGE + cols, :] = up_rows[...].astype(F32)
    values[rows + 2 : rows + 4, EDGE : EDGE + cols, :] = low_rows[...].astype(F32)
    for r, i in ((1, EDGE - 1), (rows + 2, EDGE + rows)):
        values[r, EDGE - 1 : EDGE, :] = left_cols[1, i : i + 1, :]
        values[r, EDGE + cols : EDGE + cols + 1, :] = right_cols[0, i : i + 1, :]

    def side_cells(start, count):
        for row in range(count):
            values[start + row + 2, EDGE - 1 : EDGE, :] = left_cols[1, pl.ds(start + row + EDGE, 1), :]
            values[start + row + 2, EDGE + cols : EDGE + cols + 1, :] = right_cols[
                0, pl.ds(start + row + EDGE, 1), :
            ]

    def moved_sides(start, count):
        for row in range(count):
            moved[start + row + 1, EDGE - 1 : EDGE, :] = halo_moved[0, pl.ds(start + row, 1), :]
            moved[start + row + 1, EDGE + cols : EDGE + cols + 1, :] = halo_moved[
                1, pl.ds(start + row, 1), :
            ]

    def stage(refs, row, total):
        line = SMOOTHING * total
        refs[0][row] = line
        refs[1][row * cols : (row + 1) * cols, :] = side_by_side(line)

    def stage_rows(refs, ref, start, count):
        for row in range(count):
            i = start + row
            here = ref[i, EDGE : EDGE + cols, :] + (
                ref[i - 1, EDGE : EDGE + cols, :] + ref[i + 1, EDGE : EDGE + cols, :]
            )
            near = ref[i, EDGE - 1 : EDGE - 1 + cols, :] + ref[i, EDGE + 1 : EDGE + 1 + cols, :]
            stage(refs, row, here + near)

    def note_top(q, lines):
        shape = (cols // EDGE, EDGE, levels)
        lanes = lax.broadcasted_iota(jnp.int32, (1, EDGE, levels), 2)
        kept = lines[0].reshape(shape)
        for row in range(1, CHUNK):
            moved_over = pltpu.roll(lines[row], row, 1).reshape(shape)
            kept = jnp.where(jnp.broadcast_to(lanes == row, shape), moved_over, kept)
        turned = pltpu.roll(kept.reshape(cols, levels), q * CHUNK, 1)
        here = lax.broadcasted_iota(jnp.int32, (cols, levels), 1) // CHUNK == q
        top[...] = jnp.where(here, turned, top[...])

    def mix_rows(refs, count):
        refs[2][: count * cols, :] = dot_nn(refs[1][: count * cols, :], weights[...])

    def finish(refs, row):
        part = refs[2][row * cols : (row + 1) * cols, :]
        return refs[0][row] + PHYSICS * jnp.tanh(part[:, :levels] + part[:, levels:])

    @pl.when(jnp.logical_not(ocean))
    def atmosphere():
        nearest = (left_cols.at[1], right_cols.at[0])
        beyond = (left_cols.at[0], right_cols.at[1])
        within = (own_sides.at[0], own_sides.at[3])
        for s in range(2):
            total = (
                nearest[s][EDGE : EDGE + rows, :]
                + nearest[s][EDGE - 1 : EDGE - 1 + rows, :]
                + nearest[s][EDGE + 1 : EDGE + 1 + rows, :]
            )
            stage(first, s, total + (beyond[s][EDGE : EDGE + rows, :] + within[s][...]))
        mix_rows(first, 2)
        for s in range(2):
            halo_moved[s] = finish(first, s)

        side_cells(0, 1)
        fetch(0).wait()
        fetch(1).wait()
        stage_rows(second, values, 1, 2)
        mix_rows(second, 2)
        for row in range(2):
            moved[row, EDGE : EDGE + cols, :] = finish(second, row)

        @pl.when(flags[1] == 0)
        def _():
            moved[0, EDGE : EDGE + cols, :] = jnp.zeros((cols, levels), F32)

        def begin_first(q):
            side_cells(jnp.minimum(q * CHUNK + 1, rows - CHUNK), CHUNK)
            stage_rows(first, values, q * CHUNK + 3, CHUNK)
            mix_rows(first, CHUNK)

        def end_first(q):
            for row in range(CHUNK):
                moved[q * CHUNK + row + 2, EDGE : EDGE + cols, :] = finish(first, row)

        def begin_second(q):
            moved_sides(q * CHUNK, CHUNK)
            stage_rows(second, moved, q * CHUNK + 1, CHUNK)

        def end_second(q, slot):
            for row in range(CHUNK):
                line = finish(second, row)
                staged[slot, row] = line
                both = line + moved[q * CHUNK + row + 1, EDGE : EDGE + cols, :]
                flux_pairs[row * cols : (row + 1) * cols, :] = side_by_side(both)
            put(q, slot).start()
            note_top(q, [staged[slot, row] for row in range(CHUNK)])

        def sum_fluxes(q):
            flux = dot_nt(flux_weights[...], flux_pairs[...])
            flux = flux[:flux_count] + flux[flux_count:]
            for row in range(CHUNK):
                r = q * CHUNK + row
                block = PHYSICS * flux[:, row * cols : (row + 1) * cols]
                sea = jnp.broadcast_to(mask[pl.ds(r, 1), :], block.shape)
                block = jnp.where(sea > 0.5, block, 0.0)
                fluxes[pl.ds(pl.multiple_of(r * flux_count, flux_count), flux_count), :] = block

        fetch(AHEAD).start()
        flux_pairs[...] = jnp.zeros(flux_pairs.shape, BF16)
        begin_first(0)
        end_first(0)

        def one_chunk(q, _):
            @pl.when(q + 1 < chunks)
            def _():
                fetch(q + 1).wait()

            @pl.when(q + AHEAD < chunks)
            def _():
                fetch(q + AHEAD).start()

            slot = (q - 1) % 2

            @pl.when(q >= 3)
            def _():
                put(q - 3, slot).wait()

            sum_fluxes(jnp.maximum(q - 2, 0))
            begin_first(q)
            begin_second(q - 1)
            mix_rows(second, CHUNK)
            end_first(q)
            end_second(q - 1, slot)
            return 0

        lax.fori_loop(1, chunks, one_chunk, 0)

        @pl.when(flags[2] == 0)
        def _():
            moved[rows + 1, EDGE : EDGE + cols, :] = jnp.zeros((cols, levels), F32)

        last = chunks - 1
        put(last - 2, last % 2).wait()
        sum_fluxes(last - 1)
        begin_second(last)
        mix_rows(second, CHUNK)
        end_second(last, last % 2)
        sum_fluxes(last)
        share = flux_count // comp_count
        for c in range(comp_count):
            for f in range(share):
                field = fluxes[pl.ds(c * share + f, rows, stride=flux_count), :]
                packed[c, :rows, f * cols : (f + 1) * cols] = field.astype(BF16)
            packed[c, rows:, :] = labels[...]
        put(last - 1, (last - 1) % 2).wait()
        put(last, last % 2).wait()
        surface[...] = top[...].T

    @pl.when(ocean)
    def sea_side():
        fetch(0).wait()
        lanes = lax.broadcasted_iota(jnp.int32, (CHUNK, CHUNK * levels), 1) // levels
        lines = lax.broadcasted_iota(jnp.int32, (CHUNK, CHUNK * levels), 0)
        spreader = jnp.where(lanes == lines, 1.0, 0.0).astype(F32)

        def one_chunk(q, _):
            base = q * CHUNK

            @pl.when(q + 1 < chunks)
            def _():
                fetch(q + 1).wait()

            @pl.when(q + AHEAD < chunks)
            def _():
                fetch(q + AHEAD).start()

            side_cells(base, CHUNK)
            stage_rows(first, values, base + 2, CHUNK)
            mix_rows(first, CHUNK)
            slot = q % 2

            @pl.when(q >= 2)
            def _():
                put(q - 2, slot).wait()

            sea = dot_nn(mask[pl.ds(pl.multiple_of(base, CHUNK), CHUNK), :].T, spreader)
            for row in range(CHUNK):
                chosen = sea[:, row * levels : (row + 1) * levels] > 0.5
                before = values[base + row + 2, EDGE : EDGE + cols, :]
                staged[slot, row] = jnp.where(chosen, finish(first, row), before)
            put(q, slot).start()
            note_top(q, [staged[slot, row] for row in range(CHUNK)])
            return 0

        lax.fori_loop(0, chunks, one_chunk, 0)
        put(chunks - 2, (chunks - 2) % 2).wait()
        put(chunks - 1, (chunks - 1) % 2).wait()
        surface[...] = top[...].T
        packed[...] = jnp.zeros(packed.shape, BF16)


def advance(
    flags, labels, state, halos, mask, mix_atm, mix_ocn, flux_map_t, comp_count, left_at, right_at
):
    rows, cols, levels = state.shape
    fluxes = flux_map_t.shape[0]
    vmem = pl.BlockSpec(memory_space=pltpu.VMEM)
    smem = pl.BlockSpec(memory_space=pltpu.SMEM)
    hbm = pl.BlockSpec(memory_space=pltpu.HBM)
    entry = jax.ShapeDtypeStruct(
        (comp_count, rows + labels.shape[0], fluxes // comp_count * cols), BF16
    )
    cells = rows * cols
    return pl.pallas_call(
        functools.partial(advance_kernel, comp_count, left_at, right_at),
        out_shape=(
            jax.ShapeDtypeStruct(state.shape, F32),
            jax.ShapeDtypeStruct((rows, cols), F32),
            jax.ShapeDtypeStruct((rows, cols), BF16),
            entry,
        ),
        in_specs=[smem, vmem, hbm] + [vmem] * (len(halos) + 4),
        out_specs=(hbm, vmem, vmem, vmem),
        scratch_shapes=[
            pltpu.VMEM((rows + 4, cols + 2 * EDGE, levels), F32),
            pltpu.VMEM((rows + 2, cols + 2 * EDGE, levels), F32),
            pltpu.VMEM((2, rows, levels), F32),
            pltpu.VMEM((CHUNK, cols, levels), F32),
            pltpu.VMEM((CHUNK * cols, 2 * levels), BF16),
            pltpu.VMEM((CHUNK * cols, 2 * levels), F32),
            pltpu.VMEM((CHUNK, cols, levels), F32),
            pltpu.VMEM((CHUNK * cols, 2 * levels), BF16),
            pltpu.VMEM((CHUNK * cols, 2 * levels), F32),
            pltpu.VMEM((2 * levels, 2 * levels), BF16),
            pltpu.VMEM((2 * fluxes, 2 * levels), BF16),
            pltpu.VMEM((CHUNK * cols, 2 * levels), BF16),
            pltpu.VMEM((rows * fluxes, cols), F32),
            pltpu.VMEM((2, CHUNK, cols, levels), F32),
            pltpu.VMEM((cols, levels), F32),
            pltpu.SemaphoreType.DMA((rows // CHUNK,)),
            pltpu.SemaphoreType.DMA((2,)),
        ],
        compiler_params=pltpu.CompilerParams(vmem_limit_bytes=48 * MIB),
        cost_estimate=pl.CostEstimate(
            flops=8 * cells * levels * levels, bytes_accessed=8 * cells * levels, transcendentals=0
        ),
        name="advance",
    )(flags, labels, state, *halos, mask, mix_atm, mix_ocn, flux_map_t)


BATCH = 8
LABEL_ROWS = 16


def regroup_kernel(slabs, *blocks):
    sources = slabs.shape[0] - 1
    capacity = (blocks[0].shape[0] - LABEL_ROWS) // sources
    rows = slabs.shape[1] - LABEL_ROWS
    size = len(blocks) * capacity
    heads = [slabs[c, rows:, :].astype(F32) for c in range(sources)]
    lines = [head[i : i + 1] for i in range(2) for head in heads]
    spare = jnp.zeros((LABEL_ROWS - len(lines), heads[0].shape[1]), F32)
    labels = jnp.concatenate(lines + [spare], axis=0).astype(BF16)
    spots = lax.broadcasted_iota(jnp.int32, (rows, size), 0).astype(F32)
    for c in range(sources):
        placing = jnp.where(heads[c][2:3, :size] == spots, 1.0, 0.0).T.astype(BF16)
        packed = dot_nn(placing, slabs[c, :rows, :]).astype(BF16)
        for n, block in enumerate(blocks):
            block[c * capacity : (c + 1) * capacity, :] = packed[n * capacity : (n + 1) * capacity, :]
    for block in blocks:
        block[sources * capacity :, :] = labels


def regroup(slabs, count, entry_total):
    comps, rows, width = slabs.shape
    size = entry_total // count * (comps - 1) + LABEL_ROWS
    vmem = pl.BlockSpec(memory_space=pltpu.VMEM)
    return pl.pallas_call(
        regroup_kernel,
        out_shape=(jax.ShapeDtypeStruct((size, width), BF16),) * count,
        in_specs=[vmem],
        out_specs=(vmem,) * count,
        compiler_params=pltpu.CompilerParams(vmem_limit_bytes=16 * MIB),
        name="regroup",
    )(slabs)


def regrid_body(count, comp_count, flags, ocean_first, *refs):
    blocks = refs[:count]
    seas = refs[count : count + comp_count]
    weights, surface, mask, forcing, shared, hits, entries, chosen, binned = refs[count + comp_count :]
    sources = comp_count - 1
    rows, cols = mask.shape
    share = forcing.shape[0]
    weight_count = weights.shape[0]
    capacity = (blocks[0].shape[0] - LABEL_ROWS) // sources
    size = count * capacity
    total = sources * size
    width = blocks[0].shape[1]
    for c in range(sources):
        for n in range(count):
            start = c * size + n * capacity
            entries[start : start + capacity, :] = blocks[n][c * capacity : (c + 1) * capacity, :]
    lanes = lax.broadcasted_iota(jnp.int32, (LABEL_ROWS, width), 1) // capacity
    labels = jnp.zeros((LABEL_ROWS, width), F32)
    for n in range(count):
        labels = jnp.where(lanes == n, blocks[n][sources * capacity :, :].astype(F32), labels)
    labels = labels.astype(jnp.int32)
    weight_line = jnp.concatenate([labels[c : c + 1, :size] for c in range(sources)], axis=1)
    target_line = jnp.concatenate(
        [labels[sources + c : sources + c + 1, :size] for c in range(sources)], axis=1
    )
    spots = lax.broadcasted_iota(jnp.int32, (rows, total), 0)
    by_target = jnp.where(target_line == spots, 1.0, 0.0)
    own = by_target[:, :size]
    for c in range(1, sources):
        own = jnp.where(flags[3] == c, by_target[:, c * size : (c + 1) * size], own)
    hits[...] = own.T.astype(BF16)
    by_target = by_target.astype(BF16)
    numbers = lax.broadcasted_iota(jnp.int32, (weight_count, total), 0)
    by_weight = jnp.where(weight_line == numbers, 1.0, 0.0).astype(BF16)
    for g in range(weight_count // BATCH):
        for i in range(BATCH):
            w = g * BATCH + i
            chosen[i * rows : (i + 1) * rows, :] = by_target * by_weight[w : w + 1, :]
        binned[...] = dot_nn(chosen[...], entries[...])
        wide = weights[g * BATCH : (g + 1) * BATCH].reshape(BATCH * cols, cols)
        halves = [
            [
                split_two(binned[i * rows : (i + 1) * rows, f * cols : (f + 1) * cols])
                for i in range(BATCH)
            ]
            for f in range(share)
        ]
        stacked = jnp.concatenate(
            [
                jnp.concatenate([half[k] for half in halves[f]], axis=1)
                for k in range(2)
                for f in range(share)
            ],
            axis=0,
        )
        product = dot_nn(stacked, wide)
        for f in range(share):
            part = product[f * rows : (f + 1) * rows] + product[
                (share + f) * rows : (share + f + 1) * rows
            ]
            forcing[f] = part if g == 0 else forcing[f] + part
    change = ocean_first[flags[3] * share] * forcing[0]
    for f in range(1, share):
        change = change + ocean_first[flags[3] * share + f] * forcing[f]
    sea = jnp.where(flags[0] == 1, seas[sources][...].astype(F32), 0.0)
    for c in range(sources):
        sea = sea + jnp.where(flags[3] == c, seas[c][...].astype(F32), 0.0)
    base = jnp.where(flags[0] == 1, surface[...], 0.0)
    shared[...] = base + jnp.where(sea > 0.5, change, 0.0)


def regrid(flags, ocean_first, blocks, seas, weights, surface, mask):
    comp_count = len(seas)
    sources = comp_count - 1
    rows, cols = mask.shape
    count = len(blocks)
    height, width = blocks[0].shape
    size = (height - LABEL_ROWS) // sources * count
    total = size * sources
    share = width // cols
    weight_count = weights.shape[0]
    vmem = pl.BlockSpec(memory_space=pltpu.VMEM)
    smem = pl.BlockSpec(memory_space=pltpu.SMEM)
    return pl.pallas_call(
        functools.partial(regrid_body, count, comp_count),
        out_shape=(
            jax.ShapeDtypeStruct((share, rows, cols), F32),
            jax.ShapeDtypeStruct((rows, cols), F32),
            jax.ShapeDtypeStruct((size, rows), BF16),
        ),
        in_specs=[smem, smem] + [vmem] * (count + comp_count + 3),
        out_specs=(vmem, vmem, vmem),
        scratch_shapes=[
            pltpu.VMEM((total, width), BF16),
            pltpu.VMEM((BATCH * rows, total), BF16),
            pltpu.VMEM((BATCH * rows, width), F32),
        ],
        compiler_params=pltpu.CompilerParams(vmem_limit_bytes=32 * MIB),
        cost_estimate=pl.CostEstimate(
            flops=2 * weight_count * rows * width * (total + 2 * cols),
            bytes_accessed=2 * MIB,
            transcendentals=0,
        ),
        name="regrid",
    )(flags, ocean_first, *blocks, *seas, weights, surface, mask)


def pick_kernel(count, *refs):
    parts = refs[:count]
    hits, surface = refs[count : count + 2]
    picked = refs[count + 2 :]
    now = parts[0][...]
    for part in parts[1:]:
        now = now + part[...]
    surface[...] = now
    pair = jnp.concatenate(split_two(now), axis=0)
    size = picked[0].shape[0]
    for n in range(len(picked)):
        some = hits[n * size : (n + 1) * size, :]
        picked[n][...] = dot_nn(jnp.concatenate([some, some], axis=1), pair)


def pick(parts, hits, neighbours):
    rows, cols = parts[0].shape
    size = hits.shape[0] // neighbours
    vmem = pl.BlockSpec(memory_space=pltpu.VMEM)
    return pl.pallas_call(
        functools.partial(pick_kernel, len(parts)),
        out_shape=(jax.ShapeDtypeStruct((rows, cols), F32),)
        + (jax.ShapeDtypeStruct((size, cols), F32),) * neighbours,
        in_specs=[vmem] * (len(parts) + 1),
        out_specs=(vmem,) * (1 + neighbours),
        compiler_params=pltpu.CompilerParams(vmem_limit_bytes=16 * MIB),
        name="pick",
    )(*parts, hits)


LINES = 8


def update_kernel(groups, flags, state, *refs):
    parts = refs[:groups]
    mask, ocean_map, out, token, held, table, wide, in_sems, out_sems = refs[groups:]
    rows, cols, levels = state.shape
    share = parts[0].shape[0]
    flux_count = groups * share
    chunks = rows // LINES
    depth = LINES * flux_count
    token[...] = jnp.zeros(token.shape, F32)

    def fetch(q):
        return pltpu.make_async_copy(
            state.at[pl.ds(q * LINES, LINES)], held.at[pl.ds(q * LINES, LINES)], in_sems.at[q]
        )

    def put(q):
        return pltpu.make_async_copy(
            held.at[pl.ds(q * LINES, LINES)], out.at[pl.ds(q * LINES, LINES)], out_sems.at[q]
        )

    @pl.when(flags[0] == 1)
    def ocean():
        for q in range(chunks):
            fetch(q).start()
        table[...] = jnp.zeros(table.shape, F32)
        for line in range(LINES):
            for f in range(flux_count):
                spot = f * LINES + line
                table[spot : spot + 1, line * levels : (line + 1) * levels] = ocean_map[f : f + 1]
        high, low = split_two(table[...])
        wide[:depth] = high
        wide[depth : 2 * depth] = high
        wide[2 * depth :] = low

        def one(q, _):
            start = pl.multiple_of(q * LINES, LINES)
            sea = mask[pl.ds(start, LINES), :] > 0.5
            part = jnp.concatenate(
                [
                    jnp.where(sea, parts[f // share][f % share, pl.ds(start, LINES), :], 0.0)
                    for f in range(flux_count)
                ],
                axis=0,
            )
            rough = part.astype(BF16).astype(F32)
            turned = jnp.concatenate([rough, part - rough, rough], axis=0).T.astype(BF16)
            change = dot_nn(turned, wide[...])
            fetch(q).wait()
            for line in range(LINES):
                held[start + line] += change[:, line * levels : (line + 1) * levels]
            put(q).start()
            return 0

        lax.fori_loop(0, chunks, one, 0, unroll=2)
        for q in range(chunks):
            put(q).wait()


def update(flags, state, parts, mask, ocean_map):
    rows, cols, levels = state.shape
    depth = LINES * ocean_map.shape[0]
    vmem = pl.BlockSpec(memory_space=pltpu.VMEM)
    smem = pl.BlockSpec(memory_space=pltpu.SMEM)
    hbm = pl.BlockSpec(memory_space=pltpu.HBM)
    return pl.pallas_call(
        functools.partial(update_kernel, len(parts)),
        out_shape=(
            jax.ShapeDtypeStruct(state.shape, F32),
            jax.ShapeDtypeStruct((EDGE, levels), F32),
        ),
        in_specs=[smem, hbm] + [vmem] * (len(parts) + 2),
        out_specs=(hbm, vmem),
        input_output_aliases={1: 0},
        scratch_shapes=[
            pltpu.VMEM(state.shape, F32),
            pltpu.VMEM((depth, LINES * levels), F32),
            pltpu.VMEM((3 * depth, LINES * levels), BF16),
            pltpu.SemaphoreType.DMA((rows // LINES,)),
            pltpu.SemaphoreType.DMA((rows // LINES,)),
        ],
        compiler_params=pltpu.CompilerParams(vmem_limit_bytes=24 * MIB),
        cost_estimate=pl.CostEstimate(
            flops=6 * rows * cols * depth * levels,
            bytes_accessed=8 * rows * cols * levels,
            transcendentals=0,
        ),
        name="update",
    )(flags, state, *parts, mask, ocean_map)


def returned_kernel(groups, flags, *refs):
    picked = refs[:groups]
    weight_column, row_line, weights, mask, surface, new_surface, token, out, total = refs[groups:]
    rows, cols = mask.shape
    weight_count = weights.shape[0]

    @pl.when(flags[0] == 1)
    def ocean():
        out[...] = new_surface[...]

    @pl.when(flags[0] == 0)
    def atmosphere():
        values = jnp.concatenate([p[...] for p in picked], axis=0)
        pair = side_by_side(values)
        which = jnp.broadcast_to(weight_column[...], values.shape)
        total[...] = jnp.zeros(values.shape, F32)

        def one(i, _):
            both = jnp.concatenate([weights[2 * i], weights[2 * i + 1]], axis=0)
            images = dot_nt(pair, jnp.concatenate([both, both], axis=1))
            total[...] += jnp.where(which == 2 * i, images[:, :cols], 0.0) + jnp.where(
                which == 2 * i + 1, images[:, cols:], 0.0
            )
            return 0

        lax.fori_loop(0, weight_count // 2, one, 0, unroll=8)
        spots = lax.broadcasted_iota(jnp.int32, (rows, values.shape[0]), 0)
        chosen = jnp.where(jnp.broadcast_to(row_line[...], spots.shape) == spots, 1.0, 0.0).astype(BF16)
        high, low = split_two(total[...])
        back = dot_nn(chosen, high) + dot_nn(chosen, low)
        out[...] = jnp.where(mask[...] > 0.5, back, surface[...])


def returned(flags, picked, weight_column, row_line, weights, mask, surface, new_surface, token):
    rows, cols = mask.shape
    entry_total = weight_column.shape[0]
    vmem = pl.BlockSpec(memory_space=pltpu.VMEM)
    smem = pl.BlockSpec(memory_space=pltpu.SMEM)
    return pl.pallas_call(
        functools.partial(returned_kernel, len(picked)),
        out_shape=jax.ShapeDtypeStruct((rows, cols), F32),
        in_specs=[smem] + [vmem] * (len(picked) + 7),
        out_specs=vmem,
        scratch_shapes=[pltpu.VMEM((entry_total, cols), F32)],
        compiler_params=pltpu.CompilerParams(vmem_limit_bytes=16 * MIB),
        name="returned",
    )(flags, *picked, weight_column, row_line, weights, mask, surface, new_surface, token)


def local(
    state, land_mask, intersection_list, mix_atm, mix_ocn, flux_map, ocean_map, regrid_weights
):
    rows, cols, levels = state.shape
    intersections = intersection_list.shape[2]
    comp_count = lax.axis_size("comp")
    lat_count = lax.axis_size("lat")
    lon_count = lax.axis_size("lon")
    tile_count = lat_count * lon_count
    reach = min(4, lon_count)
    neighbours = 2 * reach
    entry_total = intersections * rows
    capacity = entry_total // neighbours
    comp_index = lax.axis_index("comp")
    lat_index = lax.axis_index("lat")
    tile_index = lat_index * lon_count + lax.axis_index("lon")
    bands = comp_count * lat_count
    ocean_band = (comp_count - 1) * lat_count
    ocean_comp = comp_count - 1
    band = comp_index * lat_count + lat_index
    is_ocean = comp_index == ocean_comp
    upper_valid = (band > 0) & (band != ocean_band)
    lower_valid = (band < bands - 1) & (band != ocean_band - 1)
    flags = jnp.stack([is_ocean, upper_valid, lower_valid, comp_index]).astype(jnp.int32)
    mask = (land_mask == 1).astype(F32)

    def band_shift(value, by, lon_by):
        pairs = []
        for b in range(bands):
            target = b + by
            if 0 <= target < bands and (b >= ocean_band) == (target >= ocean_band):
                for lon in range(lon_count):
                    pairs.append(
                        (b * lon_count + lon, target * lon_count + (lon + lon_by) % lon_count)
                    )
        return lax.ppermute(value, AXES, pairs)

    first_rows, last_rows, sides = take_edges(state)
    up_rows = band_shift(last_rows, 1, 0)
    low_rows = band_shift(first_rows, -1, 0)
    framed = frame_sides(sides, up_rows, low_rows)
    if lon_count == 2:
        left_cols = right_cols = band_shift(framed, 0, 1)
        left_at, right_at = 2, 0
    else:
        left_cols = band_shift(framed[2:], 0, 1)
        right_cols = band_shift(framed[:2], 0, -1)
        left_at, right_at = 0, 0

    entry_list = intersection_list.reshape(entry_total, 3)
    owners = entry_list[:, 0]
    labels = entry_list[:, 2] * rows + entry_list[:, 1]
    offsets = [
        (n // reach * lon_count + n % reach - (reach - 1) // 2) % tile_count
        for n in range(neighbours)
    ]
    distance = (owners - tile_index + tile_count) % tile_count
    hits = distance[:, None] == jnp.array(offsets, jnp.int32)[None, :]
    neighbour_ids = jnp.sum(
        jnp.where(hits, jnp.arange(neighbours, dtype=jnp.int32)[None, :], 0), axis=1
    )
    positions = jnp.arange(entry_total, dtype=jnp.int32)
    earlier = (neighbour_ids[None, :] == neighbour_ids[:, None]) & (
        positions[None, :] < positions[:, None]
    )
    slots = neighbour_ids * capacity + jnp.sum(earlier.astype(jnp.int32), axis=1)
    placing = positions[:, None] == slots[None, :]
    sources = jnp.sum(jnp.where(placing, (positions // intersections)[None, :], 0), axis=1)
    packed_labels = jnp.sum(jnp.where(placing, labels[None, :], 0), axis=1)

    def over_comp(value):
        return lax.all_to_all(value, "comp", split_axis=0, concat_axis=0, tiled=True)

    def shifted_comp(value, shift):
        pairs = [
            (c * tile_count + t, (c + shift) % comp_count * tile_count + t)
            for c in range(comp_count)
            for t in range(tile_count)
        ]
        return lax.ppermute(value, AXES, pairs)

    def over_tiles(value, offset, comps):
        if offset % tile_count == 0:
            return value
        pairs = [
            (c * tile_count + t, c * tile_count + (t + offset) % tile_count)
            for c in range(comps)
            for t in range(tile_count)
        ]
        return lax.ppermute(value, AXES, pairs)

    def from_ocean(value, comp):
        pairs = [
            (ocean_comp * tile_count + t, comp * tile_count + t) for t in range(tile_count)
        ]
        return lax.ppermute(value, AXES, pairs)

    def to_ocean(value, comp):
        pairs = [
            (comp * tile_count + t, ocean_comp * tile_count + t) for t in range(tile_count)
        ]
        return lax.ppermute(value, AXES, pairs)

    label_lines = jnp.stack([packed_labels // rows, packed_labels % rows, sources]).astype(BF16)
    label_lines = jnp.pad(label_lines, ((0, LABEL_ROWS - 3), (0, 0)))

    halos = (up_rows, low_rows, left_cols, right_cols, sides)
    moved = advance(
        flags, label_lines, state, halos, mask, mix_atm, mix_ocn, flux_map.T,
        comp_count, left_at, right_at,
    )
    moved, surface, sea_copy, packed = moved
    slabs = over_comp(packed)
    seas = [from_ocean(sea_copy, c) for c in range(ocean_comp)] + [sea_copy]
    blocks = regroup(slabs, neighbours, entry_total)
    blocks = [over_tiles(blocks[n], offsets[n], comp_count) for n in range(neighbours)]
    forcing, shared, hits = regrid(
        flags, ocean_map[:, 0], blocks, seas, regrid_weights, surface, mask
    )
    parts = [shared] + [shifted_comp(shared, s) for s in range(1, comp_count)]
    parts[1], forcing = lax.optimization_barrier((parts[1], forcing))
    picks = pick(parts, hits, neighbours)
    new_surface, picked = picks[0], picks[1:]
    arrived = [over_tiles(picked[n], -offsets[n], ocean_comp) for n in reversed(range(neighbours))]
    arrived = arrived[::-1]
    fields = [to_ocean(forcing, c) for c in range(ocean_comp)] + [forcing]
    final_state, token = update(flags, moved, fields, mask, ocean_map)
    weight_column = (packed_labels // rows)[:, None]
    surface_out = returned(
        flags, arrived, weight_column, sources[None, :], regrid_weights, mask, surface, new_surface,
        token,
    )
    return (final_state, surface_out)


def solution(mesh):
    placed = (
        P(("comp", "lat"), "lon", None),
        P(("comp", "lat"), "lon"),
        P(("comp", "lat"), "lon", None, None),
        P(),
        P(),
        P(),
        P(),
        P(),
    )
    return jax.shard_map(
        local,
        mesh=mesh,
        in_specs=placed,
        out_specs=(P(("comp", "lat"), "lon", None), P(("comp", "lat"), "lon")),
        check_vma=False,
    )
```

```python
import functools

import jax
import jax.numpy as jnp
from jax import lax
from jax.experimental import pallas as pl
from jax.experimental.pallas import tpu as pltpu
from jax.sharding import PartitionSpec as P

SMOOTHING = 0.2
PHYSICS = 0.5
MIB = 1024 * 1024
F32 = jnp.float32
BF16 = jnp.bfloat16
EDGE = 8
AHEAD = 4
CHUNK = 8
AXES = ("comp", "lat", "lon")


def split_two(x):
    high = x.astype(BF16)
    low = (x - high.astype(F32)).astype(BF16)
    return high, low


def side_by_side(x):
    return jnp.concatenate(split_two(x), axis=1)


def dot_nt(a, b):
    return lax.dot_general(a, b, (((1,), (1,)), ((), ())), preferred_element_type=F32)


def dot_nn(a, b):
    return jnp.dot(a, b, preferred_element_type=F32)


def edges_kernel(state, first_rows, last_rows, sides, top, bottom, left, right, sems):
    rows, cols, _ = state.shape
    copies = [
        pltpu.make_async_copy(state.at[pl.ds(0, 2)], top, sems.at[0]),
        pltpu.make_async_copy(state.at[pl.ds(rows - 2, 2)], bottom, sems.at[1]),
        pltpu.make_async_copy(state.at[:, pl.ds(0, EDGE)], left, sems.at[2]),
        pltpu.make_async_copy(state.at[:, pl.ds(cols - EDGE, EDGE)], right, sems.at[3]),
    ]
    for copy in copies:
        copy.start()
    for copy in copies:
        copy.wait()
    first_rows[...] = top[...].astype(BF16)
    last_rows[...] = bottom[...].astype(BF16)
    for i in range(2):
        sides[i] = left[:, i, :]
        sides[2 + i] = right[:, EDGE - 2 + i, :]


def take_edges(state):
    rows, cols, levels = state.shape
    slab = jax.ShapeDtypeStruct((2, cols, levels), BF16)
    side = jax.ShapeDtypeStruct((4, rows, levels), F32)
    vmem = pl.BlockSpec(memory_space=pltpu.VMEM)
    return pl.pallas_call(
        edges_kernel,
        out_shape=(slab, slab, side),
        in_specs=[pl.BlockSpec(memory_space=pltpu.HBM)],
        out_specs=(vmem,) * 3,
        scratch_shapes=[
            pltpu.VMEM((2, cols, levels), F32),
            pltpu.VMEM((2, cols, levels), F32),
            pltpu.VMEM((rows, EDGE, levels), F32),
            pltpu.VMEM((rows, EDGE, levels), F32),
            pltpu.SemaphoreType.DMA((4,)),
        ],
        compiler_params=pltpu.CompilerParams(vmem_limit_bytes=50 * MIB),
        name="edges",
    )(state)


def frame_kernel(sides, up_rows, low_rows, framed):
    _, rows, levels = sides.shape
    cols = up_rows.shape[1]
    framed[...] = jnp.zeros(framed.shape, F32)
    above = up_rows[1].astype(F32)
    below = low_rows[0].astype(F32)
    for i, col in enumerate((0, 1, cols - 2, cols - 1)):
        framed[i, EDGE : EDGE + rows, :] = sides[i]
        framed[i, EDGE - 1 : EDGE, :] = above[col : col + 1, :]
        framed[i, EDGE + rows : EDGE + rows + 1, :] = below[col : col + 1, :]


def frame_sides(sides, up_rows, low_rows):
    count, rows, levels = sides.shape
    vmem = pl.BlockSpec(memory_space=pltpu.VMEM)
    return pl.pallas_call(
        frame_kernel,
        out_shape=jax.ShapeDtypeStruct((count, rows + 2 * EDGE, levels), F32),
        in_specs=[vmem] * 3,
        out_specs=vmem,
        compiler_params=pltpu.CompilerParams(vmem_limit_bytes=16 * MIB),
        name="frame",
    )(sides, up_rows, low_rows)


def advance_kernel(comp_count, left_at, right_at, *refs):
    (flags, labels, state, up_rows, low_rows, left_in, right_in, own_sides) = refs[:8]
    (mask, mix_atm, mix_ocn, flux_map) = refs[8:12]
    out, surface, sea_copy, packed = refs[12:16]
    (values, moved, halo_moved, smooth, pairs, mixed, later_smooth, later_pairs, later_mixed) = refs[16:25]
    (weights, flux_weights, flux_pairs, fluxes, staged, top, in_sems, out_sems) = refs[25:]
    left_cols = left_in.at[left_at : left_at + 2]
    right_cols = right_in.at[right_at : right_at + 2]
    first = (smooth, pairs, mixed)
    second = (later_smooth, later_pairs, later_mixed)
    rows, cols, levels = state.shape
    chunks = rows // CHUNK
    inner = pl.ds(EDGE, cols)
    flux_count = flux_map.shape[0]

    def fetch(q):
        return pltpu.make_async_copy(
            state.at[pl.ds(q * CHUNK, CHUNK)],
            values.at[pl.ds(q * CHUNK + 2, CHUNK), inner],
            in_sems.at[q],
        )

    def put(q, slot):
        return pltpu.make_async_copy(
            staged.at[slot], out.at[pl.ds(q * CHUNK, CHUNK)], out_sems.at[slot]
        )

    def begin(q, _):
        fetch(q).start()
        return 0

    lax.fori_loop(0, AHEAD, begin, 0)
    ocean = flags[0] == 1
    mix = jnp.where(ocean, mix_ocn[...], mix_atm[...])
    mix_high, mix_low = split_two(mix)
    weights[:levels, :] = mix_high
    weights[levels : 2 * levels, :] = mix_high
    weights[2 * levels :, :] = mix_low
    sea_copy[...] = mask[...].astype(BF16)
    map_high, map_low = split_two(flux_map[...])
    flux_weights[...] = jnp.concatenate(
        [
            jnp.concatenate([map_high.astype(F32), map_high.astype(F32)], axis=1),
            jnp.concatenate([map_low.astype(F32), map_low.astype(F32)], axis=1),
        ],
        axis=0,
    ).astype(BF16)
    values[0:2, EDGE : EDGE + cols, :] = up_rows[...].astype(F32)
    values[rows + 2 : rows + 4, EDGE : EDGE + cols, :] = low_rows[...].astype(F32)
    for r, i in ((1, EDGE - 1), (rows + 2, EDGE + rows)):
        values[r, EDGE - 1 : EDGE, :] = left_cols[1, i : i + 1, :]
        values[r, EDGE + cols : EDGE + cols + 1, :] = right_cols[0, i : i + 1, :]

    def side_cells(start, count):
        for row in range(count):
            values[start + row + 2, EDGE - 1 : EDGE, :] = left_cols[1, pl.ds(start + row + EDGE, 1), :]
            values[start + row + 2, EDGE + cols : EDGE + cols + 1, :] = right_cols[
                0, pl.ds(start + row + EDGE, 1), :
            ]

    def moved_sides(start, count):
        for row in range(count):
            moved[start + row + 1, EDGE - 1 : EDGE, :] = halo_moved[0, pl.ds(start + row, 1), :]
            moved[start + row + 1, EDGE + cols : EDGE + cols + 1, :] = halo_moved[
                1, pl.ds(start + row, 1), :
            ]

    def stage(refs, row, total):
        line = SMOOTHING * total
        refs[0][row] = line
        high, low = split_two(line)
        refs[1][row * cols : (row + 1) * cols, :] = jnp.concatenate([high, low, high], axis=1)

    def stage_rows(refs, ref, start, count):
        for row in range(count):
            i = start + row
            here = ref[i, EDGE : EDGE + cols, :] + (
                ref[i - 1, EDGE : EDGE + cols, :] + ref[i + 1, EDGE : EDGE + cols, :]
            )
            near = ref[i, EDGE - 1 : EDGE - 1 + cols, :] + ref[i, EDGE + 1 : EDGE + 1 + cols, :]
            stage(refs, row, here + near)

    def note_top(q, lines):
        shape = (cols // EDGE, EDGE, levels)
        lanes = lax.broadcasted_iota(jnp.int32, (1, EDGE, levels), 2)
        kept = lines[0].reshape(shape)
        for row in range(1, CHUNK):
            moved_over = pltpu.roll(lines[row], row, 1).reshape(shape)
            kept = jnp.where(jnp.broadcast_to(lanes == row, shape), moved_over, kept)
        turned = pltpu.roll(kept.reshape(cols, levels), q * CHUNK, 1)
        here = lax.broadcasted_iota(jnp.int32, (cols, levels), 1) // CHUNK == q
        top[...] = jnp.where(here, turned, top[...])

    def mix_rows(refs, count):
        refs[2][: count * cols, :] = dot_nn(refs[1][: count * cols, :], weights[...])

    def finish(refs, row):
        return refs[0][row] + PHYSICS * jnp.tanh(refs[2][row * cols : (row + 1) * cols, :])

    @pl.when(jnp.logical_not(ocean))
    def atmosphere():
        nearest = (left_cols.at[1], right_cols.at[0])
        beyond = (left_cols.at[0], right_cols.at[1])
        within = (own_sides.at[0], own_sides.at[3])
        for s in range(2):
            total = (
                nearest[s][EDGE : EDGE + rows, :]
                + nearest[s][EDGE - 1 : EDGE - 1 + rows, :]
                + nearest[s][EDGE + 1 : EDGE + 1 + rows, :]
            )
            stage(first, s, total + (beyond[s][EDGE : EDGE + rows, :] + within[s][...]))
        mix_rows(first, 2)
        for s in range(2):
            halo_moved[s] = finish(first, s)

        side_cells(0, 1)
        fetch(0).wait()
        fetch(1).wait()
        stage_rows(second, values, 1, 2)
        mix_rows(second, 2)
        for row in range(2):
            moved[row, EDGE : EDGE + cols, :] = finish(second, row)

        @pl.when(flags[1] == 0)
        def _():
            moved[0, EDGE : EDGE + cols, :] = jnp.zeros((cols, levels), F32)

        def begin_first(q):
            side_cells(jnp.minimum(q * CHUNK + 1, rows - CHUNK), CHUNK)
            stage_rows(first, values, q * CHUNK + 3, CHUNK)
            mix_rows(first, CHUNK)

        def end_first(q):
            for row in range(CHUNK):
                moved[q * CHUNK + row + 2, EDGE : EDGE + cols, :] = finish(first, row)

        def begin_second(q):
            moved_sides(q * CHUNK, CHUNK)
            stage_rows(second, moved, q * CHUNK + 1, CHUNK)

        def end_second(q, slot):
            for row in range(CHUNK):
                line = finish(second, row)
                staged[slot, row] = line
                both = line + moved[q * CHUNK + row + 1, EDGE : EDGE + cols, :]
                flux_pairs[row * cols : (row + 1) * cols, :] = side_by_side(both)
            put(q, slot).start()
            note_top(q, [staged[slot, row] for row in range(CHUNK)])

        def sum_fluxes(q):
            flux = dot_nt(flux_weights[...], flux_pairs[...])
            flux = flux[:flux_count] + flux[flux_count:]
            for row in range(CHUNK):
                r = q * CHUNK + row
                block = PHYSICS * flux[:, row * cols : (row + 1) * cols]
                sea = jnp.broadcast_to(mask[pl.ds(r, 1), :], block.shape)
                block = jnp.where(sea > 0.5, block, 0.0)
                fluxes[pl.ds(pl.multiple_of(r * flux_count, flux_count), flux_count), :] = block

        fetch(AHEAD).start()
        flux_pairs[...] = jnp.zeros(flux_pairs.shape, BF16)
        begin_first(0)
        end_first(0)

        def one_chunk(q, _):
            @pl.when(q + 1 < chunks)
            def _():
                fetch(q + 1).wait()

            @pl.when(q + AHEAD < chunks)
            def _():
                fetch(q + AHEAD).start()

            slot = (q - 1) % 2

            @pl.when(q >= 3)
            def _():
                put(q - 3, slot).wait()

            sum_fluxes(jnp.maximum(q - 2, 0))
            begin_first(q)
            begin_second(q - 1)
            mix_rows(second, CHUNK)
            end_first(q)
            end_second(q - 1, slot)
            return 0

        lax.fori_loop(1, chunks, one_chunk, 0)

        @pl.when(flags[2] == 0)
        def _():
            moved[rows + 1, EDGE : EDGE + cols, :] = jnp.zeros((cols, levels), F32)

        last = chunks - 1
        put(last - 2, last % 2).wait()
        sum_fluxes(last - 1)
        begin_second(last)
        mix_rows(second, CHUNK)
        end_second(last, last % 2)
        sum_fluxes(last)
        share = flux_count // comp_count
        for c in range(comp_count):
            for f in range(share):
                field = fluxes[pl.ds(c * share + f, rows, stride=flux_count), :]
                packed[c, :rows, f * cols : (f + 1) * cols] = field.astype(BF16)
            packed[c, rows:, :] = labels[...]
        put(last - 1, (last - 1) % 2).wait()
        put(last, last % 2).wait()
        surface[...] = top[...].T

    @pl.when(ocean)
    def sea_side():
        fetch(0).wait()
        lanes = lax.broadcasted_iota(jnp.int32, (CHUNK, CHUNK * levels), 1) // levels
        lines = lax.broadcasted_iota(jnp.int32, (CHUNK, CHUNK * levels), 0)
        spreader = jnp.where(lanes == lines, 1.0, 0.0).astype(F32)

        def one_chunk(q, _):
            base = q * CHUNK

            @pl.when(q + 1 < chunks)
            def _():
                fetch(q + 1).wait()

            @pl.when(q + AHEAD < chunks)
            def _():
                fetch(q + AHEAD).start()

            side_cells(base, CHUNK)
            stage_rows(first, values, base + 2, CHUNK)
            mix_rows(first, CHUNK)
            slot = q % 2

            @pl.when(q >= 2)
            def _():
                put(q - 2, slot).wait()

            sea = dot_nn(mask[pl.ds(pl.multiple_of(base, CHUNK), CHUNK), :].T, spreader)
            for row in range(CHUNK):
                chosen = sea[:, row * levels : (row + 1) * levels] > 0.5
                before = values[base + row + 2, EDGE : EDGE + cols, :]
                staged[slot, row] = jnp.where(chosen, finish(first, row), before)
            put(q, slot).start()
            note_top(q, [staged[slot, row] for row in range(CHUNK)])
            return 0

        lax.fori_loop(0, chunks, one_chunk, 0)
        put(chunks - 2, (chunks - 2) % 2).wait()
        put(chunks - 1, (chunks - 1) % 2).wait()
        surface[...] = top[...].T
        packed[...] = jnp.zeros(packed.shape, BF16)


def advance(
    flags, labels, state, halos, mask, mix_atm, mix_ocn, flux_map_t, comp_count, left_at, right_at
):
    rows, cols, levels = state.shape
    fluxes = flux_map_t.shape[0]
    vmem = pl.BlockSpec(memory_space=pltpu.VMEM)
    smem = pl.BlockSpec(memory_space=pltpu.SMEM)
    hbm = pl.BlockSpec(memory_space=pltpu.HBM)
    entry = jax.ShapeDtypeStruct(
        (comp_count, rows + labels.shape[0], fluxes // comp_count * cols), BF16
    )
    cells = rows * cols
    return pl.pallas_call(
        functools.partial(advance_kernel, comp_count, left_at, right_at),
        out_shape=(
            jax.ShapeDtypeStruct(state.shape, F32),
            jax.ShapeDtypeStruct((rows, cols), F32),
            jax.ShapeDtypeStruct((rows, cols), BF16),
            entry,
        ),
        in_specs=[smem, vmem, hbm] + [vmem] * (len(halos) + 4),
        out_specs=(hbm, vmem, vmem, vmem),
        scratch_shapes=[
            pltpu.VMEM((rows + 4, cols + 2 * EDGE, levels), F32),
            pltpu.VMEM((rows + 2, cols + 2 * EDGE, levels), F32),
            pltpu.VMEM((2, rows, levels), F32),
            pltpu.VMEM((CHUNK, cols, levels), F32),
            pltpu.VMEM((CHUNK * cols, 3 * levels), BF16),
            pltpu.VMEM((CHUNK * cols, levels), F32),
            pltpu.VMEM((CHUNK, cols, levels), F32),
            pltpu.VMEM((CHUNK * cols, 3 * levels), BF16),
            pltpu.VMEM((CHUNK * cols, levels), F32),
            pltpu.VMEM((3 * levels, levels), BF16),
            pltpu.VMEM((2 * fluxes, 2 * levels), BF16),
            pltpu.VMEM((CHUNK * cols, 2 * levels), BF16),
            pltpu.VMEM((rows * fluxes, cols), F32),
            pltpu.VMEM((2, CHUNK, cols, levels), F32),
            pltpu.VMEM((cols, levels), F32),
            pltpu.SemaphoreType.DMA((rows // CHUNK,)),
            pltpu.SemaphoreType.DMA((2,)),
        ],
        compiler_params=pltpu.CompilerParams(vmem_limit_bytes=48 * MIB),
        cost_estimate=pl.CostEstimate(
            flops=8 * cells * levels * levels, bytes_accessed=8 * cells * levels, transcendentals=0
        ),
        name="advance",
    )(flags, labels, state, *halos, mask, mix_atm, mix_ocn, flux_map_t)


BATCH = 8
LABEL_ROWS = 16


def regroup_kernel(slabs, *blocks):
    sources = slabs.shape[0] - 1
    capacity = (blocks[0].shape[0] - LABEL_ROWS) // sources
    rows = slabs.shape[1] - LABEL_ROWS
    size = len(blocks) * capacity
    heads = [slabs[c, rows:, :].astype(F32) for c in range(sources)]
    lines = [head[i : i + 1] for i in range(2) for head in heads]
    spare = jnp.zeros((LABEL_ROWS - len(lines), heads[0].shape[1]), F32)
    labels = jnp.concatenate(lines + [spare], axis=0).astype(BF16)
    spots = lax.broadcasted_iota(jnp.int32, (rows, size), 0).astype(F32)
    for c in range(sources):
        placing = jnp.where(heads[c][2:3, :size] == spots, 1.0, 0.0).T.astype(BF16)
        packed = dot_nn(placing, slabs[c, :rows, :]).astype(BF16)
        for n, block in enumerate(blocks):
            block[c * capacity : (c + 1) * capacity, :] = packed[n * capacity : (n + 1) * capacity, :]
    for block in blocks:
        block[sources * capacity :, :] = labels


def regroup(slabs, count, entry_total):
    comps, rows, width = slabs.shape
    size = entry_total // count * (comps - 1) + LABEL_ROWS
    vmem = pl.BlockSpec(memory_space=pltpu.VMEM)
    return pl.pallas_call(
        regroup_kernel,
        out_shape=(jax.ShapeDtypeStruct((size, width), BF16),) * count,
        in_specs=[vmem],
        out_specs=(vmem,) * count,
        compiler_params=pltpu.CompilerParams(vmem_limit_bytes=16 * MIB),
        name="regroup",
    )(slabs)


def regrid_body(count, comp_count, flags, ocean_first, *refs):
    blocks = refs[:count]
    seas = refs[count : count + comp_count]
    weights, surface, mask, forcing, shared, hits, entries, chosen, binned = refs[count + comp_count :]
    sources = comp_count - 1
    rows, cols = mask.shape
    share = forcing.shape[0]
    weight_count = weights.shape[0]
    capacity = (blocks[0].shape[0] - LABEL_ROWS) // sources
    size = count * capacity
    total = sources * size
    width = blocks[0].shape[1]
    for c in range(sources):
        for n in range(count):
            start = c * size + n * capacity
            entries[start : start + capacity, :] = blocks[n][c * capacity : (c + 1) * capacity, :]
    lanes = lax.broadcasted_iota(jnp.int32, (LABEL_ROWS, width), 1) // capacity
    labels = jnp.zeros((LABEL_ROWS, width), F32)
    for n in range(count):
        labels = jnp.where(lanes == n, blocks[n][sources * capacity :, :].astype(F32), labels)
    labels = labels.astype(jnp.int32)
    weight_line = jnp.concatenate([labels[c : c + 1, :size] for c in range(sources)], axis=1)
    target_line = jnp.concatenate(
        [labels[sources + c : sources + c + 1, :size] for c in range(sources)], axis=1
    )
    spots = lax.broadcasted_iota(jnp.int32, (rows, total), 0)
    by_target = jnp.where(target_line == spots, 1.0, 0.0)
    own = by_target[:, :size]
    for c in range(1, sources):
        own = jnp.where(flags[3] == c, by_target[:, c * size : (c + 1) * size], own)
    hits[...] = own.T.astype(BF16)
    by_target = by_target.astype(BF16)
    numbers = lax.broadcasted_iota(jnp.int32, (weight_count, total), 0)
    by_weight = jnp.where(weight_line == numbers, 1.0, 0.0).astype(BF16)
    for g in range(weight_count // BATCH):
        for i in range(BATCH):
            w = g * BATCH + i
            chosen[i * rows : (i + 1) * rows, :] = by_target * by_weight[w : w + 1, :]
        binned[...] = dot_nn(chosen[...], entries[...])
        wide = weights[g * BATCH : (g + 1) * BATCH].reshape(BATCH * cols, cols)
        halves = [
            [
                split_two(binned[i * rows : (i + 1) * rows, f * cols : (f + 1) * cols])
                for i in range(BATCH)
            ]
            for f in range(share)
        ]
        stacked = jnp.concatenate(
            [
                jnp.concatenate([half[k] for half in halves[f]], axis=1)
                for k in range(2)
                for f in range(share)
            ],
            axis=0,
        )
        product = dot_nn(stacked, wide)
        for f in range(share):
            part = product[f * rows : (f + 1) * rows] + product[
                (share + f) * rows : (share + f + 1) * rows
            ]
            forcing[f] = part if g == 0 else forcing[f] + part
    change = ocean_first[flags[3] * share] * forcing[0]
    for f in range(1, share):
        change = change + ocean_first[flags[3] * share + f] * forcing[f]
    sea = jnp.where(flags[0] == 1, seas[sources][...].astype(F32), 0.0)
    for c in range(sources):
        sea = sea + jnp.where(flags[3] == c, seas[c][...].astype(F32), 0.0)
    base = jnp.where(flags[0] == 1, surface[...], 0.0)
    shared[...] = base + jnp.where(sea > 0.5, change, 0.0)


def regrid(flags, ocean_first, blocks, seas, weights, surface, mask):
    comp_count = len(seas)
    sources = comp_count - 1
    rows, cols = mask.shape
    count = len(blocks)
    height, width = blocks[0].shape
    size = (height - LABEL_ROWS) // sources * count
    total = size * sources
    share = width // cols
    weight_count = weights.shape[0]
    vmem = pl.BlockSpec(memory_space=pltpu.VMEM)
    smem = pl.BlockSpec(memory_space=pltpu.SMEM)
    return pl.pallas_call(
        functools.partial(regrid_body, count, comp_count),
        out_shape=(
            jax.ShapeDtypeStruct((share, rows, cols), F32),
            jax.ShapeDtypeStruct((rows, cols), F32),
            jax.ShapeDtypeStruct((size, rows), BF16),
        ),
        in_specs=[smem, smem] + [vmem] * (count + comp_count + 3),
        out_specs=(vmem, vmem, vmem),
        scratch_shapes=[
            pltpu.VMEM((total, width), BF16),
            pltpu.VMEM((BATCH * rows, total), BF16),
            pltpu.VMEM((BATCH * rows, width), F32),
        ],
        compiler_params=pltpu.CompilerParams(vmem_limit_bytes=32 * MIB),
        cost_estimate=pl.CostEstimate(
            flops=2 * weight_count * rows * width * (total + 2 * cols),
            bytes_accessed=2 * MIB,
            transcendentals=0,
        ),
        name="regrid",
    )(flags, ocean_first, *blocks, *seas, weights, surface, mask)


def pick_kernel(count, *refs):
    parts = refs[:count]
    hits, surface = refs[count : count + 2]
    picked = refs[count + 2 :]
    now = parts[0][...]
    for part in parts[1:]:
        now = now + part[...]
    surface[...] = now
    pair = jnp.concatenate(split_two(now), axis=0)
    size = picked[0].shape[0]
    for n in range(len(picked)):
        some = hits[n * size : (n + 1) * size, :]
        picked[n][...] = dot_nn(jnp.concatenate([some, some], axis=1), pair)


def pick(parts, hits, neighbours):
    rows, cols = parts[0].shape
    size = hits.shape[0] // neighbours
    vmem = pl.BlockSpec(memory_space=pltpu.VMEM)
    return pl.pallas_call(
        functools.partial(pick_kernel, len(parts)),
        out_shape=(jax.ShapeDtypeStruct((rows, cols), F32),)
        + (jax.ShapeDtypeStruct((size, cols), F32),) * neighbours,
        in_specs=[vmem] * (len(parts) + 1),
        out_specs=(vmem,) * (1 + neighbours),
        compiler_params=pltpu.CompilerParams(vmem_limit_bytes=16 * MIB),
        name="pick",
    )(*parts, hits)


LINES = 8


def update_kernel(groups, flags, state, *refs):
    parts = refs[:groups]
    mask, ocean_map, out, token, held, table, wide, in_sems, out_sems = refs[groups:]
    rows, cols, levels = state.shape
    share = parts[0].shape[0]
    flux_count = groups * share
    chunks = rows // LINES
    depth = LINES * flux_count
    token[...] = jnp.zeros(token.shape, F32)

    def fetch(q):
        return pltpu.make_async_copy(
            state.at[pl.ds(q * LINES, LINES)], held.at[pl.ds(q * LINES, LINES)], in_sems.at[q]
        )

    def put(q):
        return pltpu.make_async_copy(
            held.at[pl.ds(q * LINES, LINES)], out.at[pl.ds(q * LINES, LINES)], out_sems.at[q]
        )

    @pl.when(flags[0] == 1)
    def ocean():
        for q in range(chunks):
            fetch(q).start()
        table[...] = jnp.zeros(table.shape, F32)
        for line in range(LINES):
            for f in range(flux_count):
                spot = f * LINES + line
                table[spot : spot + 1, line * levels : (line + 1) * levels] = ocean_map[f : f + 1]
        high, low = split_two(table[...])
        wide[:depth] = high
        wide[depth : 2 * depth] = high
        wide[2 * depth :] = low

        def one(q, _):
            start = pl.multiple_of(q * LINES, LINES)
            sea = mask[pl.ds(start, LINES), :] > 0.5
            part = jnp.concatenate(
                [
                    jnp.where(sea, parts[f // share][f % share, pl.ds(start, LINES), :], 0.0)
                    for f in range(flux_count)
                ],
                axis=0,
            )
            rough = part.astype(BF16).astype(F32)
            turned = jnp.concatenate([rough, part - rough, rough], axis=0).T.astype(BF16)
            change = dot_nn(turned, wide[...])
            fetch(q).wait()
            for line in range(LINES):
                held[start + line] += change[:, line * levels : (line + 1) * levels]
            put(q).start()
            return 0

        lax.fori_loop(0, chunks, one, 0, unroll=2)
        for q in range(chunks):
            put(q).wait()


def update(flags, state, parts, mask, ocean_map):
    rows, cols, levels = state.shape
    depth = LINES * ocean_map.shape[0]
    vmem = pl.BlockSpec(memory_space=pltpu.VMEM)
    smem = pl.BlockSpec(memory_space=pltpu.SMEM)
    hbm = pl.BlockSpec(memory_space=pltpu.HBM)
    return pl.pallas_call(
        functools.partial(update_kernel, len(parts)),
        out_shape=(
            jax.ShapeDtypeStruct(state.shape, F32),
            jax.ShapeDtypeStruct((EDGE, levels), F32),
        ),
        in_specs=[smem, hbm] + [vmem] * (len(parts) + 2),
        out_specs=(hbm, vmem),
        input_output_aliases={1: 0},
        scratch_shapes=[
            pltpu.VMEM(state.shape, F32),
            pltpu.VMEM((depth, LINES * levels), F32),
            pltpu.VMEM((3 * depth, LINES * levels), BF16),
            pltpu.SemaphoreType.DMA((rows // LINES,)),
            pltpu.SemaphoreType.DMA((rows // LINES,)),
        ],
        compiler_params=pltpu.CompilerParams(vmem_limit_bytes=24 * MIB),
        cost_estimate=pl.CostEstimate(
            flops=6 * rows * cols * depth * levels,
            bytes_accessed=8 * rows * cols * levels,
            transcendentals=0,
        ),
        name="update",
    )(flags, state, *parts, mask, ocean_map)


def returned_kernel(groups, flags, *refs):
    picked = refs[:groups]
    weight_column, row_line, weights, mask, surface, new_surface, token, out, total = refs[groups:]
    rows, cols = mask.shape
    weight_count = weights.shape[0]

    @pl.when(flags[0] == 1)
    def ocean():
        out[...] = new_surface[...]

    @pl.when(flags[0] == 0)
    def atmosphere():
        values = jnp.concatenate([p[...] for p in picked], axis=0)
        pair = side_by_side(values)
        which = jnp.broadcast_to(weight_column[...], values.shape)
        total[...] = jnp.zeros(values.shape, F32)

        def one(i, _):
            both = jnp.concatenate([weights[2 * i], weights[2 * i + 1]], axis=0)
            images = dot_nt(pair, jnp.concatenate([both, both], axis=1))
            total[...] += jnp.where(which == 2 * i, images[:, :cols], 0.0) + jnp.where(
                which == 2 * i + 1, images[:, cols:], 0.0
            )
            return 0

        lax.fori_loop(0, weight_count // 2, one, 0, unroll=8)
        spots = lax.broadcasted_iota(jnp.int32, (rows, values.shape[0]), 0)
        chosen = jnp.where(jnp.broadcast_to(row_line[...], spots.shape) == spots, 1.0, 0.0).astype(BF16)
        high, low = split_two(total[...])
        back = dot_nn(chosen, high) + dot_nn(chosen, low)
        out[...] = jnp.where(mask[...] > 0.5, back, surface[...])


def returned(flags, picked, weight_column, row_line, weights, mask, surface, new_surface, token):
    rows, cols = mask.shape
    entry_total = weight_column.shape[0]
    vmem = pl.BlockSpec(memory_space=pltpu.VMEM)
    smem = pl.BlockSpec(memory_space=pltpu.SMEM)
    return pl.pallas_call(
        functools.partial(returned_kernel, len(picked)),
        out_shape=jax.ShapeDtypeStruct((rows, cols), F32),
        in_specs=[smem] + [vmem] * (len(picked) + 7),
        out_specs=vmem,
        scratch_shapes=[pltpu.VMEM((entry_total, cols), F32)],
        compiler_params=pltpu.CompilerParams(vmem_limit_bytes=16 * MIB),
        name="returned",
    )(flags, *picked, weight_column, row_line, weights, mask, surface, new_surface, token)


def local(
    state, land_mask, intersection_list, mix_atm, mix_ocn, flux_map, ocean_map, regrid_weights
):
    rows, cols, levels = state.shape
    intersections = intersection_list.shape[2]
    comp_count = lax.axis_size("comp")
    lat_count = lax.axis_size("lat")
    lon_count = lax.axis_size("lon")
    tile_count = lat_count * lon_count
    reach = min(4, lon_count)
    neighbours = 2 * reach
    entry_total = intersections * rows
    capacity = entry_total // neighbours
    comp_index = lax.axis_index("comp")
    lat_index = lax.axis_index("lat")
    tile_index = lat_index * lon_count + lax.axis_index("lon")
    bands = comp_count * lat_count
    ocean_band = (comp_count - 1) * lat_count
    ocean_comp = comp_count - 1
    band = comp_index * lat_count + lat_index
    is_ocean = comp_index == ocean_comp
    upper_valid = (band > 0) & (band != ocean_band)
    lower_valid = (band < bands - 1) & (band != ocean_band - 1)
    flags = jnp.stack([is_ocean, upper_valid, lower_valid, comp_index]).astype(jnp.int32)
    mask = (land_mask == 1).astype(F32)

    def band_shift(value, by, lon_by):
        pairs = []
        for b in range(bands):
            target = b + by
            if 0 <= target < bands and (b >= ocean_band) == (target >= ocean_band):
                for lon in range(lon_count):
                    pairs.append(
                        (b * lon_count + lon, target * lon_count + (lon + lon_by) % lon_count)
                    )
        return lax.ppermute(value, AXES, pairs)

    first_rows, last_rows, sides = take_edges(state)
    up_rows = band_shift(last_rows, 1, 0)
    low_rows = band_shift(first_rows, -1, 0)
    framed = frame_sides(sides, up_rows, low_rows)
    if lon_count == 2:
        left_cols = right_cols = band_shift(framed, 0, 1)
        left_at, right_at = 2, 0
    else:
        left_cols = band_shift(framed[2:], 0, 1)
        right_cols = band_shift(framed[:2], 0, -1)
        left_at, right_at = 0, 0

    entry_list = intersection_list.reshape(entry_total, 3)
    owners = entry_list[:, 0]
    labels = entry_list[:, 2] * rows + entry_list[:, 1]
    offsets = [
        (n // reach * lon_count + n % reach - (reach - 1) // 2) % tile_count
        for n in range(neighbours)
    ]
    distance = (owners - tile_index + tile_count) % tile_count
    hits = distance[:, None] == jnp.array(offsets, jnp.int32)[None, :]
    neighbour_ids = jnp.sum(
        jnp.where(hits, jnp.arange(neighbours, dtype=jnp.int32)[None, :], 0), axis=1
    )
    positions = jnp.arange(entry_total, dtype=jnp.int32)
    earlier = (neighbour_ids[None, :] == neighbour_ids[:, None]) & (
        positions[None, :] < positions[:, None]
    )
    slots = neighbour_ids * capacity + jnp.sum(earlier.astype(jnp.int32), axis=1)
    placing = positions[:, None] == slots[None, :]
    sources = jnp.sum(jnp.where(placing, (positions // intersections)[None, :], 0), axis=1)
    packed_labels = jnp.sum(jnp.where(placing, labels[None, :], 0), axis=1)

    def over_comp(value):
        return lax.all_to_all(value, "comp", split_axis=0, concat_axis=0, tiled=True)

    def shifted_comp(value, shift):
        pairs = [
            (c * tile_count + t, (c + shift) % comp_count * tile_count + t)
            for c in range(comp_count)
            for t in range(tile_count)
        ]
        return lax.ppermute(value, AXES, pairs)

    def over_tiles(value, offset, comps):
        if offset % tile_count == 0:
            return value
        pairs = [
            (c * tile_count + t, c * tile_count + (t + offset) % tile_count)
            for c in range(comps)
            for t in range(tile_count)
        ]
        return lax.ppermute(value, AXES, pairs)

    def from_ocean(value, comp):
        pairs = [
            (ocean_comp * tile_count + t, comp * tile_count + t) for t in range(tile_count)
        ]
        return lax.ppermute(value, AXES, pairs)

    def to_ocean(value, comp):
        pairs = [
            (comp * tile_count + t, ocean_comp * tile_count + t) for t in range(tile_count)
        ]
        return lax.ppermute(value, AXES, pairs)

    label_lines = jnp.stack([packed_labels // rows, packed_labels % rows, sources]).astype(BF16)
    label_lines = jnp.pad(label_lines, ((0, LABEL_ROWS - 3), (0, 0)))

    halos = (up_rows, low_rows, left_cols, right_cols, sides)
    moved = advance(
        flags, label_lines, state, halos, mask, mix_atm, mix_ocn, flux_map.T,
        comp_count, left_at, right_at,
    )
    moved, surface, sea_copy, packed = moved
    slabs = over_comp(packed)
    seas = [from_ocean(sea_copy, c) for c in range(ocean_comp)] + [sea_copy]
    blocks = regroup(slabs, neighbours, entry_total)
    blocks = [over_tiles(blocks[n], offsets[n], comp_count) for n in range(neighbours)]
    forcing, shared, hits = regrid(
        flags, ocean_map[:, 0], blocks, seas, regrid_weights, surface, mask
    )
    parts = [shared] + [shifted_comp(shared, s) for s in range(1, comp_count)]
    parts[1], forcing = lax.optimization_barrier((parts[1], forcing))
    picks = pick(parts, hits, neighbours)
    new_surface, picked = picks[0], picks[1:]
    arrived = [over_tiles(picked[n], -offsets[n], ocean_comp) for n in reversed(range(neighbours))]
    arrived = arrived[::-1]
    fields = [to_ocean(forcing, c) for c in range(ocean_comp)] + [forcing]
    final_state, token = update(flags, moved, fields, mask, ocean_map)
    weight_column = (packed_labels // rows)[:, None]
    surface_out = returned(
        flags, arrived, weight_column, sources[None, :], regrid_weights, mask, surface, new_surface,
        token,
    )
    return (final_state, surface_out)


def solution(mesh):
    placed = (
        P(("comp", "lat"), "lon", None),
        P(("comp", "lat"), "lon"),
        P(("comp", "lat"), "lon", None, None),
        P(),
        P(),
        P(),
        P(),
        P(),
    )
    return jax.shard_map(
        local,
        mesh=mesh,
        in_specs=placed,
        out_specs=(P(("comp", "lat"), "lon", None), P(("comp", "lat"), "lon")),
        check_vma=False,
    )
```

```python
import functools

import jax
import jax.numpy as jnp
from jax import lax
from jax.experimental import pallas as pl
from jax.experimental.pallas import tpu as pltpu
from jax.sharding import PartitionSpec as P

SMOOTHING = 0.2
PHYSICS = 0.5
MIB = 1024 * 1024
F32 = jnp.float32
BF16 = jnp.bfloat16
EDGE = 8
AHEAD = 4
CHUNK = 8
AXES = ("comp", "lat", "lon")


def split_two(x):
    high = x.astype(BF16)
    low = (x - high.astype(F32)).astype(BF16)
    return high, low


def side_by_side(x):
    return jnp.concatenate(split_two(x), axis=1)


def dot_nt(a, b):
    return lax.dot_general(a, b, (((1,), (1,)), ((), ())), preferred_element_type=F32)


def dot_nn(a, b):
    return jnp.dot(a, b, preferred_element_type=F32)


def edges_kernel(state, first_rows, last_rows, sides, top, bottom, left, right, sems):
    rows, cols, _ = state.shape
    copies = [
        pltpu.make_async_copy(state.at[pl.ds(0, 2)], top, sems.at[0]),
        pltpu.make_async_copy(state.at[pl.ds(rows - 2, 2)], bottom, sems.at[1]),
        pltpu.make_async_copy(state.at[:, pl.ds(0, EDGE)], left, sems.at[2]),
        pltpu.make_async_copy(state.at[:, pl.ds(cols - EDGE, EDGE)], right, sems.at[3]),
    ]
    for copy in copies:
        copy.start()
    for copy in copies:
        copy.wait()
    first_rows[...] = top[...].astype(BF16)
    last_rows[...] = bottom[...].astype(BF16)
    for i in range(2):
        sides[i] = left[:, i, :]
        sides[2 + i] = right[:, EDGE - 2 + i, :]


def take_edges(state):
    rows, cols, levels = state.shape
    slab = jax.ShapeDtypeStruct((2, cols, levels), BF16)
    side = jax.ShapeDtypeStruct((4, rows, levels), F32)
    vmem = pl.BlockSpec(memory_space=pltpu.VMEM)
    return pl.pallas_call(
        edges_kernel,
        out_shape=(slab, slab, side),
        in_specs=[pl.BlockSpec(memory_space=pltpu.HBM)],
        out_specs=(vmem,) * 3,
        scratch_shapes=[
            pltpu.VMEM((2, cols, levels), F32),
            pltpu.VMEM((2, cols, levels), F32),
            pltpu.VMEM((rows, EDGE, levels), F32),
            pltpu.VMEM((rows, EDGE, levels), F32),
            pltpu.SemaphoreType.DMA((4,)),
        ],
        compiler_params=pltpu.CompilerParams(vmem_limit_bytes=50 * MIB),
        name="edges",
    )(state)


def frame_kernel(sides, up_rows, low_rows, framed):
    _, rows, levels = sides.shape
    cols = up_rows.shape[1]
    framed[...] = jnp.zeros(framed.shape, F32)
    above = up_rows[1].astype(F32)
    below = low_rows[0].astype(F32)
    for i, col in enumerate((0, 1, cols - 2, cols - 1)):
        framed[i, EDGE : EDGE + rows, :] = sides[i]
        framed[i, EDGE - 1 : EDGE, :] = above[col : col + 1, :]
        framed[i, EDGE + rows : EDGE + rows + 1, :] = below[col : col + 1, :]


def frame_sides(sides, up_rows, low_rows):
    count, rows, levels = sides.shape
    vmem = pl.BlockSpec(memory_space=pltpu.VMEM)
    return pl.pallas_call(
        frame_kernel,
        out_shape=jax.ShapeDtypeStruct((count, rows + 2 * EDGE, levels), F32),
        in_specs=[vmem] * 3,
        out_specs=vmem,
        compiler_params=pltpu.CompilerParams(vmem_limit_bytes=16 * MIB),
        name="frame",
    )(sides, up_rows, low_rows)


def advance_kernel(comp_count, left_at, right_at, *refs):
    (flags, labels, state, up_rows, low_rows, left_in, right_in, own_sides) = refs[:8]
    (mask, mix_atm, mix_ocn, flux_map) = refs[8:12]
    out, surface, sea_copy, packed = refs[12:16]
    (values, moved, halo_moved, smooth, pairs, mixed, later_smooth, later_pairs, later_mixed) = refs[16:25]
    (weights, flux_weights, flux_pairs, fluxes, staged, top, in_sems, out_sems) = refs[25:]
    left_cols = left_in.at[left_at : left_at + 2]
    right_cols = right_in.at[right_at : right_at + 2]
    first = (smooth, pairs, mixed)
    second = (later_smooth, later_pairs, later_mixed)
    rows, cols, levels = state.shape
    chunks = rows // CHUNK
    inner = pl.ds(EDGE, cols)
    flux_count = flux_map.shape[0]

    def fetch(q):
        return pltpu.make_async_copy(
            state.at[pl.ds(q * CHUNK, CHUNK)],
            values.at[pl.ds(q * CHUNK + 2, CHUNK), inner],
            in_sems.at[q],
        )

    def put(q, slot):
        return pltpu.make_async_copy(
            staged.at[slot], out.at[pl.ds(q * CHUNK, CHUNK)], out_sems.at[slot]
        )

    def begin(q, _):
        fetch(q).start()
        return 0

    lax.fori_loop(0, AHEAD, begin, 0)
    ocean = flags[0] == 1
    mix = jnp.where(ocean, mix_ocn[...], mix_atm[...])
    mix_high, mix_low = split_two(mix)
    weights[:levels, :levels] = mix_high
    weights[levels:, :levels] = mix_high
    weights[:levels, levels:] = mix_low
    weights[levels:, levels:] = mix_low
    sea_copy[...] = mask[...].astype(BF16)
    map_high, map_low = split_two(flux_map[...])
    flux_weights[...] = jnp.concatenate(
        [
            jnp.concatenate([map_high.astype(F32), map_high.astype(F32)], axis=1),
            jnp.concatenate([map_low.astype(F32), map_low.astype(F32)], axis=1),
        ],
        axis=0,
    ).astype(BF16)
    values[0:2, EDGE : EDGE + cols, :] = up_rows[...].astype(F32)
    values[rows + 2 : rows + 4, EDGE : EDGE + cols, :] = low_rows[...].astype(F32)
    for r, i in ((1, EDGE - 1), (rows + 2, EDGE + rows)):
        values[r, EDGE - 1 : EDGE, :] = left_cols[1, i : i + 1, :]
        values[r, EDGE + cols : EDGE + cols + 1, :] = right_cols[0, i : i + 1, :]

    def side_cells(start, count):
        for row in range(count):
            values[start + row + 2, EDGE - 1 : EDGE, :] = left_cols[1, pl.ds(start + row + EDGE, 1), :]
            values[start + row + 2, EDGE + cols : EDGE + cols + 1, :] = right_cols[
                0, pl.ds(start + row + EDGE, 1), :
            ]

    def moved_sides(start, count):
        for row in range(count):
            moved[start + row + 1, EDGE - 1 : EDGE, :] = halo_moved[0, pl.ds(start + row, 1), :]
            moved[start + row + 1, EDGE + cols : EDGE + cols + 1, :] = halo_moved[
                1, pl.ds(start + row, 1), :
            ]

    def stage(refs, row, total):
        line = SMOOTHING * total
        refs[0][row] = line
        refs[1][row * cols : (row + 1) * cols, :] = side_by_side(line)

    def stage_rows(refs, ref, start, count):
        for row in range(count):
            i = start + row
            here = ref[i, EDGE : EDGE + cols, :] + (
                ref[i - 1, EDGE : EDGE + cols, :] + ref[i + 1, EDGE : EDGE + cols, :]
            )
            near = ref[i, EDGE - 1 : EDGE - 1 + cols, :] + ref[i, EDGE + 1 : EDGE + 1 + cols, :]
            stage(refs, row, here + near)

    def note_top(q, lines):
        shape = (cols // EDGE, EDGE, levels)
        lanes = lax.broadcasted_iota(jnp.int32, (1, EDGE, levels), 2)
        kept = lines[0].reshape(shape)
        for row in range(1, CHUNK):
            moved_over = pltpu.roll(lines[row], row, 1).reshape(shape)
            kept = jnp.where(jnp.broadcast_to(lanes == row, shape), moved_over, kept)
        turned = pltpu.roll(kept.reshape(cols, levels), q * CHUNK, 1)
        here = lax.broadcasted_iota(jnp.int32, (cols, levels), 1) // CHUNK == q
        top[...] = jnp.where(here, turned, top[...])

    def mix_rows(refs, count):
        refs[2][: count * cols, :] = dot_nn(refs[1][: count * cols, :], weights[...])

    def finish(refs, row):
        part = refs[2][row * cols : (row + 1) * cols, :]
        return refs[0][row] + PHYSICS * jnp.tanh(part[:, :levels] + part[:, levels:])

    @pl.when(jnp.logical_not(ocean))
    def atmosphere():
        nearest = (left_cols.at[1], right_cols.at[0])
        beyond = (left_cols.at[0], right_cols.at[1])
        within = (own_sides.at[0], own_sides.at[3])
        for s in range(2):
            total = (
                nearest[s][EDGE : EDGE + rows, :]
                + nearest[s][EDGE - 1 : EDGE - 1 + rows, :]
                + nearest[s][EDGE + 1 : EDGE + 1 + rows, :]
            )
            stage(first, s, total + (beyond[s][EDGE : EDGE + rows, :] + within[s][...]))
        mix_rows(first, 2)
        for s in range(2):
            halo_moved[s] = finish(first, s)

        side_cells(0, 1)
        fetch(0).wait()
        fetch(1).wait()
        stage_rows(second, values, 1, 2)
        mix_rows(second, 2)
        for row in range(2):
            moved[row, EDGE : EDGE + cols, :] = finish(second, row)

        @pl.when(flags[1] == 0)
        def _():
            moved[0, EDGE : EDGE + cols, :] = jnp.zeros((cols, levels), F32)

        def begin_first(q):
            side_cells(jnp.minimum(q * CHUNK + 1, rows - CHUNK), CHUNK)
            stage_rows(first, values, q * CHUNK + 3, CHUNK)
            mix_rows(first, CHUNK)

        def end_first(q):
            for row in range(CHUNK):
                moved[q * CHUNK + row + 2, EDGE : EDGE + cols, :] = finish(first, row)

        def begin_second(q):
            moved_sides(q * CHUNK, CHUNK)
            stage_rows(second, moved, q * CHUNK + 1, CHUNK)

        def end_second(q, slot):
            for row in range(CHUNK):
                line = finish(second, row)
                staged[slot, row] = line
                both = line + moved[q * CHUNK + row + 1, EDGE : EDGE + cols, :]
                flux_pairs[row * cols : (row + 1) * cols, :] = side_by_side(both)
            put(q, slot).start()
            note_top(q, [staged[slot, row] for row in range(CHUNK)])

        def sum_fluxes(q):
            flux = dot_nt(flux_weights[...], flux_pairs[...])
            flux = flux[:flux_count] + flux[flux_count:]
            for row in range(CHUNK):
                r = q * CHUNK + row
                block = PHYSICS * flux[:, row * cols : (row + 1) * cols]
                sea = jnp.broadcast_to(mask[pl.ds(r, 1), :], block.shape)
                block = jnp.where(sea > 0.5, block, 0.0)
                fluxes[pl.ds(pl.multiple_of(r * flux_count, flux_count), flux_count), :] = block

        fetch(AHEAD).start()
        flux_pairs[...] = jnp.zeros(flux_pairs.shape, BF16)
        begin_first(0)
        end_first(0)

        def one_chunk(q, _):
            @pl.when(q + 1 < chunks)
            def _():
                fetch(q + 1).wait()

            @pl.when(q + AHEAD < chunks)
            def _():
                fetch(q + AHEAD).start()

            slot = (q - 1) % 2

            @pl.when(q >= 3)
            def _():
                put(q - 3, slot).wait()

            sum_fluxes(jnp.maximum(q - 2, 0))
            begin_first(q)
            begin_second(q - 1)
            mix_rows(second, CHUNK)
            end_first(q)
            end_second(q - 1, slot)
            return 0

        lax.fori_loop(1, chunks, one_chunk, 0)

        @pl.when(flags[2] == 0)
        def _():
            moved[rows + 1, EDGE : EDGE + cols, :] = jnp.zeros((cols, levels), F32)

        last = chunks - 1
        put(last - 2, last % 2).wait()
        sum_fluxes(last - 1)
        begin_second(last)
        mix_rows(second, CHUNK)
        end_second(last, last % 2)
        sum_fluxes(last)
        share = flux_count // comp_count
        for c in range(comp_count):
            for f in range(share):
                field = fluxes[pl.ds(c * share + f, rows, stride=flux_count), :]
                packed[c, :rows, f * cols : (f + 1) * cols] = field.astype(BF16)
            packed[c, rows:, :] = labels[...]
        put(last - 1, (last - 1) % 2).wait()
        put(last, last % 2).wait()
        surface[...] = top[...].T

    @pl.when(ocean)
    def sea_side():
        fetch(0).wait()
        lanes = lax.broadcasted_iota(jnp.int32, (CHUNK, CHUNK * levels), 1) // levels
        lines = lax.broadcasted_iota(jnp.int32, (CHUNK, CHUNK * levels), 0)
        spreader = jnp.where(lanes == lines, 1.0, 0.0).astype(F32)

        def one_chunk(q, _):
            base = q * CHUNK

            @pl.when(q + 1 < chunks)
            def _():
                fetch(q + 1).wait()

            @pl.when(q + AHEAD < chunks)
            def _():
                fetch(q + AHEAD).start()

            side_cells(base, CHUNK)
            stage_rows(first, values, base + 2, CHUNK)
            mix_rows(first, CHUNK)
            slot = q % 2

            @pl.when(q >= 2)
            def _():
                put(q - 2, slot).wait()

            sea = dot_nn(mask[pl.ds(pl.multiple_of(base, CHUNK), CHUNK), :].T, spreader)
            for row in range(CHUNK):
                chosen = sea[:, row * levels : (row + 1) * levels] > 0.5
                before = values[base + row + 2, EDGE : EDGE + cols, :]
                staged[slot, row] = jnp.where(chosen, finish(first, row), before)
            put(q, slot).start()
            note_top(q, [staged[slot, row] for row in range(CHUNK)])
            return 0

        lax.fori_loop(0, chunks, one_chunk, 0)
        put(chunks - 2, (chunks - 2) % 2).wait()
        put(chunks - 1, (chunks - 1) % 2).wait()
        surface[...] = top[...].T
        packed[...] = jnp.zeros(packed.shape, BF16)


def advance(
    flags, labels, state, halos, mask, mix_atm, mix_ocn, flux_map_t, comp_count, left_at, right_at
):
    rows, cols, levels = state.shape
    fluxes = flux_map_t.shape[0]
    vmem = pl.BlockSpec(memory_space=pltpu.VMEM)
    smem = pl.BlockSpec(memory_space=pltpu.SMEM)
    hbm = pl.BlockSpec(memory_space=pltpu.HBM)
    entry = jax.ShapeDtypeStruct(
        (comp_count, rows + labels.shape[0], fluxes // comp_count * cols), BF16
    )
    cells = rows * cols
    return pl.pallas_call(
        functools.partial(advance_kernel, comp_count, left_at, right_at),
        out_shape=(
            jax.ShapeDtypeStruct(state.shape, F32),
            jax.ShapeDtypeStruct((rows, cols), F32),
            jax.ShapeDtypeStruct((rows, cols), BF16),
            entry,
        ),
        in_specs=[smem, vmem, hbm] + [vmem] * (len(halos) + 4),
        out_specs=(hbm, vmem, vmem, vmem),
        scratch_shapes=[
            pltpu.VMEM((rows + 4, cols + 2 * EDGE, levels), F32),
            pltpu.VMEM((rows + 2, cols + 2 * EDGE, levels), F32),
            pltpu.VMEM((2, rows, levels), F32),
            pltpu.VMEM((CHUNK, cols, levels), F32),
            pltpu.VMEM((CHUNK * cols, 2 * levels), BF16),
            pltpu.VMEM((CHUNK * cols, 2 * levels), F32),
            pltpu.VMEM((CHUNK, cols, levels), F32),
            pltpu.VMEM((CHUNK * cols, 2 * levels), BF16),
            pltpu.VMEM((CHUNK * cols, 2 * levels), F32),
            pltpu.VMEM((2 * levels, 2 * levels), BF16),
            pltpu.VMEM((2 * fluxes, 2 * levels), BF16),
            pltpu.VMEM((CHUNK * cols, 2 * levels), BF16),
            pltpu.VMEM((rows * fluxes, cols), F32),
            pltpu.VMEM((2, CHUNK, cols, levels), F32),
            pltpu.VMEM((cols, levels), F32),
            pltpu.SemaphoreType.DMA((rows // CHUNK,)),
            pltpu.SemaphoreType.DMA((2,)),
        ],
        compiler_params=pltpu.CompilerParams(vmem_limit_bytes=48 * MIB),
        cost_estimate=pl.CostEstimate(
            flops=8 * cells * levels * levels, bytes_accessed=8 * cells * levels, transcendentals=0
        ),
        name="advance",
    )(flags, labels, state, *halos, mask, mix_atm, mix_ocn, flux_map_t)


BATCH = 16
LABEL_ROWS = 16


def regroup_kernel(slabs, *blocks):
    sources = slabs.shape[0] - 1
    capacity = (blocks[0].shape[0] - LABEL_ROWS) // sources
    rows = slabs.shape[1] - LABEL_ROWS
    size = len(blocks) * capacity
    heads = [slabs[c, rows:, :].astype(F32) for c in range(sources)]
    lines = [head[i : i + 1] for i in range(2) for head in heads]
    spare = jnp.zeros((LABEL_ROWS - len(lines), heads[0].shape[1]), F32)
    labels = jnp.concatenate(lines + [spare], axis=0).astype(BF16)
    spots = lax.broadcasted_iota(jnp.int32, (rows, size), 0).astype(F32)
    for c in range(sources):
        placing = jnp.where(heads[c][2:3, :size] == spots, 1.0, 0.0).T.astype(BF16)
        packed = dot_nn(placing, slabs[c, :rows, :]).astype(BF16)
        for n, block in enumerate(blocks):
            block[c * capacity : (c + 1) * capacity, :] = packed[n * capacity : (n + 1) * capacity, :]
    for block in blocks:
        block[sources * capacity :, :] = labels


def regroup(slabs, count, entry_total):
    comps, rows, width = slabs.shape
    size = entry_total // count * (comps - 1) + LABEL_ROWS
    vmem = pl.BlockSpec(memory_space=pltpu.VMEM)
    return pl.pallas_call(
        regroup_kernel,
        out_shape=(jax.ShapeDtypeStruct((size, width), BF16),) * count,
        in_specs=[vmem],
        out_specs=(vmem,) * count,
        compiler_params=pltpu.CompilerParams(vmem_limit_bytes=16 * MIB),
        name="regroup",
    )(slabs)


def regrid_body(count, comp_count, flags, ocean_first, *refs):
    blocks = refs[:count]
    seas = refs[count : count + comp_count]
    weights, surface, mask, forcing, shared, hits, entries, chosen, binned = refs[count + comp_count :]
    sources = comp_count - 1
    rows, cols = mask.shape
    share = forcing.shape[0]
    weight_count = weights.shape[0]
    capacity = (blocks[0].shape[0] - LABEL_ROWS) // sources
    size = count * capacity
    total = sources * size
    width = blocks[0].shape[1]
    for c in range(sources):
        for n in range(count):
            start = c * size + n * capacity
            entries[start : start + capacity, :] = blocks[n][c * capacity : (c + 1) * capacity, :]
    lanes = lax.broadcasted_iota(jnp.int32, (LABEL_ROWS, width), 1) // capacity
    labels = jnp.zeros((LABEL_ROWS, width), F32)
    for n in range(count):
        labels = jnp.where(lanes == n, blocks[n][sources * capacity :, :].astype(F32), labels)
    labels = labels.astype(jnp.int32)
    weight_line = jnp.concatenate([labels[c : c + 1, :size] for c in range(sources)], axis=1)
    target_line = jnp.concatenate(
        [labels[sources + c : sources + c + 1, :size] for c in range(sources)], axis=1
    )
    spots = lax.broadcasted_iota(jnp.int32, (rows, total), 0)
    by_target = jnp.where(target_line == spots, 1.0, 0.0)
    own = by_target[:, :size]
    for c in range(1, sources):
        own = jnp.where(flags[3] == c, by_target[:, c * size : (c + 1) * size], own)
    hits[...] = own.T.astype(BF16)
    by_target = by_target.astype(BF16)
    numbers = lax.broadcasted_iota(jnp.int32, (weight_count, total), 0)
    by_weight = jnp.where(weight_line == numbers, 1.0, 0.0).astype(BF16)
    for g in range(weight_count // BATCH):
        for i in range(BATCH):
            w = g * BATCH + i
            chosen[i * rows : (i + 1) * rows, :] = by_target * by_weight[w : w + 1, :]
        binned[...] = dot_nn(chosen[...], entries[...])
        wide = weights[g * BATCH : (g + 1) * BATCH].reshape(BATCH * cols, cols)
        halves = [
            [
                split_two(binned[i * rows : (i + 1) * rows, f * cols : (f + 1) * cols])
                for i in range(BATCH)
            ]
            for f in range(share)
        ]
        stacked = jnp.concatenate(
            [
                jnp.concatenate([half[k] for half in halves[f]], axis=1)
                for k in range(2)
                for f in range(share)
            ],
            axis=0,
        )
        product = dot_nn(stacked, wide)
        for f in range(share):
            part = product[f * rows : (f + 1) * rows] + product[
                (share + f) * rows : (share + f + 1) * rows
            ]
            forcing[f] = part if g == 0 else forcing[f] + part
    change = ocean_first[flags[3] * share] * forcing[0]
    for f in range(1, share):
        change = change + ocean_first[flags[3] * share + f] * forcing[f]
    sea = jnp.where(flags[0] == 1, seas[sources][...].astype(F32), 0.0)
    for c in range(sources):
        sea = sea + jnp.where(flags[3] == c, seas[c][...].astype(F32), 0.0)
    base = jnp.where(flags[0] == 1, surface[...], 0.0)
    shared[...] = base + jnp.where(sea > 0.5, change, 0.0)


def regrid(flags, ocean_first, blocks, seas, weights, surface, mask):
    comp_count = len(seas)
    sources = comp_count - 1
    rows, cols = mask.shape
    count = len(blocks)
    height, width = blocks[0].shape
    size = (height - LABEL_ROWS) // sources * count
    total = size * sources
    share = width // cols
    weight_count = weights.shape[0]
    vmem = pl.BlockSpec(memory_space=pltpu.VMEM)
    smem = pl.BlockSpec(memory_space=pltpu.SMEM)
    return pl.pallas_call(
        functools.partial(regrid_body, count, comp_count),
        out_shape=(
            jax.ShapeDtypeStruct((share, rows, cols), F32),
            jax.ShapeDtypeStruct((rows, cols), F32),
            jax.ShapeDtypeStruct((size, rows), BF16),
        ),
        in_specs=[smem, smem] + [vmem] * (count + comp_count + 3),
        out_specs=(vmem, vmem, vmem),
        scratch_shapes=[
            pltpu.VMEM((total, width), BF16),
            pltpu.VMEM((BATCH * rows, total), BF16),
            pltpu.VMEM((BATCH * rows, width), F32),
        ],
        compiler_params=pltpu.CompilerParams(vmem_limit_bytes=32 * MIB),
        cost_estimate=pl.CostEstimate(
            flops=2 * weight_count * rows * width * (total + 2 * cols),
            bytes_accessed=2 * MIB,
            transcendentals=0,
        ),
        name="regrid",
    )(flags, ocean_first, *blocks, *seas, weights, surface, mask)


def pick_kernel(count, *refs):
    parts = refs[:count]
    hits, surface = refs[count : count + 2]
    picked = refs[count + 2 :]
    now = parts[0][...]
    for part in parts[1:]:
        now = now + part[...]
    surface[...] = now
    pair = jnp.concatenate(split_two(now), axis=0)
    size = picked[0].shape[0]
    for n in range(len(picked)):
        some = hits[n * size : (n + 1) * size, :]
        picked[n][...] = dot_nn(jnp.concatenate([some, some], axis=1), pair)


def pick(parts, hits, neighbours):
    rows, cols = parts[0].shape
    size = hits.shape[0] // neighbours
    vmem = pl.BlockSpec(memory_space=pltpu.VMEM)
    return pl.pallas_call(
        functools.partial(pick_kernel, len(parts)),
        out_shape=(jax.ShapeDtypeStruct((rows, cols), F32),)
        + (jax.ShapeDtypeStruct((size, cols), F32),) * neighbours,
        in_specs=[vmem] * (len(parts) + 1),
        out_specs=(vmem,) * (1 + neighbours),
        compiler_params=pltpu.CompilerParams(vmem_limit_bytes=16 * MIB),
        name="pick",
    )(*parts, hits)


LINES = 8


def update_kernel(groups, flags, state, *refs):
    parts = refs[:groups]
    mask, ocean_map, out, token, held, table, wide, in_sems, out_sems = refs[groups:]
    rows, cols, levels = state.shape
    share = parts[0].shape[0]
    flux_count = groups * share
    chunks = rows // LINES
    depth = LINES * flux_count
    token[...] = jnp.zeros(token.shape, F32)

    def fetch(q):
        return pltpu.make_async_copy(
            state.at[pl.ds(q * LINES, LINES)], held.at[pl.ds(q * LINES, LINES)], in_sems.at[q]
        )

    def put(q):
        return pltpu.make_async_copy(
            held.at[pl.ds(q * LINES, LINES)], out.at[pl.ds(q * LINES, LINES)], out_sems.at[q]
        )

    @pl.when(flags[0] == 1)
    def ocean():
        for q in range(chunks):
            fetch(q).start()
        table[...] = jnp.zeros(table.shape, F32)
        for line in range(LINES):
            for f in range(flux_count):
                spot = f * LINES + line
                table[spot : spot + 1, line * levels : (line + 1) * levels] = ocean_map[f : f + 1]
        high, low = split_two(table[...])
        wide[:depth] = high
        wide[depth : 2 * depth] = high
        wide[2 * depth :] = low

        def one(q, _):
            start = pl.multiple_of(q * LINES, LINES)
            sea = mask[pl.ds(start, LINES), :] > 0.5
            part = jnp.concatenate(
                [
                    jnp.where(sea, parts[f // share][f % share, pl.ds(start, LINES), :], 0.0)
                    for f in range(flux_count)
                ],
                axis=0,
            )
            rough = part.astype(BF16).astype(F32)
            turned = jnp.concatenate([rough, part - rough, rough], axis=0).T.astype(BF16)
            change = dot_nn(turned, wide[...])
            fetch(q).wait()
            for line in range(LINES):
                held[start + line] += change[:, line * levels : (line + 1) * levels]
            put(q).start()
            return 0

        lax.fori_loop(0, chunks, one, 0, unroll=2)
        for q in range(chunks):
            put(q).wait()


def update(flags, state, parts, mask, ocean_map):
    rows, cols, levels = state.shape
    depth = LINES * ocean_map.shape[0]
    vmem = pl.BlockSpec(memory_space=pltpu.VMEM)
    smem = pl.BlockSpec(memory_space=pltpu.SMEM)
    hbm = pl.BlockSpec(memory_space=pltpu.HBM)
    return pl.pallas_call(
        functools.partial(update_kernel, len(parts)),
        out_shape=(
            jax.ShapeDtypeStruct(state.shape, F32),
            jax.ShapeDtypeStruct((EDGE, levels), F32),
        ),
        in_specs=[smem, hbm] + [vmem] * (len(parts) + 2),
        out_specs=(hbm, vmem),
        input_output_aliases={1: 0},
        scratch_shapes=[
            pltpu.VMEM(state.shape, F32),
            pltpu.VMEM((depth, LINES * levels), F32),
            pltpu.VMEM((3 * depth, LINES * levels), BF16),
            pltpu.SemaphoreType.DMA((rows // LINES,)),
            pltpu.SemaphoreType.DMA((rows // LINES,)),
        ],
        compiler_params=pltpu.CompilerParams(vmem_limit_bytes=24 * MIB),
        cost_estimate=pl.CostEstimate(
            flops=6 * rows * cols * depth * levels,
            bytes_accessed=8 * rows * cols * levels,
            transcendentals=0,
        ),
        name="update",
    )(flags, state, *parts, mask, ocean_map)


def returned_kernel(groups, flags, *refs):
    picked = refs[:groups]
    weight_column, row_line, weights, mask, surface, new_surface, token, out, total = refs[groups:]
    rows, cols = mask.shape
    weight_count = weights.shape[0]

    @pl.when(flags[0] == 1)
    def ocean():
        out[...] = new_surface[...]

    @pl.when(flags[0] == 0)
    def atmosphere():
        values = jnp.concatenate([p[...] for p in picked], axis=0)
        pair = side_by_side(values)
        which = jnp.broadcast_to(weight_column[...], values.shape)
        total[...] = jnp.zeros(values.shape, F32)

        def one(i, _):
            both = jnp.concatenate([weights[2 * i], weights[2 * i + 1]], axis=0)
            images = dot_nt(pair, jnp.concatenate([both, both], axis=1))
            total[...] += jnp.where(which == 2 * i, images[:, :cols], 0.0) + jnp.where(
                which == 2 * i + 1, images[:, cols:], 0.0
            )
            return 0

        lax.fori_loop(0, weight_count // 2, one, 0, unroll=8)
        spots = lax.broadcasted_iota(jnp.int32, (rows, values.shape[0]), 0)
        chosen = jnp.where(jnp.broadcast_to(row_line[...], spots.shape) == spots, 1.0, 0.0).astype(BF16)
        high, low = split_two(total[...])
        back = dot_nn(chosen, high) + dot_nn(chosen, low)
        out[...] = jnp.where(mask[...] > 0.5, back, surface[...])


def returned(flags, picked, weight_column, row_line, weights, mask, surface, new_surface, token):
    rows, cols = mask.shape
    entry_total = weight_column.shape[0]
    vmem = pl.BlockSpec(memory_space=pltpu.VMEM)
    smem = pl.BlockSpec(memory_space=pltpu.SMEM)
    return pl.pallas_call(
        functools.partial(returned_kernel, len(picked)),
        out_shape=jax.ShapeDtypeStruct((rows, cols), F32),
        in_specs=[smem] + [vmem] * (len(picked) + 7),
        out_specs=vmem,
        scratch_shapes=[pltpu.VMEM((entry_total, cols), F32)],
        compiler_params=pltpu.CompilerParams(vmem_limit_bytes=16 * MIB),
        name="returned",
    )(flags, *picked, weight_column, row_line, weights, mask, surface, new_surface, token)


def local(
    state, land_mask, intersection_list, mix_atm, mix_ocn, flux_map, ocean_map, regrid_weights
):
    rows, cols, levels = state.shape
    intersections = intersection_list.shape[2]
    comp_count = lax.axis_size("comp")
    lat_count = lax.axis_size("lat")
    lon_count = lax.axis_size("lon")
    tile_count = lat_count * lon_count
    reach = min(4, lon_count)
    neighbours = 2 * reach
    entry_total = intersections * rows
    capacity = entry_total // neighbours
    comp_index = lax.axis_index("comp")
    lat_index = lax.axis_index("lat")
    tile_index = lat_index * lon_count + lax.axis_index("lon")
    bands = comp_count * lat_count
    ocean_band = (comp_count - 1) * lat_count
    ocean_comp = comp_count - 1
    band = comp_index * lat_count + lat_index
    is_ocean = comp_index == ocean_comp
    upper_valid = (band > 0) & (band != ocean_band)
    lower_valid = (band < bands - 1) & (band != ocean_band - 1)
    flags = jnp.stack([is_ocean, upper_valid, lower_valid, comp_index]).astype(jnp.int32)
    mask = (land_mask == 1).astype(F32)

    def band_shift(value, by, lon_by):
        pairs = []
        for b in range(bands):
            target = b + by
            if 0 <= target < bands and (b >= ocean_band) == (target >= ocean_band):
                for lon in range(lon_count):
                    pairs.append(
                        (b * lon_count + lon, target * lon_count + (lon + lon_by) % lon_count)
                    )
        return lax.ppermute(value, AXES, pairs)

    first_rows, last_rows, sides = take_edges(state)
    up_rows = band_shift(last_rows, 1, 0)
    low_rows = band_shift(first_rows, -1, 0)
    framed = frame_sides(sides, up_rows, low_rows)
    if lon_count == 2:
        left_cols = right_cols = band_shift(framed, 0, 1)
        left_at, right_at = 2, 0
    else:
        left_cols = band_shift(framed[2:], 0, 1)
        right_cols = band_shift(framed[:2], 0, -1)
        left_at, right_at = 0, 0

    entry_list = intersection_list.reshape(entry_total, 3)
    owners = entry_list[:, 0]
    labels = entry_list[:, 2] * rows + entry_list[:, 1]
    offsets = [
        (n // reach * lon_count + n % reach - (reach - 1) // 2) % tile_count
        for n in range(neighbours)
    ]
    distance = (owners - tile_index + tile_count) % tile_count
    hits = distance[:, None] == jnp.array(offsets, jnp.int32)[None, :]
    neighbour_ids = jnp.sum(
        jnp.where(hits, jnp.arange(neighbours, dtype=jnp.int32)[None, :], 0), axis=1
    )
    positions = jnp.arange(entry_total, dtype=jnp.int32)
    earlier = (neighbour_ids[None, :] == neighbour_ids[:, None]) & (
        positions[None, :] < positions[:, None]
    )
    slots = neighbour_ids * capacity + jnp.sum(earlier.astype(jnp.int32), axis=1)
    placing = positions[:, None] == slots[None, :]
    sources = jnp.sum(jnp.where(placing, (positions // intersections)[None, :], 0), axis=1)
    packed_labels = jnp.sum(jnp.where(placing, labels[None, :], 0), axis=1)

    def over_comp(value):
        return lax.all_to_all(value, "comp", split_axis=0, concat_axis=0, tiled=True)

    def shifted_comp(value, shift):
        pairs = [
            (c * tile_count + t, (c + shift) % comp_count * tile_count + t)
            for c in range(comp_count)
            for t in range(tile_count)
        ]
        return lax.ppermute(value, AXES, pairs)

    def over_tiles(value, offset, comps):
        if offset % tile_count == 0:
            return value
        pairs = [
            (c * tile_count + t, c * tile_count + (t + offset) % tile_count)
            for c in range(comps)
            for t in range(tile_count)
        ]
        return lax.ppermute(value, AXES, pairs)

    def from_ocean(value, comp):
        pairs = [
            (ocean_comp * tile_count + t, comp * tile_count + t) for t in range(tile_count)
        ]
        return lax.ppermute(value, AXES, pairs)

    def to_ocean(value, comp):
        pairs = [
            (comp * tile_count + t, ocean_comp * tile_count + t) for t in range(tile_count)
        ]
        return lax.ppermute(value, AXES, pairs)

    label_lines = jnp.stack([packed_labels // rows, packed_labels % rows, sources]).astype(BF16)
    label_lines = jnp.pad(label_lines, ((0, LABEL_ROWS - 3), (0, 0)))

    halos = (up_rows, low_rows, left_cols, right_cols, sides)
    moved = advance(
        flags, label_lines, state, halos, mask, mix_atm, mix_ocn, flux_map.T,
        comp_count, left_at, right_at,
    )
    moved, surface, sea_copy, packed = moved
    slabs = over_comp(packed)
    seas = [from_ocean(sea_copy, c) for c in range(ocean_comp)] + [sea_copy]
    blocks = regroup(slabs, neighbours, entry_total)
    blocks = [over_tiles(blocks[n], offsets[n], comp_count) for n in range(neighbours)]
    forcing, shared, hits = regrid(
        flags, ocean_map[:, 0], blocks, seas, regrid_weights, surface, mask
    )
    parts = [shared] + [shifted_comp(shared, s) for s in range(1, comp_count)]
    parts[1], forcing = lax.optimization_barrier((parts[1], forcing))
    picks = pick(parts, hits, neighbours)
    new_surface, picked = picks[0], picks[1:]
    arrived = [over_tiles(picked[n], -offsets[n], ocean_comp) for n in reversed(range(neighbours))]
    arrived = arrived[::-1]
    fields = [to_ocean(forcing, c) for c in range(ocean_comp)] + [forcing]
    final_state, token = update(flags, moved, fields, mask, ocean_map)
    weight_column = (packed_labels // rows)[:, None]
    surface_out = returned(
        flags, arrived, weight_column, sources[None, :], regrid_weights, mask, surface, new_surface,
        token,
    )
    return (final_state, surface_out)


def solution(mesh):
    placed = (
        P(("comp", "lat"), "lon", None),
        P(("comp", "lat"), "lon"),
        P(("comp", "lat"), "lon", None, None),
        P(),
        P(),
        P(),
        P(),
        P(),
    )
    return jax.shard_map(
        local,
        mesh=mesh,
        in_specs=placed,
        out_specs=(P(("comp", "lat"), "lon", None), P(("comp", "lat"), "lon")),
        check_vma=False,
    )
```
